32 devices in a mesh: fx: 8 (over z, x), wy: 4 (over y, core).
Axes of the slice: x: 2, y: 2, z: 4, core: 2. Of those that a mesh axis runs over, the one named last changes fastest.
Arguments:
- displacement: float32 [3, 16, 16, 128], P(None, 'fx', 'wy'), may hold values from -6 to 6
- velocity: float32 [3, 16, 16, 128], P(None, 'fx', 'wy'), may hold values from -3 to 3
- jitter: float32 [3, 16, 16, 128], P(None, 'fx', 'wy'), may hold values from -0.3 to 0.3
- bond_masks: int32 [16, 16, 9, 128, 128], P('fx', 'wy'), may hold values from 0 to 1, as said below
- pressure: float32 [128, 128, 128], P('fx', 'wy'), may hold values from -6 to 6
- pressure_prev: float32 [128, 128, 128], P('fx', 'wy'), may hold values from -6 to 6
- speed_sq: float32 [128, 128, 128], P('fx', 'wy'), may hold values from 0.03 to 0.3
- route_device: int32 [16384, 1], P(('fx', 'wy')), may hold values from 0 to 31; in each aligned block of 512 rows (0 to 511, 512 to 1023, ...) at most 64 rows name the same one
- route_tile: int32 [16384], P(('fx', 'wy')), may hold values from 0 to 7
Outputs:
- displacement_out: float32 [3, 16, 16, 128], P(None, 'fx', 'wy')
- velocity_out: float32 [3, 16, 16, 128], P(None, 'fx', 'wy')
- pressure_out: float32 [128, 128, 128], P('fx', 'wy')
The draws below stay inside these ranges and needn't reach their ends.
Inputs may be any that keep to these rules, and one draw needn't show every extreme that they name: `bond_masks`: 0 or 1. Bonds to a neighbour tile beyond the wall's edge are 0, and some neighbour tiles have all bonds 0. `route_device`: among the 512 rows of one device, no device is named more than 64 times, and one is named exactly 64 times.
All inputs are finite; a program needn't handle non-finite values.
Results may differ from the reference program's by a relative error of at most 0.0001.
Values sent between devices are 32-bit elements; how exact they have to be, the bound alone decides.
No kernel may reach another device: no remote copies, remote signals or barrier semaphores. Data moves between devices by JAX's collectives and lax.ppermute only.
A program may use at most 64 MiB of HBM per device.

```python
import math
import jax
import jax.numpy as jnp
import numpy as np
from jax import lax

PT = 128
TLD = 2
THD = 4
CXF = 16
CYF = 32
STEPS = 2
TL = 16
TH = 16
NXF = 128
NYF = 128
FACE_DEV = 512
FACE_ROWS = 16384
CAP = 64
TILES_DEV = 8
N_FX = 8
N_WY = 4
DEVICES = 32


def draw_bond_masks(key, part):
    key = jax.random.fold_in(key, 11)
    first, second, third = jax.random.split(key, 3)
    along = jnp.arange(TL, dtype=jnp.int32)[:, None, None]
    upward = jnp.arange(TH, dtype=jnp.int32)[None, :, None]
    slot = jnp.arange(9, dtype=jnp.int32)[None, None, :]
    reach_l = along + slot // 3 - 1
    reach_h = upward + slot % 3 - 1
    inside = (reach_l >= 0) & (reach_l < TL) & (reach_h >= 0) & (reach_h < TH)
    central = (along * 3 >= TL) & (along * 3 < 2 * TL)
    broken_odds = jnp.where(central, 60, 10)
    broken = jax.random.randint(first, (TL, TH, 9), 0, 100) < broken_odds
    keep_odds = jax.random.randint(second, (TL, TH, 9), 50, 100)
    bonds = jax.random.randint(third, (TL, TH, 9, PT, PT), 0, 100) < keep_odds[..., None, None]
    live = inside & jnp.logical_not(broken)
    return (bonds & live[..., None, None]).astype(jnp.int32)


def place_ends(result, key, smallest, largest):
    dims = result.shape
    index_at = [jax.random.randint(jax.random.fold_in(key, axis), (), 0, dims[axis]) for axis in range(len(dims))]
    result = result.at[tuple(index_at)].set(smallest)
    longest = dims.index(max(dims))
    index_at[longest] = (index_at[longest] + 1) % dims[longest]
    return result.at[tuple(index_at)].set(largest)


def block_scale(key, dims, cuts, low, high):
    gain = 1.0
    for position, blocks in cuts:
        heights = jax.random.uniform(jax.random.fold_in(jax.random.fold_in(key, 6), position), (blocks,), jnp.float32, low / len(cuts), high / len(cuts))
        gain = gain * jnp.repeat(jnp.exp(heights), dims[position] // blocks).reshape((-1,) + (1,) * (len(dims) - 1 - position))
    return gain


def assign_block(rng, own, number, rows, amount, top, reach, lean):
    ranking = jax.random.permutation(rng, amount)
    heavy_load, ordinary = load_shares(amount, rows * top, reach, lean, True), load_shares(amount, rows * top, reach, lean, False)
    places = jnp.arange(amount)

    def named(lengths, turn):
        used = int((lengths > 0).sum())
        fixed = max(1, used // 4)
        moved = fixed + (places - fixed + turn * (used - fixed)) % max(1, amount - fixed)
        return jnp.zeros((amount,), jnp.int32).at[ranking[jnp.where(places < fixed, places, moved)]].set(jnp.asarray(lengths, jnp.int32))

    lengths = jnp.where(number % 4 == 0, named(heavy_load, number // 4), named(ordinary, number - number // 4 - 1))
    mixed = jax.random.permutation(jax.random.fold_in(own, 3), amount)
    donor, taker = mixed[0:amount // 2 * 2:2], mixed[1:amount // 2 * 2:2]
    margin = jnp.minimum(lengths[donor] - 1, reach - lengths[taker]) // 2
    margin = jnp.where((donor == ranking[0]) | (taker == ranking[0]) | (lengths[taker] == 0), 0, jnp.maximum(margin, 0))
    moved = jax.random.randint(jax.random.fold_in(own, 4), (amount // 2,), 0, 1 << 20) % (margin + 1)
    lengths = lengths.at[donor].add(-moved).at[taker].add(moved)
    members = jnp.searchsorted(jnp.cumsum(lengths), jnp.arange(rows * top), side="right").astype(jnp.int32)
    table = members.reshape(top, rows).T
    table = table[jax.random.permutation(jax.random.fold_in(own, 1), rows)]
    turn = jax.random.randint(jax.random.fold_in(own, 2), (rows, 1), 0, top)
    return jnp.take_along_axis(table, (jnp.arange(top)[None, :] + turn) % top, axis=1)


def load_shares(count, total, most, skew, full):
    weights = [(1 << 20) // math.isqrt(standing ** skew) + 1 for standing in range(1, count + 1)]
    largest = most if full else min(most, max(-(-total // count), total * weights[0] // sum(weights)))
    least = 1 if total - largest >= count - 1 else 0
    holding, rest = [largest] + [least] * (count - 1), total - largest - least * (count - 1)
    while rest > 0:
        candidates = [i for i in range(1, count) if holding[i] < largest] or [i for i in range(1, count) if holding[i] < most]
        pool, budget = sum([weights[i] for i in candidates]), rest
        for i in candidates:
            addition = min(most - holding[i], max(1, budget * weights[i] // pool), rest)
            holding[i] = holding[i] + addition
            rest = rest - addition
    return np.array(holding)


def centred(key, extent, width, limit, cuts=(), kind=jnp.bfloat16):
    values = width * jax.random.normal(key, extent, jnp.float32)
    if cuts:
        values = values * block_scale(key, extent, cuts, -0.22, 0.18)
    return jnp.clip(values, -limit, limit).astype(kind)


def setup_inputs(seed: int = 0) -> dict:
    key_list = jax.random.split(jax.random.key(seed), 10)
    displacement = centred(key_list[0], (3, TL, TH, PT), 1.0, 6.0, ((1, 8), (2, 4)), jnp.float32)
    velocity = centred(key_list[1], (3, TL, TH, PT), 0.5, 3.0, ((1, 8), (2, 4)), jnp.float32)
    jitter = jnp.clip(jax.random.uniform(key_list[2], (3, TL, TH, PT), jnp.float32, -0.3, 0.3) * block_scale(key_list[2], (3, TL, TH, PT), ((1, 8), (2, 4)), -0.4, 0.0), -0.3, 0.3)
    bond_masks = draw_bond_masks(jax.random.fold_in(key_list[9], 71), 0)
    pressure = centred(key_list[4], (NXF, NYF, PT), 1.0, 6.0, ((0, 8), (1, 4)), jnp.float32)
    pressure_prev = centred(key_list[5], (NXF, NYF, PT), 1.0, 6.0, ((0, 8), (1, 4)), jnp.float32)
    speed_sq = jnp.clip(jnp.exp(math.log(0.3) - 2.3025852 * jax.random.uniform(key_list[6], (NXF, NYF, PT), jnp.float32) ** block_scale(key_list[6], (NXF, NYF, PT), ((0, 8), (1, 4)), -0.2, 0.2)), 0.03, 0.3)
    route_device_keys = jax.random.split(jax.random.fold_in(key_list[7], 1), FACE_ROWS // FACE_DEV)
    route_device_turns = jax.random.permutation(jax.random.fold_in(key_list[7], 3), FACE_ROWS // FACE_DEV)
    route_device = jax.vmap(lambda own, number: assign_block(jax.random.fold_in(key_list[7], 2), own, number, FACE_DEV, DEVICES, 1, CAP, 2))(route_device_keys, route_device_turns).reshape((FACE_ROWS, 1))
    route_tile = place_ends(jax.random.randint(key_list[8], (FACE_ROWS,), 0, TILES_DEV), jax.random.fold_in(key_list[8], 1), 0, TILES_DEV - 1).astype(jnp.int32)
    return {"displacement": displacement, "velocity": velocity, "jitter": jitter, "bond_masks": bond_masks, "pressure": pressure, "pressure_prev": pressure_prev, "speed_sq": speed_sq, "route_device": route_device, "route_tile": route_tile}


STIFFNESS = 0.02
LOADING = 0.05
REACH_SQ = 9.0


def lattice(count):
    index = jnp.arange(count, dtype=jnp.int32)
    return jnp.stack([index % 8, (index // 8) % 4, index // 32]).astype(jnp.float32)


def offsets():
    table = []
    for slot in range(9):
        table.append([8.0 * (slot // 3 - 1), 4.0 * (slot % 3 - 1), 0.0])
    return jnp.array(table, dtype=jnp.float32)


def neighbours(padded, rows, cols):
    pieces = []
    for slot in range(9):
        pieces.append(padded[:, slot // 3:slot // 3 + rows, slot % 3:slot % 3 + cols, :])
    return jnp.stack(pieces)


def bond_weights(jitter_pad, masks):
    rows, cols, count = masks.shape[0], masks.shape[1], masks.shape[3]
    base = lattice(count)
    own = base[:, None, None, :] + jitter_pad[:, 1:rows + 1, 1:cols + 1, :]
    other = base[None, :, None, None, :] + offsets()[:, :, None, None, None] + neighbours(jitter_pad, rows, cols)
    other = jnp.transpose(other, (1, 2, 3, 0, 4))
    dist_sq = jnp.zeros(masks.shape, jnp.float32)
    for comp in range(3):
        diff = other[comp][:, :, :, None, :] - own[comp][:, :, None, :, None]
        dist_sq = dist_sq + diff * diff
    return masks.astype(jnp.float32) * jnp.maximum(1.0 - dist_sq / REACH_SQ, 0.0)


def bond_forces(weights, disp_pad):
    rows, cols = weights.shape[0], weights.shape[1]
    own = disp_pad[:, 1:rows + 1, 1:cols + 1, :]
    other = neighbours(disp_pad, rows, cols)
    pulled = jnp.einsum('abkij,kcabj->cabi', weights, other, precision=lax.Precision.HIGHEST)
    totals = jnp.sum(weights, axis=(2, 4))
    return STIFFNESS * (pulled - totals[None] * own)


def fluid_step(padded, pressure, previous, speed_sq):
    beside = padded[2:, 1:-1, 1:-1] + padded[:-2, 1:-1, 1:-1]
    beside = beside + padded[1:-1, 2:, 1:-1] + padded[1:-1, :-2, 1:-1]
    beside = beside + padded[1:-1, 1:-1, 2:] + padded[1:-1, 1:-1, :-2]
    return 2.0 * pressure - previous + speed_sq * (beside - 6.0 * pressure)


def wall_forces(displacement, jitter, bond_masks):
    widths = ((0, 0), (1, 1), (1, 1), (0, 0))
    disp_pad = jnp.pad(displacement, widths)
    jitter_pad = jnp.pad(jitter, widths)

    def one_row(row):
        disp_slab = lax.dynamic_slice_in_dim(disp_pad, row, 3, 1)
        jitter_slab = lax.dynamic_slice_in_dim(jitter_pad, row, 3, 1)
        mask_slab = lax.dynamic_slice_in_dim(bond_masks, row, 1, 0)
        return bond_forces(bond_weights(jitter_slab, mask_slab), disp_slab)[:, 0]

    forces = lax.map(one_row, jnp.arange(TL, dtype=jnp.int32))
    return jnp.transpose(forces, (1, 0, 2, 3))


def face_loads(pressure, route_device, route_tile):
    columns = pressure.reshape(N_FX, CXF, N_WY, CYF, PT)
    columns = jnp.transpose(columns, (0, 2, 1, 3, 4)).reshape(N_FX * N_WY * CXF * CYF, PT)
    target = route_device[:, 0] * (TLD * THD) + route_tile
    sums = jax.ops.segment_sum(columns, target, num_segments=N_FX * N_WY * TLD * THD)
    sums = sums.reshape(N_FX, N_WY, TLD, THD, PT)
    return jnp.transpose(sums, (0, 2, 1, 3, 4)).reshape(TL, TH, PT)


def reference(displacement, velocity, jitter, bond_masks, pressure, pressure_prev, speed_sq, route_device, route_tile):
    for step in range(STEPS):
        fresh = fluid_step(jnp.pad(pressure, 1), pressure, pressure_prev, speed_sq)
        pressure_prev, pressure = pressure, fresh
        loads = face_loads(pressure, route_device, route_tile)
        forces = wall_forces(displacement, jitter, bond_masks)
        forces = forces.at[0].add(LOADING * loads)
        velocity = velocity + forces
        displacement = displacement + velocity
    return displacement, velocity, pressure
```

```python
import functools

import jax
import jax.numpy as jnp
from jax import lax
from jax.experimental import pallas as pl
from jax.experimental.pallas import tpu as pltpu
from jax.sharding import PartitionSpec as P

STIFFNESS = 0.02
LOADING = 0.05
REACH = 3.0
LANES = 128
SUB = 8
VMEM_BYTES = 48 * 1024 * 1024

F32 = jnp.float32
BF16 = jnp.bfloat16


def whole(ndim):
    return pl.BlockSpec(memory_space=pltpu.VMEM)


def params(*semantics):
    return pltpu.CompilerParams(vmem_limit_bytes=VMEM_BYTES)


def even_at(axis):
    return lax.rem(lax.axis_index(axis), 2) == 0


def pair_list(count, first):
    pairs = []
    for low in range(first, count - 1, 2):
        pairs.extend([(low, low + 1), (low + 1, low)])
    return pairs


def exchange(axis, to_even, to_odd):
    count = lax.axis_size(axis)
    got_even = lax.ppermute(to_even, axis, pair_list(count, 0))
    got_odd = lax.ppermute(to_odd, axis, pair_list(count, 1))
    return got_even, got_odd


def place_edges(even, low, high, to_even, to_odd):
    @pl.when(even)
    def _():
        high(to_even)
        low(to_odd)

    @pl.when(jnp.logical_not(even))
    def _():
        low(to_even)
        high(to_odd)


def before_after(even, got_even, got_odd):
    a, b = got_even[...], got_odd[...]
    return jnp.where(even, b, a), jnp.where(even, a, b)


def pack_wy_kernel(p_lo, p_hi, q_lo, q_hi, s_lo, s_hi, jit, disp, to_even, to_odd):
    cx = p_lo.shape[0]
    rows, cols = jit.shape[1], jit.shape[2]

    def edge(p, q, s, near, far, h):
        def write(out):
            out[0:cx, :] = p[:, near, :]
            out[cx : 2 * cx, :] = p[:, far, :]
            out[2 * cx : 3 * cx, :] = q[:, near, :]
            out[3 * cx : 4 * cx, :] = s[:, near, :]
            at = 4 * cx
            for field in (jit, disp):
                for c in range(3):
                    for l in range(rows):
                        out[at : at + 1, :] = field[c, l, h : h + 1, :]
                        at += 1
            for spare in range(at, out.shape[0]):
                out[spare : spare + 1, :] = jnp.zeros((1, LANES), F32)

        return write

    place_edges(
        even_at("wy"),
        edge(p_lo, q_lo, s_lo, 0, 1, 0),
        edge(p_hi, q_hi, s_hi, SUB - 1, SUB - 2, cols - 1),
        to_even,
        to_odd,
    )


def pad8(count):
    return (count + 7) // 8 * 8


def pack_wy(p, q, s, jit, disp):
    cx, cy = p.shape[0], p.shape[1]
    rows = jit.shape[1]
    size = pad8(4 * cx + 6 * rows)
    first = pl.BlockSpec((cx, SUB, LANES), lambda i: (0, 0, 0))
    last = pl.BlockSpec((cx, SUB, LANES), lambda i: (0, cy // SUB - 1, 0))
    small = pl.BlockSpec(jit.shape, lambda i: (0, 0, 0, 0))
    out = jax.ShapeDtypeStruct((size, LANES), F32)
    spec = pl.BlockSpec((size, LANES), lambda i: (0, 0))
    return pl.pallas_call(
        pack_wy_kernel,
        grid=(1,),
        in_specs=[first, last, first, last, first, last, small, small],
        out_specs=[spec, spec],
        out_shape=[out, out],
        compiler_params=params(),
        name="pack_wy",
    )(p, p, q, q, s, s, jit, disp)


def pack_fx_kernel(
    cx, p_lo, p_hi, q_lo, q_hi, s_lo, s_hi, jit, disp, got_even, got_odd, to_even, to_odd
):
    cy = p_lo.shape[1]
    rows, cols = jit.shape[1], jit.shape[2]
    before, after = before_after(even_at("wy"), got_even, got_odd)

    def edge(p, q, s, near, far, x, l):
        def write(out):
            out[0:cy, :] = p[near]
            out[cy : 2 * cy, :] = p[far]
            out[2 * cy : 3 * cy, :] = q[0]
            out[3 * cy : 4 * cy, :] = s[0]
            at = 4 * cy
            for f, field in enumerate((jit, disp)):
                for c in range(3):
                    side = 4 * cx + (f * 3 + c) * rows + l
                    out[at : at + 1, :] = before[side : side + 1]
                    out[at + 1 : at + 1 + cols, :] = field[c, l]
                    out[at + 1 + cols : at + 2 + cols, :] = after[side : side + 1]
                    at += cols + 2
            out[at : at + 1, :] = before[x : x + 1]
            out[at + 1 : at + 2, :] = after[x : x + 1]
            for spare in range(at + 2, out.shape[0]):
                out[spare : spare + 1, :] = jnp.zeros((1, LANES), F32)

        return write

    place_edges(
        even_at("fx"),
        edge(p_lo, q_lo, s_lo, 0, 1, 0, 0),
        edge(p_hi, q_hi, s_hi, 1, 0, cx - 1, rows - 1),
        to_even,
        to_odd,
    )


def pack_fx(p, q, s, jit, disp, got_even, got_odd):
    cx, cy = p.shape[0], p.shape[1]
    cols = jit.shape[2]
    size = pad8(4 * cy + 6 * (cols + 2) + 2)

    def at(depth, index):
        return pl.BlockSpec((depth, cy, LANES), lambda i: (index, 0, 0))

    small = pl.BlockSpec(jit.shape, lambda i: (0, 0, 0, 0))
    message = pl.BlockSpec(got_even.shape, lambda i: (0, 0))
    out = jax.ShapeDtypeStruct((size, LANES), F32)
    spec = pl.BlockSpec((size, LANES), lambda i: (0, 0))
    return pl.pallas_call(
        functools.partial(pack_fx_kernel, cx),
        grid=(1,),
        in_specs=[at(2, 0), at(2, cx // 2 - 1), at(1, 0), at(1, cx - 1), at(1, 0), at(1, cx - 1)]
        + [small, small, message, message],
        out_specs=[spec, spec],
        out_shape=[out, out],
        compiler_params=params(),
        name="pack_fx",
    )(p, p, q, q, s, s, jit, disp, got_even, got_odd)


def along_z(v):
    lane = lax.broadcasted_iota(jnp.int32, v.shape, 1)
    up = jnp.where(lane == LANES - 1, 0.0, pltpu.roll(v, LANES - 1, 1))
    down = jnp.where(lane == 0, 0.0, pltpu.roll(v, 1, 1))
    return up + down


def update(v, old, speed, beside):
    return 2.0 * v - old + speed * (beside + along_z(v) - 6.0 * v)


def two_terms(v):
    high = v.astype(BF16)
    return high, (v - high.astype(F32)).astype(BF16)


def grid_kernel(p, q, s, wye, wyo, fxe, fxo, target, out, slots, s0, s1, rhs, part1, part2):
    cx, cy = p.shape[0], p.shape[1]
    ahead, behind = SUB, SUB + cy
    fx_count = part1.shape[0] // 2 - 1
    cols = 4
    tall = part2.shape[0]
    high = part1.shape[1] - 2 * SUB
    wy_count = high // cols
    before_y, after_y = before_after(even_at("wy"), wye, wyo)
    before_x, after_x = before_after(even_at("fx"), fxe, fxo)
    corner = 4 * cy + 6 * (cols + 2)

    s0[1 : cx + 1, ahead:behind, :] = p[...]
    for x, side in ((0, before_x), (cx + 1, after_x)):
        s0[x, ahead:behind, :] = side[0:cy]
        s0[x, ahead - 1 : ahead, :] = side[corner : corner + 1]
        s0[x, behind : behind + 1, :] = side[corner + 1 : corner + 2]
    s0[1 : cx + 1, ahead - 1, :] = before_y[0:cx]
    s0[1 : cx + 1, behind, :] = after_y[0:cx]

    for side, y, inner in ((before_y, ahead - 1, ahead), (after_y, behind, behind - 1)):
        near, far = side[0:cx], side[cx : 2 * cx]
        old, speed = side[2 * cx : 3 * cx], side[3 * cx : 4 * cx]
        beside = s0[0:cx, y, :] + s0[2 : cx + 2, y, :] + far + s0[1 : cx + 1, inner, :]
        s1[1 : cx + 1, y, :] = update(near, old, speed, beside)
    for side, x, inner in ((before_x, 0, 1), (after_x, cx + 1, cx)):
        near, far = side[0:cy], side[cy : 2 * cy]
        old, speed = side[2 * cy : 3 * cy], side[3 * cy : 4 * cy]
        beside = s0[x, ahead - 1 : behind - 1, :] + s0[x, ahead + 1 : behind + 1, :]
        beside = beside + far + s0[inner, ahead:behind, :]
        s1[x, ahead:behind, :] = update(near, old, speed, beside)

    def sweep(now, old, x):
        beside = now[x, ahead:behind, :] + now[x + 2, ahead:behind, :]
        beside = beside + now[x + 1, ahead - 1 : behind - 1, :]
        beside = beside + now[x + 1, ahead + 1 : behind + 1, :]
        return update(now[x + 1, ahead:behind, :], old, s[x], beside)

    for x in range(cx):
        fresh = sweep(s0, q[x], x)
        s1[x + 1, ahead:behind, :] = fresh
        a, b = two_terms(fresh)
        rhs[x * cy : (x + 1) * cy, 0:LANES] = a
        rhs[x * cy : (x + 1) * cy, LANES : 2 * LANES] = b
    for x in range(cx):
        fresh = sweep(s1, p[x], x)
        out[x] = fresh
        a, b = two_terms(fresh)
        rhs[x * cy : (x + 1) * cy, 2 * LANES : 3 * LANES] = a
        rhs[x * cy : (x + 1) * cy, 3 * LANES : 4 * LANES] = b

    part1[...] = jnp.zeros(part1.shape, F32)
    part2[:, 0:SUB, :] = jnp.zeros((tall, SUB, LANES), F32)
    chunk = 256
    for first in range(0, tall * high, chunk):
        tile = lax.broadcasted_iota(jnp.int32, (chunk, LANES), 0) + first
        picks = []
        for piece in range(target.shape[0]):
            picks.append(jnp.where(tile == target[piece : piece + 1, :], 1.0, 0.0).astype(BF16))
        sums = jnp.dot(jnp.concatenate(picks, axis=1), rhs[...], preferred_element_type=F32)
        one = sums[:, 0:LANES] + sums[:, LANES : 2 * LANES]
        two = sums[:, 2 * LANES : 3 * LANES] + sums[:, 3 * LANES : 4 * LANES]
        l = first // high
        part1[1 + l : 1 + l + chunk // high, SUB : SUB + high, :] = one.reshape(-1, high, LANES)
        part2[l : l + chunk // high, SUB : SUB + high, :] = two.reshape(-1, high, LANES)
    lower = lax.broadcasted_iota(jnp.int32, (SUB, LANES), 0) < cols + 2
    for a in range(fx_count):
        for b in range(wy_count):
            for l in range(4):
                h = SUB + cols * b
                one = part1[2 * a + l, h - 1 : h - 1 + SUB, :]
                h = h + 2 * (l % 2) - 6
                two = part2[2 * a + l // 2, h : h + SUB, :]
                slots[a * wy_count + b, l * SUB : (l + 1) * SUB, :] = jnp.where(lower, one, two)


def grid_steps(p, q, s, wy_got, fx_got, target, fx_count, wy_count):
    cx, cy = p.shape[0], p.shape[1]
    tall, high = fx_count * 2, wy_count * 4
    devices = fx_count * wy_count
    return pl.pallas_call(
        grid_kernel,
        in_specs=[whole(0)] * 8,
        out_specs=[whole(0)] * 2,
        out_shape=[
            jax.ShapeDtypeStruct(p.shape, F32),
            jax.ShapeDtypeStruct((devices, 4 * SUB, LANES), F32),
        ],
        scratch_shapes=[
            pltpu.VMEM((cx + 2, cy + 2 * SUB, LANES), F32),
            pltpu.VMEM((cx + 2, cy + 2 * SUB, LANES), F32),
            pltpu.VMEM((cx * cy, 4 * LANES), BF16),
            pltpu.VMEM((tall + 2, high + 2 * SUB, LANES), F32),
            pltpu.VMEM((tall, high + 2 * SUB, LANES), F32),
        ],
        compiler_params=params(),
        name="grid_steps",
    )(p, q, s, *wy_got, *fx_got, target)


def reached(g):
    groups = []
    for dh in (-1, 0, 1):
        if (dh == -1 and g % 4 == 3) or (dh == 1 and g % 4 == 0):
            continue
        groups.append((False, dh))
        groups.append((True, dh))
    return groups


STORED = sum(len(reached(g)) for g in range(LANES // SUB))


def tile_rows(ref, c, l, h, first_sub):
    mid, ends = {}, {}
    for dh in (-1, 0, 1):
        at = h + 1 + dh
        mid[dh] = jnp.broadcast_to(ref[c, l + 1, pl.ds(at, 1), :], (SUB, LANES))
        before = jnp.broadcast_to(ref[c, l, pl.ds(at, 1), :], (SUB, LANES))
        after = jnp.broadcast_to(ref[c, l + 2, pl.ds(at, 1), :], (SUB, LANES))
        ends[dh] = jnp.where(first_sub, before, after)
    return mid, ends


def fill_padded(pad, own, before_y, after_y, before_x, after_x, at_y, at_x):
    rows, cols = own.shape[1], own.shape[2]
    for c in range(3):
        for l in range(rows):
            row = at_y + c * rows + l
            pad[c, l + 1, 0:1, :] = before_y[row : row + 1]
            pad[c, l + 1, 1 : cols + 1, :] = own[c, l]
            pad[c, l + 1, cols + 1 : cols + 2, :] = after_y[row : row + 1]
        row = at_x + c * (cols + 2)
        pad[c, 0, 0 : cols + 2, :] = before_x[row : row + cols + 2]
        pad[c, rows + 1, 0 : cols + 2, :] = after_x[row : row + cols + 2]


def lane_sums(acc, count):
    ones = jnp.ones((2 * SUB, LANES), BF16)
    result = []
    for c in range(count):
        high, low = two_terms(acc[c])
        both = jnp.concatenate([high, low], axis=0)
        sums = lax.dot_general(
            ones, both, (((1,), (1,)), ((), ())), preferred_element_type=F32
        )
        result.append(sums[0:1, 0:LANES] + sums[0:1, LANES : 2 * LANES])
    return result


def wall_kernel(
    cx, cy, masks, jit, disp, vel, wye, wyo, fxe, fxo, weights, vel1, base1, totals, to_even, to_odd,
    jpad, dpad, acc,
):
    rows, cols = jit.shape[1], jit.shape[2]
    l, h = pl.program_id(0), pl.program_id(1)
    first_sub = lax.broadcasted_iota(jnp.int32, (SUB, LANES), 0) < SUB // 2

    @pl.when((l == 0) & (h == 0))
    def _():
        before_y, after_y = before_after(even_at("wy"), wye, wyo)
        before_x, after_x = before_after(even_at("fx"), fxe, fxo)
        fill_padded(jpad, jit, before_y, after_y, before_x, after_x, 4 * cx, 4 * cy)
        fill_padded(
            dpad, disp, before_y, after_y, before_x, after_x,
            4 * cx + 3 * rows, 4 * cy + 3 * (cols + 2),
        )

    index = lax.broadcasted_iota(jnp.int32, (1, LANES), 1)
    lattice = (index % 8, index // 8 % 4, index // 32)
    lattice = [v.astype(F32) * (1.0 / REACH) for v in lattice]
    span = 8.0 / REACH
    rise = 4.0 / REACH
    others, own = [], []
    for c in range(3):
        mid, ends = tile_rows(jpad, c, l, h, first_sub)
        for dh in (-1, 0, 1):
            mid[dh] = mid[dh] * (1.0 / REACH) + lattice[c]
            ends[dh] = ends[dh] * (1.0 / REACH) + lattice[c]
            if c == 0:
                ends[dh] = ends[dh] + jnp.where(first_sub, -span, span)
            if c == 1:
                mid[dh] = mid[dh] + rise * dh
                ends[dh] = ends[dh] + rise * dh
        own.append(mid[0])
        others.append((mid, ends))
    pulls = [tile_rows(dpad, c, l, h, first_sub) for c in range(3)]
    columns = jnp.transpose(
        jnp.concatenate([own[0], own[1], own[2]], axis=0)
    )

    place = 0
    for g in range(LANES // SUB):
        mine = [
            jnp.broadcast_to(columns[g * SUB : (g + 1) * SUB, c * SUB : c * SUB + 1], (SUB, LANES))
            for c in range(3)
        ]
        sums = [jnp.zeros((SUB, LANES), F32) for _ in range(4)]
        span_g = slice(g * SUB, (g + 1) * SUB)
        for ends, dh in reached(g):
            if ends:
                mask = jnp.where(first_sub, masks[0, 0, 1 + dh, span_g, :], masks[0, 0, 7 + dh, span_g, :])
            else:
                mask = masks[0, 0, 4 + dh, span_g, :]
            weight = mask.astype(F32)
            for c in range(3):
                diff = others[c][ends][dh] - mine[c]
                weight = weight - diff * diff
            weight = jnp.maximum(weight, 0.0)
            weights[0, 0, place] = weight
            place += 1
            for c in range(3):
                sums[c] = sums[c] + weight * pulls[c][ends][dh]
            sums[3] = sums[3] + weight
        for c in range(4):
            acc[c, span_g, :] = sums[c]
    pulled = lane_sums(acc, 4)
    totals[l, pl.ds(h, 1), :] = pulled[3]
    for c in range(3):
        mine = dpad[c, l + 1, pl.ds(h + 1, 1), :]
        force = STIFFNESS * (pulled[c] - pulled[3] * mine)
        fresh = vel[c, l, pl.ds(h, 1), :] + force
        vel1[c, l, pl.ds(h, 1), :] = fresh
        base1[c, l, pl.ds(h, 1), :] = mine + fresh

    @pl.when((l == rows - 1) & (h == cols - 1))
    def _():
        def edge(at):
            def write(out):
                for c in range(3):
                    for k in range(rows):
                        out[c * rows + k : c * rows + k + 1, :] = base1[c, k, at : at + 1, :]
                for spare in range(3 * rows, out.shape[0]):
                    out[spare : spare + 1, :] = jnp.zeros((1, LANES), F32)

            return write

        place_edges(even_at("wy"), edge(0), edge(cols - 1), to_even, to_odd)


def wall_first(cx, cy, masks, jit, disp, vel, wy_got, fx_got):
    rows, cols = jit.shape[1], jit.shape[2]
    field = pl.BlockSpec(jit.shape, lambda l, h: (0, 0, 0, 0))
    wy_spec = pl.BlockSpec(wy_got[0].shape, lambda l, h: (0, 0))
    fx_spec = pl.BlockSpec(fx_got[0].shape, lambda l, h: (0, 0))
    edge = (pad8(3 * rows), LANES)
    edge_spec = pl.BlockSpec(edge, lambda l, h: (0, 0))
    return pl.pallas_call(
        functools.partial(wall_kernel, cx, cy),
        grid=(rows, cols),
        in_specs=[
            pl.BlockSpec((1, 1, 9, LANES, LANES), lambda l, h: (l, h, 0, 0, 0)),
            field, field, field, wy_spec, wy_spec, fx_spec, fx_spec,
        ],
        out_specs=[
            pl.BlockSpec((1, 1, STORED, SUB, LANES), lambda l, h: (l, h, 0, 0, 0)),
            field, field,
            pl.BlockSpec((rows, cols, LANES), lambda l, h: (0, 0, 0)),
            edge_spec, edge_spec,
        ],
        out_shape=[
            jax.ShapeDtypeStruct((rows, cols, STORED, SUB, LANES), F32),
            jax.ShapeDtypeStruct(jit.shape, F32),
            jax.ShapeDtypeStruct(jit.shape, F32),
            jax.ShapeDtypeStruct((rows, cols, LANES), F32),
            jax.ShapeDtypeStruct(edge, F32),
            jax.ShapeDtypeStruct(edge, F32),
        ],
        scratch_shapes=[
            pltpu.VMEM((3, rows + 2, SUB, LANES), F32),
            pltpu.VMEM((3, rows + 2, SUB, LANES), F32),
            pltpu.VMEM((4, LANES, LANES), F32),
        ],
        compiler_params=params(),
        name="wall_first",
    )(masks, jit, disp, vel, *wy_got, *fx_got)


def pack_base_kernel(base1, got_even, got_odd, to_even, to_odd):
    rows, cols = base1.shape[1], base1.shape[2]
    before, after = before_after(even_at("wy"), got_even, got_odd)

    def edge(l):
        def write(out):
            at = 0
            for c in range(3):
                side = c * rows + l
                out[at : at + 1, :] = before[side : side + 1]
                out[at + 1 : at + 1 + cols, :] = base1[c, l]
                out[at + 1 + cols : at + 2 + cols, :] = after[side : side + 1]
                at += cols + 2
            for spare in range(at, out.shape[0]):
                out[spare : spare + 1, :] = jnp.zeros((1, LANES), F32)

        return write

    place_edges(even_at("fx"), edge(0), edge(rows - 1), to_even, to_odd)


def pack_base(base1, got):
    cols = base1.shape[2]
    out = jax.ShapeDtypeStruct((pad8(3 * (cols + 2)), LANES), F32)
    return pl.pallas_call(
        pack_base_kernel,
        in_specs=[whole(0)] * 3,
        out_specs=[whole(0)] * 2,
        out_shape=[out, out],
        compiler_params=params(),
        name="pack_base",
    )(base1, *got)


def last_kernel(
    weights, got, base1, vel1, totals, wye, wyo, fxe, fxo, disp_out, vel_out, dpad, loads, acc
):
    rows, cols = base1.shape[1], base1.shape[2]
    l, h = pl.program_id(0), pl.program_id(1)
    first_sub = lax.broadcasted_iota(jnp.int32, (SUB, LANES), 0) < SUB // 2

    @pl.when((l == 0) & (h == 0))
    def _():
        before_y, after_y = before_after(even_at("wy"), wye, wyo)
        before_x, after_x = before_after(even_at("fx"), fxe, fxo)
        fill_padded(dpad, base1, before_y, after_y, before_x, after_x, 0, 0)
        total = got[0]
        for d in range(1, got.shape[0]):
            total = total + got[d]
        loads[...] = total
        for k in range(rows + 2):
            here = total[k * SUB : k * SUB + cols + 2, :]
            dpad[0, k, 0 : cols + 2, :] = dpad[0, k, 0 : cols + 2, :] + LOADING * here

    pulls = [tile_rows(dpad, c, l, h, first_sub) for c in range(3)]
    place = 0
    for g in range(LANES // SUB):
        sums = [jnp.zeros((SUB, LANES), F32) for _ in range(3)]
        for ends, dh in reached(g):
            weight = weights[0, 0, place]
            place += 1
            for c in range(3):
                sums[c] = sums[c] + weight * pulls[c][ends][dh]
        for c in range(3):
            acc[c, g * SUB : (g + 1) * SUB, :] = sums[c]
    pulled = lane_sums(acc, 3)
    for c in range(3):
        mine = dpad[c, l + 1, pl.ds(h + 1, 1), :]
        force = STIFFNESS * (pulled[c] - totals[l, pl.ds(h, 1), :] * mine)
        if c == 0:
            one = loads[pl.ds((l + 1) * SUB + h + 1, 1), :]
            two = loads[pl.ds((2 * l + h // 2) * SUB + cols + 2 + h % 2, 1), :]
            force = force + LOADING * (one + two)
        fresh = vel1[c, l, pl.ds(h, 1), :] + force
        vel_out[c, l, pl.ds(h, 1), :] = fresh
        disp_out[c, l, pl.ds(h, 1), :] = mine + fresh


def wall_last(weights, got, base1, vel1, totals, wy_got, fx_got):
    rows, cols = base1.shape[1], base1.shape[2]
    field = pl.BlockSpec(base1.shape, lambda l, h: (0, 0, 0, 0))

    def flat(v):
        return pl.BlockSpec(v.shape, lambda l, h: (0,) * v.ndim)

    return pl.pallas_call(
        last_kernel,
        grid=(rows, cols),
        in_specs=[
            pl.BlockSpec((1, 1, STORED, SUB, LANES), lambda l, h: (l, h, 0, 0, 0)),
            flat(got), field, field, flat(totals),
            flat(wy_got[0]), flat(wy_got[1]), flat(fx_got[0]), flat(fx_got[1]),
        ],
        out_specs=[field, field],
        out_shape=[jax.ShapeDtypeStruct(base1.shape, F32)] * 2,
        scratch_shapes=[
            pltpu.VMEM((3, rows + 2, SUB, LANES), F32),
            pltpu.VMEM((4 * SUB, LANES), F32),
            pltpu.VMEM((3, LANES, LANES), F32),
        ],
        compiler_params=params(),
        name="wall_last",
    )(weights, got, base1, vel1, totals, *wy_got, *fx_got)


def per_device(
    displacement,
    velocity,
    jitter,
    bond_masks,
    pressure,
    pressure_prev,
    speed_sq,
    route_device,
    route_tile,
):
    fx_count, wy_count = lax.axis_size("fx"), lax.axis_size("wy")
    cols = displacement.shape[2]
    device = route_device.reshape(-1, LANES)
    tile = route_tile.reshape(-1, LANES)
    length = (device // wy_count) * 2 + tile // cols
    height = (device % wy_count) * cols + tile % cols
    target = length * (wy_count * cols) + height

    sends = pack_wy(pressure, pressure_prev, speed_sq, jitter, displacement)
    wy_got = exchange("wy", *sends)
    sends = pack_fx(pressure, pressure_prev, speed_sq, jitter, displacement, *wy_got)
    fx_got = exchange("fx", *sends)
    pressure_out, slots = grid_steps(
        pressure, pressure_prev, speed_sq, wy_got, fx_got, target, fx_count, wy_count
    )
    got = lax.all_to_all(slots, ("fx", "wy"), split_axis=0, concat_axis=0, tiled=True)
    weights, vel1, base1, totals, *sends = wall_first(
        pressure.shape[0], pressure.shape[1],
        bond_masks, jitter, displacement, velocity, wy_got, fx_got
    )
    base_wy = exchange("wy", *sends)
    sends = pack_base(base1, base_wy)
    base_fx = exchange("fx", *sends)
    disp_out, vel_out = wall_last(weights, got, base1, vel1, totals, base_wy, base_fx)
    return (disp_out, vel_out, pressure_out)


def solution(mesh):
    placed = (
        P(None, "fx", "wy", None),
        P(None, "fx", "wy", None),
        P(None, "fx", "wy", None),
        P("fx", "wy", None, None, None),
        P("fx", "wy", None),
        P("fx", "wy", None),
        P("fx", "wy", None),
        P(("fx", "wy"), None),
        P(("fx", "wy")),
    )
    return jax.shard_map(
        per_device,
        mesh=mesh,
        in_specs=placed,
        out_specs=(P(None, "fx", "wy", None), P(None, "fx", "wy", None), P("fx", "wy", None)),
        check_vma=False,
    )
```

```python
import functools

import jax
import jax.numpy as jnp
from jax import lax
from jax.experimental import pallas as pl
from jax.experimental.pallas import tpu as pltpu
from jax.sharding import PartitionSpec as P

STIFFNESS = 0.02
LOADING = 0.05
REACH = 3.0
LANES = 128
SUB = 8
VMEM_BYTES = 48 * 1024 * 1024

F32 = jnp.float32
BF16 = jnp.bfloat16


def whole():
    return pl.BlockSpec(memory_space=pltpu.VMEM)


def params():
    return pltpu.CompilerParams(vmem_limit_bytes=VMEM_BYTES)


def even_at(axis):
    return lax.rem(lax.axis_index(axis), 2) == 0


def pair_list(count, first):
    pairs = []
    for low in range(first, count - 1, 2):
        pairs.extend([(low, low + 1), (low + 1, low)])
    return pairs


def exchange(axis, to_even, to_odd):
    count = lax.axis_size(axis)
    got_odd = lax.ppermute(to_odd, axis, pair_list(count, 1))
    got_even = lax.ppermute(to_even, axis, pair_list(count, 0))
    return got_even, got_odd


def place_edges(even, low, high, to_even, to_odd):
    @pl.when(even)
    def _():
        high(to_even)
        low(to_odd)

    @pl.when(jnp.logical_not(even))
    def _():
        low(to_even)
        high(to_odd)


def before_after(even, got_even, got_odd):
    a, b = got_even[...], got_odd[...]
    return jnp.where(even, b, a), jnp.where(even, a, b)


def pack_wy_kernel(p, q, s, jit_in, disp_in, to_even, to_odd, edges, walls, sems):
    cx, cy = p.shape[0], p.shape[1]
    rows, cols = jit_in.shape[1], jit_in.shape[2]
    copies = []
    for k, field in enumerate((p, q, s)):
        for side, first in enumerate((0, cy - SUB)):
            source = field.at[:, first : first + SUB, :]
            copies.append((source, edges.at[2 * k + side], sems.at[2 * k + side]))
    copies.append((jit_in, walls.at[0], sems.at[6]))
    copies.append((disp_in, walls.at[1], sems.at[7]))
    copies = [pltpu.make_async_copy(*copy) for copy in copies]
    for copy in copies:
        copy.start()
    for copy in copies:
        copy.wait()
    p_lo, p_hi, q_lo, q_hi, s_lo, s_hi = [edges.at[k] for k in range(6)]
    jit, disp = walls.at[0], walls.at[1]

    def edge(p, q, s, near, far, h):
        def write(out):
            out[0:cx, :] = p[:, near, :]
            out[cx : 2 * cx, :] = p[:, far, :]
            out[2 * cx : 3 * cx, :] = q[:, near, :]
            out[3 * cx : 4 * cx, :] = s[:, near, :]
            at = 4 * cx
            for field in (jit, disp):
                for c in range(3):
                    for l in range(rows):
                        out[at : at + 1, :] = field[c, l, h : h + 1, :]
                        at += 1
            for spare in range(at, out.shape[0]):
                out[spare : spare + 1, :] = jnp.zeros((1, LANES), F32)

        return write

    place_edges(
        even_at("wy"),
        edge(p_lo, q_lo, s_lo, 0, 1, 0),
        edge(p_hi, q_hi, s_hi, SUB - 1, SUB - 2, cols - 1),
        to_even,
        to_odd,
    )


def pad8(count):
    return (count + 7) // 8 * 8


def pack_wy(p, q, s, jit, disp):
    cx = p.shape[0]
    rows = jit.shape[1]
    size = pad8(4 * cx + 6 * rows)
    out = jax.ShapeDtypeStruct((size, LANES), F32)
    return pl.pallas_call(
        pack_wy_kernel,
        in_specs=[pl.BlockSpec(memory_space=pltpu.HBM)] * 5,
        out_specs=[whole()] * 2,
        out_shape=[out, out],
        scratch_shapes=[
            pltpu.VMEM((6, cx, SUB, LANES), F32),
            pltpu.VMEM((2,) + jit.shape, F32),
            pltpu.SemaphoreType.DMA((8,)),
        ],
        compiler_params=params(),
        name="pack_wy",
    )(p, q, s, jit, disp)


def pack_fx_kernel(
    cx, p_lo, p_hi, q_lo, q_hi, s_lo, s_hi, jit, disp, got_even, got_odd, to_even, to_odd
):
    cy = p_lo.shape[1]
    rows, cols = jit.shape[1], jit.shape[2]
    before, after = before_after(even_at("wy"), got_even, got_odd)

    def edge(p, q, s, near, far, x, l):
        def write(out):
            out[0:cy, :] = p[near]
            out[cy : 2 * cy, :] = p[far]
            out[2 * cy : 3 * cy, :] = q[0]
            out[3 * cy : 4 * cy, :] = s[0]
            at = 4 * cy
            for f, field in enumerate((jit, disp)):
                for c in range(3):
                    side = 4 * cx + (f * 3 + c) * rows + l
                    out[at : at + 1, :] = before[side : side + 1]
                    out[at + 1 : at + 1 + cols, :] = field[c, l]
                    out[at + 1 + cols : at + 2 + cols, :] = after[side : side + 1]
                    at += cols + 2
            out[at : at + 1, :] = before[x : x + 1]
            out[at + 1 : at + 2, :] = after[x : x + 1]
            for spare in range(at + 2, out.shape[0]):
                out[spare : spare + 1, :] = jnp.zeros((1, LANES), F32)

        return write

    place_edges(
        even_at("fx"),
        edge(p_lo, q_lo, s_lo, 0, 1, 0, 0),
        edge(p_hi, q_hi, s_hi, 1, 0, cx - 1, rows - 1),
        to_even,
        to_odd,
    )


def pack_fx(p, q, s, jit, disp, got_even, got_odd):
    cx, cy = p.shape[0], p.shape[1]
    cols = jit.shape[2]
    size = pad8(4 * cy + 6 * (cols + 2) + 2)

    def at(depth, index):
        return pl.BlockSpec((depth, cy, LANES), lambda i: (index, 0, 0))

    small = pl.BlockSpec(jit.shape, lambda i: (0, 0, 0, 0))
    message = pl.BlockSpec(got_even.shape, lambda i: (0, 0))
    out = jax.ShapeDtypeStruct((size, LANES), F32)
    spec = pl.BlockSpec((size, LANES), lambda i: (0, 0))
    return pl.pallas_call(
        functools.partial(pack_fx_kernel, cx),
        grid=(1,),
        in_specs=[at(2, 0), at(2, cx // 2 - 1), at(1, 0), at(1, cx - 1), at(1, 0), at(1, cx - 1)]
        + [small, small, message, message],
        out_specs=[spec, spec],
        out_shape=[out, out],
        compiler_params=params(),
        name="pack_fx",
    )(p, p, q, q, s, s, jit, disp, got_even, got_odd)


def along_z(v):
    lane = lax.broadcasted_iota(jnp.int32, v.shape, 1)
    up = jnp.where(lane == LANES - 1, 0.0, pltpu.roll(v, LANES - 1, 1))
    down = jnp.where(lane == 0, 0.0, pltpu.roll(v, 1, 1))
    return up + down


def update(v, old, speed, beside):
    return 2.0 * v - old + speed * (beside + along_z(v) - 6.0 * v)


def two_terms(v):
    high = v.astype(BF16)
    return high, (v - high.astype(F32)).astype(BF16)


def grid_kernel(p, q, s, wye, wyo, fxe, fxo, target, out, slots, s0, s1, rhs, part1, part2):
    cx, cy = p.shape[0], p.shape[1]
    ahead, behind = SUB, SUB + cy
    fx_count = part1.shape[0] // 2 - 1
    cols = 4
    tall = part2.shape[0]
    high = part1.shape[1] - 2 * SUB
    wy_count = high // cols
    before_y, after_y = before_after(even_at("wy"), wye, wyo)
    before_x, after_x = before_after(even_at("fx"), fxe, fxo)
    corner = 4 * cy + 6 * (cols + 2)

    s0[1 : cx + 1, ahead:behind, :] = p[...]
    for x, side in ((0, before_x), (cx + 1, after_x)):
        s0[x, ahead:behind, :] = side[0:cy]
        s0[x, ahead - 1 : ahead, :] = side[corner : corner + 1]
        s0[x, behind : behind + 1, :] = side[corner + 1 : corner + 2]
    s0[1 : cx + 1, ahead - 1, :] = before_y[0:cx]
    s0[1 : cx + 1, behind, :] = after_y[0:cx]

    for side, y, inner in ((before_y, ahead - 1, ahead), (after_y, behind, behind - 1)):
        near, far = side[0:cx], side[cx : 2 * cx]
        old, speed = side[2 * cx : 3 * cx], side[3 * cx : 4 * cx]
        beside = s0[0:cx, y, :] + s0[2 : cx + 2, y, :] + far + s0[1 : cx + 1, inner, :]
        s1[1 : cx + 1, y, :] = update(near, old, speed, beside)
    for side, x, inner in ((before_x, 0, 1), (after_x, cx + 1, cx)):
        near, far = side[0:cy], side[cy : 2 * cy]
        old, speed = side[2 * cy : 3 * cy], side[3 * cy : 4 * cy]
        beside = s0[x, ahead - 1 : behind - 1, :] + s0[x, ahead + 1 : behind + 1, :]
        beside = beside + far + s0[inner, ahead:behind, :]
        s1[x, ahead:behind, :] = update(near, old, speed, beside)

    def sweep(now, old, x):
        beside = now[x, ahead:behind, :] + now[x + 2, ahead:behind, :]
        beside = beside + now[x + 1, ahead - 1 : behind - 1, :]
        beside = beside + now[x + 1, ahead + 1 : behind + 1, :]
        return update(now[x + 1, ahead:behind, :], old, s[x], beside)

    for x in range(cx):
        fresh = sweep(s0, q[x], x)
        s1[x + 1, ahead:behind, :] = fresh
        a, b = two_terms(fresh)
        rhs[x * cy : (x + 1) * cy, 0:LANES] = a
        rhs[x * cy : (x + 1) * cy, LANES : 2 * LANES] = b
    for x in range(cx):
        fresh = sweep(s1, p[x], x)
        out[x] = fresh
        a, b = two_terms(fresh)
        rhs[x * cy : (x + 1) * cy, 2 * LANES : 3 * LANES] = a
        rhs[x * cy : (x + 1) * cy, 3 * LANES : 4 * LANES] = b

    part1[...] = jnp.zeros(part1.shape, F32)
    part2[:, 0:SUB, :] = jnp.zeros((tall, SUB, LANES), F32)
    chunk = 256
    for first in range(0, tall * high, chunk):
        tile = lax.broadcasted_iota(jnp.int32, (chunk, LANES), 0) + first
        picks = []
        for piece in range(target.shape[0]):
            picks.append(jnp.where(tile == target[piece : piece + 1, :], 1.0, 0.0).astype(BF16))
        sums = jnp.dot(jnp.concatenate(picks, axis=1), rhs[...], preferred_element_type=F32)
        one = sums[:, 0:LANES] + sums[:, LANES : 2 * LANES]
        two = sums[:, 2 * LANES : 3 * LANES] + sums[:, 3 * LANES : 4 * LANES]
        l = first // high
        part1[1 + l : 1 + l + chunk // high, SUB : SUB + high, :] = one.reshape(-1, high, LANES)
        part2[l : l + chunk // high, SUB : SUB + high, :] = two.reshape(-1, high, LANES)
    lower = lax.broadcasted_iota(jnp.int32, (SUB, LANES), 0) < cols + 2
    for a in range(fx_count):
        for b in range(wy_count):
            for l in range(4):
                h = SUB + cols * b
                one = part1[2 * a + l, h - 1 : h - 1 + SUB, :]
                h = h + 2 * (l % 2) - 6
                two = part2[2 * a + l // 2, h : h + SUB, :]
                slots[a * wy_count + b, l * SUB : (l + 1) * SUB, :] = jnp.where(lower, one, two)


def grid_steps(p, q, s, wy_got, fx_got, target, fx_count, wy_count):
    cx, cy = p.shape[0], p.shape[1]
    tall, high = fx_count * 2, wy_count * 4
    devices = fx_count * wy_count
    return pl.pallas_call(
        grid_kernel,
        in_specs=[whole()] * 8,
        out_specs=[whole()] * 2,
        out_shape=[
            jax.ShapeDtypeStruct(p.shape, F32),
            jax.ShapeDtypeStruct((devices, 4 * SUB, LANES), F32),
        ],
        scratch_shapes=[
            pltpu.VMEM((cx + 2, cy + 2 * SUB, LANES), F32),
            pltpu.VMEM((cx + 2, cy + 2 * SUB, LANES), F32),
            pltpu.VMEM((cx * cy, 4 * LANES), BF16),
            pltpu.VMEM((tall + 2, high + 2 * SUB, LANES), F32),
            pltpu.VMEM((tall, high + 2 * SUB, LANES), F32),
        ],
        compiler_params=params(),
        name="grid_steps",
    )(p, q, s, *wy_got, *fx_got, target)


def reached(g):
    groups = []
    for dh in (-1, 0, 1):
        if (dh == -1 and g % 4 == 3) or (dh == 1 and g % 4 == 0):
            continue
        groups.append((False, dh))
        groups.append((True, dh))
    return groups


STORED = sum(len(reached(g)) for g in range(LANES // SUB))


def tile_rows(ref, c, l, h, first_sub):
    mid, ends = {}, {}
    for dh in (-1, 0, 1):
        at = pl.ds(h + 1 + dh, 1)
        mid[dh] = jnp.broadcast_to(ref[c, l + 1, at, :], (SUB, LANES))
        before = jnp.broadcast_to(ref[c, l, at, :], (SUB, LANES))
        after = jnp.broadcast_to(ref[c, l + 2, at, :], (SUB, LANES))
        ends[dh] = jnp.where(first_sub, before, after)
    return mid, ends


def fill_padded(pad, own, before_y, after_y, before_x, after_x, at_y, at_x):
    rows, cols = own.shape[1], own.shape[2]
    for c in range(3):
        for l in range(rows):
            row = at_y + c * rows + l
            pad[c, l + 1, 0:1, :] = before_y[row : row + 1]
            pad[c, l + 1, 1 : cols + 1, :] = own[c, l]
            pad[c, l + 1, cols + 1 : cols + 2, :] = after_y[row : row + 1]
        row = at_x + c * (cols + 2)
        pad[c, 0, 0 : cols + 2, :] = before_x[row : row + cols + 2]
        pad[c, rows + 1, 0 : cols + 2, :] = after_x[row : row + cols + 2]


def lane_sums(acc, l, cols, count):
    ones = jnp.ones((2 * SUB, LANES), BF16)
    result = [[] for _ in range(count)]
    for h in range(cols):
        terms = []
        for c in range(count):
            terms.extend(two_terms(acc[l, h, c]))
        sums = lax.dot_general(
            ones,
            jnp.concatenate(terms, axis=0),
            (((1,), (1,)), ((), ())),
            preferred_element_type=F32,
        )[0:1]
        for c in range(count):
            at = 2 * c * LANES
            result[c].append(sums[:, at : at + LANES] + sums[:, at + LANES : at + 2 * LANES])
    return [jnp.concatenate(parts, axis=0) for parts in result]


def wall_kernel(
    cx, cy, masks, jit, disp, vel, wye, wyo, fxe, fxo, weights, vel1, base1, totals, to_even, to_odd,
    jpad, dpad, acc,
):
    rows, cols = jit.shape[1], jit.shape[2]
    first_sub = lax.broadcasted_iota(jnp.int32, (SUB, LANES), 0) < SUB // 2
    before_y, after_y = before_after(even_at("wy"), wye, wyo)
    before_x, after_x = before_after(even_at("fx"), fxe, fxo)
    fill_padded(jpad, jit, before_y, after_y, before_x, after_x, 4 * cx, 4 * cy)
    fill_padded(
        dpad, disp, before_y, after_y, before_x, after_x,
        4 * cx + 3 * rows, 4 * cy + 3 * (cols + 2),
    )
    index = lax.broadcasted_iota(jnp.int32, (1, LANES), 1)
    lattice = (index % 8, index // 8 % 4, index // 32)
    lattice = [v.astype(F32) * (1.0 / REACH) for v in lattice]
    span = 8.0 / REACH
    rise = 4.0 / REACH

    def one_tile(l, h):
        others, own = [], []
        for c in range(3):
            mid, ends = tile_rows(jpad, c, l, h, first_sub)
            for dh in (-1, 0, 1):
                mid[dh] = mid[dh] * (1.0 / REACH) + lattice[c]
                ends[dh] = ends[dh] * (1.0 / REACH) + lattice[c]
                if c == 0:
                    ends[dh] = ends[dh] + jnp.where(first_sub, -span, span)
                if c == 1:
                    mid[dh] = mid[dh] + rise * dh
                    ends[dh] = ends[dh] + rise * dh
            own.append(mid[0])
            others.append((mid, ends))
        pulls = [tile_rows(dpad, c, l, h, first_sub) for c in range(3)]
        sub = lax.broadcasted_iota(jnp.int32, (SUB, LANES), 0)
        columns = jnp.transpose(
            jnp.where(sub == 0, own[0], jnp.where(sub == 1, own[1], own[2]))
        )
        place = 0
        for g in range(LANES // SUB):
            span_g = slice(g * SUB, (g + 1) * SUB)
            mine = [
                jnp.broadcast_to(columns[span_g, c : c + 1], (SUB, LANES)) for c in range(3)
            ]
            sums = [None] * 4
            for ends, dh in reached(g):
                if ends:
                    mask = jnp.where(
                        first_sub,
                        masks[l, h, 1 + dh, span_g, :],
                        masks[l, h, 7 + dh, span_g, :],
                    )
                else:
                    mask = masks[l, h, 4 + dh, span_g, :]
                weight = mask.astype(F32)
                for c in range(3):
                    diff = others[c][ends][dh] - mine[c]
                    weight = weight - diff * diff
                weight = jnp.maximum(weight, 0.0)
                weights[l, h, place] = weight
                place += 1
                terms = [weight * pulls[c][ends][dh] for c in range(3)] + [weight]
                sums = [t if v is None else v + t for v, t in zip(sums, terms)]
            for c in range(4):
                acc[l, h, c, span_g, :] = sums[c]

    @pl.loop(0, cols)
    def _(h):
        for l in range(rows):
            one_tile(l, h)

    for l in range(rows):
        pulled = lane_sums(acc, l, cols, 4)
        totals[l] = pulled[3]
        for c in range(3):
            mine = disp[c, l]
            fresh = vel[c, l] + STIFFNESS * (pulled[c] - pulled[3] * mine)
            vel1[c, l] = fresh
            base1[c, l] = mine + fresh

    def edge(at):
        def write(out):
            for c in range(3):
                for k in range(rows):
                    out[c * rows + k : c * rows + k + 1, :] = base1[c, k, at : at + 1, :]
            for spare in range(3 * rows, out.shape[0]):
                out[spare : spare + 1, :] = jnp.zeros((1, LANES), F32)

        return write

    place_edges(even_at("wy"), edge(0), edge(cols - 1), to_even, to_odd)


def wall_first(cx, cy, masks, jit, disp, vel, wy_got, fx_got):
    rows, cols = jit.shape[1], jit.shape[2]
    edge = (pad8(3 * rows), LANES)
    return pl.pallas_call(
        functools.partial(wall_kernel, cx, cy),
        in_specs=[whole()] * 8,
        out_specs=[whole()] * 6,
        out_shape=[
            jax.ShapeDtypeStruct((rows, cols, STORED, SUB, LANES), F32),
            jax.ShapeDtypeStruct(jit.shape, F32),
            jax.ShapeDtypeStruct(jit.shape, F32),
            jax.ShapeDtypeStruct((rows, cols, LANES), F32),
            jax.ShapeDtypeStruct(edge, F32),
            jax.ShapeDtypeStruct(edge, F32),
        ],
        scratch_shapes=[
            pltpu.VMEM((3, rows + 2, SUB, LANES), F32),
            pltpu.VMEM((3, rows + 2, SUB, LANES), F32),
            pltpu.VMEM((rows, cols, 4, LANES, LANES), F32),
        ],
        compiler_params=params(),
        name="wall_first",
    )(masks, jit, disp, vel, *wy_got, *fx_got)


def pack_base_kernel(base1, got_even, got_odd, to_even, to_odd):
    rows, cols = base1.shape[1], base1.shape[2]
    before, after = before_after(even_at("wy"), got_even, got_odd)

    def edge(l):
        def write(out):
            at = 0
            for c in range(3):
                side = c * rows + l
                out[at : at + 1, :] = before[side : side + 1]
                out[at + 1 : at + 1 + cols, :] = base1[c, l]
                out[at + 1 + cols : at + 2 + cols, :] = after[side : side + 1]
                at += cols + 2
            for spare in range(at, out.shape[0]):
                out[spare : spare + 1, :] = jnp.zeros((1, LANES), F32)

        return write

    place_edges(even_at("fx"), edge(0), edge(rows - 1), to_even, to_odd)


def pack_base(base1, got):
    cols = base1.shape[2]
    out = jax.ShapeDtypeStruct((pad8(3 * (cols + 2)), LANES), F32)
    return pl.pallas_call(
        pack_base_kernel,
        in_specs=[whole()] * 3,
        out_specs=[whole()] * 2,
        out_shape=[out, out],
        compiler_params=params(),
        name="pack_base",
    )(base1, *got)


def last_kernel(
    weights, got, base1, vel1, totals, wye, wyo, fxe, fxo, disp_out, vel_out, dpad, loads, acc
):
    rows, cols = base1.shape[1], base1.shape[2]
    first_sub = lax.broadcasted_iota(jnp.int32, (SUB, LANES), 0) < SUB // 2
    before_y, after_y = before_after(even_at("wy"), wye, wyo)
    before_x, after_x = before_after(even_at("fx"), fxe, fxo)
    fill_padded(dpad, base1, before_y, after_y, before_x, after_x, 0, 0)
    total = got[0]
    for d in range(1, got.shape[0]):
        total = total + got[d]
    loads[...] = total
    for k in range(rows + 2):
        here = total[k * SUB : k * SUB + cols + 2, :]
        dpad[0, k, 0 : cols + 2, :] = dpad[0, k, 0 : cols + 2, :] + LOADING * here

    def one_tile(l, h):
        pulls = [tile_rows(dpad, c, l, h, first_sub) for c in range(3)]
        place = 0
        for g in range(LANES // SUB):
            sums = [None] * 3
            for ends, dh in reached(g):
                weight = weights[l, h, place]
                place += 1
                terms = [weight * pulls[c][ends][dh] for c in range(3)]
                sums = [t if v is None else v + t for v, t in zip(sums, terms)]
            for c in range(3):
                acc[l, h, c, g * SUB : (g + 1) * SUB, :] = sums[c]

    @pl.loop(0, cols)
    def _(h):
        for l in range(rows):
            one_tile(l, h)

    for l in range(rows):
        pulled = lane_sums(acc, l, cols, 3)
        for c in range(3):
            mine = dpad[c, l + 1, 1 : cols + 1, :]
            force = STIFFNESS * (pulled[c] - totals[l] * mine)
            if c == 0:
                at = (l + 1) * SUB + 1
                force = force + LOADING * loads[at : at + cols, :]
                for half in range(2):
                    at = (2 * l + half) * SUB + cols + 2
                    two = loads[at : at + 2, :]
                    span = slice(2 * half, 2 * half + 2)
                    fresh = vel1[c, l, span, :] + force[span] + LOADING * two
                    vel_out[c, l, span, :] = fresh
                    disp_out[c, l, span, :] = mine[span] + fresh
            else:
                fresh = vel1[c, l] + force
                vel_out[c, l] = fresh
                disp_out[c, l] = mine + fresh


def wall_last(weights, got, base1, vel1, totals, wy_got, fx_got):
    rows, cols = base1.shape[1], base1.shape[2]
    return pl.pallas_call(
        last_kernel,
        in_specs=[whole()] * 9,
        out_specs=[whole()] * 2,
        out_shape=[jax.ShapeDtypeStruct(base1.shape, F32)] * 2,
        scratch_shapes=[
            pltpu.VMEM((3, rows + 2, SUB, LANES), F32),
            pltpu.VMEM((4 * SUB, LANES), F32),
            pltpu.VMEM((rows, cols, 3, LANES, LANES), F32),
        ],
        compiler_params=params(),
        name="wall_last",
    )(weights, got, base1, vel1, totals, *wy_got, *fx_got)


def per_device(
    displacement,
    velocity,
    jitter,
    bond_masks,
    pressure,
    pressure_prev,
    speed_sq,
    route_device,
    route_tile,
):
    fx_count, wy_count = lax.axis_size("fx"), lax.axis_size("wy")
    cols = displacement.shape[2]
    device = route_device.reshape(-1, LANES)
    tile = route_tile.reshape(-1, LANES)
    length = (device // wy_count) * 2 + tile // cols
    height = (device % wy_count) * cols + tile % cols
    target = length * (wy_count * cols) + height

    sends = pack_wy(pressure, pressure_prev, speed_sq, jitter, displacement)
    wy_got = exchange("wy", *sends)
    sends = pack_fx(pressure, pressure_prev, speed_sq, jitter, displacement, *wy_got)
    fx_got = exchange("fx", *sends)
    pressure_out, slots = grid_steps(
        pressure, pressure_prev, speed_sq, wy_got, fx_got, target, fx_count, wy_count
    )
    got = lax.all_to_all(slots, ("fx", "wy"), split_axis=0, concat_axis=0, tiled=True)
    weights, vel1, base1, totals, *sends = wall_first(
        pressure.shape[0], pressure.shape[1],
        bond_masks, jitter, displacement, velocity, wy_got, fx_got
    )
    base_wy = exchange("wy", *sends)
    sends = pack_base(base1, base_wy)
    base_fx = exchange("fx", *sends)
    disp_out, vel_out = wall_last(weights, got, base1, vel1, totals, base_wy, base_fx)
    return (disp_out, vel_out, pressure_out)


def solution(mesh):
    placed = (
        P(None, "fx", "wy", None),
        P(None, "fx", "wy", None),
        P(None, "fx", "wy", None),
        P("fx", "wy", None, None, None),
        P("fx", "wy", None),
        P("fx", "wy", None),
        P("fx", "wy", None),
        P(("fx", "wy"), None),
        P(("fx", "wy")),
    )
    return jax.shard_map(
        per_device,
        mesh=mesh,
        in_specs=placed,
        out_specs=(P(None, "fx", "wy", None), P(None, "fx", "wy", None), P("fx", "wy", None)),
        check_vma=False,
    )
```

```python
import functools

import jax
import jax.numpy as jnp
from jax import lax
from jax.experimental import pallas as pl
from jax.experimental.pallas import tpu as pltpu
from jax.sharding import PartitionSpec as P

STIFFNESS = 0.02
LOADING = 0.05
REACH = 3.0
LANES = 128
SUB = 8
VMEM_BYTES = 48 * 1024 * 1024
ALL_VMEM = 67_000_000
HBM = pl.BlockSpec(memory_space=pltpu.HBM)

F32 = jnp.float32
BF16 = jnp.bfloat16


def whole():
    return pl.BlockSpec(memory_space=pltpu.VMEM)


def params(limit=VMEM_BYTES):
    return pltpu.CompilerParams(vmem_limit_bytes=limit)


def even_at(axis):
    return lax.rem(lax.axis_index(axis), 2) == 0


def pair_list(count, first):
    pairs = []
    for low in range(first, count - 1, 2):
        pairs.extend([(low, low + 1), (low + 1, low)])
    return pairs


def exchange(axis, to_even, to_odd):
    count = lax.axis_size(axis)
    got_odd = lax.ppermute(to_odd, axis, pair_list(count, 1))
    got_even = lax.ppermute(to_even, axis, pair_list(count, 0))
    return got_even, got_odd


def place_edges(even, low, high, to_even, to_odd):
    @pl.when(even)
    def _():
        high(to_even)
        low(to_odd)

    @pl.when(jnp.logical_not(even))
    def _():
        low(to_even)
        high(to_odd)


def before_after(even, got_even, got_odd):
    a, b = got_even[...], got_odd[...]
    return jnp.where(even, b, a), jnp.where(even, a, b)


def pack_wy_kernel(
    p, q, s, jit_in, disp_in, vel_in, wy_even, wy_odd, fx_even, fx_odd, wall, edges, ends, sems
):
    cx, cy = p.shape[0], p.shape[1]
    rows, cols = jit_in.shape[1], jit_in.shape[2]
    pairs = []
    for k, field in enumerate((p, q, s)):
        for side, first in enumerate((0, cy - SUB)):
            pairs.append((field.at[:, first : first + SUB, :], edges.at[2 * k + side]))
    pairs.append((p.at[0:2], ends.at[0, 0:2]))
    pairs.append((p.at[cx - 2 : cx], ends.at[1, 0:2]))
    for k, field in enumerate((q, s)):
        pairs.append((field.at[0], ends.at[0, 2 + k]))
        pairs.append((field.at[cx - 1], ends.at[1, 2 + k]))
    for k, field in enumerate((jit_in, disp_in, vel_in)):
        pairs.append((field, wall.at[k]))
    copies = [pltpu.make_async_copy(a, b, sems.at[k]) for k, (a, b) in enumerate(pairs)]
    for copy in copies:
        copy.start()
    for copy in copies:
        copy.wait()

    def edge(side, near, far, h):
        def write(out):
            out[0:cx, :] = edges[side, :, near, :]
            out[cx : 2 * cx, :] = edges[side, :, far, :]
            out[2 * cx : 3 * cx, :] = edges[2 + side, :, near, :]
            out[3 * cx : 4 * cx, :] = edges[4 + side, :, near, :]
            at = 4 * cx
            for field in range(2):
                for c in range(3):
                    for l in range(rows):
                        out[at : at + 1, :] = wall[field, c, l, h : h + 1, :]
                        at += 1
            for spare in range(at, out.shape[0]):
                out[spare : spare + 1, :] = jnp.zeros((1, LANES), F32)

        return write

    place_edges(
        even_at("wy"),
        edge(0, 0, 1, 0),
        edge(1, SUB - 1, SUB - 2, cols - 1),
        wy_even,
        wy_odd,
    )

    def end(side, near, far, l):
        def write(out):
            out[0:cy, :] = ends[side, near]
            out[cy : 2 * cy, :] = ends[side, far]
            out[2 * cy : 3 * cy, :] = ends[side, 2]
            out[3 * cy : 4 * cy, :] = ends[side, 3]
            at = 4 * cy
            for field in range(2):
                for c in range(3):
                    out[at + 1 : at + 1 + cols, :] = wall[field, c, l]
                    at += cols + 2

        return write

    place_edges(even_at("fx"), end(0, 0, 1, 0), end(1, 1, 0, rows - 1), fx_even, fx_odd)


def pad8(count):
    return (count + 7) // 8 * 8


def pack_wy(p, q, s, jit, disp, vel):
    cx, cy = p.shape[0], p.shape[1]
    rows, cols = jit.shape[1], jit.shape[2]
    wy_out = jax.ShapeDtypeStruct((pad8(4 * cx + 6 * rows), LANES), F32)
    fx_out = jax.ShapeDtypeStruct((pad8(4 * cy + 6 * (cols + 2) + 2), LANES), F32)
    return pl.pallas_call(
        pack_wy_kernel,
        in_specs=[HBM] * 6,
        out_specs=[whole()] * 5,
        out_shape=[wy_out, wy_out, fx_out, fx_out, jax.ShapeDtypeStruct((3,) + jit.shape, F32)],
        scratch_shapes=[
            pltpu.VMEM((6, cx, SUB, LANES), F32),
            pltpu.VMEM((2, 4, cy, LANES), F32),
            pltpu.SemaphoreType.DMA((15,)),
        ],
        compiler_params=params(ALL_VMEM),
        name="pack_wy",
    )(p, q, s, jit, disp, vel)


def pack_fx_kernel(cx, cy, rows, cols, part_even, part_odd, got_even, got_odd, to_even, to_odd):
    before, after = before_after(even_at("wy"), got_even, got_odd)
    to_even[...] = part_even[...]
    to_odd[...] = part_odd[...]

    def corners(x, l):
        def write(out):
            at = 4 * cy
            for k in range(6):
                side = 4 * cx + k * rows + l
                out[at : at + 1, :] = before[side : side + 1]
                out[at + 1 + cols : at + 2 + cols, :] = after[side : side + 1]
                at += cols + 2
            out[at : at + 1, :] = before[x : x + 1]
            out[at + 1 : at + 2, :] = after[x : x + 1]

        return write

    place_edges(even_at("fx"), corners(0, 0), corners(cx - 1, rows - 1), to_even, to_odd)


def pack_fx(sizes, parts, got):
    out = jax.ShapeDtypeStruct(parts[0].shape, F32)
    return pl.pallas_call(
        functools.partial(pack_fx_kernel, *sizes),
        in_specs=[whole()] * 4,
        out_specs=[whole()] * 2,
        out_shape=[out, out],
        compiler_params=params(),
        name="pack_fx",
    )(*parts, *got)


def along_z(v):
    lane = lax.broadcasted_iota(jnp.int32, v.shape, 1)
    up = jnp.where(lane == LANES - 1, 0.0, pltpu.roll(v, LANES - 1, 1))
    down = jnp.where(lane == 0, 0.0, pltpu.roll(v, 1, 1))
    return up + down


def update(v, old, speed, beside):
    return 2.0 * v - old + speed * (beside + along_z(v) - 6.0 * v)


def two_terms(v):
    high = v.astype(BF16)
    return high, (v - high.astype(F32)).astype(BF16)


def grid_kernel(p, q, s, wye, wyo, fxe, fxo, target, out, slots, s0, s1, rhs, part1, part2):
    cx, cy = p.shape[0], p.shape[1]
    ahead, behind = SUB, SUB + cy
    fx_count = part1.shape[0] // 2 - 1
    cols = 4
    tall = part2.shape[0]
    high = part1.shape[1] - 2 * SUB
    wy_count = high // cols
    before_y, after_y = before_after(even_at("wy"), wye, wyo)
    before_x, after_x = before_after(even_at("fx"), fxe, fxo)
    corner = 4 * cy + 6 * (cols + 2)

    s0[1 : cx + 1, ahead:behind, :] = p[...]
    for x, side in ((0, before_x), (cx + 1, after_x)):
        s0[x, ahead:behind, :] = side[0:cy]
        s0[x, ahead - 1 : ahead, :] = side[corner : corner + 1]
        s0[x, behind : behind + 1, :] = side[corner + 1 : corner + 2]
    s0[1 : cx + 1, ahead - 1, :] = before_y[0:cx]
    s0[1 : cx + 1, behind, :] = after_y[0:cx]

    for side, y, inner in ((before_y, ahead - 1, ahead), (after_y, behind, behind - 1)):
        near, far = side[0:cx], side[cx : 2 * cx]
        old, speed = side[2 * cx : 3 * cx], side[3 * cx : 4 * cx]
        beside = s0[0:cx, y, :] + s0[2 : cx + 2, y, :] + far + s0[1 : cx + 1, inner, :]
        s1[1 : cx + 1, y, :] = update(near, old, speed, beside)
    for side, x, inner in ((before_x, 0, 1), (after_x, cx + 1, cx)):
        near, far = side[0:cy], side[cy : 2 * cy]
        old, speed = side[2 * cy : 3 * cy], side[3 * cy : 4 * cy]
        beside = s0[x, ahead - 1 : behind - 1, :] + s0[x, ahead + 1 : behind + 1, :]
        beside = beside + far + s0[inner, ahead:behind, :]
        s1[x, ahead:behind, :] = update(near, old, speed, beside)

    def sweep(now, old, x):
        beside = now[x, ahead:behind, :] + now[x + 2, ahead:behind, :]
        beside = beside + now[x + 1, ahead - 1 : behind - 1, :]
        beside = beside + now[x + 1, ahead + 1 : behind + 1, :]
        return update(now[x + 1, ahead:behind, :], old, s[x], beside)

    for x in range(cx):
        fresh = sweep(s0, q[x], x)
        s1[x + 1, ahead:behind, :] = fresh
        a, b = two_terms(fresh)
        rhs[x * cy : (x + 1) * cy, 0:LANES] = a
        rhs[x * cy : (x + 1) * cy, LANES : 2 * LANES] = b
    for x in range(cx):
        fresh = sweep(s1, p[x], x)
        out[x] = fresh
        a, b = two_terms(fresh)
        rhs[x * cy : (x + 1) * cy, 2 * LANES : 3 * LANES] = a
        rhs[x * cy : (x + 1) * cy, 3 * LANES : 4 * LANES] = b

    part1[...] = jnp.zeros(part1.shape, F32)
    part2[:, 0:SUB, :] = jnp.zeros((tall, SUB, LANES), F32)
    chunk = 256
    for first in range(0, tall * high, chunk):
        tile = lax.broadcasted_iota(jnp.int32, (chunk, LANES), 0) + first
        picks = []
        for piece in range(target.shape[0]):
            picks.append(jnp.where(tile == target[piece : piece + 1, :], 1.0, 0.0).astype(BF16))
        sums = jnp.dot(jnp.concatenate(picks, axis=1), rhs[...], preferred_element_type=F32)
        one = sums[:, 0:LANES] + sums[:, LANES : 2 * LANES]
        two = sums[:, 2 * LANES : 3 * LANES] + sums[:, 3 * LANES : 4 * LANES]
        l = first // high
        part1[1 + l : 1 + l + chunk // high, SUB : SUB + high, :] = one.reshape(-1, high, LANES)
        part2[l : l + chunk // high, SUB : SUB + high, :] = two.reshape(-1, high, LANES)
    lower = lax.broadcasted_iota(jnp.int32, (SUB, LANES), 0) < cols + 2
    for a in range(fx_count):
        for b in range(wy_count):
            for l in range(4):
                h = SUB + cols * b
                one = part1[2 * a + l, h - 1 : h - 1 + SUB, :]
                h = h + 2 * (l % 2) - 6
                two = part2[2 * a + l // 2, h : h + SUB, :]
                slots[a * wy_count + b, l * SUB : (l + 1) * SUB, :] = jnp.where(lower, one, two)


def grid_steps(p, q, s, wy_got, fx_got, target, fx_count, wy_count):
    cx, cy = p.shape[0], p.shape[1]
    tall, high = fx_count * 2, wy_count * 4
    devices = fx_count * wy_count
    return pl.pallas_call(
        grid_kernel,
        in_specs=[whole()] * 8,
        out_specs=[whole()] * 2,
        out_shape=[
            jax.ShapeDtypeStruct(p.shape, F32),
            jax.ShapeDtypeStruct((devices, 4 * SUB, LANES), F32),
        ],
        scratch_shapes=[
            pltpu.VMEM((cx + 2, cy + 2 * SUB, LANES), F32),
            pltpu.VMEM((cx + 2, cy + 2 * SUB, LANES), F32),
            pltpu.VMEM((cx * cy, 4 * LANES), BF16),
            pltpu.VMEM((tall + 2, high + 2 * SUB, LANES), F32),
            pltpu.VMEM((tall, high + 2 * SUB, LANES), F32),
        ],
        compiler_params=params(),
        name="grid_steps",
    )(p, q, s, *wy_got, *fx_got, target)


def reached(g):
    groups = []
    for dh in (-1, 0, 1):
        if (dh == -1 and g % 4 == 3) or (dh == 1 and g % 4 == 0):
            continue
        groups.append(dh)
    return groups


STORED = sum(len(reached(g)) for g in range(LANES // SUB))


def mid_rows(ref, c, l, h):
    rows = {}
    for dh in (-1, 0, 1):
        row = ref[c, l + 1, pl.ds(h + 1 + dh, 1), :]
        rows[dh] = jnp.broadcast_to(row, (SUB, LANES))
    return rows


def end_rows(ref, c, l, h, first_sub):
    rows = {}
    for dh in (-1, 0, 1):
        at = pl.ds(h + 1 + dh, 1)
        before = jnp.broadcast_to(ref[c, l, at, :], (SUB, LANES))
        after = jnp.broadcast_to(ref[c, l + 2, at, :], (SUB, LANES))
        rows[dh] = jnp.where(first_sub, before, after)
    return rows


def fill_y(pad, own, before, after, at):
    rows, cols = own.shape[1], own.shape[2]
    for c in range(3):
        for l in range(rows):
            row = at + c * rows + l
            pad[c, l + 1, 0:1, :] = before[row : row + 1]
            pad[c, l + 1, 1 : cols + 1, :] = own[c, l]
            pad[c, l + 1, cols + 1 : cols + 2, :] = after[row : row + 1]


def fill_x(pad, rows, cols, before, after, at):
    for c in range(3):
        row = at + c * (cols + 2)
        pad[c, 0, 0 : cols + 2, :] = before[row : row + cols + 2]
        pad[c, rows + 1, 0 : cols + 2, :] = after[row : row + cols + 2]


def lattice_rows():
    index = lax.broadcasted_iota(jnp.int32, (1, LANES), 1)
    places = (index % 8, index // 8 % 4, index // 32)
    return [v.astype(F32) * (1.0 / REACH) for v in places]


SPAN = 8.0 / REACH
RISE = 4.0 / REACH


def mine_columns(ref, lattice, l, h):
    sub = lax.broadcasted_iota(jnp.int32, (SUB, LANES), 0)
    own = []
    for c in range(3):
        row = ref[c, l + 1, pl.ds(h + 1, 1), :] * (1.0 / REACH) + lattice[c]
        own.append(jnp.broadcast_to(row, (SUB, LANES)))
    return jnp.transpose(jnp.where(sub == 0, own[0], jnp.where(sub == 1, own[1], own[2])))


def bond_row(weight, others, mine):
    for c in range(3):
        diff = others[c] - mine[c]
        weight = weight - diff * diff
    return jnp.maximum(weight, 0.0)


def tile_pass(l, h, columns, others, pulls, mask_at, weights, sums_in, acc):
    place = 0
    for g in range(LANES // SUB):
        span = slice(g * SUB, (g + 1) * SUB)
        mine = [jnp.broadcast_to(columns[span, c : c + 1], (SUB, LANES)) for c in range(3)]
        sums = [None if sums_in is None else sums_in[l, h, c, span, :] for c in range(4)]
        for dh in reached(g):
            here = [others[c][dh] for c in range(3)]
            weight = bond_row(mask_at(dh, span, place), here, mine)
            weights[l, h, place] = weight
            place += 1
            terms = [weight * pulls[c][dh] for c in range(3)] + [weight]
            sums = [t if v is None else v + t for v, t in zip(sums, terms)]
        for c in range(4):
            acc[l, h, c, span, :] = sums[c]


def lane_sums(acc, l, cols, count):
    ones = jnp.ones((2 * SUB, LANES), BF16)
    result = [[] for _ in range(count)]
    for h in range(cols):
        terms = []
        for c in range(count):
            terms.extend(two_terms(acc[l, h, c]))
        sums = lax.dot_general(
            ones,
            jnp.concatenate(terms, axis=0),
            (((1,), (1,)), ((), ())),
            preferred_element_type=F32,
        )[0:1]
        for c in range(count):
            at = 2 * c * LANES
            result[c].append(sums[:, at : at + LANES] + sums[:, at + LANES : at + 2 * LANES])
    return [jnp.concatenate(parts, axis=0) for parts in result]


def center_kernel(
    cx, masks_in, wall, wye, wyo, weights, acc, end_masks, jpad, dpad, masks, sems
):
    rows, cols = wall.shape[2], wall.shape[3]
    copies = {}
    for h in range(cols):
        for l in range(rows):
            copies[l, h] = pltpu.make_async_copy(
                masks_in.at[l, h], masks.at[l, h], sems.at[l * cols + h]
            )
            copies[l, h].start()
    first_sub = lax.broadcasted_iota(jnp.int32, (SUB, LANES), 0) < SUB // 2
    before, after = before_after(even_at("wy"), wye, wyo)
    fill_y(jpad, wall.at[0], before, after, 4 * cx)
    fill_y(dpad, wall.at[1], before, after, 4 * cx + 3 * rows)
    lattice = lattice_rows()

    def one_tile(l, h):
        columns = mine_columns(jpad, lattice, l, h)
        others = []
        for c in range(3):
            mid = mid_rows(jpad, c, l, h)
            for dh in (-1, 0, 1):
                mid[dh] = mid[dh] * (1.0 / REACH) + lattice[c]
                if c == 1:
                    mid[dh] = mid[dh] + RISE * dh
            others.append(mid)
        pulls = [mid_rows(dpad, c, l, h) for c in range(3)]

        def mask_at(dh, span, place):
            before = masks[l, h, 1 + dh, span, :]
            after = masks[l, h, 7 + dh, span, :]
            end_masks[l, h, place] = jnp.where(first_sub, before, after).astype(F32)
            return masks[l, h, 4 + dh, span, :].astype(F32)

        tile_pass(l, h, columns, others, pulls, mask_at, weights, None, acc)

    for h in range(cols):
        for l in range(rows):
            copies[l, h].wait()
            one_tile(l, h)


def wall_center(cx, masks, wall, wy_got):
    rows, cols = wall.shape[2], wall.shape[3]
    stored = jax.ShapeDtypeStruct((rows, cols, STORED, SUB, LANES), F32)
    return pl.pallas_call(
        functools.partial(center_kernel, cx),
        in_specs=[HBM] + [whole()] * 3,
        out_specs=[whole()] * 3,
        out_shape=[stored, jax.ShapeDtypeStruct((rows, cols, 4, LANES, LANES), F32), stored],
        scratch_shapes=[
            pltpu.VMEM((3, rows + 2, SUB, LANES), F32),
            pltpu.VMEM((3, rows + 2, SUB, LANES), F32),
            pltpu.VMEM(masks.shape, jnp.int32),
            pltpu.SemaphoreType.DMA((rows * cols,)),
        ],
        compiler_params=params(),
        name="wall_center",
    )(masks, wall, *wy_got)


def wall_kernel(
    cx, cy, wall, wye, wyo, fxe, fxo, part, end_masks, weights, vel1, base1, totals, to_even, to_odd,
    jpad, dpad, acc,
):
    rows, cols = wall.shape[2], wall.shape[3]
    first_sub = lax.broadcasted_iota(jnp.int32, (SUB, LANES), 0) < SUB // 2
    before, after = before_after(even_at("wy"), wye, wyo)
    fill_y(jpad, wall.at[0], before, after, 4 * cx)
    fill_y(dpad, wall.at[1], before, after, 4 * cx + 3 * rows)
    before, after = before_after(even_at("fx"), fxe, fxo)
    fill_x(jpad, rows, cols, before, after, 4 * cy)
    fill_x(dpad, rows, cols, before, after, 4 * cy + 3 * (cols + 2))
    lattice = lattice_rows()

    def one_tile(l, h):
        columns = mine_columns(jpad, lattice, l, h)
        others = []
        for c in range(3):
            ends = end_rows(jpad, c, l, h, first_sub)
            for dh in (-1, 0, 1):
                ends[dh] = ends[dh] * (1.0 / REACH) + lattice[c]
                if c == 0:
                    ends[dh] = ends[dh] + jnp.where(first_sub, -SPAN, SPAN)
                if c == 1:
                    ends[dh] = ends[dh] + RISE * dh
            others.append(ends)
        pulls = [end_rows(dpad, c, l, h, first_sub) for c in range(3)]

        def mask_at(dh, span, place):
            return end_masks[l, h, place]

        tile_pass(l, h, columns, others, pulls, mask_at, weights, part, acc)

    @pl.loop(0, cols)
    def _(h):
        for l in range(rows):
            one_tile(l, h)

    for l in range(rows):
        pulled = lane_sums(acc, l, cols, 4)
        totals[l] = pulled[3]
        for c in range(3):
            mine = wall[1, c, l]
            fresh = wall[2, c, l] + STIFFNESS * (pulled[c] - pulled[3] * mine)
            vel1[c, l] = fresh
            base1[c, l] = mine + fresh

    def edge(at):
        def write(out):
            for c in range(3):
                for k in range(rows):
                    out[c * rows + k : c * rows + k + 1, :] = base1[c, k, at : at + 1, :]
            for spare in range(3 * rows, out.shape[0]):
                out[spare : spare + 1, :] = jnp.zeros((1, LANES), F32)

        return write

    place_edges(even_at("wy"), edge(0), edge(cols - 1), to_even, to_odd)


def wall_first(cx, cy, wall, wy_got, fx_got, part, end_masks):
    rows, cols = wall.shape[2], wall.shape[3]
    edge = (pad8(3 * rows), LANES)
    field = jax.ShapeDtypeStruct(wall.shape[1:], F32)
    return pl.pallas_call(
        functools.partial(wall_kernel, cx, cy),
        in_specs=[whole()] * 7,
        out_specs=[whole()] * 6,
        out_shape=[
            jax.ShapeDtypeStruct((rows, cols, STORED, SUB, LANES), F32),
            field,
            field,
            jax.ShapeDtypeStruct((rows, cols, LANES), F32),
            jax.ShapeDtypeStruct(edge, F32),
            jax.ShapeDtypeStruct(edge, F32),
        ],
        scratch_shapes=[
            pltpu.VMEM((3, rows + 2, SUB, LANES), F32),
            pltpu.VMEM((3, rows + 2, SUB, LANES), F32),
            pltpu.VMEM((rows, cols, 4, LANES, LANES), F32),
        ],
        compiler_params=params(),
        name="wall_first",
    )(wall, *wy_got, *fx_got, part, end_masks)


def pack_base_kernel(base1, got_even, got_odd, to_even, to_odd):
    rows, cols = base1.shape[1], base1.shape[2]
    before, after = before_after(even_at("wy"), got_even, got_odd)

    def edge(l):
        def write(out):
            at = 0
            for c in range(3):
                side = c * rows + l
                out[at : at + 1, :] = before[side : side + 1]
                out[at + 1 : at + 1 + cols, :] = base1[c, l]
                out[at + 1 + cols : at + 2 + cols, :] = after[side : side + 1]
                at += cols + 2
            for spare in range(at, out.shape[0]):
                out[spare : spare + 1, :] = jnp.zeros((1, LANES), F32)

        return write

    place_edges(even_at("fx"), edge(0), edge(rows - 1), to_even, to_odd)


def pack_base(base1, got):
    cols = base1.shape[2]
    out = jax.ShapeDtypeStruct((pad8(3 * (cols + 2)), LANES), F32)
    return pl.pallas_call(
        pack_base_kernel,
        in_specs=[whole()] * 3,
        out_specs=[whole()] * 2,
        out_shape=[out, out],
        compiler_params=params(),
        name="pack_base",
    )(base1, *got)


def last_kernel(
    weights, end_weights, got, base1, vel1, totals, wye, wyo, fxe, fxo, disp_out, vel_out,
    dpad, loads, acc,
):
    rows, cols = base1.shape[1], base1.shape[2]
    first_sub = lax.broadcasted_iota(jnp.int32, (SUB, LANES), 0) < SUB // 2
    before, after = before_after(even_at("wy"), wye, wyo)
    fill_y(dpad, base1, before, after, 0)
    before, after = before_after(even_at("fx"), fxe, fxo)
    fill_x(dpad, rows, cols, before, after, 0)
    total = got[0]
    for d in range(1, got.shape[0]):
        total = total + got[d]
    loads[...] = total
    for k in range(rows + 2):
        here = total[k * SUB : k * SUB + cols + 2, :]
        dpad[0, k, 0 : cols + 2, :] = dpad[0, k, 0 : cols + 2, :] + LOADING * here

    def one_tile(l, h):
        mids = [mid_rows(dpad, c, l, h) for c in range(3)]
        ends = [end_rows(dpad, c, l, h, first_sub) for c in range(3)]
        place = 0
        for g in range(LANES // SUB):
            sums = [None] * 3
            for dh in reached(g):
                for weight, pulls in (
                    (weights[l, h, place], mids), (end_weights[l, h, place], ends)
                ):
                    terms = [weight * pulls[c][dh] for c in range(3)]
                    sums = [t if v is None else v + t for v, t in zip(sums, terms)]
                place += 1
            for c in range(3):
                acc[l, h, c, g * SUB : (g + 1) * SUB, :] = sums[c]

    @pl.loop(0, cols)
    def _(h):
        for l in range(rows):
            one_tile(l, h)

    for l in range(rows):
        pulled = lane_sums(acc, l, cols, 3)
        for c in range(3):
            mine = dpad[c, l + 1, 1 : cols + 1, :]
            force = STIFFNESS * (pulled[c] - totals[l] * mine)
            if c == 0:
                at = (l + 1) * SUB + 1
                force = force + LOADING * loads[at : at + cols, :]
                for half in range(2):
                    at = (2 * l + half) * SUB + cols + 2
                    two = loads[at : at + 2, :]
                    span = slice(2 * half, 2 * half + 2)
                    fresh = vel1[c, l, span, :] + force[span] + LOADING * two
                    vel_out[c, l, span, :] = fresh
                    disp_out[c, l, span, :] = mine[span] + fresh
            else:
                fresh = vel1[c, l] + force
                vel_out[c, l] = fresh
                disp_out[c, l] = mine + fresh


def wall_last(weights, end_weights, got, base1, vel1, totals, wy_got, fx_got):
    rows, cols = base1.shape[1], base1.shape[2]
    return pl.pallas_call(
        last_kernel,
        in_specs=[whole()] * 10,
        out_specs=[whole()] * 2,
        out_shape=[jax.ShapeDtypeStruct(base1.shape, F32)] * 2,
        scratch_shapes=[
            pltpu.VMEM((3, rows + 2, SUB, LANES), F32),
            pltpu.VMEM((4 * SUB, LANES), F32),
            pltpu.VMEM((rows, cols, 3, LANES, LANES), F32),
        ],
        compiler_params=params(),
        name="wall_last",
    )(weights, end_weights, got, base1, vel1, totals, *wy_got, *fx_got)


def per_device(
    displacement,
    velocity,
    jitter,
    bond_masks,
    pressure,
    pressure_prev,
    speed_sq,
    route_device,
    route_tile,
):
    fx_count, wy_count = lax.axis_size("fx"), lax.axis_size("wy")
    cols = displacement.shape[2]
    device = route_device.reshape(-1, LANES)
    tile = route_tile.reshape(-1, LANES)
    length = (device // wy_count) * 2 + tile // cols
    height = (device % wy_count) * cols + tile % cols
    target = length * (wy_count * cols) + height

    cx, cy = pressure.shape[0], pressure.shape[1]
    rows = displacement.shape[1]
    *sends, part_even, part_odd, wall = pack_wy(
        pressure, pressure_prev, speed_sq, jitter, displacement, velocity
    )
    wy_got = exchange("wy", *sends)
    sends = pack_fx((cx, cy, rows, cols), (part_even, part_odd), wy_got)
    fx_got = exchange("fx", *sends)
    weights, part, end_masks = wall_center(cx, bond_masks, wall, wy_got)
    pressure_out, slots = grid_steps(
        pressure, pressure_prev, speed_sq, wy_got, fx_got, target, fx_count, wy_count
    )
    got = lax.all_to_all(slots, ("fx", "wy"), split_axis=0, concat_axis=0, tiled=True)
    end_weights, vel1, base1, totals, *sends = wall_first(
        cx, cy, wall, wy_got, fx_got, part, end_masks
    )
    base_wy = exchange("wy", *sends)
    sends = pack_base(base1, base_wy)
    base_fx = exchange("fx", *sends)
    disp_out, vel_out = wall_last(
        weights, end_weights, got, base1, vel1, totals, base_wy, base_fx
    )
    return (disp_out, vel_out, pressure_out)


def solution(mesh):
    placed = (
        P(None, "fx", "wy", None),
        P(None, "fx", "wy", None),
        P(None, "fx", "wy", None),
        P("fx", "wy", None, None, None),
        P("fx", "wy", None),
        P("fx", "wy", None),
        P("fx", "wy", None),
        P(("fx", "wy"), None),
        P(("fx", "wy")),
    )
    return jax.shard_map(
        per_device,
        mesh=mesh,
        in_specs=placed,
        out_specs=(P(None, "fx", "wy", None), P(None, "fx", "wy", None), P("fx", "wy", None)),
        check_vma=False,
    )
```

```python
import functools

import jax
import jax.numpy as jnp
from jax import lax
from jax.experimental import pallas as pl
from jax.experimental.pallas import tpu as pltpu
from jax.sharding import PartitionSpec as P

STIFFNESS = 0.02
LOADING = 0.05
REACH = 3.0
LANES = 128
SUB = 8
VMEM_BYTES = 48 * 1024 * 1024
HBM = pl.BlockSpec(memory_space=pltpu.HBM)

F32 = jnp.float32
BF16 = jnp.bfloat16


def whole():
    return pl.BlockSpec(memory_space=pltpu.VMEM)


def params():
    return pltpu.CompilerParams(vmem_limit_bytes=VMEM_BYTES)


def vmem(*shape):
    return pltpu.VMEM(shape, F32)


def even_at(axis):
    return lax.rem(lax.axis_index(axis), 2) == 0


def pair_list(count, first):
    pairs = []
    for low in range(first, count - 1, 2):
        pairs.extend([(low, low + 1), (low + 1, low)])
    return pairs


def exchange(axis, to_even, to_odd):
    count = lax.axis_size(axis)
    got_odd = lax.ppermute(to_odd, axis, pair_list(count, 1))
    got_even = lax.ppermute(to_even, axis, pair_list(count, 0))
    return got_even, got_odd


def place_edges(even, low, high, to_even, to_odd):
    @pl.when(even)
    def _():
        high(to_even)
        low(to_odd)

    @pl.when(jnp.logical_not(even))
    def _():
        low(to_even)
        high(to_odd)


def before_after(even, got_even, got_odd):
    a, b = got_even[...], got_odd[...]
    return jnp.where(even, b, a), jnp.where(even, a, b)


def pack_wy_kernel(
    p, q, s, jit_in, disp_in, vel_in, wy_even, wy_odd, fx_even, fx_odd, wall, edges, ends, sems
):
    cx, cy = p.shape[0], p.shape[1]
    rows, cols = jit_in.shape[1], jit_in.shape[2]
    pairs = []
    for k, field in enumerate((p, q, s)):
        for side, first in enumerate((0, cy - SUB)):
            pairs.append((field.at[:, first : first + SUB, :], edges.at[2 * k + side]))
    pairs.append((p.at[0:2], ends.at[0, 0:2]))
    pairs.append((p.at[cx - 2 : cx], ends.at[1, 0:2]))
    for k, field in enumerate((q, s)):
        pairs.append((field.at[0], ends.at[0, 2 + k]))
        pairs.append((field.at[cx - 1], ends.at[1, 2 + k]))
    for k, field in enumerate((jit_in, disp_in, vel_in)):
        pairs.append((field, wall.at[k]))
    copies = [pltpu.make_async_copy(a, b, sems.at[k]) for k, (a, b) in enumerate(pairs)]
    for copy in copies:
        copy.start()
    for copy in copies:
        copy.wait()

    def edge(side, near, far, h):
        def write(out):
            out[0:cx, :] = edges[side, :, near, :]
            out[cx : 2 * cx, :] = edges[side, :, far, :]
            out[2 * cx : 3 * cx, :] = edges[2 + side, :, near, :]
            out[3 * cx : 4 * cx, :] = edges[4 + side, :, near, :]
            at = 4 * cx
            for field in range(2):
                for c in range(3):
                    for l in range(rows):
                        out[at : at + 1, :] = wall[field, c, l, h : h + 1, :]
                        at += 1
            for spare in range(at, out.shape[0]):
                out[spare : spare + 1, :] = jnp.zeros((1, LANES), F32)

        return write

    place_edges(
        even_at("wy"),
        edge(0, 0, 1, 0),
        edge(1, SUB - 1, SUB - 2, cols - 1),
        wy_even,
        wy_odd,
    )

    def end(side, near, far, l):
        def write(out):
            out[0:cy, :] = ends[side, near]
            out[cy : 2 * cy, :] = ends[side, far]
            out[2 * cy : 3 * cy, :] = ends[side, 2]
            out[3 * cy : 4 * cy, :] = ends[side, 3]
            at = 4 * cy
            for field in range(2):
                for c in range(3):
                    out[at + 1 : at + 1 + cols, :] = wall[field, c, l]
                    at += cols + 2

        return write

    place_edges(even_at("fx"), end(0, 0, 1, 0), end(1, 1, 0, rows - 1), fx_even, fx_odd)


def in_hbm(*arrays):
    return [pltpu.with_memory_space_constraint(v, pltpu.HBM) for v in arrays]


def pad8(count):
    return (count + 7) // 8 * 8


def pack_wy(p, q, s, jit, disp, vel):
    cx, cy = p.shape[0], p.shape[1]
    rows, cols = jit.shape[1], jit.shape[2]
    wy_out = vmem(pad8(4 * cx + 6 * rows), LANES)
    fx_out = vmem(pad8(4 * cy + 6 * (cols + 2) + 2), LANES)
    return pl.pallas_call(
        pack_wy_kernel,
        in_specs=[HBM] * 6,
        out_specs=[whole()] * 5,
        out_shape=[wy_out, wy_out, fx_out, fx_out, vmem(3, *jit.shape)],
        scratch_shapes=[
            pltpu.VMEM((6, cx, SUB, LANES), F32),
            pltpu.VMEM((2, 4, cy, LANES), F32),
            pltpu.SemaphoreType.DMA((15,)),
        ],
        compiler_params=params(),
        name="pack_wy",
    )(*in_hbm(p, q, s, jit, disp, vel))


def pack_fx_kernel(cx, cy, rows, cols, part_even, part_odd, got_even, got_odd, to_even, to_odd):
    before, after = before_after(even_at("wy"), got_even, got_odd)
    to_even[...] = part_even[...]
    to_odd[...] = part_odd[...]

    def corners(x, l):
        def write(out):
            at = 4 * cy
            for k in range(6):
                side = 4 * cx + k * rows + l
                out[at : at + 1, :] = before[side : side + 1]
                out[at + 1 + cols : at + 2 + cols, :] = after[side : side + 1]
                at += cols + 2
            out[at : at + 1, :] = before[x : x + 1]
            out[at + 1 : at + 2, :] = after[x : x + 1]

        return write

    place_edges(even_at("fx"), corners(0, 0), corners(cx - 1, rows - 1), to_even, to_odd)


def pack_fx(sizes, parts, got):
    out = vmem(*parts[0].shape)
    return pl.pallas_call(
        functools.partial(pack_fx_kernel, *sizes),
        in_specs=[whole()] * 4,
        out_specs=[whole()] * 2,
        out_shape=[out, out],
        compiler_params=params(),
        name="pack_fx",
    )(*parts, *got)


def along_z(v):
    lane = lax.broadcasted_iota(jnp.int32, v.shape, 1)
    up = jnp.where(lane == LANES - 1, 0.0, pltpu.roll(v, LANES - 1, 1))
    down = jnp.where(lane == 0, 0.0, pltpu.roll(v, 1, 1))
    return up + down


def update(v, old, speed, beside):
    return 2.0 * v - old + speed * (beside + along_z(v) - 6.0 * v)


def two_terms(v):
    high = v.astype(BF16)
    return high, (v - high.astype(F32)).astype(BF16)


def grid_kernel(p, q, s, wye, wyo, fxe, fxo, target, out, slots, s0, s1, rhs, part1, part2):
    cx, cy = p.shape[0], p.shape[1]
    ahead, behind = SUB, SUB + cy
    fx_count = part1.shape[0] // 2 - 1
    cols = 4
    tall = part2.shape[0]
    high = part1.shape[1] - 2 * SUB
    wy_count = high // cols
    before_y, after_y = before_after(even_at("wy"), wye, wyo)
    before_x, after_x = before_after(even_at("fx"), fxe, fxo)
    corner = 4 * cy + 6 * (cols + 2)

    s0[1 : cx + 1, ahead:behind, :] = p[...]
    for x, side in ((0, before_x), (cx + 1, after_x)):
        s0[x, ahead:behind, :] = side[0:cy]
        s0[x, ahead - 1 : ahead, :] = side[corner : corner + 1]
        s0[x, behind : behind + 1, :] = side[corner + 1 : corner + 2]
    s0[1 : cx + 1, ahead - 1, :] = before_y[0:cx]
    s0[1 : cx + 1, behind, :] = after_y[0:cx]

    for side, y, inner in ((before_y, ahead - 1, ahead), (after_y, behind, behind - 1)):
        near, far = side[0:cx], side[cx : 2 * cx]
        old, speed = side[2 * cx : 3 * cx], side[3 * cx : 4 * cx]
        beside = s0[0:cx, y, :] + s0[2 : cx + 2, y, :] + far + s0[1 : cx + 1, inner, :]
        s1[1 : cx + 1, y, :] = update(near, old, speed, beside)
    for side, x, inner in ((before_x, 0, 1), (after_x, cx + 1, cx)):
        near, far = side[0:cy], side[cy : 2 * cy]
        old, speed = side[2 * cy : 3 * cy], side[3 * cy : 4 * cy]
        beside = s0[x, ahead - 1 : behind - 1, :] + s0[x, ahead + 1 : behind + 1, :]
        beside = beside + far + s0[inner, ahead:behind, :]
        s1[x, ahead:behind, :] = update(near, old, speed, beside)

    def sweep(now, old, x):
        beside = now[x, ahead:behind, :] + now[x + 2, ahead:behind, :]
        beside = beside + now[x + 1, ahead - 1 : behind - 1, :]
        beside = beside + now[x + 1, ahead + 1 : behind + 1, :]
        return update(now[x + 1, ahead:behind, :], old, s[x], beside)

    for x in range(cx):
        fresh = sweep(s0, q[x], x)
        s1[x + 1, ahead:behind, :] = fresh
        a, b = two_terms(fresh)
        rhs[x * cy : (x + 1) * cy, 0:LANES] = a
        rhs[x * cy : (x + 1) * cy, LANES : 2 * LANES] = b
    for x in range(cx):
        fresh = sweep(s1, p[x], x)
        out[x] = fresh
        a, b = two_terms(fresh)
        rhs[x * cy : (x + 1) * cy, 2 * LANES : 3 * LANES] = a
        rhs[x * cy : (x + 1) * cy, 3 * LANES : 4 * LANES] = b

    part1[...] = jnp.zeros(part1.shape, F32)
    part2[:, 0:SUB, :] = jnp.zeros((tall, SUB, LANES), F32)
    chunk = 256
    for first in range(0, tall * high, chunk):
        tile = lax.broadcasted_iota(jnp.int32, (chunk, LANES), 0) + first
        picks = []
        for piece in range(target.shape[0]):
            picks.append(jnp.where(tile == target[piece : piece + 1, :], 1.0, 0.0).astype(BF16))
        sums = jnp.dot(jnp.concatenate(picks, axis=1), rhs[...], preferred_element_type=F32)
        one = sums[:, 0:LANES] + sums[:, LANES : 2 * LANES]
        two = sums[:, 2 * LANES : 3 * LANES] + sums[:, 3 * LANES : 4 * LANES]
        l = first // high
        part1[1 + l : 1 + l + chunk // high, SUB : SUB + high, :] = one.reshape(-1, high, LANES)
        part2[l : l + chunk // high, SUB : SUB + high, :] = two.reshape(-1, high, LANES)
    lower = lax.broadcasted_iota(jnp.int32, (SUB, LANES), 0) < cols + 2
    for a in range(fx_count):
        for b in range(wy_count):
            for l in range(4):
                h = SUB + cols * b
                one = part1[2 * a + l, h - 1 : h - 1 + SUB, :]
                h = h + 2 * (l % 2) - 6
                two = part2[2 * a + l // 2, h : h + SUB, :]
                slots[a * wy_count + b, l * SUB : (l + 1) * SUB, :] = jnp.where(lower, one, two)


def grid_steps(p, q, s, wy_got, fx_got, target, fx_count, wy_count):
    cx, cy = p.shape[0], p.shape[1]
    tall, high = fx_count * 2, wy_count * 4
    devices = fx_count * wy_count
    return pl.pallas_call(
        grid_kernel,
        in_specs=[whole()] * 8,
        out_specs=[whole()] * 2,
        out_shape=[
            jax.ShapeDtypeStruct(p.shape, F32),
            vmem(devices, 4 * SUB, LANES),
        ],
        scratch_shapes=[
            pltpu.VMEM((cx + 2, cy + 2 * SUB, LANES), F32),
            pltpu.VMEM((cx + 2, cy + 2 * SUB, LANES), F32),
            pltpu.VMEM((cx * cy, 4 * LANES), BF16),
            pltpu.VMEM((tall + 2, high + 2 * SUB, LANES), F32),
            pltpu.VMEM((tall, high + 2 * SUB, LANES), F32),
        ],
        compiler_params=params(),
        name="grid_steps",
    )(p, q, s, *wy_got, *fx_got, target)


def reached(g):
    groups = []
    for dh in (-1, 0, 1):
        if (dh == -1 and g % 4 == 3) or (dh == 1 and g % 4 == 0):
            continue
        groups.append(dh)
    return groups


STORED = sum(len(reached(g)) for g in range(LANES // SUB))


def mid_rows(ref, c, l, h):
    rows = {}
    for dh in (-1, 0, 1):
        row = ref[c, l + 1, pl.ds(h + 1 + dh, 1), :]
        rows[dh] = jnp.broadcast_to(row, (SUB, LANES))
    return rows


def end_rows(ref, c, l, h, first_sub):
    rows = {}
    for dh in (-1, 0, 1):
        at = pl.ds(h + 1 + dh, 1)
        before = jnp.broadcast_to(ref[c, l, at, :], (SUB, LANES))
        after = jnp.broadcast_to(ref[c, l + 2, at, :], (SUB, LANES))
        rows[dh] = jnp.where(first_sub, before, after)
    return rows


def fill_y(pad, own, before, after, at):
    rows, cols = own.shape[1], own.shape[2]
    for c in range(3):
        for l in range(rows):
            row = at + c * rows + l
            pad[c, l + 1, 0:1, :] = before[row : row + 1]
            pad[c, l + 1, 1 : cols + 1, :] = own[c, l]
            pad[c, l + 1, cols + 1 : cols + 2, :] = after[row : row + 1]


def fill_x(pad, rows, cols, before, after, at):
    for c in range(3):
        row = at + c * (cols + 2)
        pad[c, 0, 0 : cols + 2, :] = before[row : row + cols + 2]
        pad[c, rows + 1, 0 : cols + 2, :] = after[row : row + cols + 2]


def lattice_rows():
    index = lax.broadcasted_iota(jnp.int32, (1, LANES), 1)
    places = (index % 8, index // 8 % 4, index // 32)
    return [v.astype(F32) * (1.0 / REACH) for v in places]


SPAN = 8.0 / REACH
RISE = 4.0 / REACH


def mine_columns(ref, lattice, l, h):
    sub = lax.broadcasted_iota(jnp.int32, (SUB, LANES), 0)
    own = []
    for c in range(3):
        row = ref[c, l + 1, pl.ds(h + 1, 1), :] * (1.0 / REACH) + lattice[c]
        own.append(jnp.broadcast_to(row, (SUB, LANES)))
    return jnp.transpose(jnp.where(sub == 0, own[0], jnp.where(sub == 1, own[1], own[2])))


def bond_row(weight, others, mine):
    for c in range(3):
        diff = others[c] - mine[c]
        weight = weight - diff * diff
    return jnp.maximum(weight, 0.0)


def tile_pass(l, h, columns, others, pulls, mask_at, weights, sums_in, acc):
    place = 0
    for g in range(LANES // SUB):
        span = slice(g * SUB, (g + 1) * SUB)
        mine = [jnp.broadcast_to(columns[span, c : c + 1], (SUB, LANES)) for c in range(3)]
        sums = [None if sums_in is None else sums_in[l, h, c, span, :] for c in range(4)]
        for dh in reached(g):
            here = [others[c][dh] for c in range(3)]
            weight = bond_row(mask_at(dh, span, place), here, mine)
            weights[l, h, place] = weight
            place += 1
            terms = [weight * pulls[c][dh] for c in range(3)] + [weight]
            sums = [t if v is None else v + t for v, t in zip(sums, terms)]
        for c in range(4):
            acc[l, h, c, span, :] = sums[c]


def lane_sums(acc, l, cols, count):
    ones = jnp.ones((2 * SUB, LANES), BF16)
    result = [[] for _ in range(count)]
    for h in range(cols):
        terms = []
        for c in range(count):
            terms.extend(two_terms(acc[l, h, c]))
        sums = lax.dot_general(
            ones,
            jnp.concatenate(terms, axis=0),
            (((1,), (1,)), ((), ())),
            preferred_element_type=F32,
        )[0:1]
        for c in range(count):
            at = 2 * c * LANES
            result[c].append(sums[:, at : at + LANES] + sums[:, at + LANES : at + 2 * LANES])
    return [jnp.concatenate(parts, axis=0) for parts in result]


def center_kernel(
    masks_in, p_in, q_in, s_in, wall, wye, wyo, weights, acc, end_masks, p, q, s,
    jpad, dpad, masks, sems,
):
    rows, cols = wall.shape[2], wall.shape[3]
    cx = p.shape[0]
    copies = {}
    for k, pair in enumerate(((p_in, p), (q_in, q), (s_in, s))):
        copies[k] = pltpu.make_async_copy(*pair, sems.at[rows * cols + k])
    for h in range(cols):
        for l in range(rows):
            copies[l, h] = pltpu.make_async_copy(
                masks_in.at[l, h], masks.at[l, h], sems.at[l * cols + h]
            )
    for copy in copies.values():
        copy.start()
    first_sub = lax.broadcasted_iota(jnp.int32, (SUB, LANES), 0) < SUB // 2
    before, after = before_after(even_at("wy"), wye, wyo)
    fill_y(jpad, wall.at[0], before, after, 4 * cx)
    fill_y(dpad, wall.at[1], before, after, 4 * cx + 3 * rows)
    lattice = lattice_rows()

    def one_tile(l, h):
        columns = mine_columns(jpad, lattice, l, h)
        others = []
        for c in range(3):
            mid = mid_rows(jpad, c, l, h)
            for dh in (-1, 0, 1):
                mid[dh] = mid[dh] * (1.0 / REACH) + lattice[c]
                if c == 1:
                    mid[dh] = mid[dh] + RISE * dh
            others.append(mid)
        pulls = [mid_rows(dpad, c, l, h) for c in range(3)]

        def mask_at(dh, span, place):
            before = masks[l, h, 1 + dh, span, :]
            after = masks[l, h, 7 + dh, span, :]
            end_masks[l, h, place] = jnp.where(first_sub, before, after).astype(F32)
            return masks[l, h, 4 + dh, span, :].astype(F32)

        tile_pass(l, h, columns, others, pulls, mask_at, weights, None, acc)

    for h in range(cols):
        for l in range(rows):
            copies[l, h].wait()
            one_tile(l, h)
    for k in range(3):
        copies[k].wait()


def wall_center(masks, grids, wall, wy_got):
    rows, cols = wall.shape[2], wall.shape[3]
    stored = vmem(rows, cols, STORED, SUB, LANES)
    return pl.pallas_call(
        center_kernel,
        in_specs=[HBM] * 4 + [whole()] * 3,
        out_specs=[whole()] * 6,
        out_shape=[stored, vmem(rows, cols, 4, LANES, LANES), stored] + [vmem(*grids[0].shape)] * 3,
        scratch_shapes=[
            vmem(3, rows + 2, SUB, LANES),
            vmem(3, rows + 2, SUB, LANES),
            pltpu.VMEM(masks.shape, jnp.int32),
            pltpu.SemaphoreType.DMA((rows * cols + 3,)),
        ],
        compiler_params=params(),
        name="wall_center",
    )(*in_hbm(masks, *grids), wall, *wy_got)


def wall_kernel(
    cx, cy, wall, wye, wyo, fxe, fxo, part, end_masks, weights, vel1, base1, totals, to_even, to_odd,
    jpad, dpad, acc,
):
    rows, cols = wall.shape[2], wall.shape[3]
    first_sub = lax.broadcasted_iota(jnp.int32, (SUB, LANES), 0) < SUB // 2
    before, after = before_after(even_at("wy"), wye, wyo)
    fill_y(jpad, wall.at[0], before, after, 4 * cx)
    fill_y(dpad, wall.at[1], before, after, 4 * cx + 3 * rows)
    before, after = before_after(even_at("fx"), fxe, fxo)
    fill_x(jpad, rows, cols, before, after, 4 * cy)
    fill_x(dpad, rows, cols, before, after, 4 * cy + 3 * (cols + 2))
    lattice = lattice_rows()

    def one_tile(l, h):
        columns = mine_columns(jpad, lattice, l, h)
        others = []
        for c in range(3):
            ends = end_rows(jpad, c, l, h, first_sub)
            for dh in (-1, 0, 1):
                ends[dh] = ends[dh] * (1.0 / REACH) + lattice[c]
                if c == 0:
                    ends[dh] = ends[dh] + jnp.where(first_sub, -SPAN, SPAN)
                if c == 1:
                    ends[dh] = ends[dh] + RISE * dh
            others.append(ends)
        pulls = [end_rows(dpad, c, l, h, first_sub) for c in range(3)]

        def mask_at(dh, span, place):
            return end_masks[l, h, place]

        tile_pass(l, h, columns, others, pulls, mask_at, weights, part, acc)

    @pl.loop(0, cols)
    def _(h):
        for l in range(rows):
            one_tile(l, h)

    for l in range(rows):
        pulled = lane_sums(acc, l, cols, 4)
        totals[l] = pulled[3]
        for c in range(3):
            mine = wall[1, c, l]
            fresh = wall[2, c, l] + STIFFNESS * (pulled[c] - pulled[3] * mine)
            vel1[c, l] = fresh
            base1[c, l] = mine + fresh

    def edge(at):
        def write(out):
            for c in range(3):
                for k in range(rows):
                    out[c * rows + k : c * rows + k + 1, :] = base1[c, k, at : at + 1, :]
            for spare in range(3 * rows, out.shape[0]):
                out[spare : spare + 1, :] = jnp.zeros((1, LANES), F32)

        return write

    place_edges(even_at("wy"), edge(0), edge(cols - 1), to_even, to_odd)


def wall_first(cx, cy, wall, wy_got, fx_got, part, end_masks):
    rows, cols = wall.shape[2], wall.shape[3]
    edge = (pad8(3 * rows), LANES)
    field = vmem(*wall.shape[1:])
    return pl.pallas_call(
        functools.partial(wall_kernel, cx, cy),
        in_specs=[whole()] * 7,
        out_specs=[whole()] * 6,
        out_shape=[
            vmem(rows, cols, STORED, SUB, LANES),
            field,
            field,
            vmem(rows, cols, LANES),
            vmem(*edge),
            vmem(*edge),
        ],
        scratch_shapes=[
            pltpu.VMEM((3, rows + 2, SUB, LANES), F32),
            pltpu.VMEM((3, rows + 2, SUB, LANES), F32),
            pltpu.VMEM((rows, cols, 4, LANES, LANES), F32),
        ],
        compiler_params=params(),
        name="wall_first",
    )(wall, *wy_got, *fx_got, part, end_masks)


def pack_base_kernel(base1, got_even, got_odd, to_even, to_odd):
    rows, cols = base1.shape[1], base1.shape[2]
    before, after = before_after(even_at("wy"), got_even, got_odd)

    def edge(l):
        def write(out):
            at = 0
            for c in range(3):
                side = c * rows + l
                out[at : at + 1, :] = before[side : side + 1]
                out[at + 1 : at + 1 + cols, :] = base1[c, l]
                out[at + 1 + cols : at + 2 + cols, :] = after[side : side + 1]
                at += cols + 2
            for spare in range(at, out.shape[0]):
                out[spare : spare + 1, :] = jnp.zeros((1, LANES), F32)

        return write

    place_edges(even_at("fx"), edge(0), edge(rows - 1), to_even, to_odd)


def pack_base(base1, got):
    cols = base1.shape[2]
    out = vmem(pad8(3 * (cols + 2)), LANES)
    return pl.pallas_call(
        pack_base_kernel,
        in_specs=[whole()] * 3,
        out_specs=[whole()] * 2,
        out_shape=[out, out],
        compiler_params=params(),
        name="pack_base",
    )(base1, *got)


def last_kernel(
    weights, end_weights, got, base1, vel1, totals, wye, wyo, fxe, fxo, disp_out, vel_out,
    dpad, loads, acc,
):
    rows, cols = base1.shape[1], base1.shape[2]
    first_sub = lax.broadcasted_iota(jnp.int32, (SUB, LANES), 0) < SUB // 2
    before, after = before_after(even_at("wy"), wye, wyo)
    fill_y(dpad, base1, before, after, 0)
    before, after = before_after(even_at("fx"), fxe, fxo)
    fill_x(dpad, rows, cols, before, after, 0)
    total = got[0]
    for d in range(1, got.shape[0]):
        total = total + got[d]
    loads[...] = total
    for k in range(rows + 2):
        here = total[k * SUB : k * SUB + cols + 2, :]
        dpad[0, k, 0 : cols + 2, :] = dpad[0, k, 0 : cols + 2, :] + LOADING * here

    def one_tile(l, h):
        mids = [mid_rows(dpad, c, l, h) for c in range(3)]
        ends = [end_rows(dpad, c, l, h, first_sub) for c in range(3)]
        place = 0
        for g in range(LANES // SUB):
            sums = [None] * 3
            for dh in reached(g):
                for weight, pulls in (
                    (weights[l, h, place], mids), (end_weights[l, h, place], ends)
                ):
                    terms = [weight * pulls[c][dh] for c in range(3)]
                    sums = [t if v is None else v + t for v, t in zip(sums, terms)]
                place += 1
            for c in range(3):
                acc[l, h, c, g * SUB : (g + 1) * SUB, :] = sums[c]

    @pl.loop(0, cols)
    def _(h):
        for l in range(rows):
            one_tile(l, h)

    for l in range(rows):
        pulled = lane_sums(acc, l, cols, 3)
        for c in range(3):
            mine = dpad[c, l + 1, 1 : cols + 1, :]
            force = STIFFNESS * (pulled[c] - totals[l] * mine)
            if c == 0:
                at = (l + 1) * SUB + 1
                force = force + LOADING * loads[at : at + cols, :]
                for half in range(2):
                    at = (2 * l + half) * SUB + cols + 2
                    two = loads[at : at + 2, :]
                    span = slice(2 * half, 2 * half + 2)
                    fresh = vel1[c, l, span, :] + force[span] + LOADING * two
                    vel_out[c, l, span, :] = fresh
                    disp_out[c, l, span, :] = mine[span] + fresh
            else:
                fresh = vel1[c, l] + force
                vel_out[c, l] = fresh
                disp_out[c, l] = mine + fresh


def wall_last(weights, end_weights, got, base1, vel1, totals, wy_got, fx_got):
    rows, cols = base1.shape[1], base1.shape[2]
    return pl.pallas_call(
        last_kernel,
        in_specs=[whole()] * 10,
        out_specs=[whole()] * 2,
        out_shape=[jax.ShapeDtypeStruct(base1.shape, F32)] * 2,
        scratch_shapes=[
            pltpu.VMEM((3, rows + 2, SUB, LANES), F32),
            pltpu.VMEM((4 * SUB, LANES), F32),
            pltpu.VMEM((rows, cols, 3, LANES, LANES), F32),
        ],
        compiler_params=params(),
        name="wall_last",
    )(weights, end_weights, got, base1, vel1, totals, *wy_got, *fx_got)


def per_device(
    displacement,
    velocity,
    jitter,
    bond_masks,
    pressure,
    pressure_prev,
    speed_sq,
    route_device,
    route_tile,
):
    fx_count, wy_count = lax.axis_size("fx"), lax.axis_size("wy")
    cols = displacement.shape[2]
    device = route_device.reshape(-1, LANES)
    tile = route_tile.reshape(-1, LANES)
    length = (device // wy_count) * 2 + tile // cols
    height = (device % wy_count) * cols + tile % cols
    target = length * (wy_count * cols) + height

    cx, cy = pressure.shape[0], pressure.shape[1]
    rows = displacement.shape[1]
    *sends, part_even, part_odd, wall = pack_wy(
        pressure, pressure_prev, speed_sq, jitter, displacement, velocity
    )
    wy_got = exchange("wy", *sends)
    sends = pack_fx((cx, cy, rows, cols), (part_even, part_odd), wy_got)
    fx_got = exchange("fx", *sends)
    grids = (pressure, pressure_prev, speed_sq)
    weights, part, end_masks, *grids = wall_center(bond_masks, grids, wall, wy_got)
    pressure_out, slots = grid_steps(*grids, wy_got, fx_got, target, fx_count, wy_count)
    got = lax.all_to_all(slots, ("fx", "wy"), split_axis=0, concat_axis=0, tiled=True)
    end_weights, vel1, base1, totals, *sends = wall_first(
        cx, cy, wall, wy_got, fx_got, part, end_masks
    )
    base_wy = exchange("wy", *sends)
    sends = pack_base(base1, base_wy)
    base_fx = exchange("fx", *sends)
    disp_out, vel_out = wall_last(
        weights, end_weights, got, base1, vel1, totals, base_wy, base_fx
    )
    return (disp_out, vel_out, pressure_out)


def solution(mesh):
    placed = (
        P(None, "fx", "wy", None),
        P(None, "fx", "wy", None),
        P(None, "fx", "wy", None),
        P("fx", "wy", None, None, None),
        P("fx", "wy", None),
        P("fx", "wy", None),
        P("fx", "wy", None),
        P(("fx", "wy"), None),
        P(("fx", "wy")),
    )
    return jax.shard_map(
        per_device,
        mesh=mesh,
        in_specs=placed,
        out_specs=(P(None, "fx", "wy", None), P(None, "fx", "wy", None), P("fx", "wy", None)),
        check_vma=False,
    )
```

```python
import functools

import jax
import jax.numpy as jnp
from jax import lax
from jax.experimental import pallas as pl
from jax.experimental.pallas import tpu as pltpu
from jax.sharding import PartitionSpec as P

STIFFNESS = 0.02
LOADING = 0.05
REACH = 3.0
LANES = 128
SUB = 8
VMEM_BYTES = 32 * 1024 * 1024
HBM = pl.BlockSpec(memory_space=pltpu.HBM)

F32 = jnp.float32
BF16 = jnp.bfloat16


def whole():
    return pl.BlockSpec(memory_space=pltpu.VMEM)


def params():
    return pltpu.CompilerParams(vmem_limit_bytes=VMEM_BYTES)


def vmem(*shape):
    return pltpu.VMEM(shape, F32)


def even_at(axis):
    return lax.rem(lax.axis_index(axis), 2) == 0


def pair_list(count, first):
    pairs = []
    for low in range(first, count - 1, 2):
        pairs.extend([(low, low + 1), (low + 1, low)])
    return pairs


def exchange(axis, to_even, to_odd):
    count = lax.axis_size(axis)
    got_odd = lax.ppermute(to_odd, axis, pair_list(count, 1))
    got_even = lax.ppermute(to_even, axis, pair_list(count, 0))
    return got_even, got_odd


def place_edges(even, low, high, to_even, to_odd):
    @pl.when(even)
    def _():
        high(to_even)
        low(to_odd)

    @pl.when(jnp.logical_not(even))
    def _():
        low(to_even)
        high(to_odd)


def before_after(even, got_even, got_odd):
    a, b = got_even[...], got_odd[...]
    return jnp.where(even, b, a), jnp.where(even, a, b)


def pack_wy_kernel(
    p, q, s, jit_in, disp_in, vel_in, wy_even, wy_odd, fx_even, fx_odd, wall, edges, ends, sems
):
    cx, cy = p.shape[0], p.shape[1]
    rows, cols = jit_in.shape[1], jit_in.shape[2]
    pairs = []
    for k, field in enumerate((p, q, s)):
        for side, first in enumerate((0, cy - SUB)):
            pairs.append((field.at[:, first : first + SUB, :], edges.at[2 * k + side]))
    pairs.append((p.at[0:2], ends.at[0, 0:2]))
    pairs.append((p.at[cx - 2 : cx], ends.at[1, 0:2]))
    for k, field in enumerate((q, s)):
        pairs.append((field.at[0], ends.at[0, 2 + k]))
        pairs.append((field.at[cx - 1], ends.at[1, 2 + k]))
    for k, field in enumerate((jit_in, disp_in, vel_in)):
        pairs.append((field, wall.at[k]))
    copies = [pltpu.make_async_copy(a, b, sems.at[k]) for k, (a, b) in enumerate(pairs)]
    for copy in copies:
        copy.start()
    for copy in copies:
        copy.wait()

    def edge(side, near, far, h):
        def write(out):
            out[0:cx, :] = edges[side, :, near, :]
            out[cx : 2 * cx, :] = edges[side, :, far, :]
            out[2 * cx : 3 * cx, :] = edges[2 + side, :, near, :]
            out[3 * cx : 4 * cx, :] = edges[4 + side, :, near, :]
            at = 4 * cx
            for field in range(2):
                for c in range(3):
                    for l in range(rows):
                        out[at : at + 1, :] = wall[field, c, l, h : h + 1, :]
                        at += 1
            for spare in range(at, out.shape[0]):
                out[spare : spare + 1, :] = jnp.zeros((1, LANES), F32)

        return write

    place_edges(
        even_at("wy"),
        edge(0, 0, 1, 0),
        edge(1, SUB - 1, SUB - 2, cols - 1),
        wy_even,
        wy_odd,
    )

    def end(side, near, far, l):
        def write(out):
            out[0:cy, :] = ends[side, near]
            out[cy : 2 * cy, :] = ends[side, far]
            out[2 * cy : 3 * cy, :] = ends[side, 2]
            out[3 * cy : 4 * cy, :] = ends[side, 3]
            at = 4 * cy
            for field in range(2):
                for c in range(3):
                    out[at + 1 : at + 1 + cols, :] = wall[field, c, l]
                    at += cols + 2

        return write

    place_edges(even_at("fx"), end(0, 0, 1, 0), end(1, 1, 0, rows - 1), fx_even, fx_odd)


def in_hbm(*arrays):
    return [pltpu.with_memory_space_constraint(v, pltpu.HBM) for v in arrays]


def pad8(count):
    return (count + 7) // 8 * 8


def pack_wy(p, q, s, jit, disp, vel):
    cx, cy = p.shape[0], p.shape[1]
    rows, cols = jit.shape[1], jit.shape[2]
    wy_out = vmem(pad8(4 * cx + 6 * rows), LANES)
    fx_out = vmem(pad8(4 * cy + 6 * (cols + 2) + 2), LANES)
    return pl.pallas_call(
        pack_wy_kernel,
        in_specs=[HBM] * 6,
        out_specs=[whole()] * 5,
        out_shape=[wy_out, wy_out, fx_out, fx_out, vmem(3, *jit.shape)],
        scratch_shapes=[
            pltpu.VMEM((6, cx, SUB, LANES), F32),
            pltpu.VMEM((2, 4, cy, LANES), F32),
            pltpu.SemaphoreType.DMA((15,)),
        ],
        compiler_params=params(),
        name="pack_wy",
    )(*in_hbm(p, q, s, jit, disp, vel))


def pack_fx_kernel(cx, cy, rows, cols, part_even, part_odd, got_even, got_odd, to_even, to_odd):
    before, after = before_after(even_at("wy"), got_even, got_odd)
    to_even[...] = part_even[...]
    to_odd[...] = part_odd[...]

    def corners(x, l):
        def write(out):
            at = 4 * cy
            for k in range(6):
                side = 4 * cx + k * rows + l
                out[at : at + 1, :] = before[side : side + 1]
                out[at + 1 + cols : at + 2 + cols, :] = after[side : side + 1]
                at += cols + 2
            out[at : at + 1, :] = before[x : x + 1]
            out[at + 1 : at + 2, :] = after[x : x + 1]

        return write

    place_edges(even_at("fx"), corners(0, 0), corners(cx - 1, rows - 1), to_even, to_odd)


def pack_fx(sizes, parts, got):
    out = vmem(*parts[0].shape)
    return pl.pallas_call(
        functools.partial(pack_fx_kernel, *sizes),
        in_specs=[whole()] * 4,
        out_specs=[whole()] * 2,
        out_shape=[out, out],
        compiler_params=params(),
        name="pack_fx",
    )(*parts, *got)


def along_z(v):
    lane = lax.broadcasted_iota(jnp.int32, v.shape, 1)
    up = jnp.where(lane == LANES - 1, 0.0, pltpu.roll(v, LANES - 1, 1))
    down = jnp.where(lane == 0, 0.0, pltpu.roll(v, 1, 1))
    return up + down


def update(v, old, speed, beside):
    return 2.0 * v - old + speed * (beside + along_z(v) - 6.0 * v)


def two_terms(v):
    high = v.astype(BF16)
    return high, (v - high.astype(F32)).astype(BF16)


def grid_kernel(p, q, s, wye, wyo, fxe, fxo, target, out, slots, s0, s1, rhs, part1, part2):
    cx, cy = p.shape[0], p.shape[1]
    ahead, behind = SUB, SUB + cy
    fx_count = part1.shape[0] // 2 - 1
    cols = 4
    tall = part2.shape[0]
    high = part1.shape[1] - 2 * SUB
    wy_count = high // cols
    before_y, after_y = before_after(even_at("wy"), wye, wyo)
    before_x, after_x = before_after(even_at("fx"), fxe, fxo)
    corner = 4 * cy + 6 * (cols + 2)

    s0[1 : cx + 1, ahead:behind, :] = p[...]
    for x, side in ((0, before_x), (cx + 1, after_x)):
        s0[x, ahead:behind, :] = side[0:cy]
        s0[x, ahead - 1 : ahead, :] = side[corner : corner + 1]
        s0[x, behind : behind + 1, :] = side[corner + 1 : corner + 2]
    s0[1 : cx + 1, ahead - 1, :] = before_y[0:cx]
    s0[1 : cx + 1, behind, :] = after_y[0:cx]

    for side, y, inner in ((before_y, ahead - 1, ahead), (after_y, behind, behind - 1)):
        near, far = side[0:cx], side[cx : 2 * cx]
        old, speed = side[2 * cx : 3 * cx], side[3 * cx : 4 * cx]
        beside = s0[0:cx, y, :] + s0[2 : cx + 2, y, :] + far + s0[1 : cx + 1, inner, :]
        s1[1 : cx + 1, y, :] = update(near, old, speed, beside)
    for side, x, inner in ((before_x, 0, 1), (after_x, cx + 1, cx)):
        near, far = side[0:cy], side[cy : 2 * cy]
        old, speed = side[2 * cy : 3 * cy], side[3 * cy : 4 * cy]
        beside = s0[x, ahead - 1 : behind - 1, :] + s0[x, ahead + 1 : behind + 1, :]
        beside = beside + far + s0[inner, ahead:behind, :]
        s1[x, ahead:behind, :] = update(near, old, speed, beside)

    def sweep(now, old, x):
        beside = now[x, ahead:behind, :] + now[x + 2, ahead:behind, :]
        beside = beside + now[x + 1, ahead - 1 : behind - 1, :]
        beside = beside + now[x + 1, ahead + 1 : behind + 1, :]
        return update(now[x + 1, ahead:behind, :], old, s[x], beside)

    for x in range(cx):
        fresh = sweep(s0, q[x], x)
        s1[x + 1, ahead:behind, :] = fresh
        a, b = two_terms(fresh)
        rhs[x * cy : (x + 1) * cy, 0:LANES] = a
        rhs[x * cy : (x + 1) * cy, LANES : 2 * LANES] = b
    for x in range(cx):
        fresh = sweep(s1, p[x], x)
        out[x] = fresh
        a, b = two_terms(fresh)
        rhs[x * cy : (x + 1) * cy, 2 * LANES : 3 * LANES] = a
        rhs[x * cy : (x + 1) * cy, 3 * LANES : 4 * LANES] = b

    part1[...] = jnp.zeros(part1.shape, F32)
    part2[:, 0:SUB, :] = jnp.zeros((tall, SUB, LANES), F32)
    chunk = 256
    for first in range(0, tall * high, chunk):
        tile = lax.broadcasted_iota(jnp.int32, (chunk, LANES), 0) + first
        picks = []
        for piece in range(target.shape[0]):
            picks.append(jnp.where(tile == target[piece : piece + 1, :], 1.0, 0.0).astype(BF16))
        sums = jnp.dot(jnp.concatenate(picks, axis=1), rhs[...], preferred_element_type=F32)
        one = sums[:, 0:LANES] + sums[:, LANES : 2 * LANES]
        two = sums[:, 2 * LANES : 3 * LANES] + sums[:, 3 * LANES : 4 * LANES]
        l = first // high
        part1[1 + l : 1 + l + chunk // high, SUB : SUB + high, :] = one.reshape(-1, high, LANES)
        part2[l : l + chunk // high, SUB : SUB + high, :] = two.reshape(-1, high, LANES)
    lower = lax.broadcasted_iota(jnp.int32, (SUB, LANES), 0) < cols + 2
    for a in range(fx_count):
        for b in range(wy_count):
            for l in range(4):
                h = SUB + cols * b
                one = part1[2 * a + l, h - 1 : h - 1 + SUB, :]
                h = h + 2 * (l % 2) - 6
                two = part2[2 * a + l // 2, h : h + SUB, :]
                slots[a * wy_count + b, l * SUB : (l + 1) * SUB, :] = jnp.where(lower, one, two)


def grid_steps(p, q, s, wy_got, fx_got, target, fx_count, wy_count):
    cx, cy = p.shape[0], p.shape[1]
    tall, high = fx_count * 2, wy_count * 4
    devices = fx_count * wy_count
    return pl.pallas_call(
        grid_kernel,
        in_specs=[whole()] * 8,
        out_specs=[whole()] * 2,
        out_shape=[
            jax.ShapeDtypeStruct(p.shape, F32),
            vmem(devices, 4 * SUB, LANES),
        ],
        scratch_shapes=[
            pltpu.VMEM((cx + 2, cy + 2 * SUB, LANES), F32),
            pltpu.VMEM((cx + 2, cy + 2 * SUB, LANES), F32),
            pltpu.VMEM((cx * cy, 4 * LANES), BF16),
            pltpu.VMEM((tall + 2, high + 2 * SUB, LANES), F32),
            pltpu.VMEM((tall, high + 2 * SUB, LANES), F32),
        ],
        compiler_params=params(),
        name="grid_steps",
    )(p, q, s, *wy_got, *fx_got, target)


def reached(g):
    groups = []
    for dh in (-1, 0, 1):
        if (dh == -1 and g % 4 == 3) or (dh == 1 and g % 4 == 0):
            continue
        groups.append(dh)
    return groups


STORED = sum(len(reached(g)) for g in range(LANES // SUB))


def mid_rows(ref, c, l, h):
    rows = {}
    for dh in (-1, 0, 1):
        row = ref[c, l + 1, pl.ds(h + 1 + dh, 1), :]
        rows[dh] = jnp.broadcast_to(row, (SUB, LANES))
    return rows


def end_rows(ref, c, l, h, first_sub):
    rows = {}
    for dh in (-1, 0, 1):
        at = pl.ds(h + 1 + dh, 1)
        before = jnp.broadcast_to(ref[c, l, at, :], (SUB, LANES))
        after = jnp.broadcast_to(ref[c, l + 2, at, :], (SUB, LANES))
        rows[dh] = jnp.where(first_sub, before, after)
    return rows


def fill_y(pad, own, before, after, at):
    rows, cols = own.shape[1], own.shape[2]
    for c in range(3):
        for l in range(rows):
            row = at + c * rows + l
            pad[c, l + 1, 0:1, :] = before[row : row + 1]
            pad[c, l + 1, 1 : cols + 1, :] = own[c, l]
            pad[c, l + 1, cols + 1 : cols + 2, :] = after[row : row + 1]


def fill_x(pad, rows, cols, before, after, at):
    for c in range(3):
        row = at + c * (cols + 2)
        pad[c, 0, 0 : cols + 2, :] = before[row : row + cols + 2]
        pad[c, rows + 1, 0 : cols + 2, :] = after[row : row + cols + 2]


def lattice_rows():
    index = lax.broadcasted_iota(jnp.int32, (1, LANES), 1)
    places = (index % 8, index // 8 % 4, index // 32)
    return [v.astype(F32) * (1.0 / REACH) for v in places]


SPAN = 8.0 / REACH
RISE = 4.0 / REACH


def mine_columns(ref, lattice, l, h):
    sub = lax.broadcasted_iota(jnp.int32, (SUB, LANES), 0)
    own = []
    for c in range(3):
        row = ref[c, l + 1, pl.ds(h + 1, 1), :] * (1.0 / REACH) + lattice[c]
        own.append(jnp.broadcast_to(row, (SUB, LANES)))
    return jnp.transpose(jnp.where(sub == 0, own[0], jnp.where(sub == 1, own[1], own[2])))


def bond_row(weight, others, mine):
    for c in range(3):
        diff = others[c] - mine[c]
        weight = weight - diff * diff
    return jnp.maximum(weight, 0.0)


def tile_pass(l, h, columns, others, pulls, mask_at, weights, sums_in, acc):
    place = 0
    for g in range(LANES // SUB):
        span = slice(g * SUB, (g + 1) * SUB)
        mine = [jnp.broadcast_to(columns[span, c : c + 1], (SUB, LANES)) for c in range(3)]
        sums = [None if sums_in is None else sums_in[l, h, c, span, :] for c in range(4)]
        for dh in reached(g):
            here = [others[c][dh] for c in range(3)]
            weight = bond_row(mask_at(dh, span, place), here, mine)
            weights[l, h, place] = weight
            place += 1
            terms = [weight * pulls[c][dh] for c in range(3)] + [weight]
            sums = [t if v is None else v + t for v, t in zip(sums, terms)]
        for c in range(4):
            acc[l, h, c, span, :] = sums[c]


def lane_sums(acc, l, cols, count):
    ones = jnp.ones((2 * SUB, LANES), BF16)
    result = [[] for _ in range(count)]
    for h in range(cols):
        terms = []
        for c in range(count):
            terms.extend(two_terms(acc[l, h, c]))
        sums = lax.dot_general(
            ones,
            jnp.concatenate(terms, axis=0),
            (((1,), (1,)), ((), ())),
            preferred_element_type=F32,
        )[0:1]
        for c in range(count):
            at = 2 * c * LANES
            result[c].append(sums[:, at : at + LANES] + sums[:, at + LANES : at + 2 * LANES])
    return [jnp.concatenate(parts, axis=0) for parts in result]


def center_kernel(
    masks_in, p_in, q_in, s_in, wall, wye, wyo, weights, acc, end_masks, p, q, s,
    jpad, dpad, masks, sems,
):
    rows, cols = wall.shape[2], wall.shape[3]
    cx = p.shape[0]
    copies = {}
    for k, pair in enumerate(((p_in, p), (q_in, q), (s_in, s))):
        copies[k] = pltpu.make_async_copy(*pair, sems.at[rows * cols + k])
    for h in range(cols):
        for l in range(rows):
            copies[l, h] = pltpu.make_async_copy(
                masks_in.at[l, h], masks.at[l, h], sems.at[l * cols + h]
            )
    for copy in copies.values():
        copy.start()
    first_sub = lax.broadcasted_iota(jnp.int32, (SUB, LANES), 0) < SUB // 2
    before, after = before_after(even_at("wy"), wye, wyo)
    fill_y(jpad, wall.at[0], before, after, 4 * cx)
    fill_y(dpad, wall.at[1], before, after, 4 * cx + 3 * rows)
    lattice = lattice_rows()

    def one_tile(l, h):
        columns = mine_columns(jpad, lattice, l, h)
        others = []
        for c in range(3):
            mid = mid_rows(jpad, c, l, h)
            for dh in (-1, 0, 1):
                mid[dh] = mid[dh] * (1.0 / REACH) + lattice[c]
                if c == 1:
                    mid[dh] = mid[dh] + RISE * dh
            others.append(mid)
        pulls = [mid_rows(dpad, c, l, h) for c in range(3)]

        def mask_at(dh, span, place):
            before = masks[l, h, 1 + dh, span, :]
            after = masks[l, h, 7 + dh, span, :]
            end_masks[l, h, place] = jnp.where(first_sub, before, after).astype(F32)
            return masks[l, h, 4 + dh, span, :].astype(F32)

        tile_pass(l, h, columns, others, pulls, mask_at, weights, None, acc)

    for h in range(cols):
        for l in range(rows):
            copies[l, h].wait()
            one_tile(l, h)
    for k in range(3):
        copies[k].wait()


def wall_center(masks, grids, wall, wy_got):
    rows, cols = wall.shape[2], wall.shape[3]
    stored = jax.ShapeDtypeStruct((rows, cols, STORED, SUB, LANES), F32)
    sums = jax.ShapeDtypeStruct((rows, cols, 4, LANES, LANES), F32)
    return pl.pallas_call(
        center_kernel,
        in_specs=[HBM] * 4 + [whole()] * 3,
        out_specs=[whole()] * 6,
        out_shape=[stored, sums, stored] + [vmem(*grids[0].shape)] * 3,
        scratch_shapes=[
            vmem(3, rows + 2, SUB, LANES),
            vmem(3, rows + 2, SUB, LANES),
            pltpu.VMEM(masks.shape, jnp.int32),
            pltpu.SemaphoreType.DMA((rows * cols + 3,)),
        ],
        compiler_params=params(),
        name="wall_center",
    )(*in_hbm(masks, *grids), wall, *wy_got)


def wall_kernel(
    cx, cy, wall, wye, wyo, fxe, fxo, part, end_masks, weights, vel1, base1, totals, to_even, to_odd,
    jpad, dpad, acc,
):
    rows, cols = wall.shape[2], wall.shape[3]
    first_sub = lax.broadcasted_iota(jnp.int32, (SUB, LANES), 0) < SUB // 2
    before, after = before_after(even_at("wy"), wye, wyo)
    fill_y(jpad, wall.at[0], before, after, 4 * cx)
    fill_y(dpad, wall.at[1], before, after, 4 * cx + 3 * rows)
    before, after = before_after(even_at("fx"), fxe, fxo)
    fill_x(jpad, rows, cols, before, after, 4 * cy)
    fill_x(dpad, rows, cols, before, after, 4 * cy + 3 * (cols + 2))
    lattice = lattice_rows()

    def one_tile(l, h):
        columns = mine_columns(jpad, lattice, l, h)
        others = []
        for c in range(3):
            ends = end_rows(jpad, c, l, h, first_sub)
            for dh in (-1, 0, 1):
                ends[dh] = ends[dh] * (1.0 / REACH) + lattice[c]
                if c == 0:
                    ends[dh] = ends[dh] + jnp.where(first_sub, -SPAN, SPAN)
                if c == 1:
                    ends[dh] = ends[dh] + RISE * dh
            others.append(ends)
        pulls = [end_rows(dpad, c, l, h, first_sub) for c in range(3)]

        def mask_at(dh, span, place):
            return end_masks[l, h, place]

        tile_pass(l, h, columns, others, pulls, mask_at, weights, part, acc)

    @pl.loop(0, cols)
    def _(h):
        for l in range(rows):
            one_tile(l, h)

    for l in range(rows):
        pulled = lane_sums(acc, l, cols, 4)
        totals[l] = pulled[3]
        for c in range(3):
            mine = wall[1, c, l]
            fresh = wall[2, c, l] + STIFFNESS * (pulled[c] - pulled[3] * mine)
            vel1[c, l] = fresh
            base1[c, l] = mine + fresh

    def edge(at):
        def write(out):
            for c in range(3):
                for k in range(rows):
                    out[c * rows + k : c * rows + k + 1, :] = base1[c, k, at : at + 1, :]
            for spare in range(3 * rows, out.shape[0]):
                out[spare : spare + 1, :] = jnp.zeros((1, LANES), F32)

        return write

    place_edges(even_at("wy"), edge(0), edge(cols - 1), to_even, to_odd)


def wall_first(cx, cy, wall, wy_got, fx_got, part, end_masks):
    rows, cols = wall.shape[2], wall.shape[3]
    edge = (pad8(3 * rows), LANES)
    field = vmem(*wall.shape[1:])
    return pl.pallas_call(
        functools.partial(wall_kernel, cx, cy),
        in_specs=[whole()] * 7,
        out_specs=[whole()] * 6,
        out_shape=[
            jax.ShapeDtypeStruct((rows, cols, STORED, SUB, LANES), F32),
            field,
            field,
            vmem(rows, cols, LANES),
            vmem(*edge),
            vmem(*edge),
        ],
        scratch_shapes=[
            pltpu.VMEM((3, rows + 2, SUB, LANES), F32),
            pltpu.VMEM((3, rows + 2, SUB, LANES), F32),
            pltpu.VMEM((rows, cols, 4, LANES, LANES), F32),
        ],
        compiler_params=params(),
        name="wall_first",
    )(wall, *wy_got, *fx_got, part, end_masks)


def pack_base_kernel(base1, got_even, got_odd, to_even, to_odd):
    rows, cols = base1.shape[1], base1.shape[2]
    before, after = before_after(even_at("wy"), got_even, got_odd)

    def edge(l):
        def write(out):
            at = 0
            for c in range(3):
                side = c * rows + l
                out[at : at + 1, :] = before[side : side + 1]
                out[at + 1 : at + 1 + cols, :] = base1[c, l]
                out[at + 1 + cols : at + 2 + cols, :] = after[side : side + 1]
                at += cols + 2
            for spare in range(at, out.shape[0]):
                out[spare : spare + 1, :] = jnp.zeros((1, LANES), F32)

        return write

    place_edges(even_at("fx"), edge(0), edge(rows - 1), to_even, to_odd)


def pack_base(base1, got):
    cols = base1.shape[2]
    out = vmem(pad8(3 * (cols + 2)), LANES)
    return pl.pallas_call(
        pack_base_kernel,
        in_specs=[whole()] * 3,
        out_specs=[whole()] * 2,
        out_shape=[out, out],
        compiler_params=params(),
        name="pack_base",
    )(base1, *got)


def last_kernel(
    weights, end_weights, got, base1, vel1, totals, wye, wyo, fxe, fxo, disp_out, vel_out,
    dpad, loads, acc,
):
    rows, cols = base1.shape[1], base1.shape[2]
    first_sub = lax.broadcasted_iota(jnp.int32, (SUB, LANES), 0) < SUB // 2
    before, after = before_after(even_at("wy"), wye, wyo)
    fill_y(dpad, base1, before, after, 0)
    before, after = before_after(even_at("fx"), fxe, fxo)
    fill_x(dpad, rows, cols, before, after, 0)
    total = got[0]
    for d in range(1, got.shape[0]):
        total = total + got[d]
    loads[...] = total
    for k in range(rows + 2):
        here = total[k * SUB : k * SUB + cols + 2, :]
        dpad[0, k, 0 : cols + 2, :] = dpad[0, k, 0 : cols + 2, :] + LOADING * here

    def one_tile(l, h):
        mids = [mid_rows(dpad, c, l, h) for c in range(3)]
        ends = [end_rows(dpad, c, l, h, first_sub) for c in range(3)]
        place = 0
        for g in range(LANES // SUB):
            sums = [None] * 3
            for dh in reached(g):
                for weight, pulls in (
                    (weights[l, h, place], mids), (end_weights[l, h, place], ends)
                ):
                    terms = [weight * pulls[c][dh] for c in range(3)]
                    sums = [t if v is None else v + t for v, t in zip(sums, terms)]
                place += 1
            for c in range(3):
                acc[l, h, c, g * SUB : (g + 1) * SUB, :] = sums[c]

    @pl.loop(0, cols)
    def _(h):
        for l in range(rows):
            one_tile(l, h)

    for l in range(rows):
        pulled = lane_sums(acc, l, cols, 3)
        for c in range(3):
            mine = dpad[c, l + 1, 1 : cols + 1, :]
            force = STIFFNESS * (pulled[c] - totals[l] * mine)
            if c == 0:
                at = (l + 1) * SUB + 1
                force = force + LOADING * loads[at : at + cols, :]
                for half in range(2):
                    at = (2 * l + half) * SUB + cols + 2
                    two = loads[at : at + 2, :]
                    span = slice(2 * half, 2 * half + 2)
                    fresh = vel1[c, l, span, :] + force[span] + LOADING * two
                    vel_out[c, l, span, :] = fresh
                    disp_out[c, l, span, :] = mine[span] + fresh
            else:
                fresh = vel1[c, l] + force
                vel_out[c, l] = fresh
                disp_out[c, l] = mine + fresh


def wall_last(weights, end_weights, got, base1, vel1, totals, wy_got, fx_got):
    rows, cols = base1.shape[1], base1.shape[2]
    return pl.pallas_call(
        last_kernel,
        in_specs=[whole()] * 10,
        out_specs=[whole()] * 2,
        out_shape=[jax.ShapeDtypeStruct(base1.shape, F32)] * 2,
        scratch_shapes=[
            pltpu.VMEM((3, rows + 2, SUB, LANES), F32),
            pltpu.VMEM((4 * SUB, LANES), F32),
            pltpu.VMEM((rows, cols, 3, LANES, LANES), F32),
        ],
        compiler_params=params(),
        name="wall_last",
    )(weights, end_weights, got, base1, vel1, totals, *wy_got, *fx_got)


def per_device(
    displacement,
    velocity,
    jitter,
    bond_masks,
    pressure,
    pressure_prev,
    speed_sq,
    route_device,
    route_tile,
):
    fx_count, wy_count = lax.axis_size("fx"), lax.axis_size("wy")
    cols = displacement.shape[2]
    device = route_device.reshape(-1, LANES)
    tile = route_tile.reshape(-1, LANES)
    length = (device // wy_count) * 2 + tile // cols
    height = (device % wy_count) * cols + tile % cols
    target = length * (wy_count * cols) + height

    cx, cy = pressure.shape[0], pressure.shape[1]
    rows = displacement.shape[1]
    *sends, part_even, part_odd, wall = pack_wy(
        pressure, pressure_prev, speed_sq, jitter, displacement, velocity
    )
    wy_got = exchange("wy", *sends)
    sends = pack_fx((cx, cy, rows, cols), (part_even, part_odd), wy_got)
    fx_got = exchange("fx", *sends)
    grids = (pressure, pressure_prev, speed_sq)
    weights, part, end_masks, *grids = wall_center(bond_masks, grids, wall, wy_got)
    pressure_out, slots = grid_steps(*grids, wy_got, fx_got, target, fx_count, wy_count)
    got = lax.all_to_all(slots, ("fx", "wy"), split_axis=0, concat_axis=0, tiled=True)
    end_weights, vel1, base1, totals, *sends = wall_first(
        cx, cy, wall, wy_got, fx_got, part, end_masks
    )
    base_wy = exchange("wy", *sends)
    sends = pack_base(base1, base_wy)
    base_fx = exchange("fx", *sends)
    disp_out, vel_out = wall_last(
        weights, end_weights, got, base1, vel1, totals, base_wy, base_fx
    )
    return (disp_out, vel_out, pressure_out)


def solution(mesh):
    placed = (
        P(None, "fx", "wy", None),
        P(None, "fx", "wy", None),
        P(None, "fx", "wy", None),
        P("fx", "wy", None, None, None),
        P("fx", "wy", None),
        P("fx", "wy", None),
        P("fx", "wy", None),
        P(("fx", "wy"), None),
        P(("fx", "wy")),
    )
    return jax.shard_map(
        per_device,
        mesh=mesh,
        in_specs=placed,
        out_specs=(P(None, "fx", "wy", None), P(None, "fx", "wy", None), P("fx", "wy", None)),
        check_vma=False,
    )
```

```python
import functools

import jax
import jax.numpy as jnp
from jax import lax
from jax.experimental import pallas as pl
from jax.experimental.pallas import tpu as pltpu
from jax.sharding import PartitionSpec as P

STIFFNESS = 0.02
LOADING = 0.05
REACH = 3.0
LANES = 128
SUB = 8
VMEM_BYTES = 32 * 1024 * 1024
HBM = pl.BlockSpec(memory_space=pltpu.HBM)

F32 = jnp.float32
BF16 = jnp.bfloat16


def whole():
    return pl.BlockSpec(memory_space=pltpu.VMEM)


def params():
    return pltpu.CompilerParams(vmem_limit_bytes=VMEM_BYTES)


def vmem(*shape):
    return pltpu.VMEM(shape, F32)


def even_at(axis):
    return lax.rem(lax.axis_index(axis), 2) == 0


def pair_list(count, first):
    pairs = []
    for low in range(first, count - 1, 2):
        pairs.extend([(low, low + 1), (low + 1, low)])
    return pairs


def exchange(axis, to_odd, to_even):
    count = lax.axis_size(axis)
    got_odd = lax.ppermute(to_odd, axis, pair_list(count, 1))
    got_even = lax.ppermute(to_even, axis, pair_list(count, 0))
    return got_odd, got_even


def place_edges(even, low, high, to_even, to_odd):
    @pl.when(even)
    def _():
        high(to_even)
        low(to_odd)

    @pl.when(jnp.logical_not(even))
    def _():
        low(to_even)
        high(to_odd)


def before_after(even, got_even, got_odd):
    a, b = got_even[...], got_odd[...]
    return jnp.where(even, b, a), jnp.where(even, a, b)


def pack_wy_kernel(
    p, q, s, jit_in, disp_in, vel_in, wy_odd, wy_even, fx_odd, fx_even, wall, edges, ends, sems
):
    cx, cy = p.shape[0], p.shape[1]
    rows, cols = jit_in.shape[1], jit_in.shape[2]
    pairs = []
    for k, field in enumerate((p, q, s)):
        for side, first in enumerate((0, cy - SUB)):
            pairs.append((field.at[:, first : first + SUB, :], edges.at[2 * k + side]))
    pairs.append((p.at[0:2], ends.at[0, 0:2]))
    pairs.append((p.at[cx - 2 : cx], ends.at[1, 0:2]))
    for k, field in enumerate((q, s)):
        pairs.append((field.at[0], ends.at[0, 2 + k]))
        pairs.append((field.at[cx - 1], ends.at[1, 2 + k]))
    for k, field in enumerate((jit_in, disp_in, vel_in)):
        pairs.append((field, wall.at[k]))
    copies = [pltpu.make_async_copy(a, b, sems.at[k]) for k, (a, b) in enumerate(pairs)]
    for copy in copies:
        copy.start()
    for copy in copies:
        copy.wait()

    def edge(side, near, far, h):
        def write(out):
            out[0:cx, :] = edges[side, :, near, :]
            out[cx : 2 * cx, :] = edges[side, :, far, :]
            out[2 * cx : 3 * cx, :] = edges[2 + side, :, near, :]
            out[3 * cx : 4 * cx, :] = edges[4 + side, :, near, :]
            at = 4 * cx
            for field in range(2):
                for c in range(3):
                    for l in range(rows):
                        out[at : at + 1, :] = wall[field, c, l, h : h + 1, :]
                        at += 1
            for spare in range(at, out.shape[0]):
                out[spare : spare + 1, :] = jnp.zeros((1, LANES), F32)

        return write

    place_edges(
        even_at("wy"),
        edge(0, 0, 1, 0),
        edge(1, SUB - 1, SUB - 2, cols - 1),
        wy_even,
        wy_odd,
    )

    def end(side, near, far, l):
        def write(out):
            out[0:cy, :] = ends[side, near]
            out[cy : 2 * cy, :] = ends[side, far]
            out[2 * cy : 3 * cy, :] = ends[side, 2]
            out[3 * cy : 4 * cy, :] = ends[side, 3]
            at = 4 * cy
            for field in range(2):
                for c in range(3):
                    out[at + 1 : at + 1 + cols, :] = wall[field, c, l]
                    at += cols + 2

        return write

    place_edges(even_at("fx"), end(0, 0, 1, 0), end(1, 1, 0, rows - 1), fx_even, fx_odd)


def in_hbm(*arrays):
    return [pltpu.with_memory_space_constraint(v, pltpu.HBM) for v in arrays]


def pad8(count):
    return (count + 7) // 8 * 8


def pack_wy(p, q, s, jit, disp, vel):
    cx, cy = p.shape[0], p.shape[1]
    rows, cols = jit.shape[1], jit.shape[2]
    wy_out = vmem(pad8(4 * cx + 6 * rows), LANES)
    fx_out = vmem(pad8(4 * cy + 6 * (cols + 2) + 2), LANES)
    return pl.pallas_call(
        pack_wy_kernel,
        in_specs=[HBM] * 6,
        out_specs=[whole()] * 5,
        out_shape=[wy_out, wy_out, fx_out, fx_out, vmem(3, *jit.shape)],
        scratch_shapes=[
            pltpu.VMEM((6, cx, SUB, LANES), F32),
            pltpu.VMEM((2, 4, cy, LANES), F32),
            pltpu.SemaphoreType.DMA((15,)),
        ],
        compiler_params=params(),
        name="pack_wy",
    )(*in_hbm(p, q, s, jit, disp, vel))


def pack_fx_kernel(cx, cy, rows, cols, part_odd, part_even, got_odd, got_even, to_odd, to_even):
    before, after = before_after(even_at("wy"), got_even, got_odd)
    to_even[...] = part_even[...]
    to_odd[...] = part_odd[...]

    def corners(x, l):
        def write(out):
            at = 4 * cy
            for k in range(6):
                side = 4 * cx + k * rows + l
                out[at : at + 1, :] = before[side : side + 1]
                out[at + 1 + cols : at + 2 + cols, :] = after[side : side + 1]
                at += cols + 2
            out[at : at + 1, :] = before[x : x + 1]
            out[at + 1 : at + 2, :] = after[x : x + 1]

        return write

    place_edges(even_at("fx"), corners(0, 0), corners(cx - 1, rows - 1), to_even, to_odd)


def pack_fx(sizes, parts, got):
    out = vmem(*parts[0].shape)
    return pl.pallas_call(
        functools.partial(pack_fx_kernel, *sizes),
        in_specs=[whole()] * 4,
        out_specs=[whole()] * 2,
        out_shape=[out, out],
        compiler_params=params(),
        name="pack_fx",
    )(*parts, *got)


def along_z(v):
    lane = lax.broadcasted_iota(jnp.int32, v.shape, 1)
    up = jnp.where(lane == LANES - 1, 0.0, pltpu.roll(v, LANES - 1, 1))
    down = jnp.where(lane == 0, 0.0, pltpu.roll(v, 1, 1))
    return up + down


def update(v, old, speed, beside):
    return 2.0 * v - old + speed * (beside + along_z(v) - 6.0 * v)


def two_terms(v):
    high = v.astype(BF16)
    return high, (v - high.astype(F32)).astype(BF16)


def grid_kernel(p, q, s, wyo, wye, fxo, fxe, target, out, slots, s0, s1, rhs, part1, part2):
    cx, cy = p.shape[0], p.shape[1]
    ahead, behind = SUB, SUB + cy
    fx_count = part1.shape[0] // 2 - 1
    cols = 4
    tall = part2.shape[0]
    high = part1.shape[1] - 2 * SUB
    wy_count = high // cols
    before_y, after_y = before_after(even_at("wy"), wye, wyo)
    before_x, after_x = before_after(even_at("fx"), fxe, fxo)
    corner = 4 * cy + 6 * (cols + 2)

    s0[1 : cx + 1, ahead:behind, :] = p[...]
    for x, side in ((0, before_x), (cx + 1, after_x)):
        s0[x, ahead:behind, :] = side[0:cy]
        s0[x, ahead - 1 : ahead, :] = side[corner : corner + 1]
        s0[x, behind : behind + 1, :] = side[corner + 1 : corner + 2]
    s0[1 : cx + 1, ahead - 1, :] = before_y[0:cx]
    s0[1 : cx + 1, behind, :] = after_y[0:cx]

    for side, y, inner in ((before_y, ahead - 1, ahead), (after_y, behind, behind - 1)):
        near, far = side[0:cx], side[cx : 2 * cx]
        old, speed = side[2 * cx : 3 * cx], side[3 * cx : 4 * cx]
        beside = s0[0:cx, y, :] + s0[2 : cx + 2, y, :] + far + s0[1 : cx + 1, inner, :]
        s1[1 : cx + 1, y, :] = update(near, old, speed, beside)
    for side, x, inner in ((before_x, 0, 1), (after_x, cx + 1, cx)):
        near, far = side[0:cy], side[cy : 2 * cy]
        old, speed = side[2 * cy : 3 * cy], side[3 * cy : 4 * cy]
        beside = s0[x, ahead - 1 : behind - 1, :] + s0[x, ahead + 1 : behind + 1, :]
        beside = beside + far + s0[inner, ahead:behind, :]
        s1[x, ahead:behind, :] = update(near, old, speed, beside)

    def sweep(now, old, x):
        beside = now[x, ahead:behind, :] + now[x + 2, ahead:behind, :]
        beside = beside + now[x + 1, ahead - 1 : behind - 1, :]
        beside = beside + now[x + 1, ahead + 1 : behind + 1, :]
        return update(now[x + 1, ahead:behind, :], old, s[x], beside)

    for x in range(cx):
        fresh = sweep(s0, q[x], x)
        s1[x + 1, ahead:behind, :] = fresh
        a, b = two_terms(fresh)
        rhs[x * cy : (x + 1) * cy, 0:LANES] = a
        rhs[x * cy : (x + 1) * cy, LANES : 2 * LANES] = b
    for x in range(cx):
        fresh = sweep(s1, p[x], x)
        out[x] = fresh
        a, b = two_terms(fresh)
        rhs[x * cy : (x + 1) * cy, 2 * LANES : 3 * LANES] = a
        rhs[x * cy : (x + 1) * cy, 3 * LANES : 4 * LANES] = b

    part1[...] = jnp.zeros(part1.shape, F32)
    part2[:, 0:SUB, :] = jnp.zeros((tall, SUB, LANES), F32)
    chunk = 256
    for first in range(0, tall * high, chunk):
        tile = lax.broadcasted_iota(jnp.int32, (chunk, LANES), 0) + first
        picks = []
        for piece in range(target.shape[0]):
            picks.append(jnp.where(tile == target[piece : piece + 1, :], 1.0, 0.0).astype(BF16))
        sums = jnp.dot(jnp.concatenate(picks, axis=1), rhs[...], preferred_element_type=F32)
        one = sums[:, 0:LANES] + sums[:, LANES : 2 * LANES]
        two = sums[:, 2 * LANES : 3 * LANES] + sums[:, 3 * LANES : 4 * LANES]
        l = first // high
        part1[1 + l : 1 + l + chunk // high, SUB : SUB + high, :] = one.reshape(-1, high, LANES)
        part2[l : l + chunk // high, SUB : SUB + high, :] = two.reshape(-1, high, LANES)
    sub = lax.broadcasted_iota(jnp.int32, (SUB, LANES), 0)
    lane = lax.broadcasted_iota(jnp.int32, (SUB, LANES), 1)
    step1 = sub < cols + 2
    for a in range(fx_count):
        for b in range(wy_count):
            h = SUB + cols * b
            slot = a * wy_count + b
            one = [part1[2 * a + l, h - 1 : h - 1 + SUB, :] for l in range(4)]
            ends = jnp.where(lane % 8 < 4, one[3], one[0])
            two = [
                part2[2 * a + l, h + at - 6 : h + at - 6 + SUB, :]
                for l, at in ((0, 0), (0, 2), (1, 0))
            ]
            x = jnp.broadcast_to(part2[2 * a + 1, h + 2 : h + 3, :], (SUB, LANES))
            y = jnp.broadcast_to(part2[2 * a + 1, h + 3 : h + 4, :], (SUB, LANES))
            for r in range(4):
                moved = pltpu.roll(y, (3 - 2 * r) % LANES, 1)
                ends = jnp.where((sub == 1 + r) & free_ends(lane), moved, ends)
            low, high_free = (sub == 0) & (lane // 8 % 4 == 0), (sub == cols + 1) & (lane // 8 % 4 == 3)
            own0 = jnp.where(low | high_free, x, one[1])
            own1 = jnp.where(low, pltpu.roll(x, LANES - 8, 1), one[2])
            own1 = jnp.where(high_free, pltpu.roll(x, 8, 1), own1)
            for k, group in enumerate((ends, own0, own1)):
                slots[slot, k * SUB : (k + 1) * SUB, :] = jnp.where(step1, group, two[k])


def free_ends(lane):
    return (lane % 8 == 3) | (lane % 8 == 4)


def unpack_slots(total, cols):
    ends, own0, own1 = [total[k * SUB : (k + 1) * SUB] for k in range(3)]
    lane = lax.broadcasted_iota(jnp.int32, (1, LANES), 1)
    two = [[ends[6:7], ends[7:8], own0[6:7], own0[7:8]], [own1[6:7], own1[7:8]]]
    q = lane // 8 % 4
    last = cols + 1
    x = jnp.where(q == 0, own0[0:1], own0[last : last + 1])
    x = jnp.where(q == 1, pltpu.roll(own1[0:1], 8, 1), x)
    x = jnp.where(q == 2, pltpu.roll(own1[last : last + 1], LANES - 8, 1), x)
    y = None
    for r in range(4):
        moved = pltpu.roll(ends[1 + r : 2 + r], (2 * r - 3) % LANES, 1)
        y = moved if y is None else jnp.where(lane % 8 // 2 == r, moved, y)
    two[1].extend([x, y])
    two = [jnp.concatenate(v, axis=0) for v in two]
    return (ends, own0, own1, ends), two


def grid_steps(p, q, s, wy_got, fx_got, target, fx_count, wy_count):
    cx, cy = p.shape[0], p.shape[1]
    tall, high = fx_count * 2, wy_count * 4
    devices = fx_count * wy_count
    return pl.pallas_call(
        grid_kernel,
        in_specs=[whole()] * 8,
        out_specs=[whole()] * 2,
        out_shape=[
            jax.ShapeDtypeStruct(p.shape, F32),
            vmem(devices, 3 * SUB, LANES),
        ],
        scratch_shapes=[
            pltpu.VMEM((cx + 2, cy + 2 * SUB, LANES), F32),
            pltpu.VMEM((cx + 2, cy + 2 * SUB, LANES), F32),
            pltpu.VMEM((cx * cy, 4 * LANES), BF16),
            pltpu.VMEM((tall + 2, high + 2 * SUB, LANES), F32),
            pltpu.VMEM((tall, high + 2 * SUB, LANES), F32),
        ],
        compiler_params=params(),
        name="grid_steps",
    )(p, q, s, *wy_got, *fx_got, target)


def reached(g):
    groups = []
    for dh in (-1, 0, 1):
        if (dh == -1 and g % 4 == 3) or (dh == 1 and g % 4 == 0):
            continue
        groups.append(dh)
    return groups


STORED = sum(len(reached(g)) for g in range(LANES // SUB))


def mid_rows(ref, c, l, h):
    rows = {}
    for dh in (-1, 0, 1):
        row = ref[c, l + 1, pl.ds(h + 1 + dh, 1), :]
        rows[dh] = jnp.broadcast_to(row, (SUB, LANES))
    return rows


def end_rows(ref, c, l, h, first_sub):
    rows = {}
    for dh in (-1, 0, 1):
        at = pl.ds(h + 1 + dh, 1)
        before = jnp.broadcast_to(ref[c, l, at, :], (SUB, LANES))
        after = jnp.broadcast_to(ref[c, l + 2, at, :], (SUB, LANES))
        rows[dh] = jnp.where(first_sub, before, after)
    return rows


def fill_y(pad, own, before, after, at):
    rows, cols = own.shape[1], own.shape[2]
    for c in range(3):
        for l in range(rows):
            row = at + c * rows + l
            pad[c, l + 1, 0:1, :] = before[row : row + 1]
            pad[c, l + 1, 1 : cols + 1, :] = own[c, l]
            pad[c, l + 1, cols + 1 : cols + 2, :] = after[row : row + 1]


def fill_x(pad, rows, cols, before, after, at):
    for c in range(3):
        row = at + c * (cols + 2)
        pad[c, 0, 0 : cols + 2, :] = before[row : row + cols + 2]
        pad[c, rows + 1, 0 : cols + 2, :] = after[row : row + cols + 2]


def lattice_rows():
    index = lax.broadcasted_iota(jnp.int32, (1, LANES), 1)
    places = (index % 8, index // 8 % 4, index // 32)
    return [v.astype(F32) * (1.0 / REACH) for v in places]


SPAN = 8.0 / REACH
RISE = 4.0 / REACH


def mine_columns(ref, lattice, l, h):
    sub = lax.broadcasted_iota(jnp.int32, (SUB, LANES), 0)
    own = []
    for c in range(3):
        row = ref[c, l + 1, pl.ds(h + 1, 1), :] * (1.0 / REACH) + lattice[c]
        own.append(jnp.broadcast_to(row, (SUB, LANES)))
    return jnp.transpose(jnp.where(sub == 0, own[0], jnp.where(sub == 1, own[1], own[2])))


def bond_row(weight, others, mine):
    for c in range(3):
        diff = others[c] - mine[c]
        weight = weight - diff * diff
    return jnp.maximum(weight, 0.0)


def tile_pass(l, h, columns, others, pulls, weight_of, weights, acc):
    place = 0
    for g in range(LANES // SUB):
        span = slice(g * SUB, (g + 1) * SUB)
        mine = [jnp.broadcast_to(columns[span, c : c + 1], (SUB, LANES)) for c in range(3)]
        sums = [None] * 4
        for order, dh in enumerate(reached(g)):
            here = [others[c][dh] for c in range(3)]
            weight = weight_of(g, order, dh, here, mine)
            weights[l, h, place] = weight
            place += 1
            terms = [weight * pulls[c][dh] for c in range(3)] + [weight]
            sums = [t if v is None else v + t for v, t in zip(sums, terms)]
        for c in range(4):
            acc[l, h, c, span, :] = sums[c]


def lane_sums(acc, l, cols, count):
    ones = jnp.ones((2 * SUB, LANES), BF16)
    result = [[] for _ in range(count)]
    for h in range(cols):
        terms = []
        for c in range(count):
            terms.extend(two_terms(acc[l, h, c]))
        sums = lax.dot_general(
            ones,
            jnp.concatenate(terms, axis=0),
            (((1,), (1,)), ((), ())),
            preferred_element_type=F32,
        )[0:1]
        for c in range(count):
            at = 2 * c * LANES
            result[c].append(sums[:, at : at + LANES] + sums[:, at + LANES : at + 2 * LANES])
    return [jnp.concatenate(parts, axis=0) for parts in result]


def quotient(v, n):
    return ((v.astype(F32) + 0.5) * (1.0 / n)).astype(jnp.int32)


def center_kernel(
    wy_count, masks_in, p_in, q_in, s_in, device_in, tile_in, wall, wyo, wye,
    weights, part, bits, target, p, q, s, jpad, dpad, acc, masks, route, sems,
):
    rows, cols = wall.shape[2], wall.shape[3]
    cx = p.shape[0]
    copies = {}
    pairs = [(device_in, route.at[0]), (tile_in, route.at[1])]
    pairs = [(p_in, p), (q_in, q), (s_in, s)] + pairs
    for k, pair in enumerate(pairs):
        copies[k] = pltpu.make_async_copy(*pair, sems.at[rows * cols + k])
    for h in range(cols):
        for l in range(rows):
            copies[l, h] = pltpu.make_async_copy(
                masks_in.at[l, h], masks.at[l, h], sems.at[l * cols + h]
            )
    for copy in copies.values():
        copy.start()
    first_sub = lax.broadcasted_iota(jnp.int32, (SUB, LANES), 0) < SUB // 2
    copies[3].wait()
    copies[4].wait()
    device, tile = route[0], route[1]
    a, t = quotient(device, wy_count), quotient(tile, cols)
    b, u = device - a * wy_count, tile - t * cols
    target[...] = (a * rows + t) * (wy_count * cols) + b * cols + u
    before, after = before_after(even_at("wy"), wye, wyo)
    fill_y(jpad, wall.at[0], before, after, 4 * cx)
    fill_y(dpad, wall.at[1], before, after, 4 * cx + 3 * rows)
    lattice = lattice_rows()

    def one_tile(l, h):
        columns = mine_columns(jpad, lattice, l, h)
        others = []
        for c in range(3):
            mid = mid_rows(jpad, c, l, h)
            for dh in (-1, 0, 1):
                mid[dh] = mid[dh] * (1.0 / REACH) + lattice[c]
                if c == 1:
                    mid[dh] = mid[dh] + RISE * dh
            others.append(mid)
        pulls = [mid_rows(dpad, c, l, h) for c in range(3)]

        def weight_of(g, order, dh, here, mine):
            span = slice(g * SUB, (g + 1) * SUB)
            before = masks[l, h, 1 + dh, span, :]
            after = masks[l, h, 7 + dh, span, :]
            bit = jnp.where(first_sub, before, after) * (1 << order)
            bits[l, h, g] = bit if order == 0 else bits[l, h, g] + bit
            return bond_row(masks[l, h, 4 + dh, span, :].astype(F32), here, mine)

        tile_pass(l, h, columns, others, pulls, weight_of, weights, acc)

    for h in range(cols):
        for l in range(rows):
            copies[l, h].wait()
            one_tile(l, h)
    for l in range(rows):
        for c, sums in enumerate(lane_sums(acc, l, cols, 4)):
            part[l, c] = sums
    for k in range(3):
        copies[k].wait()


def wall_center(wy_count, masks, grids, device, tile, wall, wy_got):
    rows, cols = wall.shape[2], wall.shape[3]
    groups = LANES // SUB
    return pl.pallas_call(
        functools.partial(center_kernel, wy_count),
        in_specs=[HBM] * 6 + [whole()] * 3,
        out_specs=[whole()] * 7,
        out_shape=[
            jax.ShapeDtypeStruct((rows, cols, STORED, SUB, LANES), F32),
            vmem(rows, 4, cols, LANES),
            jax.ShapeDtypeStruct((rows, cols, groups, SUB, LANES), jnp.int32),
            pltpu.VMEM(device.shape, jnp.int32),
        ]
        + [vmem(*grids[0].shape)] * 3,
        scratch_shapes=[
            vmem(3, rows + 2, SUB, LANES),
            vmem(3, rows + 2, SUB, LANES),
            vmem(rows, cols, 4, LANES, LANES),
            pltpu.VMEM(masks.shape, jnp.int32),
            pltpu.VMEM((2,) + device.shape, jnp.int32),
            pltpu.SemaphoreType.DMA((rows * cols + 5,)),
        ],
        compiler_params=params(),
        name="wall_center",
    )(*in_hbm(masks, *grids, device, tile), wall, *wy_got)


def wall_kernel(
    cx, cy, wall, wyo, wye, fxo, fxe, part, bits, weights, vel1, base1, totals, to_odd, to_even,
    jpad, dpad, acc,
):
    rows, cols = wall.shape[2], wall.shape[3]
    first_sub = lax.broadcasted_iota(jnp.int32, (SUB, LANES), 0) < SUB // 2
    before, after = before_after(even_at("wy"), wye, wyo)
    fill_y(jpad, wall.at[0], before, after, 4 * cx)
    fill_y(dpad, wall.at[1], before, after, 4 * cx + 3 * rows)
    before, after = before_after(even_at("fx"), fxe, fxo)
    fill_x(jpad, rows, cols, before, after, 4 * cy)
    fill_x(dpad, rows, cols, before, after, 4 * cy + 3 * (cols + 2))
    lattice = lattice_rows()

    def one_tile(l, h):
        columns = mine_columns(jpad, lattice, l, h)
        others = []
        for c in range(3):
            ends = end_rows(jpad, c, l, h, first_sub)
            for dh in (-1, 0, 1):
                ends[dh] = ends[dh] * (1.0 / REACH) + lattice[c]
                if c == 0:
                    ends[dh] = ends[dh] + jnp.where(first_sub, -SPAN, SPAN)
                if c == 1:
                    ends[dh] = ends[dh] + RISE * dh
            others.append(ends)
        pulls = [end_rows(dpad, c, l, h, first_sub) for c in range(3)]

        def weight_of(g, order, dh, here, mine):
            bonded = (bits[l, h, g] & (1 << order)) != 0
            return jnp.where(bonded, bond_row(1.0, here, mine), 0.0)

        tile_pass(l, h, columns, others, pulls, weight_of, weights, acc)

    @pl.loop(0, cols)
    def _(h):
        for l in range(rows):
            one_tile(l, h)

    for l in range(rows):
        pulled = [v + part[l, c] for c, v in enumerate(lane_sums(acc, l, cols, 4))]
        totals[l] = pulled[3]
        for c in range(3):
            mine = wall[1, c, l]
            fresh = wall[2, c, l] + STIFFNESS * (pulled[c] - pulled[3] * mine)
            vel1[c, l] = fresh
            base1[c, l] = mine + fresh

    def edge(at):
        def write(out):
            for c in range(3):
                for k in range(rows):
                    out[c * rows + k : c * rows + k + 1, :] = base1[c, k, at : at + 1, :]
            for spare in range(3 * rows, out.shape[0]):
                out[spare : spare + 1, :] = jnp.zeros((1, LANES), F32)

        return write

    place_edges(even_at("wy"), edge(0), edge(cols - 1), to_even, to_odd)


def wall_first(cx, cy, wall, wy_got, fx_got, part, bits):
    rows, cols = wall.shape[2], wall.shape[3]
    edge = (pad8(3 * rows), LANES)
    field = vmem(*wall.shape[1:])
    return pl.pallas_call(
        functools.partial(wall_kernel, cx, cy),
        in_specs=[whole()] * 7,
        out_specs=[whole()] * 6,
        out_shape=[
            jax.ShapeDtypeStruct((rows, cols, STORED, SUB, LANES), F32),
            field,
            field,
            vmem(rows, cols, LANES),
            vmem(*edge),
            vmem(*edge),
        ],
        scratch_shapes=[
            pltpu.VMEM((3, rows + 2, SUB, LANES), F32),
            pltpu.VMEM((3, rows + 2, SUB, LANES), F32),
            pltpu.VMEM((rows, cols, 4, LANES, LANES), F32),
        ],
        compiler_params=params(),
        name="wall_first",
    )(wall, *wy_got, *fx_got, part, bits)


def pack_base_kernel(base1, got_odd, got_even, to_odd, to_even):
    rows, cols = base1.shape[1], base1.shape[2]
    before, after = before_after(even_at("wy"), got_even, got_odd)

    def edge(l):
        def write(out):
            at = 0
            for c in range(3):
                side = c * rows + l
                out[at : at + 1, :] = before[side : side + 1]
                out[at + 1 : at + 1 + cols, :] = base1[c, l]
                out[at + 1 + cols : at + 2 + cols, :] = after[side : side + 1]
                at += cols + 2
            for spare in range(at, out.shape[0]):
                out[spare : spare + 1, :] = jnp.zeros((1, LANES), F32)

        return write

    place_edges(even_at("fx"), edge(0), edge(rows - 1), to_even, to_odd)


def pack_base(base1, got):
    cols = base1.shape[2]
    out = vmem(pad8(3 * (cols + 2)), LANES)
    return pl.pallas_call(
        pack_base_kernel,
        in_specs=[whole()] * 3,
        out_specs=[whole()] * 2,
        out_shape=[out, out],
        compiler_params=params(),
        name="pack_base",
    )(base1, *got)


def last_kernel(
    weights, end_weights, got, base1, vel1, totals, wyo, wye, fxo, fxe, disp_out, vel_out,
    dpad, acc,
):
    rows, cols = base1.shape[1], base1.shape[2]
    first_sub = lax.broadcasted_iota(jnp.int32, (SUB, LANES), 0) < SUB // 2
    before, after = before_after(even_at("wy"), wye, wyo)
    fill_y(dpad, base1, before, after, 0)
    before, after = before_after(even_at("fx"), fxe, fxo)
    fill_x(dpad, rows, cols, before, after, 0)
    total = got[0]
    for d in range(1, got.shape[0]):
        total = total + got[d]
    one, two = unpack_slots(total, cols)
    for k in range(rows + 2):
        here = dpad[0, k, 0 : cols + 2, :] + LOADING * one[k][0 : cols + 2]
        dpad[0, k, 0 : cols + 2, :] = here

    def one_tile(l, h):
        mids = [mid_rows(dpad, c, l, h) for c in range(3)]
        ends = [end_rows(dpad, c, l, h, first_sub) for c in range(3)]
        place = 0
        for g in range(LANES // SUB):
            sums = [None] * 3
            for dh in reached(g):
                for weight, pulls in (
                    (weights[l, h, place], mids), (end_weights[l, h, place], ends)
                ):
                    terms = [weight * pulls[c][dh] for c in range(3)]
                    sums = [t if v is None else v + t for v, t in zip(sums, terms)]
                place += 1
            for c in range(3):
                acc[l, h, c, g * SUB : (g + 1) * SUB, :] = sums[c]

    @pl.loop(0, cols)
    def _(h):
        for l in range(rows):
            one_tile(l, h)

    for l in range(rows):
        pulled = lane_sums(acc, l, cols, 3)
        for c in range(3):
            mine = dpad[c, l + 1, 1 : cols + 1, :]
            force = STIFFNESS * (pulled[c] - totals[l] * mine)
            if c == 0:
                force = force + LOADING * (one[l + 1][1 : cols + 1] + two[l])
            fresh = vel1[c, l] + force
            vel_out[c, l] = fresh
            disp_out[c, l] = mine + fresh


def wall_last(weights, end_weights, got, base1, vel1, totals, wy_got, fx_got):
    rows, cols = base1.shape[1], base1.shape[2]
    return pl.pallas_call(
        last_kernel,
        in_specs=[whole()] * 10,
        out_specs=[whole()] * 2,
        out_shape=[jax.ShapeDtypeStruct(base1.shape, F32)] * 2,
        scratch_shapes=[
            pltpu.VMEM((3, rows + 2, SUB, LANES), F32),
            pltpu.VMEM((rows, cols, 3, LANES, LANES), F32),
        ],
        compiler_params=params(),
        name="wall_last",
    )(weights, end_weights, got, base1, vel1, totals, *wy_got, *fx_got)


def per_device(
    displacement,
    velocity,
    jitter,
    bond_masks,
    pressure,
    pressure_prev,
    speed_sq,
    route_device,
    route_tile,
):
    fx_count, wy_count = lax.axis_size("fx"), lax.axis_size("wy")
    cols = displacement.shape[2]
    device = route_device.reshape(-1, LANES)
    tile = route_tile.reshape(-1, LANES)
    cx, cy = pressure.shape[0], pressure.shape[1]
    rows = displacement.shape[1]
    *sends, part_odd, part_even, wall = pack_wy(
        pressure, pressure_prev, speed_sq, jitter, displacement, velocity
    )
    wy_got = exchange("wy", *sends)
    sends = pack_fx((cx, cy, rows, cols), (part_odd, part_even), wy_got)
    fx_got = exchange("fx", *sends)
    grids = (pressure, pressure_prev, speed_sq)
    weights, part, bits, target, *grids = wall_center(
        wy_count, bond_masks, grids, device, tile, wall, wy_got
    )
    pressure_out, slots = grid_steps(*grids, wy_got, fx_got, target, fx_count, wy_count)
    got = lax.all_to_all(slots, ("fx", "wy"), split_axis=0, concat_axis=0, tiled=True)
    end_weights, vel1, base1, totals, *sends = wall_first(
        cx, cy, wall, wy_got, fx_got, part, bits
    )
    base_wy = exchange("wy", *sends)
    sends = pack_base(base1, base_wy)
    base_fx = exchange("fx", *sends)
    disp_out, vel_out = wall_last(
        weights, end_weights, got, base1, vel1, totals, base_wy, base_fx
    )
    return (disp_out, vel_out, pressure_out)


def solution(mesh):
    placed = (
        P(None, "fx", "wy", None),
        P(None, "fx", "wy", None),
        P(None, "fx", "wy", None),
        P("fx", "wy", None, None, None),
        P("fx", "wy", None),
        P("fx", "wy", None),
        P("fx", "wy", None),
        P(("fx", "wy"), None),
        P(("fx", "wy")),
    )
    return jax.shard_map(
        per_device,
        mesh=mesh,
        in_specs=placed,
        out_specs=(P(None, "fx", "wy", None), P(None, "fx", "wy", None), P("fx", "wy", None)),
        check_vma=False,
    )
```

```python
import functools

import jax
import jax.numpy as jnp
from jax import lax
from jax.experimental import pallas as pl
from jax.experimental.pallas import tpu as pltpu
from jax.sharding import PartitionSpec as P

STIFFNESS = 0.02
LOADING = 0.05
REACH = 3.0
LANES = 128
SUB = 8
VMEM_BYTES = 32 * 1024 * 1024
HBM = pl.BlockSpec(memory_space=pltpu.HBM)

F32 = jnp.float32
BF16 = jnp.bfloat16


def whole():
    return pl.BlockSpec(memory_space=pltpu.VMEM)


def params():
    return pltpu.CompilerParams(vmem_limit_bytes=VMEM_BYTES)


def vmem(*shape):
    return pltpu.VMEM(shape, F32)


def even_at(axis):
    return lax.rem(lax.axis_index(axis), 2) == 0


def pair_list(count, first):
    pairs = []
    for low in range(first, count - 1, 2):
        pairs.extend([(low, low + 1), (low + 1, low)])
    if first == 1 and count % 2 == 0 and count > 2:
        pairs.extend([(0, count - 1), (count - 1, 0)])
    return pairs


def exchange(axis, to_odd, to_even):
    count = lax.axis_size(axis)
    got_odd = lax.ppermute(to_odd, axis, pair_list(count, 1))
    got_even = lax.ppermute(to_even, axis, pair_list(count, 0))
    return got_odd, got_even


def place_edges(even, low, high, to_even, to_odd):
    @pl.when(even)
    def _():
        high(to_even)
        low(to_odd)

    @pl.when(jnp.logical_not(even))
    def _():
        low(to_even)
        high(to_odd)


def before_after(axis, got_even, got_odd):
    even = even_at(axis)
    place, last = lax.axis_index(axis), lax.axis_size(axis) - 1
    a, b = got_even[...], got_odd[...]
    before = jnp.where(place == 0, 0.0, jnp.where(even, b, a))
    after = jnp.where(place == last, 0.0, jnp.where(even, a, b))
    return before, after


def pack_wy_kernel(
    p, q, s, jit_in, disp_in, vel_in, wy_odd, wy_even, fx_odd, fx_even, wall, edges, ends, sems
):
    cx, cy = p.shape[0], p.shape[1]
    rows, cols = jit_in.shape[1], jit_in.shape[2]
    pairs = []
    for k, field in enumerate((p, q, s)):
        for side, first in enumerate((0, cy - SUB)):
            pairs.append((field.at[:, first : first + SUB, :], edges.at[2 * k + side]))
    pairs.append((p.at[0:2], ends.at[0, 0:2]))
    pairs.append((p.at[cx - 2 : cx], ends.at[1, 0:2]))
    for k, field in enumerate((q, s)):
        pairs.append((field.at[0], ends.at[0, 2 + k]))
        pairs.append((field.at[cx - 1], ends.at[1, 2 + k]))
    for k, field in enumerate((jit_in, disp_in, vel_in)):
        pairs.append((field, wall.at[k]))
    copies = [pltpu.make_async_copy(a, b, sems.at[k]) for k, (a, b) in enumerate(pairs)]
    for copy in copies:
        copy.start()
    for copy in copies:
        copy.wait()

    def edge(side, near, far, h):
        def write(out):
            out[0:cx, :] = edges[side, :, near, :]
            out[cx : 2 * cx, :] = edges[side, :, far, :]
            out[2 * cx : 3 * cx, :] = edges[2 + side, :, near, :]
            out[3 * cx : 4 * cx, :] = edges[4 + side, :, near, :]
            at = 4 * cx
            for field in range(2):
                for c in range(3):
                    for l in range(rows):
                        out[at : at + 1, :] = wall[field, c, l, h : h + 1, :]
                        at += 1
            for spare in range(at, out.shape[0]):
                out[spare : spare + 1, :] = jnp.zeros((1, LANES), F32)

        return write

    place_edges(
        even_at("wy"),
        edge(0, 0, 1, 0),
        edge(1, SUB - 1, SUB - 2, cols - 1),
        wy_even,
        wy_odd,
    )

    def end(side, near, far, l):
        def write(out):
            out[0:cy, :] = ends[side, near]
            out[cy : 2 * cy, :] = ends[side, far]
            out[2 * cy : 3 * cy, :] = ends[side, 2]
            out[3 * cy : 4 * cy, :] = ends[side, 3]
            at = 4 * cy
            for field in range(2):
                for c in range(3):
                    out[at + 1 : at + 1 + cols, :] = wall[field, c, l]
                    at += cols + 2

        return write

    place_edges(even_at("fx"), end(0, 0, 1, 0), end(1, 1, 0, rows - 1), fx_even, fx_odd)


def in_hbm(*arrays):
    return [pltpu.with_memory_space_constraint(v, pltpu.HBM) for v in arrays]


def pad8(count):
    return (count + 7) // 8 * 8


def pack_wy(p, q, s, jit, disp, vel):
    cx, cy = p.shape[0], p.shape[1]
    rows, cols = jit.shape[1], jit.shape[2]
    wy_out = vmem(pad8(4 * cx + 6 * rows), LANES)
    fx_out = vmem(pad8(4 * cy + 6 * (cols + 2) + 2), LANES)
    return pl.pallas_call(
        pack_wy_kernel,
        in_specs=[HBM] * 6,
        out_specs=[whole()] * 5,
        out_shape=[wy_out, wy_out, fx_out, fx_out, vmem(3, *jit.shape)],
        scratch_shapes=[
            pltpu.VMEM((6, cx, SUB, LANES), F32),
            pltpu.VMEM((2, 4, cy, LANES), F32),
            pltpu.SemaphoreType.DMA((15,)),
        ],
        compiler_params=params(),
        name="pack_wy",
    )(*in_hbm(p, q, s, jit, disp, vel))


def pack_fx_kernel(cx, cy, rows, cols, part_odd, part_even, got_odd, got_even, to_odd, to_even):
    before, after = before_after("wy", got_even, got_odd)
    to_even[...] = part_even[...]
    to_odd[...] = part_odd[...]

    def corners(x, l):
        def write(out):
            at = 4 * cy
            for k in range(6):
                side = 4 * cx + k * rows + l
                out[at : at + 1, :] = before[side : side + 1]
                out[at + 1 + cols : at + 2 + cols, :] = after[side : side + 1]
                at += cols + 2
            out[at : at + 1, :] = before[x : x + 1]
            out[at + 1 : at + 2, :] = after[x : x + 1]

        return write

    place_edges(even_at("fx"), corners(0, 0), corners(cx - 1, rows - 1), to_even, to_odd)


def pack_fx(sizes, parts, got):
    out = vmem(*parts[0].shape)
    return pl.pallas_call(
        functools.partial(pack_fx_kernel, *sizes),
        in_specs=[whole()] * 4,
        out_specs=[whole()] * 2,
        out_shape=[out, out],
        compiler_params=params(),
        name="pack_fx",
    )(*parts, *got)


def along_z(v):
    lane = lax.broadcasted_iota(jnp.int32, v.shape, 1)
    up = jnp.where(lane == LANES - 1, 0.0, pltpu.roll(v, LANES - 1, 1))
    down = jnp.where(lane == 0, 0.0, pltpu.roll(v, 1, 1))
    return up + down


def update(v, old, speed, beside):
    return 2.0 * v - old + speed * (beside + along_z(v) - 6.0 * v)


def two_terms(v):
    high = v.astype(BF16)
    return high, (v - high.astype(F32)).astype(BF16)


def grid_kernel(p, q, s, wyo, wye, fxo, fxe, target, out, slots, s0, s1, rhs, part1, part2):
    cx, cy = p.shape[0], p.shape[1]
    ahead, behind = SUB, SUB + cy
    fx_count = part1.shape[0] // 2 - 1
    cols = 4
    tall = part2.shape[0]
    high = part1.shape[1] - 2 * SUB
    wy_count = high // cols
    before_y, after_y = before_after("wy", wye, wyo)
    before_x, after_x = before_after("fx", fxe, fxo)
    corner = 4 * cy + 6 * (cols + 2)

    s0[1 : cx + 1, ahead:behind, :] = p[...]
    for x, side in ((0, before_x), (cx + 1, after_x)):
        s0[x, ahead:behind, :] = side[0:cy]
        s0[x, ahead - 1 : ahead, :] = side[corner : corner + 1]
        s0[x, behind : behind + 1, :] = side[corner + 1 : corner + 2]
    s0[1 : cx + 1, ahead - 1, :] = before_y[0:cx]
    s0[1 : cx + 1, behind, :] = after_y[0:cx]

    for side, y, inner in ((before_y, ahead - 1, ahead), (after_y, behind, behind - 1)):
        near, far = side[0:cx], side[cx : 2 * cx]
        old, speed = side[2 * cx : 3 * cx], side[3 * cx : 4 * cx]
        beside = s0[0:cx, y, :] + s0[2 : cx + 2, y, :] + far + s0[1 : cx + 1, inner, :]
        s1[1 : cx + 1, y, :] = update(near, old, speed, beside)
    for side, x, inner in ((before_x, 0, 1), (after_x, cx + 1, cx)):
        near, far = side[0:cy], side[cy : 2 * cy]
        old, speed = side[2 * cy : 3 * cy], side[3 * cy : 4 * cy]
        beside = s0[x, ahead - 1 : behind - 1, :] + s0[x, ahead + 1 : behind + 1, :]
        beside = beside + far + s0[inner, ahead:behind, :]
        s1[x, ahead:behind, :] = update(near, old, speed, beside)

    def sweep(now, old, x):
        beside = now[x, ahead:behind, :] + now[x + 2, ahead:behind, :]
        beside = beside + now[x + 1, ahead - 1 : behind - 1, :]
        beside = beside + now[x + 1, ahead + 1 : behind + 1, :]
        return update(now[x + 1, ahead:behind, :], old, s[x], beside)

    for x in range(cx):
        fresh = sweep(s0, q[x], x)
        s1[x + 1, ahead:behind, :] = fresh
        a, b = two_terms(fresh)
        rhs[x * cy : (x + 1) * cy, 0:LANES] = a
        rhs[x * cy : (x + 1) * cy, LANES : 2 * LANES] = b
    for x in range(cx):
        fresh = sweep(s1, p[x], x)
        out[x] = fresh
        a, b = two_terms(fresh)
        rhs[x * cy : (x + 1) * cy, 2 * LANES : 3 * LANES] = a
        rhs[x * cy : (x + 1) * cy, 3 * LANES : 4 * LANES] = b

    part1[...] = jnp.zeros(part1.shape, F32)
    part2[:, 0:SUB, :] = jnp.zeros((tall, SUB, LANES), F32)
    chunk = 256
    for first in range(0, tall * high, chunk):
        tile = lax.broadcasted_iota(jnp.int32, (chunk, LANES), 0) + first
        picks = []
        for piece in range(target.shape[0]):
            picks.append(jnp.where(tile == target[piece : piece + 1, :], 1.0, 0.0).astype(BF16))
        sums = jnp.dot(jnp.concatenate(picks, axis=1), rhs[...], preferred_element_type=F32)
        one = sums[:, 0:LANES] + sums[:, LANES : 2 * LANES]
        two = sums[:, 2 * LANES : 3 * LANES] + sums[:, 3 * LANES : 4 * LANES]
        l = first // high
        part1[1 + l : 1 + l + chunk // high, SUB : SUB + high, :] = one.reshape(-1, high, LANES)
        part2[l : l + chunk // high, SUB : SUB + high, :] = two.reshape(-1, high, LANES)
    sub = lax.broadcasted_iota(jnp.int32, (SUB, LANES), 0)
    lane = lax.broadcasted_iota(jnp.int32, (SUB, LANES), 1)
    step1 = sub < cols + 2
    for a in range(fx_count):
        for b in range(wy_count):
            h = SUB + cols * b
            slot = a * wy_count + b
            one = [part1[2 * a + l, h - 1 : h - 1 + SUB, :] for l in range(4)]
            ends = jnp.where(lane % 8 < 4, one[3], one[0])
            two = [
                part2[2 * a + l, h + at - 6 : h + at - 6 + SUB, :]
                for l, at in ((0, 0), (0, 2), (1, 0))
            ]
            x = jnp.broadcast_to(part2[2 * a + 1, h + 2 : h + 3, :], (SUB, LANES))
            y = jnp.broadcast_to(part2[2 * a + 1, h + 3 : h + 4, :], (SUB, LANES))
            for r in range(4):
                moved = pltpu.roll(y, (3 - 2 * r) % LANES, 1)
                ends = jnp.where((sub == 1 + r) & free_ends(lane), moved, ends)
            low, high_free = (sub == 0) & (lane // 8 % 4 == 0), (sub == cols + 1) & (lane // 8 % 4 == 3)
            own0 = jnp.where(low | high_free, x, one[1])
            own1 = jnp.where(low, pltpu.roll(x, LANES - 8, 1), one[2])
            own1 = jnp.where(high_free, pltpu.roll(x, 8, 1), own1)
            for k, group in enumerate((ends, own0, own1)):
                slots[slot, k * SUB : (k + 1) * SUB, :] = jnp.where(step1, group, two[k])


def free_ends(lane):
    return (lane % 8 == 3) | (lane % 8 == 4)


def unpack_slots(total, cols):
    ends, own0, own1 = [total[k * SUB : (k + 1) * SUB] for k in range(3)]
    lane = lax.broadcasted_iota(jnp.int32, (1, LANES), 1)
    two = [[ends[6:7], ends[7:8], own0[6:7], own0[7:8]], [own1[6:7], own1[7:8]]]
    q = lane // 8 % 4
    last = cols + 1
    x = jnp.where(q == 0, own0[0:1], own0[last : last + 1])
    x = jnp.where(q == 1, pltpu.roll(own1[0:1], 8, 1), x)
    x = jnp.where(q == 2, pltpu.roll(own1[last : last + 1], LANES - 8, 1), x)
    y = None
    for r in range(4):
        moved = pltpu.roll(ends[1 + r : 2 + r], (2 * r - 3) % LANES, 1)
        y = moved if y is None else jnp.where(lane % 8 // 2 == r, moved, y)
    two[1].extend([x, y])
    two = [jnp.concatenate(v, axis=0) for v in two]
    return (ends, own0, own1, ends), two


def grid_steps(p, q, s, wy_got, fx_got, target, fx_count, wy_count):
    cx, cy = p.shape[0], p.shape[1]
    tall, high = fx_count * 2, wy_count * 4
    devices = fx_count * wy_count
    return pl.pallas_call(
        grid_kernel,
        in_specs=[whole()] * 8,
        out_specs=[whole()] * 2,
        out_shape=[
            jax.ShapeDtypeStruct(p.shape, F32),
            vmem(devices, 3 * SUB, LANES),
        ],
        scratch_shapes=[
            pltpu.VMEM((cx + 2, cy + 2 * SUB, LANES), F32),
            pltpu.VMEM((cx + 2, cy + 2 * SUB, LANES), F32),
            pltpu.VMEM((cx * cy, 4 * LANES), BF16),
            pltpu.VMEM((tall + 2, high + 2 * SUB, LANES), F32),
            pltpu.VMEM((tall, high + 2 * SUB, LANES), F32),
        ],
        compiler_params=params(),
        name="grid_steps",
    )(p, q, s, *wy_got, *fx_got, target)


def reached(g):
    groups = []
    for dh in (-1, 0, 1):
        if (dh == -1 and g % 4 == 3) or (dh == 1 and g % 4 == 0):
            continue
        groups.append(dh)
    return groups


STORED = sum(len(reached(g)) for g in range(LANES // SUB))


def mid_rows(ref, c, l, h):
    rows = {}
    for dh in (-1, 0, 1):
        row = ref[c, l + 1, pl.ds(h + 1 + dh, 1), :]
        rows[dh] = jnp.broadcast_to(row, (SUB, LANES))
    return rows


def end_rows(ref, c, l, h, first_sub):
    rows = {}
    for dh in (-1, 0, 1):
        at = pl.ds(h + 1 + dh, 1)
        before = jnp.broadcast_to(ref[c, l, at, :], (SUB, LANES))
        after = jnp.broadcast_to(ref[c, l + 2, at, :], (SUB, LANES))
        rows[dh] = jnp.where(first_sub, before, after)
    return rows


def fill_y(pad, own, before, after, at):
    rows, cols = own.shape[1], own.shape[2]
    for c in range(3):
        for l in range(rows):
            row = at + c * rows + l
            pad[c, l + 1, 0:1, :] = before[row : row + 1]
            pad[c, l + 1, 1 : cols + 1, :] = own[c, l]
            pad[c, l + 1, cols + 1 : cols + 2, :] = after[row : row + 1]


def fill_x(pad, rows, cols, before, after, at):
    for c in range(3):
        row = at + c * (cols + 2)
        pad[c, 0, 0 : cols + 2, :] = before[row : row + cols + 2]
        pad[c, rows + 1, 0 : cols + 2, :] = after[row : row + cols + 2]


def lattice_rows():
    index = lax.broadcasted_iota(jnp.int32, (1, LANES), 1)
    places = (index % 8, index // 8 % 4, index // 32)
    return [v.astype(F32) * (1.0 / REACH) for v in places]


SPAN = 8.0 / REACH
RISE = 4.0 / REACH


def mine_columns(ref, lattice, l, h):
    sub = lax.broadcasted_iota(jnp.int32, (SUB, LANES), 0)
    own = []
    for c in range(3):
        row = ref[c, l + 1, pl.ds(h + 1, 1), :] * (1.0 / REACH) + lattice[c]
        own.append(jnp.broadcast_to(row, (SUB, LANES)))
    return jnp.transpose(jnp.where(sub == 0, own[0], jnp.where(sub == 1, own[1], own[2])))


def bond_row(weight, others, mine):
    for c in range(3):
        diff = others[c] - mine[c]
        weight = weight - diff * diff
    return jnp.maximum(weight, 0.0)


def tile_pass(l, h, columns, others, pulls, weight_of, weights, acc):
    place = 0
    for g in range(LANES // SUB):
        span = slice(g * SUB, (g + 1) * SUB)
        mine = [jnp.broadcast_to(columns[span, c : c + 1], (SUB, LANES)) for c in range(3)]
        sums = [None] * 4
        for order, dh in enumerate(reached(g)):
            here = [others[c][dh] for c in range(3)]
            weight = weight_of(g, order, dh, here, mine)
            weights[l, h, place] = weight
            place += 1
            terms = [weight * pulls[c][dh] for c in range(3)] + [weight]
            sums = [t if v is None else v + t for v, t in zip(sums, terms)]
        for c in range(4):
            acc[l, h, c, span, :] = sums[c]


def lane_sums(acc, l, cols, count):
    ones = jnp.ones((2 * SUB, LANES), BF16)
    result = [[] for _ in range(count)]
    for h in range(cols):
        terms = []
        for c in range(count):
            terms.extend(two_terms(acc[l, h, c]))
        sums = lax.dot_general(
            ones,
            jnp.concatenate(terms, axis=0),
            (((1,), (1,)), ((), ())),
            preferred_element_type=F32,
        )[0:1]
        for c in range(count):
            at = 2 * c * LANES
            result[c].append(sums[:, at : at + LANES] + sums[:, at + LANES : at + 2 * LANES])
    return [jnp.concatenate(parts, axis=0) for parts in result]


def quotient(v, n):
    return ((v.astype(F32) + 0.5) * (1.0 / n)).astype(jnp.int32)


def center_kernel(
    wy_count, masks_in, p_in, q_in, s_in, device_in, tile_in, wall, wyo, wye,
    weights, part, bits, target, p, q, s, jpad, dpad, acc, masks, route, sems,
):
    rows, cols = wall.shape[2], wall.shape[3]
    cx = p.shape[0]
    copies = {}
    pairs = [(device_in, route.at[0]), (tile_in, route.at[1])]
    pairs = [(p_in, p), (q_in, q), (s_in, s)] + pairs
    for k, pair in enumerate(pairs):
        copies[k] = pltpu.make_async_copy(*pair, sems.at[rows * cols + k])
    for h in range(cols):
        for l in range(rows):
            copies[l, h] = pltpu.make_async_copy(
                masks_in.at[l, h], masks.at[l, h], sems.at[l * cols + h]
            )
    for copy in copies.values():
        copy.start()
    first_sub = lax.broadcasted_iota(jnp.int32, (SUB, LANES), 0) < SUB // 2
    copies[3].wait()
    copies[4].wait()
    device, tile = route[0], route[1]
    a, t = quotient(device, wy_count), quotient(tile, cols)
    b, u = device - a * wy_count, tile - t * cols
    target[...] = (a * rows + t) * (wy_count * cols) + b * cols + u
    before, after = before_after("wy", wye, wyo)
    fill_y(jpad, wall.at[0], before, after, 4 * cx)
    fill_y(dpad, wall.at[1], before, after, 4 * cx + 3 * rows)
    lattice = lattice_rows()

    def one_tile(l, h):
        columns = mine_columns(jpad, lattice, l, h)
        others = []
        for c in range(3):
            mid = mid_rows(jpad, c, l, h)
            for dh in (-1, 0, 1):
                mid[dh] = mid[dh] * (1.0 / REACH) + lattice[c]
                if c == 1:
                    mid[dh] = mid[dh] + RISE * dh
            others.append(mid)
        pulls = [mid_rows(dpad, c, l, h) for c in range(3)]
        words = [jnp.zeros((SUB, LANES), jnp.int32) for _ in range(2)]

        def weight_of(g, order, dh, here, mine):
            span = slice(g * SUB, (g + 1) * SUB)
            before = masks[l, h, 1 + dh, span, :]
            after = masks[l, h, 7 + dh, span, :]
            place = 3 * (g % 8) + order
            words[g // 8] = words[g // 8] + jnp.where(first_sub, before, after) * (1 << place)
            return bond_row(masks[l, h, 4 + dh, span, :].astype(F32), here, mine)

        tile_pass(l, h, columns, others, pulls, weight_of, weights, acc)
        for k in range(2):
            bits[l, h, k] = words[k]

    for h in range(cols):
        for l in range(rows):
            copies[l, h].wait()
            one_tile(l, h)
    for l in range(rows):
        for c, sums in enumerate(lane_sums(acc, l, cols, 4)):
            part[l, c] = sums
    for k in range(3):
        copies[k].wait()


def wall_center(wy_count, masks, grids, device, tile, wall, wy_got):
    rows, cols = wall.shape[2], wall.shape[3]
    return pl.pallas_call(
        functools.partial(center_kernel, wy_count),
        in_specs=[HBM] * 6 + [whole()] * 3,
        out_specs=[whole()] * 7,
        out_shape=[
            jax.ShapeDtypeStruct((rows, cols, STORED, SUB, LANES), F32),
            vmem(rows, 4, cols, LANES),
            pltpu.VMEM((rows, cols, 2, SUB, LANES), jnp.int32),
            pltpu.VMEM(device.shape, jnp.int32),
        ]
        + [vmem(*grids[0].shape)] * 3,
        scratch_shapes=[
            vmem(3, rows + 2, SUB, LANES),
            vmem(3, rows + 2, SUB, LANES),
            vmem(rows, cols, 4, LANES, LANES),
            pltpu.VMEM(masks.shape, jnp.int32),
            pltpu.VMEM((2,) + device.shape, jnp.int32),
            pltpu.SemaphoreType.DMA((rows * cols + 5,)),
        ],
        compiler_params=params(),
        name="wall_center",
    )(*in_hbm(masks, *grids, device, tile), wall, *wy_got)


def wall_kernel(
    cx, cy, wall, wyo, wye, fxo, fxe, part, bits, weights, vel1, base1, totals, to_odd, to_even,
    jpad, dpad, acc,
):
    rows, cols = wall.shape[2], wall.shape[3]
    first_sub = lax.broadcasted_iota(jnp.int32, (SUB, LANES), 0) < SUB // 2
    before, after = before_after("wy", wye, wyo)
    fill_y(jpad, wall.at[0], before, after, 4 * cx)
    fill_y(dpad, wall.at[1], before, after, 4 * cx + 3 * rows)
    before, after = before_after("fx", fxe, fxo)
    fill_x(jpad, rows, cols, before, after, 4 * cy)
    fill_x(dpad, rows, cols, before, after, 4 * cy + 3 * (cols + 2))
    lattice = lattice_rows()

    def one_tile(l, h):
        columns = mine_columns(jpad, lattice, l, h)
        others = []
        for c in range(3):
            ends = end_rows(jpad, c, l, h, first_sub)
            for dh in (-1, 0, 1):
                ends[dh] = ends[dh] * (1.0 / REACH) + lattice[c]
                if c == 0:
                    ends[dh] = ends[dh] + jnp.where(first_sub, -SPAN, SPAN)
                if c == 1:
                    ends[dh] = ends[dh] + RISE * dh
            others.append(ends)
        pulls = [end_rows(dpad, c, l, h, first_sub) for c in range(3)]

        def weight_of(g, order, dh, here, mine):
            bonded = (bits[l, h, g // 8] & (1 << (3 * (g % 8) + order))) != 0
            return jnp.where(bonded, bond_row(1.0, here, mine), 0.0)

        tile_pass(l, h, columns, others, pulls, weight_of, weights, acc)

    @pl.loop(0, cols)
    def _(h):
        for l in range(rows):
            one_tile(l, h)

    for l in range(rows):
        pulled = [v + part[l, c] for c, v in enumerate(lane_sums(acc, l, cols, 4))]
        totals[l] = pulled[3]
        for c in range(3):
            mine = wall[1, c, l]
            fresh = wall[2, c, l] + STIFFNESS * (pulled[c] - pulled[3] * mine)
            vel1[c, l] = fresh
            base1[c, l] = mine + fresh

    def edge(at):
        def write(out):
            for c in range(3):
                for k in range(rows):
                    out[c * rows + k : c * rows + k + 1, :] = base1[c, k, at : at + 1, :]
            for spare in range(3 * rows, out.shape[0]):
                out[spare : spare + 1, :] = jnp.zeros((1, LANES), F32)

        return write

    place_edges(even_at("wy"), edge(0), edge(cols - 1), to_even, to_odd)


def wall_first(cx, cy, wall, wy_got, fx_got, part, bits):
    rows, cols = wall.shape[2], wall.shape[3]
    edge = (pad8(3 * rows), LANES)
    field = vmem(*wall.shape[1:])
    return pl.pallas_call(
        functools.partial(wall_kernel, cx, cy),
        in_specs=[whole()] * 7,
        out_specs=[whole()] * 6,
        out_shape=[
            jax.ShapeDtypeStruct((rows, cols, STORED, SUB, LANES), F32),
            field,
            field,
            vmem(rows, cols, LANES),
            vmem(*edge),
            vmem(*edge),
        ],
        scratch_shapes=[
            pltpu.VMEM((3, rows + 2, SUB, LANES), F32),
            pltpu.VMEM((3, rows + 2, SUB, LANES), F32),
            pltpu.VMEM((rows, cols, 4, LANES, LANES), F32),
        ],
        compiler_params=params(),
        name="wall_first",
    )(wall, *wy_got, *fx_got, part, bits)


def pack_base_kernel(base1, got_odd, got_even, to_odd, to_even):
    rows, cols = base1.shape[1], base1.shape[2]
    before, after = before_after("wy", got_even, got_odd)

    def edge(l):
        def write(out):
            at = 0
            for c in range(3):
                side = c * rows + l
                out[at : at + 1, :] = before[side : side + 1]
                out[at + 1 : at + 1 + cols, :] = base1[c, l]
                out[at + 1 + cols : at + 2 + cols, :] = after[side : side + 1]
                at += cols + 2
            for spare in range(at, out.shape[0]):
                out[spare : spare + 1, :] = jnp.zeros((1, LANES), F32)

        return write

    place_edges(even_at("fx"), edge(0), edge(rows - 1), to_even, to_odd)


def pack_base(base1, got):
    cols = base1.shape[2]
    out = vmem(pad8(3 * (cols + 2)), LANES)
    return pl.pallas_call(
        pack_base_kernel,
        in_specs=[whole()] * 3,
        out_specs=[whole()] * 2,
        out_shape=[out, out],
        compiler_params=params(),
        name="pack_base",
    )(base1, *got)


def last_kernel(
    weights, end_weights, got, base1, vel1, totals, wyo, wye, fxo, fxe, disp_out, vel_out,
    dpad, acc,
):
    rows, cols = base1.shape[1], base1.shape[2]
    first_sub = lax.broadcasted_iota(jnp.int32, (SUB, LANES), 0) < SUB // 2
    before, after = before_after("wy", wye, wyo)
    fill_y(dpad, base1, before, after, 0)
    before, after = before_after("fx", fxe, fxo)
    fill_x(dpad, rows, cols, before, after, 0)
    total = got[0]
    for d in range(1, got.shape[0]):
        total = total + got[d]
    one, two = unpack_slots(total, cols)
    for k in range(rows + 2):
        here = dpad[0, k, 0 : cols + 2, :] + LOADING * one[k][0 : cols + 2]
        dpad[0, k, 0 : cols + 2, :] = here

    def one_tile(l, h):
        mids = [mid_rows(dpad, c, l, h) for c in range(3)]
        ends = [end_rows(dpad, c, l, h, first_sub) for c in range(3)]
        place = 0
        for g in range(LANES // SUB):
            sums = [None] * 3
            for dh in reached(g):
                for weight, pulls in (
                    (weights[l, h, place], mids), (end_weights[l, h, place], ends)
                ):
                    terms = [weight * pulls[c][dh] for c in range(3)]
                    sums = [t if v is None else v + t for v, t in zip(sums, terms)]
                place += 1
            for c in range(3):
                acc[l, h, c, g * SUB : (g + 1) * SUB, :] = sums[c]

    @pl.loop(0, cols)
    def _(h):
        for l in range(rows):
            one_tile(l, h)

    for l in range(rows):
        pulled = lane_sums(acc, l, cols, 3)
        for c in range(3):
            mine = dpad[c, l + 1, 1 : cols + 1, :]
            force = STIFFNESS * (pulled[c] - totals[l] * mine)
            if c == 0:
                force = force + LOADING * (one[l + 1][1 : cols + 1] + two[l])
            fresh = vel1[c, l] + force
            vel_out[c, l] = fresh
            disp_out[c, l] = mine + fresh


def wall_last(weights, end_weights, got, base1, vel1, totals, wy_got, fx_got):
    rows, cols = base1.shape[1], base1.shape[2]
    return pl.pallas_call(
        last_kernel,
        in_specs=[whole()] * 10,
        out_specs=[whole()] * 2,
        out_shape=[jax.ShapeDtypeStruct(base1.shape, F32)] * 2,
        scratch_shapes=[
            pltpu.VMEM((3, rows + 2, SUB, LANES), F32),
            pltpu.VMEM((rows, cols, 3, LANES, LANES), F32),
        ],
        compiler_params=params(),
        name="wall_last",
    )(weights, end_weights, got, base1, vel1, totals, *wy_got, *fx_got)


def per_device(
    displacement,
    velocity,
    jitter,
    bond_masks,
    pressure,
    pressure_prev,
    speed_sq,
    route_device,
    route_tile,
):
    fx_count, wy_count = lax.axis_size("fx"), lax.axis_size("wy")
    cols = displacement.shape[2]
    device = route_device.reshape(-1, LANES)
    tile = route_tile.reshape(-1, LANES)
    cx, cy = pressure.shape[0], pressure.shape[1]
    rows = displacement.shape[1]
    *sends, part_odd, part_even, wall = pack_wy(
        pressure, pressure_prev, speed_sq, jitter, displacement, velocity
    )
    wy_got = exchange("wy", *sends)
    sends = pack_fx((cx, cy, rows, cols), (part_odd, part_even), wy_got)
    fx_got = exchange("fx", *sends)
    grids = (pressure, pressure_prev, speed_sq)
    weights, part, bits, target, *grids = wall_center(
        wy_count, bond_masks, grids, device, tile, wall, wy_got
    )
    pressure_out, slots = grid_steps(*grids, wy_got, fx_got, target, fx_count, wy_count)
    got = lax.all_to_all(slots, ("fx", "wy"), split_axis=0, concat_axis=0, tiled=True)
    end_weights, vel1, base1, totals, *sends = wall_first(
        cx, cy, wall, wy_got, fx_got, part, bits
    )
    base_wy = exchange("wy", *sends)
    sends = pack_base(base1, base_wy)
    base_fx = exchange("fx", *sends)
    disp_out, vel_out = wall_last(
        weights, end_weights, got, base1, vel1, totals, base_wy, base_fx
    )
    return (disp_out, vel_out, pressure_out)


def solution(mesh):
    placed = (
        P(None, "fx", "wy", None),
        P(None, "fx", "wy", None),
        P(None, "fx", "wy", None),
        P("fx", "wy", None, None, None),
        P("fx", "wy", None),
        P("fx", "wy", None),
        P("fx", "wy", None),
        P(("fx", "wy"), None),
        P(("fx", "wy")),
    )
    return jax.shard_map(
        per_device,
        mesh=mesh,
        in_specs=placed,
        out_specs=(P(None, "fx", "wy", None), P(None, "fx", "wy", None), P("fx", "wy", None)),
        check_vma=False,
    )
```

```python
import functools

import jax
import jax.numpy as jnp
from jax import lax
from jax.experimental import pallas as pl
from jax.experimental.pallas import tpu as pltpu
from jax.sharding import PartitionSpec as P

STIFFNESS = 0.02
LOADING = 0.05
REACH = 3.0
LANES = 128
SUB = 8
VMEM_BYTES = 32 * 1024 * 1024
HBM = pl.BlockSpec(memory_space=pltpu.HBM)

F32 = jnp.float32
BF16 = jnp.bfloat16


def whole():
    return pl.BlockSpec(memory_space=pltpu.VMEM)


def params():
    return pltpu.CompilerParams(vmem_limit_bytes=VMEM_BYTES)


def vmem(*shape):
    return pltpu.VMEM(shape, F32)


def even_at(axis):
    return lax.rem(lax.axis_index(axis), 2) == 0


def swap_pairs(axis, sizes, first):
    count, others = sizes[axis], sizes[1 - axis]
    pairs = []

    def join(*two):
        a, b = [place * sizes[1] + other for place, other in two]
        pairs.extend([(a, b), (b, a)])

    def at(place, other):
        return (place, other) if axis == 0 else (other, place)

    met = set()
    for low in range(first, count - 1, 2):
        met.update((low, low + 1))
        for other in range(others):
            join(at(low, other), at(low + 1, other))
    for place in range(count):
        if place not in met and others % 2 == 0:
            for other in range(0, others, 2):
                join(at(place, other), at(place, other + 1))
    return pairs


def exchange(axis, to_odd, to_even):
    names = ("fx", "wy")
    sizes = [lax.axis_size(name) for name in names]
    along = names.index(axis)
    got_odd = lax.ppermute(to_odd, names, swap_pairs(along, sizes, 1))
    got_even = lax.ppermute(to_even, names, swap_pairs(along, sizes, 0))
    return got_odd, got_even


def place_edges(even, low, high, to_even, to_odd):
    @pl.when(even)
    def _():
        high(to_even)
        low(to_odd)

    @pl.when(jnp.logical_not(even))
    def _():
        low(to_even)
        high(to_odd)


def before_after(axis, got_even, got_odd):
    even = even_at(axis)
    place, last = lax.axis_index(axis), lax.axis_size(axis) - 1
    a, b = got_even[...], got_odd[...]
    before = jnp.where(place == 0, 0.0, jnp.where(even, b, a))
    after = jnp.where(place == last, 0.0, jnp.where(even, a, b))
    return before, after


def pack_wy_kernel(
    p, q, s, jit_in, disp_in, vel_in, wy_odd, wy_even, fx_odd, fx_even, wall, edges, ends, sems
):
    cx, cy = p.shape[0], p.shape[1]
    rows, cols = jit_in.shape[1], jit_in.shape[2]
    pairs = []
    for k, field in enumerate((p, q, s)):
        for side, first in enumerate((0, cy - SUB)):
            pairs.append((field.at[:, first : first + SUB, :], edges.at[2 * k + side]))
    pairs.append((p.at[0:2], ends.at[0, 0:2]))
    pairs.append((p.at[cx - 2 : cx], ends.at[1, 0:2]))
    for k, field in enumerate((q, s)):
        pairs.append((field.at[0], ends.at[0, 2 + k]))
        pairs.append((field.at[cx - 1], ends.at[1, 2 + k]))
    for k, field in enumerate((jit_in, disp_in, vel_in)):
        pairs.append((field, wall.at[k]))
    copies = [pltpu.make_async_copy(a, b, sems.at[k]) for k, (a, b) in enumerate(pairs)]
    for copy in copies:
        copy.start()
    for copy in copies:
        copy.wait()

    def edge(side, near, far, h):
        def write(out):
            out[0:cx, :] = edges[side, :, near, :]
            out[cx : 2 * cx, :] = edges[side, :, far, :]
            out[2 * cx : 3 * cx, :] = edges[2 + side, :, near, :]
            out[3 * cx : 4 * cx, :] = edges[4 + side, :, near, :]
            at = 4 * cx
            for field in range(2):
                for c in range(3):
                    for l in range(rows):
                        out[at : at + 1, :] = wall[field, c, l, h : h + 1, :]
                        at += 1
            for spare in range(at, out.shape[0]):
                out[spare : spare + 1, :] = jnp.zeros((1, LANES), F32)

        return write

    place_edges(
        even_at("wy"),
        edge(0, 0, 1, 0),
        edge(1, SUB - 1, SUB - 2, cols - 1),
        wy_even,
        wy_odd,
    )

    def end(side, near, far, l):
        def write(out):
            out[0:cy, :] = ends[side, near]
            out[cy : 2 * cy, :] = ends[side, far]
            out[2 * cy : 3 * cy, :] = ends[side, 2]
            out[3 * cy : 4 * cy, :] = ends[side, 3]
            at = 4 * cy
            for field in range(2):
                for c in range(3):
                    out[at + 1 : at + 1 + cols, :] = wall[field, c, l]
                    at += cols + 2

        return write

    place_edges(even_at("fx"), end(0, 0, 1, 0), end(1, 1, 0, rows - 1), fx_even, fx_odd)


def in_hbm(*arrays):
    return [pltpu.with_memory_space_constraint(v, pltpu.HBM) for v in arrays]


def pad8(count):
    return (count + 7) // 8 * 8


def pack_wy(p, q, s, jit, disp, vel):
    cx, cy = p.shape[0], p.shape[1]
    rows, cols = jit.shape[1], jit.shape[2]
    wy_out = vmem(pad8(4 * cx + 6 * rows), LANES)
    fx_out = vmem(pad8(4 * cy + 6 * (cols + 2) + 2), LANES)
    return pl.pallas_call(
        pack_wy_kernel,
        in_specs=[HBM] * 6,
        out_specs=[whole()] * 5,
        out_shape=[wy_out, wy_out, fx_out, fx_out, vmem(3, *jit.shape)],
        scratch_shapes=[
            pltpu.VMEM((6, cx, SUB, LANES), F32),
            pltpu.VMEM((2, 4, cy, LANES), F32),
            pltpu.SemaphoreType.DMA((15,)),
        ],
        compiler_params=params(),
        name="pack_wy",
    )(*in_hbm(p, q, s, jit, disp, vel))


def pack_fx_kernel(cx, cy, rows, cols, part_odd, part_even, got_odd, got_even, to_odd, to_even):
    before, after = before_after("wy", got_even, got_odd)
    to_even[...] = part_even[...]
    to_odd[...] = part_odd[...]

    def corners(x, l):
        def write(out):
            at = 4 * cy
            for k in range(6):
                side = 4 * cx + k * rows + l
                out[at : at + 1, :] = before[side : side + 1]
                out[at + 1 + cols : at + 2 + cols, :] = after[side : side + 1]
                at += cols + 2
            out[at : at + 1, :] = before[x : x + 1]
            out[at + 1 : at + 2, :] = after[x : x + 1]

        return write

    place_edges(even_at("fx"), corners(0, 0), corners(cx - 1, rows - 1), to_even, to_odd)


def pack_fx(sizes, parts, got):
    out = vmem(*parts[0].shape)
    return pl.pallas_call(
        functools.partial(pack_fx_kernel, *sizes),
        in_specs=[whole()] * 4,
        out_specs=[whole()] * 2,
        out_shape=[out, out],
        compiler_params=params(),
        name="pack_fx",
    )(*parts, *got)


def along_z(v):
    lane = lax.broadcasted_iota(jnp.int32, v.shape, 1)
    up = jnp.where(lane == LANES - 1, 0.0, pltpu.roll(v, LANES - 1, 1))
    down = jnp.where(lane == 0, 0.0, pltpu.roll(v, 1, 1))
    return up + down


def update(v, old, speed, beside):
    return 2.0 * v - old + speed * (beside + along_z(v) - 6.0 * v)


def two_terms(v):
    high = v.astype(BF16)
    return high, (v - high.astype(F32)).astype(BF16)


def grid_kernel(p, q, s, wyo, wye, fxo, fxe, target, out, slots, s0, s1, rhs, part1, part2):
    cx, cy = p.shape[0], p.shape[1]
    ahead, behind = SUB, SUB + cy
    fx_count = part1.shape[0] // 2 - 1
    cols = 4
    tall = part2.shape[0]
    high = part1.shape[1] - 2 * SUB
    wy_count = high // cols
    before_y, after_y = before_after("wy", wye, wyo)
    before_x, after_x = before_after("fx", fxe, fxo)
    corner = 4 * cy + 6 * (cols + 2)

    s0[1 : cx + 1, ahead:behind, :] = p[...]
    for x, side in ((0, before_x), (cx + 1, after_x)):
        s0[x, ahead:behind, :] = side[0:cy]
        s0[x, ahead - 1 : ahead, :] = side[corner : corner + 1]
        s0[x, behind : behind + 1, :] = side[corner + 1 : corner + 2]
    s0[1 : cx + 1, ahead - 1, :] = before_y[0:cx]
    s0[1 : cx + 1, behind, :] = after_y[0:cx]

    for side, y, inner in ((before_y, ahead - 1, ahead), (after_y, behind, behind - 1)):
        near, far = side[0:cx], side[cx : 2 * cx]
        old, speed = side[2 * cx : 3 * cx], side[3 * cx : 4 * cx]
        beside = s0[0:cx, y, :] + s0[2 : cx + 2, y, :] + far + s0[1 : cx + 1, inner, :]
        s1[1 : cx + 1, y, :] = update(near, old, speed, beside)
    for side, x, inner in ((before_x, 0, 1), (after_x, cx + 1, cx)):
        near, far = side[0:cy], side[cy : 2 * cy]
        old, speed = side[2 * cy : 3 * cy], side[3 * cy : 4 * cy]
        beside = s0[x, ahead - 1 : behind - 1, :] + s0[x, ahead + 1 : behind + 1, :]
        beside = beside + far + s0[inner, ahead:behind, :]
        s1[x, ahead:behind, :] = update(near, old, speed, beside)

    def sweep(now, old, x):
        beside = now[x, ahead:behind, :] + now[x + 2, ahead:behind, :]
        beside = beside + now[x + 1, ahead - 1 : behind - 1, :]
        beside = beside + now[x + 1, ahead + 1 : behind + 1, :]
        return update(now[x + 1, ahead:behind, :], old, s[x], beside)

    for x in range(cx):
        fresh = sweep(s0, q[x], x)
        s1[x + 1, ahead:behind, :] = fresh
        a, b = two_terms(fresh)
        rhs[x * cy : (x + 1) * cy, 0:LANES] = a
        rhs[x * cy : (x + 1) * cy, LANES : 2 * LANES] = b
    for x in range(cx):
        fresh = sweep(s1, p[x], x)
        out[x] = fresh
        a, b = two_terms(fresh)
        rhs[x * cy : (x + 1) * cy, 2 * LANES : 3 * LANES] = a
        rhs[x * cy : (x + 1) * cy, 3 * LANES : 4 * LANES] = b

    part1[...] = jnp.zeros(part1.shape, F32)
    part2[:, 0:SUB, :] = jnp.zeros((tall, SUB, LANES), F32)
    chunk = 256
    for first in range(0, tall * high, chunk):
        tile = lax.broadcasted_iota(jnp.int32, (chunk, LANES), 0) + first
        picks = []
        for piece in range(target.shape[0]):
            picks.append(jnp.where(tile == target[piece : piece + 1, :], 1.0, 0.0).astype(BF16))
        sums = jnp.dot(jnp.concatenate(picks, axis=1), rhs[...], preferred_element_type=F32)
        one = sums[:, 0:LANES] + sums[:, LANES : 2 * LANES]
        two = sums[:, 2 * LANES : 3 * LANES] + sums[:, 3 * LANES : 4 * LANES]
        l = first // high
        part1[1 + l : 1 + l + chunk // high, SUB : SUB + high, :] = one.reshape(-1, high, LANES)
        part2[l : l + chunk // high, SUB : SUB + high, :] = two.reshape(-1, high, LANES)
    sub = lax.broadcasted_iota(jnp.int32, (SUB, LANES), 0)
    lane = lax.broadcasted_iota(jnp.int32, (SUB, LANES), 1)
    step1 = sub < cols + 2
    for a in range(fx_count):
        for b in range(wy_count):
            h = SUB + cols * b
            slot = a * wy_count + b
            one = [part1[2 * a + l, h - 1 : h - 1 + SUB, :] for l in range(4)]
            ends = jnp.where(lane % 8 < 4, one[3], one[0])
            two = [
                part2[2 * a + l, h + at - 6 : h + at - 6 + SUB, :]
                for l, at in ((0, 0), (0, 2), (1, 0))
            ]
            x = jnp.broadcast_to(part2[2 * a + 1, h + 2 : h + 3, :], (SUB, LANES))
            y = jnp.broadcast_to(part2[2 * a + 1, h + 3 : h + 4, :], (SUB, LANES))
            for r in range(4):
                moved = pltpu.roll(y, (3 - 2 * r) % LANES, 1)
                ends = jnp.where((sub == 1 + r) & free_ends(lane), moved, ends)
            low, high_free = (sub == 0) & (lane // 8 % 4 == 0), (sub == cols + 1) & (lane // 8 % 4 == 3)
            own0 = jnp.where(low | high_free, x, one[1])
            own1 = jnp.where(low, pltpu.roll(x, LANES - 8, 1), one[2])
            own1 = jnp.where(high_free, pltpu.roll(x, 8, 1), own1)
            for k, group in enumerate((ends, own0, own1)):
                slots[slot, k * SUB : (k + 1) * SUB, :] = jnp.where(step1, group, two[k])


def free_ends(lane):
    return (lane % 8 == 3) | (lane % 8 == 4)


def unpack_slots(total, cols):
    ends, own0, own1 = [total[k * SUB : (k + 1) * SUB] for k in range(3)]
    lane = lax.broadcasted_iota(jnp.int32, (1, LANES), 1)
    two = [[ends[6:7], ends[7:8], own0[6:7], own0[7:8]], [own1[6:7], own1[7:8]]]
    q = lane // 8 % 4
    last = cols + 1
    x = jnp.where(q == 0, own0[0:1], own0[last : last + 1])
    x = jnp.where(q == 1, pltpu.roll(own1[0:1], 8, 1), x)
    x = jnp.where(q == 2, pltpu.roll(own1[last : last + 1], LANES - 8, 1), x)
    y = None
    for r in range(4):
        moved = pltpu.roll(ends[1 + r : 2 + r], (2 * r - 3) % LANES, 1)
        y = moved if y is None else jnp.where(lane % 8 // 2 == r, moved, y)
    two[1].extend([x, y])
    two = [jnp.concatenate(v, axis=0) for v in two]
    return (ends, own0, own1, ends), two


def grid_steps(p, q, s, wy_got, fx_got, target, fx_count, wy_count):
    cx, cy = p.shape[0], p.shape[1]
    tall, high = fx_count * 2, wy_count * 4
    devices = fx_count * wy_count
    return pl.pallas_call(
        grid_kernel,
        in_specs=[whole()] * 8,
        out_specs=[whole()] * 2,
        out_shape=[
            jax.ShapeDtypeStruct(p.shape, F32),
            vmem(devices, 3 * SUB, LANES),
        ],
        scratch_shapes=[
            pltpu.VMEM((cx + 2, cy + 2 * SUB, LANES), F32),
            pltpu.VMEM((cx + 2, cy + 2 * SUB, LANES), F32),
            pltpu.VMEM((cx * cy, 4 * LANES), BF16),
            pltpu.VMEM((tall + 2, high + 2 * SUB, LANES), F32),
            pltpu.VMEM((tall, high + 2 * SUB, LANES), F32),
        ],
        compiler_params=params(),
        name="grid_steps",
    )(p, q, s, *wy_got, *fx_got, target)


def reached(g):
    groups = []
    for dh in (-1, 0, 1):
        if (dh == -1 and g % 4 == 3) or (dh == 1 and g % 4 == 0):
            continue
        groups.append(dh)
    return groups


STORED = sum(len(reached(g)) for g in range(LANES // SUB))


def mid_rows(ref, c, l, h):
    rows = {}
    for dh in (-1, 0, 1):
        row = ref[c, l + 1, pl.ds(h + 1 + dh, 1), :]
        rows[dh] = jnp.broadcast_to(row, (SUB, LANES))
    return rows


def end_rows(ref, c, l, h, first_sub):
    rows = {}
    for dh in (-1, 0, 1):
        at = pl.ds(h + 1 + dh, 1)
        before = jnp.broadcast_to(ref[c, l, at, :], (SUB, LANES))
        after = jnp.broadcast_to(ref[c, l + 2, at, :], (SUB, LANES))
        rows[dh] = jnp.where(first_sub, before, after)
    return rows


def fill_y(pad, own, before, after, at):
    rows, cols = own.shape[1], own.shape[2]
    for c in range(3):
        for l in range(rows):
            row = at + c * rows + l
            pad[c, l + 1, 0:1, :] = before[row : row + 1]
            pad[c, l + 1, 1 : cols + 1, :] = own[c, l]
            pad[c, l + 1, cols + 1 : cols + 2, :] = after[row : row + 1]


def fill_x(pad, rows, cols, before, after, at):
    for c in range(3):
        row = at + c * (cols + 2)
        pad[c, 0, 0 : cols + 2, :] = before[row : row + cols + 2]
        pad[c, rows + 1, 0 : cols + 2, :] = after[row : row + cols + 2]


def lattice_rows():
    index = lax.broadcasted_iota(jnp.int32, (1, LANES), 1)
    places = (index % 8, index // 8 % 4, index // 32)
    return [v.astype(F32) * (1.0 / REACH) for v in places]


SPAN = 8.0 / REACH
RISE = 4.0 / REACH


def mine_columns(ref, lattice, l, h):
    sub = lax.broadcasted_iota(jnp.int32, (SUB, LANES), 0)
    own = []
    for c in range(3):
        row = ref[c, l + 1, pl.ds(h + 1, 1), :] * (1.0 / REACH) + lattice[c]
        own.append(jnp.broadcast_to(row, (SUB, LANES)))
    return jnp.transpose(jnp.where(sub == 0, own[0], jnp.where(sub == 1, own[1], own[2])))


def bond_row(weight, others, mine):
    for c in range(3):
        diff = others[c] - mine[c]
        weight = weight - diff * diff
    return jnp.maximum(weight, 0.0)


def tile_pass(l, h, columns, others, pulls, weight_of, weights, acc):
    place = 0
    for g in range(LANES // SUB):
        span = slice(g * SUB, (g + 1) * SUB)
        mine = [jnp.broadcast_to(columns[span, c : c + 1], (SUB, LANES)) for c in range(3)]
        sums = [None] * 4
        for order, dh in enumerate(reached(g)):
            here = [others[c][dh] for c in range(3)]
            weight = weight_of(g, order, dh, here, mine)
            weights[l, h, place] = weight
            place += 1
            terms = [weight * pulls[c][dh] for c in range(3)] + [weight]
            sums = [t if v is None else v + t for v, t in zip(sums, terms)]
        for c in range(4):
            acc[l, h, c, span, :] = sums[c]


def lane_sums(acc, l, cols, count):
    ones = jnp.ones((2 * SUB, LANES), BF16)
    result = [[] for _ in range(count)]
    for h in range(cols):
        terms = []
        for c in range(count):
            terms.extend(two_terms(acc[l, h, c]))
        sums = lax.dot_general(
            ones,
            jnp.concatenate(terms, axis=0),
            (((1,), (1,)), ((), ())),
            preferred_element_type=F32,
        )[0:1]
        for c in range(count):
            at = 2 * c * LANES
            result[c].append(sums[:, at : at + LANES] + sums[:, at + LANES : at + 2 * LANES])
    return [jnp.concatenate(parts, axis=0) for parts in result]


def quotient(v, n):
    return ((v.astype(F32) + 0.5) * (1.0 / n)).astype(jnp.int32)


def center_kernel(
    wy_count, masks_in, p_in, q_in, s_in, device_in, tile_in, wall, wyo, wye,
    weights, part, bits, target, p, q, s, jpad, dpad, acc, masks, route, sems,
):
    rows, cols = wall.shape[2], wall.shape[3]
    cx = p.shape[0]
    copies = {}
    pairs = [(device_in, route.at[0]), (tile_in, route.at[1])]
    pairs = [(p_in, p), (q_in, q), (s_in, s)] + pairs
    for k, pair in enumerate(pairs):
        copies[k] = pltpu.make_async_copy(*pair, sems.at[rows * cols + k])
    for h in range(cols):
        for l in range(rows):
            copies[l, h] = pltpu.make_async_copy(
                masks_in.at[l, h], masks.at[l, h], sems.at[l * cols + h]
            )
    for copy in copies.values():
        copy.start()
    first_sub = lax.broadcasted_iota(jnp.int32, (SUB, LANES), 0) < SUB // 2
    copies[3].wait()
    copies[4].wait()
    device, tile = route[0], route[1]
    a, t = quotient(device, wy_count), quotient(tile, cols)
    b, u = device - a * wy_count, tile - t * cols
    target[...] = (a * rows + t) * (wy_count * cols) + b * cols + u
    before, after = before_after("wy", wye, wyo)
    fill_y(jpad, wall.at[0], before, after, 4 * cx)
    fill_y(dpad, wall.at[1], before, after, 4 * cx + 3 * rows)
    lattice = lattice_rows()

    def one_tile(l, h):
        columns = mine_columns(jpad, lattice, l, h)
        others = []
        for c in range(3):
            mid = mid_rows(jpad, c, l, h)
            for dh in (-1, 0, 1):
                mid[dh] = mid[dh] * (1.0 / REACH) + lattice[c]
                if c == 1:
                    mid[dh] = mid[dh] + RISE * dh
            others.append(mid)
        pulls = [mid_rows(dpad, c, l, h) for c in range(3)]
        words = [jnp.zeros((SUB, LANES), jnp.int32) for _ in range(2)]

        def weight_of(g, order, dh, here, mine):
            span = slice(g * SUB, (g + 1) * SUB)
            before = masks[l, h, 1 + dh, span, :]
            after = masks[l, h, 7 + dh, span, :]
            place = 3 * (g % 8) + order
            words[g // 8] = words[g // 8] + jnp.where(first_sub, before, after) * (1 << place)
            return bond_row(masks[l, h, 4 + dh, span, :].astype(F32), here, mine)

        tile_pass(l, h, columns, others, pulls, weight_of, weights, acc)
        for k in range(2):
            bits[l, h, k] = words[k]

    for h in range(cols):
        for l in range(rows):
            copies[l, h].wait()
            one_tile(l, h)
    for l in range(rows):
        for c, sums in enumerate(lane_sums(acc, l, cols, 4)):
            part[l, c] = sums
    for k in range(3):
        copies[k].wait()


def wall_center(wy_count, masks, grids, device, tile, wall, wy_got):
    rows, cols = wall.shape[2], wall.shape[3]
    return pl.pallas_call(
        functools.partial(center_kernel, wy_count),
        in_specs=[HBM] * 6 + [whole()] * 3,
        out_specs=[whole()] * 7,
        out_shape=[
            jax.ShapeDtypeStruct((rows, cols, STORED, SUB, LANES), F32),
            vmem(rows, 4, cols, LANES),
            pltpu.VMEM((rows, cols, 2, SUB, LANES), jnp.int32),
            pltpu.VMEM(device.shape, jnp.int32),
        ]
        + [vmem(*grids[0].shape)] * 3,
        scratch_shapes=[
            vmem(3, rows + 2, SUB, LANES),
            vmem(3, rows + 2, SUB, LANES),
            vmem(rows, cols, 4, LANES, LANES),
            pltpu.VMEM(masks.shape, jnp.int32),
            pltpu.VMEM((2,) + device.shape, jnp.int32),
            pltpu.SemaphoreType.DMA((rows * cols + 5,)),
        ],
        compiler_params=params(),
        name="wall_center",
    )(*in_hbm(masks, *grids, device, tile), wall, *wy_got)


def wall_kernel(
    cx, cy, wall, wyo, wye, fxo, fxe, part, bits, weights, vel1, base1, totals, to_odd, to_even,
    jpad, dpad, acc,
):
    rows, cols = wall.shape[2], wall.shape[3]
    first_sub = lax.broadcasted_iota(jnp.int32, (SUB, LANES), 0) < SUB // 2
    before, after = before_after("wy", wye, wyo)
    fill_y(jpad, wall.at[0], before, after, 4 * cx)
    fill_y(dpad, wall.at[1], before, after, 4 * cx + 3 * rows)
    before, after = before_after("fx", fxe, fxo)
    fill_x(jpad, rows, cols, before, after, 4 * cy)
    fill_x(dpad, rows, cols, before, after, 4 * cy + 3 * (cols + 2))
    lattice = lattice_rows()

    def one_tile(l, h):
        columns = mine_columns(jpad, lattice, l, h)
        others = []
        for c in range(3):
            ends = end_rows(jpad, c, l, h, first_sub)
            for dh in (-1, 0, 1):
                ends[dh] = ends[dh] * (1.0 / REACH) + lattice[c]
                if c == 0:
                    ends[dh] = ends[dh] + jnp.where(first_sub, -SPAN, SPAN)
                if c == 1:
                    ends[dh] = ends[dh] + RISE * dh
            others.append(ends)
        pulls = [end_rows(dpad, c, l, h, first_sub) for c in range(3)]

        def weight_of(g, order, dh, here, mine):
            bonded = (bits[l, h, g // 8] & (1 << (3 * (g % 8) + order))) != 0
            return jnp.where(bonded, bond_row(1.0, here, mine), 0.0)

        tile_pass(l, h, columns, others, pulls, weight_of, weights, acc)

    @pl.loop(0, cols)
    def _(h):
        for l in range(rows):
            one_tile(l, h)

    for l in range(rows):
        pulled = [v + part[l, c] for c, v in enumerate(lane_sums(acc, l, cols, 4))]
        totals[l] = pulled[3]
        for c in range(3):
            mine = wall[1, c, l]
            fresh = wall[2, c, l] + STIFFNESS * (pulled[c] - pulled[3] * mine)
            vel1[c, l] = fresh
            base1[c, l] = mine + fresh

    def edge(at):
        def write(out):
            for c in range(3):
                for k in range(rows):
                    out[c * rows + k : c * rows + k + 1, :] = base1[c, k, at : at + 1, :]
            for spare in range(3 * rows, out.shape[0]):
                out[spare : spare + 1, :] = jnp.zeros((1, LANES), F32)

        return write

    place_edges(even_at("wy"), edge(0), edge(cols - 1), to_even, to_odd)


def wall_first(cx, cy, wall, wy_got, fx_got, part, bits):
    rows, cols = wall.shape[2], wall.shape[3]
    edge = (pad8(3 * rows), LANES)
    field = vmem(*wall.shape[1:])
    return pl.pallas_call(
        functools.partial(wall_kernel, cx, cy),
        in_specs=[whole()] * 7,
        out_specs=[whole()] * 6,
        out_shape=[
            jax.ShapeDtypeStruct((rows, cols, STORED, SUB, LANES), F32),
            field,
            field,
            vmem(rows, cols, LANES),
            vmem(*edge),
            vmem(*edge),
        ],
        scratch_shapes=[
            pltpu.VMEM((3, rows + 2, SUB, LANES), F32),
            pltpu.VMEM((3, rows + 2, SUB, LANES), F32),
            pltpu.VMEM((rows, cols, 4, LANES, LANES), F32),
        ],
        compiler_params=params(),
        name="wall_first",
    )(wall, *wy_got, *fx_got, part, bits)


def pack_base_kernel(base1, got_odd, got_even, to_odd, to_even):
    rows, cols = base1.shape[1], base1.shape[2]
    before, after = before_after("wy", got_even, got_odd)

    def edge(l):
        def write(out):
            at = 0
            for c in range(3):
                side = c * rows + l
                out[at : at + 1, :] = before[side : side + 1]
                out[at + 1 : at + 1 + cols, :] = base1[c, l]
                out[at + 1 + cols : at + 2 + cols, :] = after[side : side + 1]
                at += cols + 2
            for spare in range(at, out.shape[0]):
                out[spare : spare + 1, :] = jnp.zeros((1, LANES), F32)

        return write

    place_edges(even_at("fx"), edge(0), edge(rows - 1), to_even, to_odd)


def pack_base(base1, got):
    cols = base1.shape[2]
    out = vmem(pad8(3 * (cols + 2)), LANES)
    return pl.pallas_call(
        pack_base_kernel,
        in_specs=[whole()] * 3,
        out_specs=[whole()] * 2,
        out_shape=[out, out],
        compiler_params=params(),
        name="pack_base",
    )(base1, *got)


def last_kernel(
    weights, end_weights, got, base1, vel1, totals, wyo, wye, fxo, fxe, disp_out, vel_out,
    dpad, acc,
):
    rows, cols = base1.shape[1], base1.shape[2]
    first_sub = lax.broadcasted_iota(jnp.int32, (SUB, LANES), 0) < SUB // 2
    before, after = before_after("wy", wye, wyo)
    fill_y(dpad, base1, before, after, 0)
    before, after = before_after("fx", fxe, fxo)
    fill_x(dpad, rows, cols, before, after, 0)
    total = got[0]
    for d in range(1, got.shape[0]):
        total = total + got[d]
    one, two = unpack_slots(total, cols)
    for k in range(rows + 2):
        here = dpad[0, k, 0 : cols + 2, :] + LOADING * one[k][0 : cols + 2]
        dpad[0, k, 0 : cols + 2, :] = here

    def one_tile(l, h):
        mids = [mid_rows(dpad, c, l, h) for c in range(3)]
        ends = [end_rows(dpad, c, l, h, first_sub) for c in range(3)]
        place = 0
        for g in range(LANES // SUB):
            sums = [None] * 3
            for dh in reached(g):
                for weight, pulls in (
                    (weights[l, h, place], mids), (end_weights[l, h, place], ends)
                ):
                    terms = [weight * pulls[c][dh] for c in range(3)]
                    sums = [t if v is None else v + t for v, t in zip(sums, terms)]
                place += 1
            for c in range(3):
                acc[l, h, c, g * SUB : (g + 1) * SUB, :] = sums[c]

    @pl.loop(0, cols)
    def _(h):
        for l in range(rows):
            one_tile(l, h)

    for l in range(rows):
        pulled = lane_sums(acc, l, cols, 3)
        for c in range(3):
            mine = dpad[c, l + 1, 1 : cols + 1, :]
            force = STIFFNESS * (pulled[c] - totals[l] * mine)
            if c == 0:
                force = force + LOADING * (one[l + 1][1 : cols + 1] + two[l])
            fresh = vel1[c, l] + force
            vel_out[c, l] = fresh
            disp_out[c, l] = mine + fresh


def wall_last(weights, end_weights, got, base1, vel1, totals, wy_got, fx_got):
    rows, cols = base1.shape[1], base1.shape[2]
    return pl.pallas_call(
        last_kernel,
        in_specs=[whole()] * 10,
        out_specs=[whole()] * 2,
        out_shape=[jax.ShapeDtypeStruct(base1.shape, F32)] * 2,
        scratch_shapes=[
            pltpu.VMEM((3, rows + 2, SUB, LANES), F32),
            pltpu.VMEM((rows, cols, 3, LANES, LANES), F32),
        ],
        compiler_params=params(),
        name="wall_last",
    )(weights, end_weights, got, base1, vel1, totals, *wy_got, *fx_got)


def per_device(
    displacement,
    velocity,
    jitter,
    bond_masks,
    pressure,
    pressure_prev,
    speed_sq,
    route_device,
    route_tile,
):
    fx_count, wy_count = lax.axis_size("fx"), lax.axis_size("wy")
    cols = displacement.shape[2]
    device = route_device.reshape(-1, LANES)
    tile = route_tile.reshape(-1, LANES)
    cx, cy = pressure.shape[0], pressure.shape[1]
    rows = displacement.shape[1]
    *sends, part_odd, part_even, wall = pack_wy(
        pressure, pressure_prev, speed_sq, jitter, displacement, velocity
    )
    wy_got = exchange("wy", *sends)
    sends = pack_fx((cx, cy, rows, cols), (part_odd, part_even), wy_got)
    fx_got = exchange("fx", *sends)
    grids = (pressure, pressure_prev, speed_sq)
    weights, part, bits, target, *grids = wall_center(
        wy_count, bond_masks, grids, device, tile, wall, wy_got
    )
    pressure_out, slots = grid_steps(*grids, wy_got, fx_got, target, fx_count, wy_count)
    got = lax.all_to_all(slots, ("fx", "wy"), split_axis=0, concat_axis=0, tiled=True)
    end_weights, vel1, base1, totals, *sends = wall_first(
        cx, cy, wall, wy_got, fx_got, part, bits
    )
    base_wy = exchange("wy", *sends)
    sends = pack_base(base1, base_wy)
    base_fx = exchange("fx", *sends)
    disp_out, vel_out = wall_last(
        weights, end_weights, got, base1, vel1, totals, base_wy, base_fx
    )
    return (disp_out, vel_out, pressure_out)


def solution(mesh):
    placed = (
        P(None, "fx", "wy", None),
        P(None, "fx", "wy", None),
        P(None, "fx", "wy", None),
        P("fx", "wy", None, None, None),
        P("fx", "wy", None),
        P("fx", "wy", None),
        P("fx", "wy", None),
        P(("fx", "wy"), None),
        P(("fx", "wy")),
    )
    return jax.shard_map(
        per_device,
        mesh=mesh,
        in_specs=placed,
        out_specs=(P(None, "fx", "wy", None), P(None, "fx", "wy", None), P("fx", "wy", None)),
        check_vma=False,
    )
```

```python
import functools

import jax
import jax.numpy as jnp
from jax import lax
from jax.experimental import pallas as pl
from jax.experimental.pallas import tpu as pltpu
from jax.sharding import PartitionSpec as P

STIFFNESS = 0.02
LOADING = 0.05
REACH = 3.0
LANES = 128
SUB = 8
VMEM_BYTES = 32 * 1024 * 1024
HBM = pl.BlockSpec(memory_space=pltpu.HBM)

F32 = jnp.float32
BF16 = jnp.bfloat16


def whole():
    return pl.BlockSpec(memory_space=pltpu.VMEM)


def params():
    return pltpu.CompilerParams(vmem_limit_bytes=VMEM_BYTES)


def vmem(*shape):
    return pltpu.VMEM(shape, F32)


def even_at(axis):
    return lax.rem(lax.axis_index(axis), 2) == 0


def swap_pairs(axis, sizes, first):
    count, others = sizes[axis], sizes[1 - axis]
    pairs = []

    def join(*two):
        a, b = [place * sizes[1] + other for place, other in two]
        pairs.extend([(a, b), (b, a)])

    def at(place, other):
        return (place, other) if axis == 0 else (other, place)

    met = set()
    for low in range(first, count - 1, 2):
        met.update((low, low + 1))
        for other in range(others):
            join(at(low, other), at(low + 1, other))
    for place in range(count):
        if place not in met and others % 2 == 0:
            for other in range(0, others, 2):
                join(at(place, other), at(place, other + 1))
    return pairs


def exchange(axis, to_odd, to_even):
    names = ("fx", "wy")
    sizes = [lax.axis_size(name) for name in names]
    along = names.index(axis)
    got_odd = lax.ppermute(to_odd, names, swap_pairs(along, sizes, 1))
    got_even = lax.ppermute(to_even, names, swap_pairs(along, sizes, 0))
    return got_odd, got_even


def place_edges(even, low, high, to_even, to_odd):
    @pl.when(even)
    def _():
        high(to_even)
        low(to_odd)

    @pl.when(jnp.logical_not(even))
    def _():
        low(to_even)
        high(to_odd)


def before_after(axis, got_even, got_odd):
    even = even_at(axis)
    place, last = lax.axis_index(axis), lax.axis_size(axis) - 1
    a, b = got_even[...], got_odd[...]
    before = jnp.where(place == 0, 0.0, jnp.where(even, b, a))
    after = jnp.where(place == last, 0.0, jnp.where(even, a, b))
    return before, after


def pack_wy_kernel(
    p, q, s, jit_in, disp_in, vel_in, wy_odd, wy_even, ends, wall, edges, sems
):
    cx, cy = p.shape[0], p.shape[1]
    rows, cols = jit_in.shape[1], jit_in.shape[2]
    pairs = []
    for k, field in enumerate((p, q, s)):
        for side, first in enumerate((0, cy - SUB)):
            pairs.append((field.at[:, first : first + SUB, :], edges.at[2 * k + side]))
    pairs.append((p.at[0:2], ends.at[0, 0:2]))
    pairs.append((p.at[cx - 2 : cx], ends.at[1, 0:2]))
    for k, field in enumerate((q, s)):
        pairs.append((field.at[0], ends.at[0, 2 + k]))
        pairs.append((field.at[cx - 1], ends.at[1, 2 + k]))
    for k, field in enumerate((jit_in, disp_in, vel_in)):
        pairs.append((field, wall.at[k]))
    copies = [pltpu.make_async_copy(a, b, sems.at[k]) for k, (a, b) in enumerate(pairs)]
    for copy in copies:
        copy.start()
    for copy in copies:
        copy.wait()

    def edge(side, near, far, h):
        def write(out):
            out[0:cx, :] = edges[side, :, near, :]
            out[cx : 2 * cx, :] = edges[side, :, far, :]
            out[2 * cx : 3 * cx, :] = edges[2 + side, :, near, :]
            out[3 * cx : 4 * cx, :] = edges[4 + side, :, near, :]
            at = 4 * cx
            for field in range(2):
                for c in range(3):
                    for l in range(rows):
                        out[at : at + 1, :] = wall[field, c, l, h : h + 1, :]
                        at += 1
            for spare in range(at, out.shape[0]):
                out[spare : spare + 1, :] = jnp.zeros((1, LANES), F32)

        return write

    place_edges(
        even_at("wy"),
        edge(0, 0, 1, 0),
        edge(1, SUB - 1, SUB - 2, cols - 1),
        wy_even,
        wy_odd,
    )


def in_hbm(*arrays):
    return [pltpu.with_memory_space_constraint(v, pltpu.HBM) for v in arrays]


def pad8(count):
    return (count + 7) // 8 * 8


def pack_wy(p, q, s, jit, disp, vel):
    cx, cy = p.shape[0], p.shape[1]
    rows = jit.shape[1]
    wy_out = vmem(pad8(4 * cx + 6 * rows), LANES)
    return pl.pallas_call(
        pack_wy_kernel,
        in_specs=[HBM] * 6,
        out_specs=[whole()] * 4,
        out_shape=[wy_out, wy_out, vmem(2, 4, cy, LANES), vmem(3, *jit.shape)],
        scratch_shapes=[
            pltpu.VMEM((6, cx, SUB, LANES), F32),
            pltpu.SemaphoreType.DMA((15,)),
        ],
        compiler_params=params(),
        name="pack_wy",
    )(*in_hbm(p, q, s, jit, disp, vel))


def wall_lanes(field, low):
    lane = lax.broadcasted_iota(jnp.int32, field.shape, 1) % 8
    return lane < 3 if low else lane > 4


def pack_fx_kernel(cx, ends, wall, got_odd, got_even, to_odd, to_even, line):
    cy = ends.shape[2]
    rows, cols = wall.shape[2], wall.shape[3]
    before, after = before_after("wy", got_even, got_odd)

    def edge(side, near, far, x, l):
        def write(out):
            line[SUB - 1 : SUB, :] = before[x : x + 1]
            line[SUB : SUB + cy, :] = ends[side, near]
            line[SUB + cy : SUB + cy + 1, :] = after[x : x + 1]
            mine, speed = ends[side, near], ends[side, 3]
            beside = ends[side, far] + line[SUB - 1 : SUB - 1 + cy, :] + line[SUB + 1 : SUB + 1 + cy, :]
            out[0:cy, :] = mine
            out[cy : 2 * cy, :] = update(mine, ends[side, 2], speed, beside)
            out[2 * cy : 3 * cy, :] = speed
            at = 3 * cy
            for c in range(3):
                pair = []
                for field in range(2):
                    row = 4 * cx + (field * 3 + c) * rows + l
                    parts = (before[row : row + 1], wall[field, c, l], after[row : row + 1])
                    pair.append(jnp.concatenate(parts, axis=0))
                moved = pltpu.roll(pair[1], 3 if side == 0 else LANES - 3, 1)
                out[at : at + cols + 2, :] = jnp.where(wall_lanes(moved, side == 0), pair[0], moved)
                at += cols + 2
            out[at : at + 1, :] = before[x : x + 1]
            out[at + 1 : at + 2, :] = after[x : x + 1]
            for spare in range(at + 2, out.shape[0]):
                out[spare : spare + 1, :] = jnp.zeros((1, LANES), F32)

        return write

    place_edges(
        even_at("fx"), edge(0, 0, 1, 0, 0), edge(1, 1, 0, cx - 1, rows - 1), to_even, to_odd
    )


def pack_fx(cx, ends, wall, got):
    cy, cols = ends.shape[2], wall.shape[3]
    out = vmem(pad8(3 * cy + 3 * (cols + 2) + 2), LANES)
    return pl.pallas_call(
        functools.partial(pack_fx_kernel, cx),
        in_specs=[whole()] * 4,
        out_specs=[whole()] * 2,
        out_shape=[out, out],
        scratch_shapes=[vmem(cy + 2 * SUB, LANES)],
        compiler_params=params(),
        name="pack_fx",
    )(ends, wall, *got)


def along_z(v):
    lane = lax.broadcasted_iota(jnp.int32, v.shape, 1)
    up = jnp.where(lane == LANES - 1, 0.0, pltpu.roll(v, LANES - 1, 1))
    down = jnp.where(lane == 0, 0.0, pltpu.roll(v, 1, 1))
    return up + down


def update(v, old, speed, beside):
    return 2.0 * v - old + speed * (beside + along_z(v) - 6.0 * v)


def two_terms(v):
    high = v.astype(BF16)
    return high, (v - high.astype(F32)).astype(BF16)


def grid_kernel(p, q, s, wyo, wye, fxo, fxe, target, out, slots, s0, s1, rhs, part1, part2):
    cx, cy = p.shape[0], p.shape[1]
    ahead, behind = SUB, SUB + cy
    fx_count = part1.shape[0] // 2 - 1
    cols = 4
    tall = part2.shape[0]
    high = part1.shape[1] - 2 * SUB
    wy_count = high // cols
    before_y, after_y = before_after("wy", wye, wyo)
    before_x, after_x = before_after("fx", fxe, fxo)
    corner = 3 * cy + 3 * (cols + 2)

    s0[1 : cx + 1, ahead:behind, :] = p[...]
    for x, side in ((0, before_x), (cx + 1, after_x)):
        s0[x, ahead:behind, :] = side[0:cy]
        s0[x, ahead - 1 : ahead, :] = side[corner : corner + 1]
        s0[x, behind : behind + 1, :] = side[corner + 1 : corner + 2]
    s0[1 : cx + 1, ahead - 1, :] = before_y[0:cx]
    s0[1 : cx + 1, behind, :] = after_y[0:cx]

    for side, y, inner in ((before_y, ahead - 1, ahead), (after_y, behind, behind - 1)):
        near, far = side[0:cx], side[cx : 2 * cx]
        old, speed = side[2 * cx : 3 * cx], side[3 * cx : 4 * cx]
        beside = s0[0:cx, y, :] + s0[2 : cx + 2, y, :] + far + s0[1 : cx + 1, inner, :]
        s1[1 : cx + 1, y, :] = update(near, old, speed, beside)
    for side, x, inner in ((before_x, 0, 1), (after_x, cx + 1, cx)):
        part, speed = side[cy : 2 * cy], side[2 * cy : 3 * cy]
        s1[x, ahead:behind, :] = part + speed * s0[inner, ahead:behind, :]

    def sweep(now, old, x):
        beside = now[x, ahead:behind, :] + now[x + 2, ahead:behind, :]
        beside = beside + now[x + 1, ahead - 1 : behind - 1, :]
        beside = beside + now[x + 1, ahead + 1 : behind + 1, :]
        return update(now[x + 1, ahead:behind, :], old, s[x], beside)

    for x in range(cx):
        fresh = sweep(s0, q[x], x)
        s1[x + 1, ahead:behind, :] = fresh
        a, b = two_terms(fresh)
        rhs[x * cy : (x + 1) * cy, 0:LANES] = a
        rhs[x * cy : (x + 1) * cy, LANES : 2 * LANES] = b
    for x in range(cx):
        fresh = sweep(s1, p[x], x)
        out[x] = fresh
        a, b = two_terms(fresh)
        rhs[x * cy : (x + 1) * cy, 2 * LANES : 3 * LANES] = a
        rhs[x * cy : (x + 1) * cy, 3 * LANES : 4 * LANES] = b

    part1[...] = jnp.zeros(part1.shape, F32)
    part2[:, 0:SUB, :] = jnp.zeros((tall, SUB, LANES), F32)
    chunk = 256
    for first in range(0, tall * high, chunk):
        tile = lax.broadcasted_iota(jnp.int32, (chunk, LANES), 0) + first
        picks = []
        for piece in range(target.shape[0]):
            picks.append(jnp.where(tile == target[piece : piece + 1, :], 1.0, 0.0).astype(BF16))
        sums = jnp.dot(jnp.concatenate(picks, axis=1), rhs[...], preferred_element_type=F32)
        one = sums[:, 0:LANES] + sums[:, LANES : 2 * LANES]
        two = sums[:, 2 * LANES : 3 * LANES] + sums[:, 3 * LANES : 4 * LANES]
        l = first // high
        part1[1 + l : 1 + l + chunk // high, SUB : SUB + high, :] = one.reshape(-1, high, LANES)
        part2[l : l + chunk // high, SUB : SUB + high, :] = two.reshape(-1, high, LANES)
    sub = lax.broadcasted_iota(jnp.int32, (SUB, LANES), 0)
    lane = lax.broadcasted_iota(jnp.int32, (SUB, LANES), 1)
    step1 = sub < cols + 2
    for a in range(fx_count):
        for b in range(wy_count):
            h = SUB + cols * b
            slot = a * wy_count + b
            one = [part1[2 * a + l, h - 1 : h - 1 + SUB, :] for l in range(4)]
            ends = jnp.where(lane % 8 < 4, one[3], one[0])
            two = [
                part2[2 * a + l, h + at - 6 : h + at - 6 + SUB, :]
                for l, at in ((0, 0), (0, 2), (1, 0))
            ]
            x = jnp.broadcast_to(part2[2 * a + 1, h + 2 : h + 3, :], (SUB, LANES))
            y = jnp.broadcast_to(part2[2 * a + 1, h + 3 : h + 4, :], (SUB, LANES))
            for r in range(4):
                moved = pltpu.roll(y, (3 - 2 * r) % LANES, 1)
                ends = jnp.where((sub == 1 + r) & free_ends(lane), moved, ends)
            low, high_free = (sub == 0) & (lane // 8 % 4 == 0), (sub == cols + 1) & (lane // 8 % 4 == 3)
            own0 = jnp.where(low | high_free, x, one[1])
            own1 = jnp.where(low, pltpu.roll(x, LANES - 8, 1), one[2])
            own1 = jnp.where(high_free, pltpu.roll(x, 8, 1), own1)
            for k, group in enumerate((ends, own0, own1)):
                slots[slot, k * SUB : (k + 1) * SUB, :] = jnp.where(step1, group, two[k])


def free_ends(lane):
    return (lane % 8 == 3) | (lane % 8 == 4)


def unpack_slots(total, cols):
    ends, own0, own1 = [total[k * SUB : (k + 1) * SUB] for k in range(3)]
    lane = lax.broadcasted_iota(jnp.int32, (1, LANES), 1)
    two = [[ends[6:7], ends[7:8], own0[6:7], own0[7:8]], [own1[6:7], own1[7:8]]]
    q = lane // 8 % 4
    last = cols + 1
    x = jnp.where(q == 0, own0[0:1], own0[last : last + 1])
    x = jnp.where(q == 1, pltpu.roll(own1[0:1], 8, 1), x)
    x = jnp.where(q == 2, pltpu.roll(own1[last : last + 1], LANES - 8, 1), x)
    y = None
    for r in range(4):
        moved = pltpu.roll(ends[1 + r : 2 + r], (2 * r - 3) % LANES, 1)
        y = moved if y is None else jnp.where(lane % 8 // 2 == r, moved, y)
    two[1].extend([x, y])
    two = [jnp.concatenate(v, axis=0) for v in two]
    return (ends, own0, own1, ends), two


def grid_steps(p, q, s, wy_got, fx_got, target, fx_count, wy_count):
    cx, cy = p.shape[0], p.shape[1]
    tall, high = fx_count * 2, wy_count * 4
    devices = fx_count * wy_count
    return pl.pallas_call(
        grid_kernel,
        in_specs=[whole()] * 8,
        out_specs=[whole()] * 2,
        out_shape=[
            jax.ShapeDtypeStruct(p.shape, F32),
            vmem(devices, 3 * SUB, LANES),
        ],
        scratch_shapes=[
            pltpu.VMEM((cx + 2, cy + 2 * SUB, LANES), F32),
            pltpu.VMEM((cx + 2, cy + 2 * SUB, LANES), F32),
            pltpu.VMEM((cx * cy, 4 * LANES), BF16),
            pltpu.VMEM((tall + 2, high + 2 * SUB, LANES), F32),
            pltpu.VMEM((tall, high + 2 * SUB, LANES), F32),
        ],
        compiler_params=params(),
        name="grid_steps",
    )(p, q, s, *wy_got, *fx_got, target)


def reached(g):
    groups = []
    for dh in (-1, 0, 1):
        if (dh == -1 and g % 4 == 3) or (dh == 1 and g % 4 == 0):
            continue
        groups.append(dh)
    return groups


STORED = sum(len(reached(g)) for g in range(LANES // SUB))


def mid_rows(ref, c, l, h):
    rows = {}
    for dh in (-1, 0, 1):
        row = ref[c, l + 1, pl.ds(h + 1 + dh, 1), :]
        rows[dh] = jnp.broadcast_to(row, (SUB, LANES))
    return rows


def end_rows(ref, c, l, h, first_sub):
    rows = {}
    for dh in (-1, 0, 1):
        at = pl.ds(h + 1 + dh, 1)
        before = jnp.broadcast_to(ref[c, l, at, :], (SUB, LANES))
        after = jnp.broadcast_to(ref[c, l + 2, at, :], (SUB, LANES))
        rows[dh] = jnp.where(first_sub, before, after)
    return rows


def fill_y(pad, own, before, after, at):
    rows, cols = own.shape[1], own.shape[2]
    for c in range(3):
        for l in range(rows):
            row = at + c * rows + l
            pad[c, l + 1, 0:1, :] = before[row : row + 1]
            pad[c, l + 1, 1 : cols + 1, :] = own[c, l]
            pad[c, l + 1, cols + 1 : cols + 2, :] = after[row : row + 1]


def fill_x(pad, rows, cols, before, after, at):
    for c in range(3):
        row = at + c * (cols + 2)
        pad[c, 0, 0 : cols + 2, :] = before[row : row + cols + 2]
        pad[c, rows + 1, 0 : cols + 2, :] = after[row : row + cols + 2]


def fill_x_shared(jpad, dpad, rows, cols, before, after, at):
    for c in range(3):
        row = at + c * (cols + 2)
        for message, l, low in ((before, 0, False), (after, rows + 1, True)):
            both = message[row : row + cols + 2]
            jpad[c, l, 0 : cols + 2, :] = jnp.where(wall_lanes(both, low), both, 0.0)
            moved = pltpu.roll(both, LANES - 3 if low else 3, 1)
            dpad[c, l, 0 : cols + 2, :] = moved


def lattice_rows():
    index = lax.broadcasted_iota(jnp.int32, (1, LANES), 1)
    places = (index % 8, index // 8 % 4, index // 32)
    return [v.astype(F32) * (1.0 / REACH) for v in places]


SPAN = 8.0 / REACH
RISE = 4.0 / REACH


def spread_mine(ref, lattice, l, h):
    own = []
    for c in range(3):
        own.append(ref[c, l + 1, pl.ds(h + 1, 1), :] * (1.0 / REACH) + lattice[c])
    rest = jnp.concatenate(own + [jnp.zeros((1, LANES), F32)], axis=0)
    terms = []
    for _ in range(3):
        term = rest.astype(BF16).astype(F32)
        terms.append(term)
        rest = rest - term
    terms.append(jnp.zeros((4, LANES), F32))
    columns = jnp.transpose(jnp.concatenate(terms, axis=0)).astype(BF16)
    row = lax.broadcasted_iota(jnp.int32, (16, 3 * LANES), 0)
    lane = lax.broadcasted_iota(jnp.int32, (16, 3 * LANES), 1)
    ones = jnp.where((row % 4 == lane // LANES) & (row < 12), 1.0, 0.0).astype(BF16)
    return jnp.dot(columns, ones, preferred_element_type=F32)


def bond_row(weight, others, mine):
    for c in range(3):
        diff = others[c] - mine[c]
        weight = weight - diff * diff
    return jnp.maximum(weight, 0.0)


def tile_pass(l, h, columns, others, pulls, weight_of, weights, acc):
    place = 0
    for g in range(LANES // SUB):
        span = slice(g * SUB, (g + 1) * SUB)
        mine = [columns[span, c * LANES : (c + 1) * LANES] for c in range(3)]
        sums = [None] * 4
        for order, dh in enumerate(reached(g)):
            here = [others[c][dh] for c in range(3)]
            weight = weight_of(g, order, dh, here, mine)
            weights[l, h, place] = weight
            place += 1
            terms = [weight * pulls[c][dh] for c in range(3)] + [weight]
            sums = [t if v is None else v + t for v, t in zip(sums, terms)]
        for c in range(4):
            acc[l, h, c, span, :] = sums[c]


def tile_sums(acc, l, h, count):
    ones = jnp.ones((2 * SUB, 2 * LANES), BF16)
    terms = [jnp.concatenate(two_terms(acc[l, h, c]), axis=1) for c in range(count)]
    sums = lax.dot_general(
        ones,
        jnp.concatenate(terms, axis=0),
        (((1,), (1,)), ((), ())),
        preferred_element_type=F32,
    )[0:1]
    return [sums[:, c * LANES : (c + 1) * LANES] for c in range(count)]


def lane_sums(acc, l, cols, count):
    tiles = [tile_sums(acc, l, h, count) for h in range(cols)]
    return [jnp.concatenate(rows, axis=0) for rows in zip(*tiles)]


def quotient(v, n):
    return ((v.astype(F32) + 0.5) * (1.0 / n)).astype(jnp.int32)


def center_kernel(
    wy_count, masks_in, p_in, q_in, s_in, device_in, tile_in, wall, wyo, wye,
    weights, part, bits, target, p, q, s, jpad, dpad, acc, masks, route, sems,
):
    rows, cols = wall.shape[2], wall.shape[3]
    cx = p.shape[0]
    copies = {}
    pairs = [(device_in, route.at[0]), (tile_in, route.at[1])]
    pairs = [(p_in, p), (q_in, q), (s_in, s)] + pairs
    for k, pair in enumerate(pairs):
        copies[k] = pltpu.make_async_copy(*pair, sems.at[k])
    tiles = [(l, h) for h in range(cols) for l in range(rows)]
    at = rows * cols
    for k, first in enumerate((3, 0, 6)):
        for n, (l, h) in enumerate(tiles):
            copies[l, h, first] = pltpu.make_async_copy(
                masks_in.at[l, h, first : first + 3],
                masks.at[l, h, first : first + 3],
                sems.at[5 + k * at + n],
            )
    order = [copies[k] for k in (3, 4)]
    order += [copies[l, h, 3] for l, h in tiles]
    order += [copies[l, h, first] for l, h in tiles for first in (0, 6)]
    order += [copies[k] for k in range(3)]
    for copy in order:
        copy.start()
    first_sub = lax.broadcasted_iota(jnp.int32, (SUB, LANES), 0) < SUB // 2
    copies[3].wait()
    copies[4].wait()
    device, tile = route[0], route[1]
    a, t = quotient(device, wy_count), quotient(tile, cols)
    b, u = device - a * wy_count, tile - t * cols
    target[...] = (a * rows + t) * (wy_count * cols) + b * cols + u
    before, after = before_after("wy", wye, wyo)
    fill_y(jpad, wall.at[0], before, after, 4 * cx)
    fill_y(dpad, wall.at[1], before, after, 4 * cx + 3 * rows)
    lattice = lattice_rows()

    def one_tile(l, h):
        columns = spread_mine(jpad, lattice, l, h)
        others = []
        for c in range(3):
            mid = mid_rows(jpad, c, l, h)
            for dh in (-1, 0, 1):
                mid[dh] = mid[dh] * (1.0 / REACH) + lattice[c]
                if c == 1:
                    mid[dh] = mid[dh] + RISE * dh
            others.append(mid)
        pulls = [mid_rows(dpad, c, l, h) for c in range(3)]

        def weight_of(g, order, dh, here, mine):
            span = slice(g * SUB, (g + 1) * SUB)
            return bond_row(masks[l, h, 4 + dh, span, :].astype(F32), here, mine)

        tile_pass(l, h, columns, others, pulls, weight_of, weights, acc)

    def put_sums(l, h):
        for c, sums in enumerate(tile_sums(acc, l, h, 4)):
            part[l, c, h : h + 1, :] = sums

    def put_bits(l, h):
        words = [jnp.zeros((SUB, LANES), jnp.int32) for _ in range(2)]
        for g in range(LANES // SUB):
            span = slice(g * SUB, (g + 1) * SUB)
            for order, dh in enumerate(reached(g)):
                before = masks[l, h, 1 + dh, span, :]
                after = masks[l, h, 7 + dh, span, :]
                place = 3 * (g % 8) + order
                words[g // 8] = words[g // 8] + jnp.where(first_sub, before, after) * (1 << place)
        for k in range(2):
            bits[l, h, k] = words[k]

    for n, (l, h) in enumerate(tiles):
        copies[l, h, 3].wait()
        one_tile(l, h)
        if n > 0:
            put_sums(*tiles[n - 1])
    put_sums(*tiles[-1])
    for l, h in tiles:
        copies[l, h, 0].wait()
        copies[l, h, 6].wait()
        put_bits(l, h)
    for k in range(3):
        copies[k].wait()


def wall_center(wy_count, masks, grids, device, tile, wall, wy_got):
    rows, cols = wall.shape[2], wall.shape[3]
    return pl.pallas_call(
        functools.partial(center_kernel, wy_count),
        in_specs=[HBM] * 6 + [whole()] * 3,
        out_specs=[whole()] * 7,
        out_shape=[
            jax.ShapeDtypeStruct((rows, cols, STORED, SUB, LANES), F32),
            vmem(rows, 4, cols, LANES),
            pltpu.VMEM((rows, cols, 2, SUB, LANES), jnp.int32),
            pltpu.VMEM(device.shape, jnp.int32),
        ]
        + [vmem(*grids[0].shape)] * 3,
        scratch_shapes=[
            vmem(3, rows + 2, SUB, LANES),
            vmem(3, rows + 2, SUB, LANES),
            vmem(rows, cols, 4, LANES, LANES),
            pltpu.VMEM(masks.shape, jnp.int32),
            pltpu.VMEM((2,) + device.shape, jnp.int32),
            pltpu.SemaphoreType.DMA((5 + 3 * rows * cols,)),
        ],
        compiler_params=params(),
        name="wall_center",
    )(*in_hbm(masks, *grids, device, tile), wall, *wy_got)


def wall_kernel(
    cx, cy, wall, wyo, wye, fxo, fxe, part, bits, weights, vel1, base1, totals, to_odd, to_even,
    jpad, dpad, acc,
):
    rows, cols = wall.shape[2], wall.shape[3]
    first_sub = lax.broadcasted_iota(jnp.int32, (SUB, LANES), 0) < SUB // 2
    before, after = before_after("wy", wye, wyo)
    fill_y(jpad, wall.at[0], before, after, 4 * cx)
    fill_y(dpad, wall.at[1], before, after, 4 * cx + 3 * rows)
    before, after = before_after("fx", fxe, fxo)
    fill_x_shared(jpad, dpad, rows, cols, before, after, 3 * cy)
    lattice = lattice_rows()

    def one_tile(l, h):
        columns = spread_mine(jpad, lattice, l, h)
        others = []
        for c in range(3):
            ends = end_rows(jpad, c, l, h, first_sub)
            for dh in (-1, 0, 1):
                ends[dh] = ends[dh] * (1.0 / REACH) + lattice[c]
                if c == 0:
                    ends[dh] = ends[dh] + jnp.where(first_sub, -SPAN, SPAN)
                if c == 1:
                    ends[dh] = ends[dh] + RISE * dh
            others.append(ends)
        pulls = [end_rows(dpad, c, l, h, first_sub) for c in range(3)]

        def weight_of(g, order, dh, here, mine):
            bonded = (bits[l, h, g // 8] & (1 << (3 * (g % 8) + order))) != 0
            return jnp.where(bonded, bond_row(1.0, here, mine), 0.0)

        tile_pass(l, h, columns, others, pulls, weight_of, weights, acc)

    @pl.loop(0, cols)
    def _(h):
        for l in range(rows):
            one_tile(l, h)

    for l in range(rows):
        pulled = [v + part[l, c] for c, v in enumerate(lane_sums(acc, l, cols, 4))]
        totals[l] = pulled[3]
        for c in range(3):
            mine = wall[1, c, l]
            fresh = wall[2, c, l] + STIFFNESS * (pulled[c] - pulled[3] * mine)
            vel1[c, l] = fresh
            base1[c, l] = mine + fresh

    def edge(at):
        def write(out):
            for c in range(3):
                for k in range(rows):
                    out[c * rows + k : c * rows + k + 1, :] = base1[c, k, at : at + 1, :]
            for spare in range(3 * rows, out.shape[0]):
                out[spare : spare + 1, :] = jnp.zeros((1, LANES), F32)

        return write

    place_edges(even_at("wy"), edge(0), edge(cols - 1), to_even, to_odd)


def wall_first(cx, cy, wall, wy_got, fx_got, part, bits):
    rows, cols = wall.shape[2], wall.shape[3]
    edge = (pad8(3 * rows), LANES)
    field = vmem(*wall.shape[1:])
    return pl.pallas_call(
        functools.partial(wall_kernel, cx, cy),
        in_specs=[whole()] * 7,
        out_specs=[whole()] * 6,
        out_shape=[
            jax.ShapeDtypeStruct((rows, cols, STORED, SUB, LANES), F32),
            field,
            field,
            vmem(rows, cols, LANES),
            vmem(*edge),
            vmem(*edge),
        ],
        scratch_shapes=[
            pltpu.VMEM((3, rows + 2, SUB, LANES), F32),
            pltpu.VMEM((3, rows + 2, SUB, LANES), F32),
            pltpu.VMEM((rows, cols, 4, LANES, LANES), F32),
        ],
        compiler_params=params(),
        name="wall_first",
    )(wall, *wy_got, *fx_got, part, bits)


def pack_base_kernel(base1, got_odd, got_even, to_odd, to_even):
    rows, cols = base1.shape[1], base1.shape[2]
    before, after = before_after("wy", got_even, got_odd)

    def edge(l):
        def write(out):
            at = 0
            for c in range(3):
                side = c * rows + l
                out[at : at + 1, :] = before[side : side + 1]
                out[at + 1 : at + 1 + cols, :] = base1[c, l]
                out[at + 1 + cols : at + 2 + cols, :] = after[side : side + 1]
                at += cols + 2
            for spare in range(at, out.shape[0]):
                out[spare : spare + 1, :] = jnp.zeros((1, LANES), F32)

        return write

    place_edges(even_at("fx"), edge(0), edge(rows - 1), to_even, to_odd)


def pack_base(base1, got):
    cols = base1.shape[2]
    out = vmem(pad8(3 * (cols + 2)), LANES)
    return pl.pallas_call(
        pack_base_kernel,
        in_specs=[whole()] * 3,
        out_specs=[whole()] * 2,
        out_shape=[out, out],
        compiler_params=params(),
        name="pack_base",
    )(base1, *got)


def last_kernel(
    weights, end_weights, got, base1, vel1, totals, wyo, wye, fxo, fxe, disp_out, vel_out,
    dpad, acc,
):
    rows, cols = base1.shape[1], base1.shape[2]
    first_sub = lax.broadcasted_iota(jnp.int32, (SUB, LANES), 0) < SUB // 2
    before, after = before_after("wy", wye, wyo)
    fill_y(dpad, base1, before, after, 0)
    before, after = before_after("fx", fxe, fxo)
    fill_x(dpad, rows, cols, before, after, 0)
    total = got[0]
    for d in range(1, got.shape[0]):
        total = total + got[d]
    one, two = unpack_slots(total, cols)
    for k in range(rows + 2):
        here = dpad[0, k, 0 : cols + 2, :] + LOADING * one[k][0 : cols + 2]
        dpad[0, k, 0 : cols + 2, :] = here

    def one_tile(l, h):
        mids = [mid_rows(dpad, c, l, h) for c in range(3)]
        ends = [end_rows(dpad, c, l, h, first_sub) for c in range(3)]
        place = 0
        for g in range(LANES // SUB):
            sums = [None] * 3
            for dh in reached(g):
                for weight, pulls in (
                    (weights[l, h, place], mids), (end_weights[l, h, place], ends)
                ):
                    terms = [weight * pulls[c][dh] for c in range(3)]
                    sums = [t if v is None else v + t for v, t in zip(sums, terms)]
                place += 1
            for c in range(3):
                acc[l, h, c, g * SUB : (g + 1) * SUB, :] = sums[c]

    @pl.loop(0, cols)
    def _(h):
        for l in range(rows):
            one_tile(l, h)

    for l in range(rows):
        pulled = lane_sums(acc, l, cols, 3)
        for c in range(3):
            mine = dpad[c, l + 1, 1 : cols + 1, :]
            force = STIFFNESS * (pulled[c] - totals[l] * mine)
            if c == 0:
                force = force + LOADING * (one[l + 1][1 : cols + 1] + two[l])
            fresh = vel1[c, l] + force
            vel_out[c, l] = fresh
            disp_out[c, l] = mine + fresh


def wall_last(weights, end_weights, got, base1, vel1, totals, wy_got, fx_got):
    rows, cols = base1.shape[1], base1.shape[2]
    return pl.pallas_call(
        last_kernel,
        in_specs=[whole()] * 10,
        out_specs=[whole()] * 2,
        out_shape=[jax.ShapeDtypeStruct(base1.shape, F32)] * 2,
        scratch_shapes=[
            pltpu.VMEM((3, rows + 2, SUB, LANES), F32),
            pltpu.VMEM((rows, cols, 3, LANES, LANES), F32),
        ],
        compiler_params=params(),
        name="wall_last",
    )(weights, end_weights, got, base1, vel1, totals, *wy_got, *fx_got)


def per_device(
    displacement,
    velocity,
    jitter,
    bond_masks,
    pressure,
    pressure_prev,
    speed_sq,
    route_device,
    route_tile,
):
    fx_count, wy_count = lax.axis_size("fx"), lax.axis_size("wy")
    cols = displacement.shape[2]
    device = route_device.reshape(-1, LANES)
    tile = route_tile.reshape(-1, LANES)
    cx, cy = pressure.shape[0], pressure.shape[1]
    *sends, ends, wall = pack_wy(
        pressure, pressure_prev, speed_sq, jitter, displacement, velocity
    )
    wy_got = exchange("wy", *sends)
    sends = pack_fx(cx, ends, wall, wy_got)
    fx_got = exchange("fx", *sends)
    grids = (pressure, pressure_prev, speed_sq)
    weights, part, bits, target, *grids = wall_center(
        wy_count, bond_masks, grids, device, tile, wall, wy_got
    )
    pressure_out, slots = grid_steps(*grids, wy_got, fx_got, target, fx_count, wy_count)
    got = lax.all_to_all(slots, ("fx", "wy"), split_axis=0, concat_axis=0, tiled=True)
    end_weights, vel1, base1, totals, *sends = wall_first(
        cx, cy, wall, wy_got, fx_got, part, bits
    )
    base_wy = exchange("wy", *sends)
    sends = pack_base(base1, base_wy)
    base_fx = exchange("fx", *sends)
    disp_out, vel_out = wall_last(
        weights, end_weights, got, base1, vel1, totals, base_wy, base_fx
    )
    return (disp_out, vel_out, pressure_out)


def solution(mesh):
    placed = (
        P(None, "fx", "wy", None),
        P(None, "fx", "wy", None),
        P(None, "fx", "wy", None),
        P("fx", "wy", None, None, None),
        P("fx", "wy", None),
        P("fx", "wy", None),
        P("fx", "wy", None),
        P(("fx", "wy"), None),
        P(("fx", "wy")),
    )
    return jax.shard_map(
        per_device,
        mesh=mesh,
        in_specs=placed,
        out_specs=(P(None, "fx", "wy", None), P(None, "fx", "wy", None), P("fx", "wy", None)),
        check_vma=False,
    )
```

```python
import functools

import jax
import jax.numpy as jnp
from jax import lax
from jax.experimental import pallas as pl
from jax.experimental.pallas import tpu as pltpu
from jax.sharding import PartitionSpec as P

STIFFNESS = 0.02
LOADING = 0.05
REACH = 3.0
LANES = 128
SUB = 8
VMEM_BYTES = 32 * 1024 * 1024
HBM = pl.BlockSpec(memory_space=pltpu.HBM)

F32 = jnp.float32
BF16 = jnp.bfloat16


def whole():
    return pl.BlockSpec(memory_space=pltpu.VMEM)


def params():
    return pltpu.CompilerParams(vmem_limit_bytes=VMEM_BYTES)


def vmem(*shape):
    return pltpu.VMEM(shape, F32)


def even_at(axis):
    return lax.rem(lax.axis_index(axis), 2) == 0


def swap_pairs(axis, sizes, first):
    count, others = sizes[axis], sizes[1 - axis]
    pairs = []

    def join(*two):
        a, b = [place * sizes[1] + other for place, other in two]
        pairs.extend([(a, b), (b, a)])

    def at(place, other):
        return (place, other) if axis == 0 else (other, place)

    met = set()
    for low in range(first, count - 1, 2):
        met.update((low, low + 1))
        for other in range(others):
            join(at(low, other), at(low + 1, other))
    for place in range(count):
        if place not in met and others % 2 == 0:
            for other in range(0, others, 2):
                join(at(place, other), at(place, other + 1))
    return pairs


def exchange(axis, to_odd, to_even):
    names = ("fx", "wy")
    sizes = [lax.axis_size(name) for name in names]
    along = names.index(axis)
    got_odd = lax.ppermute(to_odd, names, swap_pairs(along, sizes, 1))
    got_even = lax.ppermute(to_even, names, swap_pairs(along, sizes, 0))
    return got_odd, got_even


def place_edges(even, low, high, to_even, to_odd):
    @pl.when(even)
    def _():
        high(to_even)
        low(to_odd)

    @pl.when(jnp.logical_not(even))
    def _():
        low(to_even)
        high(to_odd)


def before_after(axis, got_even, got_odd):
    even = even_at(axis)
    place, last = lax.axis_index(axis), lax.axis_size(axis) - 1
    a, b = got_even[...], got_odd[...]
    before = jnp.where(place == 0, 0.0, jnp.where(even, b, a))
    after = jnp.where(place == last, 0.0, jnp.where(even, a, b))
    return before, after


def pack_wy_kernel(
    p, q, s, jit_in, disp_in, vel_in, wy_odd, wy_even, ends, wall, edges, sems
):
    cx, cy = p.shape[0], p.shape[1]
    rows, cols = jit_in.shape[1], jit_in.shape[2]
    pairs = []
    for k, field in enumerate((p, q, s)):
        for side, first in enumerate((0, cy - SUB)):
            pairs.append((field.at[:, first : first + SUB, :], edges.at[2 * k + side]))
    pairs.append((p.at[0:2], ends.at[0, 0:2]))
    pairs.append((p.at[cx - 2 : cx], ends.at[1, 0:2]))
    for k, field in enumerate((q, s)):
        pairs.append((field.at[0], ends.at[0, 2 + k]))
        pairs.append((field.at[cx - 1], ends.at[1, 2 + k]))
    for k, field in enumerate((jit_in, disp_in, vel_in)):
        pairs.append((field, wall.at[k]))
    copies = [pltpu.make_async_copy(a, b, sems.at[k]) for k, (a, b) in enumerate(pairs)]
    for copy in copies:
        copy.start()
    for copy in copies:
        copy.wait()

    def edge(side, near, far, h):
        def write(out):
            out[0:cx, :] = edges[side, :, near, :]
            out[cx : 2 * cx, :] = edges[side, :, far, :]
            out[2 * cx : 3 * cx, :] = edges[2 + side, :, near, :]
            out[3 * cx : 4 * cx, :] = edges[4 + side, :, near, :]
            at = 4 * cx
            for field in range(2):
                for c in range(3):
                    for l in range(rows):
                        out[at : at + 1, :] = wall[field, c, l, h : h + 1, :]
                        at += 1
            for spare in range(at, out.shape[0]):
                out[spare : spare + 1, :] = jnp.zeros((1, LANES), F32)

        return write

    place_edges(
        even_at("wy"),
        edge(0, 0, 1, 0),
        edge(1, SUB - 1, SUB - 2, cols - 1),
        wy_even,
        wy_odd,
    )


def in_hbm(*arrays):
    return [pltpu.with_memory_space_constraint(v, pltpu.HBM) for v in arrays]


def pad8(count):
    return (count + 7) // 8 * 8


def pack_wy(p, q, s, jit, disp, vel):
    cx, cy = p.shape[0], p.shape[1]
    rows = jit.shape[1]
    wy_out = vmem(pad8(4 * cx + 6 * rows), LANES)
    return pl.pallas_call(
        pack_wy_kernel,
        in_specs=[HBM] * 6,
        out_specs=[whole()] * 4,
        out_shape=[wy_out, wy_out, vmem(2, 4, cy, LANES), vmem(3, *jit.shape)],
        scratch_shapes=[
            pltpu.VMEM((6, cx, SUB, LANES), F32),
            pltpu.SemaphoreType.DMA((15,)),
        ],
        compiler_params=params(),
        name="pack_wy",
    )(*in_hbm(p, q, s, jit, disp, vel))


def wall_lanes(field, low):
    lane = lax.broadcasted_iota(jnp.int32, field.shape, 1) % 8
    return lane < 3 if low else lane > 4


def pack_fx_kernel(cx, ends, wall, got_odd, got_even, to_odd, to_even, line):
    cy = ends.shape[2]
    rows, cols = wall.shape[2], wall.shape[3]
    before, after = before_after("wy", got_even, got_odd)

    def edge(side, near, far, x, l):
        def write(out):
            line[SUB - 1 : SUB, :] = before[x : x + 1]
            line[SUB : SUB + cy, :] = ends[side, near]
            line[SUB + cy : SUB + cy + 1, :] = after[x : x + 1]
            mine, speed = ends[side, near], ends[side, 3]
            beside = ends[side, far] + line[SUB - 1 : SUB - 1 + cy, :] + line[SUB + 1 : SUB + 1 + cy, :]
            out[0:cy, :] = mine
            out[cy : 2 * cy, :] = update(mine, ends[side, 2], speed, beside)
            out[2 * cy : 3 * cy, :] = speed
            at = 3 * cy
            for c in range(3):
                pair = []
                for field in range(2):
                    row = 4 * cx + (field * 3 + c) * rows + l
                    parts = (before[row : row + 1], wall[field, c, l], after[row : row + 1])
                    pair.append(jnp.concatenate(parts, axis=0))
                moved = pltpu.roll(pair[1], 3 if side == 0 else LANES - 3, 1)
                out[at : at + cols + 2, :] = jnp.where(wall_lanes(moved, side == 0), pair[0], moved)
                at += cols + 2
            out[at : at + 1, :] = before[x : x + 1]
            out[at + 1 : at + 2, :] = after[x : x + 1]
            for spare in range(at + 2, out.shape[0]):
                out[spare : spare + 1, :] = jnp.zeros((1, LANES), F32)

        return write

    place_edges(
        even_at("fx"), edge(0, 0, 1, 0, 0), edge(1, 1, 0, cx - 1, rows - 1), to_even, to_odd
    )


def pack_fx(cx, ends, wall, got):
    cy, cols = ends.shape[2], wall.shape[3]
    out = vmem(pad8(3 * cy + 3 * (cols + 2) + 2), LANES)
    return pl.pallas_call(
        functools.partial(pack_fx_kernel, cx),
        in_specs=[whole()] * 4,
        out_specs=[whole()] * 2,
        out_shape=[out, out],
        scratch_shapes=[vmem(cy + 2 * SUB, LANES)],
        compiler_params=params(),
        name="pack_fx",
    )(ends, wall, *got)


def along_z(v):
    lane = lax.broadcasted_iota(jnp.int32, v.shape, 1)
    up = jnp.where(lane == LANES - 1, 0.0, pltpu.roll(v, LANES - 1, 1))
    down = jnp.where(lane == 0, 0.0, pltpu.roll(v, 1, 1))
    return up + down


def update(v, old, speed, beside):
    return 2.0 * v - old + speed * (beside + along_z(v) - 6.0 * v)


def two_terms(v):
    high = v.astype(BF16)
    return high, (v - high.astype(F32)).astype(BF16)


def grid_kernel(p, q, s, wyo, wye, fxo, fxe, target, out, slots, s0, s1, rhs, part1, part2):
    cx, cy = p.shape[0], p.shape[1]
    ahead, behind = SUB, SUB + cy
    fx_count = part1.shape[0] // 2 - 1
    cols = 4
    tall = part2.shape[0]
    high = part1.shape[1] - 2 * SUB
    wy_count = high // cols
    before_y, after_y = before_after("wy", wye, wyo)
    before_x, after_x = before_after("fx", fxe, fxo)
    corner = 3 * cy + 3 * (cols + 2)

    s0[1 : cx + 1, ahead:behind, :] = p[...]
    for x, side in ((0, before_x), (cx + 1, after_x)):
        s0[x, ahead:behind, :] = side[0:cy]
        s0[x, ahead - 1 : ahead, :] = side[corner : corner + 1]
        s0[x, behind : behind + 1, :] = side[corner + 1 : corner + 2]
    s0[1 : cx + 1, ahead - 1, :] = before_y[0:cx]
    s0[1 : cx + 1, behind, :] = after_y[0:cx]

    for side, y, inner in ((before_y, ahead - 1, ahead), (after_y, behind, behind - 1)):
        near, far = side[0:cx], side[cx : 2 * cx]
        old, speed = side[2 * cx : 3 * cx], side[3 * cx : 4 * cx]
        beside = s0[0:cx, y, :] + s0[2 : cx + 2, y, :] + far + s0[1 : cx + 1, inner, :]
        s1[1 : cx + 1, y, :] = update(near, old, speed, beside)
    for side, x, inner in ((before_x, 0, 1), (after_x, cx + 1, cx)):
        part, speed = side[cy : 2 * cy], side[2 * cy : 3 * cy]
        s1[x, ahead:behind, :] = part + speed * s0[inner, ahead:behind, :]

    def sweep(now, old, x):
        beside = now[x, ahead:behind, :] + now[x + 2, ahead:behind, :]
        beside = beside + now[x + 1, ahead - 1 : behind - 1, :]
        beside = beside + now[x + 1, ahead + 1 : behind + 1, :]
        return update(now[x + 1, ahead:behind, :], old, s[x], beside)

    for x in range(cx):
        fresh = sweep(s0, q[x], x)
        s1[x + 1, ahead:behind, :] = fresh
        a, b = two_terms(fresh)
        rhs[x * cy : (x + 1) * cy, 0:LANES] = a
        rhs[x * cy : (x + 1) * cy, LANES : 2 * LANES] = b
    for x in range(cx):
        fresh = sweep(s1, p[x], x)
        out[x] = fresh
        a, b = two_terms(fresh)
        rhs[x * cy : (x + 1) * cy, 2 * LANES : 3 * LANES] = a
        rhs[x * cy : (x + 1) * cy, 3 * LANES : 4 * LANES] = b

    part1[...] = jnp.zeros(part1.shape, F32)
    part2[:, 0:SUB, :] = jnp.zeros((tall, SUB, LANES), F32)
    chunk = 256
    for first in range(0, tall * high, chunk):
        tile = lax.broadcasted_iota(jnp.int32, (chunk, LANES), 0) + first
        picks = []
        for piece in range(target.shape[0]):
            picks.append(jnp.where(tile == target[piece : piece + 1, :], 1.0, 0.0).astype(BF16))
        sums = jnp.dot(jnp.concatenate(picks, axis=1), rhs[...], preferred_element_type=F32)
        one = sums[:, 0:LANES] + sums[:, LANES : 2 * LANES]
        two = sums[:, 2 * LANES : 3 * LANES] + sums[:, 3 * LANES : 4 * LANES]
        l = first // high
        part1[1 + l : 1 + l + chunk // high, SUB : SUB + high, :] = one.reshape(-1, high, LANES)
        part2[l : l + chunk // high, SUB : SUB + high, :] = two.reshape(-1, high, LANES)
    sub = lax.broadcasted_iota(jnp.int32, (SUB, LANES), 0)
    lane = lax.broadcasted_iota(jnp.int32, (SUB, LANES), 1)
    step1 = sub < cols + 2
    for a in range(fx_count):
        for b in range(wy_count):
            h = SUB + cols * b
            slot = a * wy_count + b
            one = [part1[2 * a + l, h - 1 : h - 1 + SUB, :] for l in range(4)]
            ends = jnp.where(lane % 8 < 4, one[3], one[0])
            two = [
                part2[2 * a + l, h + at - 6 : h + at - 6 + SUB, :]
                for l, at in ((0, 0), (0, 2), (1, 0))
            ]
            x = jnp.broadcast_to(part2[2 * a + 1, h + 2 : h + 3, :], (SUB, LANES))
            y = jnp.broadcast_to(part2[2 * a + 1, h + 3 : h + 4, :], (SUB, LANES))
            for r in range(4):
                moved = pltpu.roll(y, (3 - 2 * r) % LANES, 1)
                ends = jnp.where((sub == 1 + r) & free_ends(lane), moved, ends)
            low, high_free = (sub == 0) & (lane // 8 % 4 == 0), (sub == cols + 1) & (lane // 8 % 4 == 3)
            own0 = jnp.where(low | high_free, x, one[1])
            own1 = jnp.where(low, pltpu.roll(x, LANES - 8, 1), one[2])
            own1 = jnp.where(high_free, pltpu.roll(x, 8, 1), own1)
            for k, group in enumerate((ends, own0, own1)):
                slots[slot, k * SUB : (k + 1) * SUB, :] = jnp.where(step1, group, two[k])


def free_ends(lane):
    return (lane % 8 == 3) | (lane % 8 == 4)


def unpack_slots(total, cols):
    ends, own0, own1 = [total[k * SUB : (k + 1) * SUB] for k in range(3)]
    lane = lax.broadcasted_iota(jnp.int32, (1, LANES), 1)
    two = [[ends[6:7], ends[7:8], own0[6:7], own0[7:8]], [own1[6:7], own1[7:8]]]
    q = lane // 8 % 4
    last = cols + 1
    x = jnp.where(q == 0, own0[0:1], own0[last : last + 1])
    x = jnp.where(q == 1, pltpu.roll(own1[0:1], 8, 1), x)
    x = jnp.where(q == 2, pltpu.roll(own1[last : last + 1], LANES - 8, 1), x)
    y = None
    for r in range(4):
        moved = pltpu.roll(ends[1 + r : 2 + r], (2 * r - 3) % LANES, 1)
        y = moved if y is None else jnp.where(lane % 8 // 2 == r, moved, y)
    two[1].extend([x, y])
    two = [jnp.concatenate(v, axis=0) for v in two]
    return (ends, own0, own1, ends), two


def grid_steps(p, q, s, wy_got, fx_got, target, fx_count, wy_count):
    cx, cy = p.shape[0], p.shape[1]
    tall, high = fx_count * 2, wy_count * 4
    devices = fx_count * wy_count
    return pl.pallas_call(
        grid_kernel,
        in_specs=[whole()] * 8,
        out_specs=[whole()] * 2,
        out_shape=[
            jax.ShapeDtypeStruct(p.shape, F32),
            vmem(devices, 3 * SUB, LANES),
        ],
        scratch_shapes=[
            pltpu.VMEM((cx + 2, cy + 2 * SUB, LANES), F32),
            pltpu.VMEM((cx + 2, cy + 2 * SUB, LANES), F32),
            pltpu.VMEM((cx * cy, 4 * LANES), BF16),
            pltpu.VMEM((tall + 2, high + 2 * SUB, LANES), F32),
            pltpu.VMEM((tall, high + 2 * SUB, LANES), F32),
        ],
        compiler_params=params(),
        name="grid_steps",
    )(p, q, s, *wy_got, *fx_got, target)


def reached(g):
    groups = []
    for dh in (-1, 0, 1):
        if (dh == -1 and g % 4 == 3) or (dh == 1 and g % 4 == 0):
            continue
        groups.append(dh)
    return groups


STORED = sum(len(reached(g)) for g in range(LANES // SUB))


def mid_rows(ref, c, l, h):
    rows = {}
    for dh in (-1, 0, 1):
        row = ref[c, l + 1, pl.ds(h + 1 + dh, 1), :]
        rows[dh] = jnp.broadcast_to(row, (SUB, LANES))
    return rows


def end_rows(ref, c, l, h, first_sub):
    rows = {}
    for dh in (-1, 0, 1):
        at = pl.ds(h + 1 + dh, 1)
        before = jnp.broadcast_to(ref[c, l, at, :], (SUB, LANES))
        after = jnp.broadcast_to(ref[c, l + 2, at, :], (SUB, LANES))
        rows[dh] = jnp.where(first_sub, before, after)
    return rows


def fill_y(pad, own, before, after, at):
    rows, cols = own.shape[1], own.shape[2]
    for c in range(3):
        for l in range(rows):
            row = at + c * rows + l
            pad[c, l + 1, 0:1, :] = before[row : row + 1]
            pad[c, l + 1, 1 : cols + 1, :] = own[c, l]
            pad[c, l + 1, cols + 1 : cols + 2, :] = after[row : row + 1]


def fill_x(pad, rows, cols, before, after, at):
    for c in range(3):
        row = at + c * (cols + 2)
        pad[c, 0, 0 : cols + 2, :] = before[row : row + cols + 2]
        pad[c, rows + 1, 0 : cols + 2, :] = after[row : row + cols + 2]


def fill_x_shared(jpad, dpad, rows, cols, before, after, at):
    for c in range(3):
        row = at + c * (cols + 2)
        for message, l, low in ((before, 0, False), (after, rows + 1, True)):
            both = message[row : row + cols + 2]
            jpad[c, l, 0 : cols + 2, :] = jnp.where(wall_lanes(both, low), both, 0.0)
            moved = pltpu.roll(both, LANES - 3 if low else 3, 1)
            dpad[c, l, 0 : cols + 2, :] = moved


def lattice_rows():
    index = lax.broadcasted_iota(jnp.int32, (1, LANES), 1)
    places = (index % 8, index // 8 % 4, index // 32)
    return [v.astype(F32) * (1.0 / REACH) for v in places]


SPAN = 8.0 / REACH
RISE = 4.0 / REACH


def own_columns(ref, lattice, rows, cols):
    places = []
    for l in range(rows):
        for h in range(cols):
            for c in range(3):
                places.append(ref[c, l + 1, h + 1 : h + 2, :] * (1.0 / REACH) + lattice[c])
    spare = -len(places) % SUB
    if spare:
        places.append(jnp.zeros((spare, LANES), F32))
    return jnp.transpose(jnp.concatenate(places, axis=0))


def bond_row(weight, others, mine):
    for c in range(3):
        diff = others[c] - mine[c]
        weight = weight - diff * diff
    return jnp.maximum(weight, 0.0)


def tile_pass(l, h, cols, columns, others, pulls, weight_of, weights, acc):
    place = 0
    first = 3 * (l * cols + h)
    for g in range(LANES // SUB):
        span = slice(g * SUB, (g + 1) * SUB)
        mine = [jnp.broadcast_to(columns[span, first + c : first + c + 1], (SUB, LANES)) for c in range(3)]
        sums = [None] * 4
        for order, dh in enumerate(reached(g)):
            here = [others[c][dh] for c in range(3)]
            weight = weight_of(g, order, dh, here, mine)
            weights[l, h, place] = weight
            place += 1
            terms = [weight * pulls[c][dh] for c in range(3)] + [weight]
            sums = [t if v is None else v + t for v, t in zip(sums, terms)]
        for c in range(4):
            acc[l, h, c, span, :] = sums[c]


def tile_sums(acc, l, h, count):
    ones = jnp.ones((2 * SUB, 2 * LANES), BF16)
    terms = [jnp.concatenate(two_terms(acc[l, h, c]), axis=1) for c in range(count)]
    sums = lax.dot_general(
        ones,
        jnp.concatenate(terms, axis=0),
        (((1,), (1,)), ((), ())),
        preferred_element_type=F32,
    )[0:1]
    return [sums[:, c * LANES : (c + 1) * LANES] for c in range(count)]


def by_quantity(tiles):
    return [jnp.concatenate(rows, axis=0) for rows in zip(*tiles)]


def quotient(v, n):
    return ((v.astype(F32) + 0.5) * (1.0 / n)).astype(jnp.int32)


def center_kernel(
    wy_count, masks_in, p_in, q_in, s_in, device_in, tile_in, wall, wyo, wye,
    weights, part, bits, target, columns, p, q, s, jpad, dpad, acc, masks, route, sems,
):
    rows, cols = wall.shape[2], wall.shape[3]
    cx = p.shape[0]
    copies = {}
    pairs = [(device_in, route.at[0]), (tile_in, route.at[1])]
    pairs = [(p_in, p), (q_in, q), (s_in, s)] + pairs
    for k, pair in enumerate(pairs):
        copies[k] = pltpu.make_async_copy(*pair, sems.at[k])
    for k, first in enumerate((3, 0, 6)):
        span = slice(first, first + 3)
        copies["masks", first] = pltpu.make_async_copy(
            masks_in.at[:, :, span], masks.at[:, :, span], sems.at[5 + k]
        )
    order = [3, 4, ("masks", 3), ("masks", 0), ("masks", 6), 0, 1, 2]
    for k in order:
        copies[k].start()
    first_sub = lax.broadcasted_iota(jnp.int32, (SUB, LANES), 0) < SUB // 2
    copies[3].wait()
    copies[4].wait()
    device, tile = route[0], route[1]
    a, t = quotient(device, wy_count), quotient(tile, cols)
    b, u = device - a * wy_count, tile - t * cols
    target[...] = (a * rows + t) * (wy_count * cols) + b * cols + u
    before, after = before_after("wy", wye, wyo)
    fill_y(jpad, wall.at[0], before, after, 4 * cx)
    fill_y(dpad, wall.at[1], before, after, 4 * cx + 3 * rows)
    lattice = lattice_rows()
    columns[...] = own_columns(jpad, lattice, rows, cols)

    def one_tile(l, h):
        others = []
        for c in range(3):
            mid = mid_rows(jpad, c, l, h)
            for dh in (-1, 0, 1):
                mid[dh] = mid[dh] * (1.0 / REACH) + lattice[c]
                if c == 1:
                    mid[dh] = mid[dh] + RISE * dh
            others.append(mid)
        pulls = [mid_rows(dpad, c, l, h) for c in range(3)]

        def weight_of(g, order, dh, here, mine):
            span = slice(g * SUB, (g + 1) * SUB)
            return bond_row(masks[l, h, 4 + dh, span, :].astype(F32), here, mine)

        tile_pass(l, h, cols, columns, others, pulls, weight_of, weights, acc)

    def put_sums(l, h):
        for c, sums in enumerate(tile_sums(acc, l, h, 4)):
            part[l, c, h : h + 1, :] = sums

    def put_bits(l, h):
        words = [jnp.zeros((SUB, LANES), jnp.int32) for _ in range(2)]
        for g in range(LANES // SUB):
            span = slice(g * SUB, (g + 1) * SUB)
            for order, dh in enumerate(reached(g)):
                before = masks[l, h, 1 + dh, span, :]
                after = masks[l, h, 7 + dh, span, :]
                place = 3 * (g % 8) + order
                words[g // 8] = words[g // 8] + jnp.where(first_sub, before, after) * (1 << place)
        for k in range(2):
            bits[l, h, k] = words[k]

    tiles = [(l, h) for l in range(rows) for h in range(cols)]
    copies["masks", 3].wait()
    for l, h in tiles:
        one_tile(l, h)
        put_sums(l, h)
    copies["masks", 0].wait()
    copies["masks", 6].wait()
    for l, h in tiles:
        put_bits(l, h)
    for k in range(3):
        copies[k].wait()


def wall_center(wy_count, masks, grids, device, tile, wall, wy_got):
    rows, cols = wall.shape[2], wall.shape[3]
    return pl.pallas_call(
        functools.partial(center_kernel, wy_count),
        in_specs=[HBM] * 6 + [whole()] * 3,
        out_specs=[whole()] * 8,
        out_shape=[
            jax.ShapeDtypeStruct((rows, cols, STORED, SUB, LANES), F32),
            vmem(rows, 4, cols, LANES),
            pltpu.VMEM((rows, cols, 2, SUB, LANES), jnp.int32),
            pltpu.VMEM(device.shape, jnp.int32),
            vmem(LANES, pad8(3 * rows * cols)),
        ]
        + [vmem(*grids[0].shape)] * 3,
        scratch_shapes=[
            vmem(3, rows + 2, SUB, LANES),
            vmem(3, rows + 2, SUB, LANES),
            vmem(rows, cols, 4, LANES, LANES),
            pltpu.VMEM(masks.shape, jnp.int32),
            pltpu.VMEM((2,) + device.shape, jnp.int32),
            pltpu.SemaphoreType.DMA((8,)),
        ],
        compiler_params=params(),
        name="wall_center",
    )(*in_hbm(masks, *grids, device, tile), wall, *wy_got)


def wall_kernel(
    cx, cy, wall, wyo, wye, fxo, fxe, part, bits, columns, weights, vel1, base1, totals, to_odd, to_even,
    jpad, dpad, acc,
):
    rows, cols = wall.shape[2], wall.shape[3]
    first_sub = lax.broadcasted_iota(jnp.int32, (SUB, LANES), 0) < SUB // 2
    before, after = before_after("wy", wye, wyo)
    fill_y(jpad, wall.at[0], before, after, 4 * cx)
    fill_y(dpad, wall.at[1], before, after, 4 * cx + 3 * rows)
    before, after = before_after("fx", fxe, fxo)
    fill_x_shared(jpad, dpad, rows, cols, before, after, 3 * cy)
    lattice = lattice_rows()

    def one_tile(l, h):
        others = []
        for c in range(3):
            ends = end_rows(jpad, c, l, h, first_sub)
            for dh in (-1, 0, 1):
                ends[dh] = ends[dh] * (1.0 / REACH) + lattice[c]
                if c == 0:
                    ends[dh] = ends[dh] + jnp.where(first_sub, -SPAN, SPAN)
                if c == 1:
                    ends[dh] = ends[dh] + RISE * dh
            others.append(ends)
        pulls = [end_rows(dpad, c, l, h, first_sub) for c in range(3)]

        def weight_of(g, order, dh, here, mine):
            bonded = (bits[l, h, g // 8] & (1 << (3 * (g % 8) + order))) != 0
            return jnp.where(bonded, bond_row(1.0, here, mine), 0.0)

        tile_pass(l, h, cols, columns, others, pulls, weight_of, weights, acc)

    for l in range(rows):
        sums = []
        for h in range(cols):
            one_tile(l, h)
            sums.append(tile_sums(acc, l, h, 4))
        pulled = [v + part[l, c] for c, v in enumerate(by_quantity(sums))]
        totals[l] = pulled[3]
        for c in range(3):
            mine = wall[1, c, l]
            fresh = wall[2, c, l] + STIFFNESS * (pulled[c] - pulled[3] * mine)
            vel1[c, l] = fresh
            base1[c, l] = mine + fresh

    def edge(at):
        def write(out):
            for c in range(3):
                for k in range(rows):
                    out[c * rows + k : c * rows + k + 1, :] = base1[c, k, at : at + 1, :]
            for spare in range(3 * rows, out.shape[0]):
                out[spare : spare + 1, :] = jnp.zeros((1, LANES), F32)

        return write

    place_edges(even_at("wy"), edge(0), edge(cols - 1), to_even, to_odd)


def wall_first(cx, cy, wall, wy_got, fx_got, part, bits, columns):
    rows, cols = wall.shape[2], wall.shape[3]
    edge = (pad8(3 * rows), LANES)
    field = vmem(*wall.shape[1:])
    return pl.pallas_call(
        functools.partial(wall_kernel, cx, cy),
        in_specs=[whole()] * 8,
        out_specs=[whole()] * 6,
        out_shape=[
            jax.ShapeDtypeStruct((rows, cols, STORED, SUB, LANES), F32),
            field,
            field,
            vmem(rows, cols, LANES),
            vmem(*edge),
            vmem(*edge),
        ],
        scratch_shapes=[
            pltpu.VMEM((3, rows + 2, SUB, LANES), F32),
            pltpu.VMEM((3, rows + 2, SUB, LANES), F32),
            pltpu.VMEM((rows, cols, 4, LANES, LANES), F32),
        ],
        compiler_params=params(),
        name="wall_first",
    )(wall, *wy_got, *fx_got, part, bits, columns)


def pack_base_kernel(base1, got_odd, got_even, to_odd, to_even):
    rows, cols = base1.shape[1], base1.shape[2]
    before, after = before_after("wy", got_even, got_odd)

    def edge(l):
        def write(out):
            at = 0
            for c in range(3):
                side = c * rows + l
                out[at : at + 1, :] = before[side : side + 1]
                out[at + 1 : at + 1 + cols, :] = base1[c, l]
                out[at + 1 + cols : at + 2 + cols, :] = after[side : side + 1]
                at += cols + 2
            for spare in range(at, out.shape[0]):
                out[spare : spare + 1, :] = jnp.zeros((1, LANES), F32)

        return write

    place_edges(even_at("fx"), edge(0), edge(rows - 1), to_even, to_odd)


def pack_base(base1, got):
    cols = base1.shape[2]
    out = vmem(pad8(3 * (cols + 2)), LANES)
    return pl.pallas_call(
        pack_base_kernel,
        in_specs=[whole()] * 3,
        out_specs=[whole()] * 2,
        out_shape=[out, out],
        compiler_params=params(),
        name="pack_base",
    )(base1, *got)


def last_kernel(
    weights, end_weights, got, base1, vel1, totals, wyo, wye, fxo, fxe, disp_out, vel_out,
    dpad, acc,
):
    rows, cols = base1.shape[1], base1.shape[2]
    first_sub = lax.broadcasted_iota(jnp.int32, (SUB, LANES), 0) < SUB // 2
    before, after = before_after("wy", wye, wyo)
    fill_y(dpad, base1, before, after, 0)
    before, after = before_after("fx", fxe, fxo)
    fill_x(dpad, rows, cols, before, after, 0)
    total = got[0]
    for d in range(1, got.shape[0]):
        total = total + got[d]
    one, two = unpack_slots(total, cols)
    for k in range(rows + 2):
        here = dpad[0, k, 0 : cols + 2, :] + LOADING * one[k][0 : cols + 2]
        dpad[0, k, 0 : cols + 2, :] = here

    def one_tile(l, h):
        mids = [mid_rows(dpad, c, l, h) for c in range(3)]
        ends = [end_rows(dpad, c, l, h, first_sub) for c in range(3)]
        place = 0
        for g in range(LANES // SUB):
            sums = [None] * 3
            for dh in reached(g):
                for weight, pulls in (
                    (weights[l, h, place], mids), (end_weights[l, h, place], ends)
                ):
                    terms = [weight * pulls[c][dh] for c in range(3)]
                    sums = [t if v is None else v + t for v, t in zip(sums, terms)]
                place += 1
            for c in range(3):
                acc[l, h, c, g * SUB : (g + 1) * SUB, :] = sums[c]

    for l in range(rows):
        sums = []
        for h in range(cols):
            one_tile(l, h)
            sums.append(tile_sums(acc, l, h, 3))
        pulled = by_quantity(sums)
        for c in range(3):
            mine = dpad[c, l + 1, 1 : cols + 1, :]
            force = STIFFNESS * (pulled[c] - totals[l] * mine)
            if c == 0:
                force = force + LOADING * (one[l + 1][1 : cols + 1] + two[l])
            fresh = vel1[c, l] + force
            vel_out[c, l] = fresh
            disp_out[c, l] = mine + fresh


def wall_last(weights, end_weights, got, base1, vel1, totals, wy_got, fx_got):
    rows, cols = base1.shape[1], base1.shape[2]
    return pl.pallas_call(
        last_kernel,
        in_specs=[whole()] * 10,
        out_specs=[whole()] * 2,
        out_shape=[jax.ShapeDtypeStruct(base1.shape, F32)] * 2,
        scratch_shapes=[
            pltpu.VMEM((3, rows + 2, SUB, LANES), F32),
            pltpu.VMEM((rows, cols, 3, LANES, LANES), F32),
        ],
        compiler_params=params(),
        name="wall_last",
    )(weights, end_weights, got, base1, vel1, totals, *wy_got, *fx_got)


def per_device(
    displacement,
    velocity,
    jitter,
    bond_masks,
    pressure,
    pressure_prev,
    speed_sq,
    route_device,
    route_tile,
):
    fx_count, wy_count = lax.axis_size("fx"), lax.axis_size("wy")
    cols = displacement.shape[2]
    device = route_device.reshape(-1, LANES)
    tile = route_tile.reshape(-1, LANES)
    cx, cy = pressure.shape[0], pressure.shape[1]
    *sends, ends, wall = pack_wy(
        pressure, pressure_prev, speed_sq, jitter, displacement, velocity
    )
    wy_got = exchange("wy", *sends)
    sends = pack_fx(cx, ends, wall, wy_got)
    fx_got = exchange("fx", *sends)
    grids = (pressure, pressure_prev, speed_sq)
    weights, part, bits, target, columns, *grids = wall_center(
        wy_count, bond_masks, grids, device, tile, wall, wy_got
    )
    pressure_out, slots = grid_steps(*grids, wy_got, fx_got, target, fx_count, wy_count)
    got = lax.all_to_all(slots, ("fx", "wy"), split_axis=0, concat_axis=0, tiled=True)
    end_weights, vel1, base1, totals, *sends = wall_first(
        cx, cy, wall, wy_got, fx_got, part, bits, columns
    )
    base_wy = exchange("wy", *sends)
    sends = pack_base(base1, base_wy)
    base_fx = exchange("fx", *sends)
    disp_out, vel_out = wall_last(
        weights, end_weights, got, base1, vel1, totals, base_wy, base_fx
    )
    return (disp_out, vel_out, pressure_out)


def solution(mesh):
    placed = (
        P(None, "fx", "wy", None),
        P(None, "fx", "wy", None),
        P(None, "fx", "wy", None),
        P("fx", "wy", None, None, None),
        P("fx", "wy", None),
        P("fx", "wy", None),
        P("fx", "wy", None),
        P(("fx", "wy"), None),
        P(("fx", "wy")),
    )
    return jax.shard_map(
        per_device,
        mesh=mesh,
        in_specs=placed,
        out_specs=(P(None, "fx", "wy", None), P(None, "fx", "wy", None), P("fx", "wy", None)),
        check_vma=False,
    )
```

```python
import functools

import jax
import jax.numpy as jnp
from jax import lax
from jax.experimental import pallas as pl
from jax.experimental.pallas import tpu as pltpu
from jax.sharding import PartitionSpec as P

STIFFNESS = 0.02
LOADING = 0.05
REACH = 3.0
LANES = 128
SUB = 8
VMEM_BYTES = 32 * 1024 * 1024
HBM = pl.BlockSpec(memory_space=pltpu.HBM)

F32 = jnp.float32
BF16 = jnp.bfloat16


def whole():
    return pl.BlockSpec(memory_space=pltpu.VMEM)


def params():
    return pltpu.CompilerParams(vmem_limit_bytes=VMEM_BYTES)


def vmem(*shape):
    return pltpu.VMEM(shape, F32)


def even_at(axis):
    return lax.rem(lax.axis_index(axis), 2) == 0


def swap_pairs(axis, sizes, first):
    count, others = sizes[axis], sizes[1 - axis]
    pairs = []

    def join(*two):
        a, b = [place * sizes[1] + other for place, other in two]
        pairs.extend([(a, b), (b, a)])

    def at(place, other):
        return (place, other) if axis == 0 else (other, place)

    met = set()
    for low in range(first, count - 1, 2):
        met.update((low, low + 1))
        for other in range(others):
            join(at(low, other), at(low + 1, other))
    for place in range(count):
        if place not in met and others % 2 == 0:
            for other in range(0, others, 2):
                join(at(place, other), at(place, other + 1))
    return pairs


def exchange(axis, to_odd, to_even):
    names = ("fx", "wy")
    sizes = [lax.axis_size(name) for name in names]
    along = names.index(axis)
    got_odd = lax.ppermute(to_odd, names, swap_pairs(along, sizes, 1))
    got_even = lax.ppermute(to_even, names, swap_pairs(along, sizes, 0))
    return got_odd, got_even


def place_edges(even, low, high, to_even, to_odd):
    @pl.when(even)
    def _():
        high(to_even)
        low(to_odd)

    @pl.when(jnp.logical_not(even))
    def _():
        low(to_even)
        high(to_odd)


def before_after(axis, got_even, got_odd):
    even = even_at(axis)
    place, last = lax.axis_index(axis), lax.axis_size(axis) - 1
    a, b = got_even[...], got_odd[...]
    before = jnp.where(place == 0, 0.0, jnp.where(even, b, a))
    after = jnp.where(place == last, 0.0, jnp.where(even, a, b))
    return before, after


def pack_wy_kernel(
    p, q, s, jit_in, disp_in, vel_in, wy_odd, wy_even, ends, wall, edges, sems
):
    cx, cy = p.shape[0], p.shape[1]
    rows, cols = jit_in.shape[1], jit_in.shape[2]
    pairs = []
    for k, field in enumerate((p, q, s)):
        for side, first in enumerate((0, cy - SUB)):
            pairs.append((field.at[:, first : first + SUB, :], edges.at[2 * k + side]))
    pairs.append((p.at[0:2], ends.at[0, 0:2]))
    pairs.append((p.at[cx - 2 : cx], ends.at[1, 0:2]))
    for k, field in enumerate((q, s)):
        pairs.append((field.at[0], ends.at[0, 2 + k]))
        pairs.append((field.at[cx - 1], ends.at[1, 2 + k]))
    for k, field in enumerate((jit_in, disp_in, vel_in)):
        pairs.append((field, wall.at[k]))
    copies = [pltpu.make_async_copy(a, b, sems.at[k]) for k, (a, b) in enumerate(pairs)]
    for copy in copies:
        copy.start()
    for copy in copies:
        copy.wait()

    def edge(side, near, far, h):
        def write(out):
            out[0:cx, :] = edges[side, :, near, :]
            out[cx : 2 * cx, :] = edges[side, :, far, :]
            out[2 * cx : 3 * cx, :] = edges[2 + side, :, near, :]
            out[3 * cx : 4 * cx, :] = edges[4 + side, :, near, :]
            at = 4 * cx
            for field in range(2):
                for c in range(3):
                    for l in range(rows):
                        out[at : at + 1, :] = wall[field, c, l, h : h + 1, :]
                        at += 1
            for spare in range(at, out.shape[0]):
                out[spare : spare + 1, :] = jnp.zeros((1, LANES), F32)

        return write

    place_edges(
        even_at("wy"),
        edge(0, 0, 1, 0),
        edge(1, SUB - 1, SUB - 2, cols - 1),
        wy_even,
        wy_odd,
    )


def in_hbm(*arrays):
    return [pltpu.with_memory_space_constraint(v, pltpu.HBM) for v in arrays]


def pad8(count):
    return (count + 7) // 8 * 8


def pack_wy(p, q, s, jit, disp, vel):
    cx, cy = p.shape[0], p.shape[1]
    rows = jit.shape[1]
    wy_out = vmem(pad8(4 * cx + 6 * rows), LANES)
    return pl.pallas_call(
        pack_wy_kernel,
        in_specs=[HBM] * 6,
        out_specs=[whole()] * 4,
        out_shape=[wy_out, wy_out, vmem(2, 4, cy, LANES), vmem(3, *jit.shape)],
        scratch_shapes=[
            pltpu.VMEM((6, cx, SUB, LANES), F32),
            pltpu.SemaphoreType.DMA((15,)),
        ],
        compiler_params=params(),
        name="pack_wy",
    )(*in_hbm(p, q, s, jit, disp, vel))


def wall_lanes(field, low):
    lane = lax.broadcasted_iota(jnp.int32, field.shape, 1) % 8
    return lane < 3 if low else lane > 4


def pack_fx_kernel(cx, ends, wall, got_odd, got_even, to_odd, to_even, line):
    cy = ends.shape[2]
    rows, cols = wall.shape[2], wall.shape[3]
    before, after = before_after("wy", got_even, got_odd)

    def edge(side, near, far, x, l):
        def write(out):
            line[SUB - 1 : SUB, :] = before[x : x + 1]
            line[SUB : SUB + cy, :] = ends[side, near]
            line[SUB + cy : SUB + cy + 1, :] = after[x : x + 1]
            mine, speed = ends[side, near], ends[side, 3]
            beside = ends[side, far] + line[SUB - 1 : SUB - 1 + cy, :] + line[SUB + 1 : SUB + 1 + cy, :]
            out[0:cy, :] = mine
            out[cy : 2 * cy, :] = update(mine, ends[side, 2], speed, beside)
            out[2 * cy : 3 * cy, :] = speed
            at = 3 * cy
            for c in range(3):
                pair = []
                for field in range(2):
                    row = 4 * cx + (field * 3 + c) * rows + l
                    parts = (before[row : row + 1], wall[field, c, l], after[row : row + 1])
                    pair.append(jnp.concatenate(parts, axis=0))
                moved = pltpu.roll(pair[1], 3 if side == 0 else LANES - 3, 1)
                out[at : at + cols + 2, :] = jnp.where(wall_lanes(moved, side == 0), pair[0], moved)
                at += cols + 2
            out[at : at + 1, :] = before[x : x + 1]
            out[at + 1 : at + 2, :] = after[x : x + 1]
            for spare in range(at + 2, out.shape[0]):
                out[spare : spare + 1, :] = jnp.zeros((1, LANES), F32)

        return write

    place_edges(
        even_at("fx"), edge(0, 0, 1, 0, 0), edge(1, 1, 0, cx - 1, rows - 1), to_even, to_odd
    )


def pack_fx(cx, ends, wall, got):
    cy, cols = ends.shape[2], wall.shape[3]
    out = vmem(pad8(3 * cy + 3 * (cols + 2) + 2), LANES)
    return pl.pallas_call(
        functools.partial(pack_fx_kernel, cx),
        in_specs=[whole()] * 4,
        out_specs=[whole()] * 2,
        out_shape=[out, out],
        scratch_shapes=[vmem(cy + 2 * SUB, LANES)],
        compiler_params=params(),
        name="pack_fx",
    )(ends, wall, *got)


def along_z(v):
    lane = lax.broadcasted_iota(jnp.int32, v.shape, 1)
    up = jnp.where(lane == LANES - 1, 0.0, pltpu.roll(v, LANES - 1, 1))
    down = jnp.where(lane == 0, 0.0, pltpu.roll(v, 1, 1))
    return up + down


def update(v, old, speed, beside):
    return 2.0 * v - old + speed * (beside + along_z(v) - 6.0 * v)


def two_terms(v):
    high = v.astype(BF16)
    return high, (v - high.astype(F32)).astype(BF16)


def grid_kernel(
    p, q, s, wyo, wye, fxo, fxe, target, out_to, slots_to, s0, s1, rhs, part1, part2, out, slots, sems
):
    cx, cy = p.shape[0], p.shape[1]
    ahead, behind = SUB, SUB + cy
    fx_count = part1.shape[0] // 2 - 1
    cols = 4
    tall = part2.shape[0]
    high = part1.shape[1] - 2 * SUB
    wy_count = high // cols
    before_y, after_y = before_after("wy", wye, wyo)
    before_x, after_x = before_after("fx", fxe, fxo)
    corner = 3 * cy + 3 * (cols + 2)

    s0[1 : cx + 1, ahead:behind, :] = p[...]
    for x, side in ((0, before_x), (cx + 1, after_x)):
        s0[x, ahead:behind, :] = side[0:cy]
        s0[x, ahead - 1 : ahead, :] = side[corner : corner + 1]
        s0[x, behind : behind + 1, :] = side[corner + 1 : corner + 2]
    s0[1 : cx + 1, ahead - 1, :] = before_y[0:cx]
    s0[1 : cx + 1, behind, :] = after_y[0:cx]

    for side, y, inner in ((before_y, ahead - 1, ahead), (after_y, behind, behind - 1)):
        near, far = side[0:cx], side[cx : 2 * cx]
        old, speed = side[2 * cx : 3 * cx], side[3 * cx : 4 * cx]
        beside = s0[0:cx, y, :] + s0[2 : cx + 2, y, :] + far + s0[1 : cx + 1, inner, :]
        s1[1 : cx + 1, y, :] = update(near, old, speed, beside)
    for side, x, inner in ((before_x, 0, 1), (after_x, cx + 1, cx)):
        part, speed = side[cy : 2 * cy], side[2 * cy : 3 * cy]
        s1[x, ahead:behind, :] = part + speed * s0[inner, ahead:behind, :]

    def sweep(now, old, x):
        beside = now[x, ahead:behind, :] + now[x + 2, ahead:behind, :]
        beside = beside + now[x + 1, ahead - 1 : behind - 1, :]
        beside = beside + now[x + 1, ahead + 1 : behind + 1, :]
        return update(now[x + 1, ahead:behind, :], old, s[x], beside)

    for x in range(cx):
        fresh = sweep(s0, q[x], x)
        s1[x + 1, ahead:behind, :] = fresh
        a, b = two_terms(fresh)
        rhs[x * cy : (x + 1) * cy, 0:LANES] = a
        rhs[x * cy : (x + 1) * cy, LANES : 2 * LANES] = b
    for x in range(cx):
        fresh = sweep(s1, p[x], x)
        out[x] = fresh
        a, b = two_terms(fresh)
        rhs[x * cy : (x + 1) * cy, 2 * LANES : 3 * LANES] = a
        rhs[x * cy : (x + 1) * cy, 3 * LANES : 4 * LANES] = b

    out_copy = pltpu.make_async_copy(out, out_to, sems.at[0])
    out_copy.start()

    part1[...] = jnp.zeros(part1.shape, F32)
    part2[:, 0:SUB, :] = jnp.zeros((tall, SUB, LANES), F32)
    chunk = 256
    for first in range(0, tall * high, chunk):
        tile = lax.broadcasted_iota(jnp.int32, (chunk, LANES), 0) + first
        picks = []
        for piece in range(target.shape[0]):
            picks.append(jnp.where(tile == target[piece : piece + 1, :], 1.0, 0.0).astype(BF16))
        sums = jnp.dot(jnp.concatenate(picks, axis=1), rhs[...], preferred_element_type=F32)
        one = sums[:, 0:LANES] + sums[:, LANES : 2 * LANES]
        two = sums[:, 2 * LANES : 3 * LANES] + sums[:, 3 * LANES : 4 * LANES]
        l = first // high
        part1[1 + l : 1 + l + chunk // high, SUB : SUB + high, :] = one.reshape(-1, high, LANES)
        part2[l : l + chunk // high, SUB : SUB + high, :] = two.reshape(-1, high, LANES)
    sub = lax.broadcasted_iota(jnp.int32, (SUB, LANES), 0)
    lane = lax.broadcasted_iota(jnp.int32, (SUB, LANES), 1)
    step1 = sub < cols + 2
    copies = [out_copy]
    batch = max(1, fx_count // 4)
    for a in range(fx_count):
        for b in range(wy_count):
            h = SUB + cols * b
            slot = a * wy_count + b
            one = [part1[2 * a + l, h - 1 : h - 1 + SUB, :] for l in range(4)]
            ends = jnp.where(lane % 8 < 4, one[3], one[0])
            two = [
                part2[2 * a + l, h + at - 6 : h + at - 6 + SUB, :]
                for l, at in ((0, 0), (0, 2), (1, 0))
            ]
            x = jnp.broadcast_to(part2[2 * a + 1, h + 2 : h + 3, :], (SUB, LANES))
            y = jnp.broadcast_to(part2[2 * a + 1, h + 3 : h + 4, :], (SUB, LANES))
            for r in range(4):
                moved = pltpu.roll(y, (3 - 2 * r) % LANES, 1)
                ends = jnp.where((sub == 1 + r) & free_ends(lane), moved, ends)
            low, high_free = (sub == 0) & (lane // 8 % 4 == 0), (sub == cols + 1) & (lane // 8 % 4 == 3)
            own0 = jnp.where(low | high_free, x, one[1])
            own1 = jnp.where(low, pltpu.roll(x, LANES - 8, 1), one[2])
            own1 = jnp.where(high_free, pltpu.roll(x, 8, 1), own1)
            for k, group in enumerate((ends, own0, own1)):
                slots[slot, k * SUB : (k + 1) * SUB, :] = jnp.where(step1, group, two[k])
        if a % batch == batch - 1 or a == fx_count - 1:
            done = (a + 1) * wy_count
            span = slice((a // batch) * batch * wy_count, done)
            sem = sems.at[len(copies)]
            copies.append(pltpu.make_async_copy(slots.at[span], slots_to.at[span], sem))
            copies[-1].start()
    for copy in copies:
        copy.wait()


def free_ends(lane):
    return (lane % 8 == 3) | (lane % 8 == 4)


def unpack_slots(total, cols):
    ends, own0, own1 = [total[k * SUB : (k + 1) * SUB] for k in range(3)]
    lane = lax.broadcasted_iota(jnp.int32, (1, LANES), 1)
    two = [[ends[6:7], ends[7:8], own0[6:7], own0[7:8]], [own1[6:7], own1[7:8]]]
    q = lane // 8 % 4
    last = cols + 1
    x = jnp.where(q == 0, own0[0:1], own0[last : last + 1])
    x = jnp.where(q == 1, pltpu.roll(own1[0:1], 8, 1), x)
    x = jnp.where(q == 2, pltpu.roll(own1[last : last + 1], LANES - 8, 1), x)
    y = None
    for r in range(4):
        moved = pltpu.roll(ends[1 + r : 2 + r], (2 * r - 3) % LANES, 1)
        y = moved if y is None else jnp.where(lane % 8 // 2 == r, moved, y)
    two[1].extend([x, y])
    two = [jnp.concatenate(v, axis=0) for v in two]
    return (ends, own0, own1, ends), two


def grid_steps(p, q, s, wy_got, fx_got, target, fx_count, wy_count):
    cx, cy = p.shape[0], p.shape[1]
    tall, high = fx_count * 2, wy_count * 4
    devices = fx_count * wy_count
    return pl.pallas_call(
        grid_kernel,
        in_specs=[whole()] * 8,
        out_specs=[HBM] * 2,
        out_shape=[
            jax.ShapeDtypeStruct(p.shape, F32),
            jax.ShapeDtypeStruct((devices, 3 * SUB, LANES), F32),
        ],
        scratch_shapes=[
            pltpu.VMEM((cx + 2, cy + 2 * SUB, LANES), F32),
            pltpu.VMEM((cx + 2, cy + 2 * SUB, LANES), F32),
            pltpu.VMEM((cx * cy, 4 * LANES), BF16),
            pltpu.VMEM((tall + 2, high + 2 * SUB, LANES), F32),
            pltpu.VMEM((tall, high + 2 * SUB, LANES), F32),
            vmem(*p.shape),
            vmem(devices, 3 * SUB, LANES),
            pltpu.SemaphoreType.DMA((8,)),
        ],
        compiler_params=params(),
        name="grid_steps",
    )(p, q, s, *wy_got, *fx_got, target)


def reached(g):
    groups = []
    for dh in (-1, 0, 1):
        if (dh == -1 and g % 4 == 3) or (dh == 1 and g % 4 == 0):
            continue
        groups.append(dh)
    return groups


STORED = sum(len(reached(g)) for g in range(LANES // SUB))


def mid_rows(ref, c, l, h):
    rows = {}
    for dh in (-1, 0, 1):
        row = ref[c, l + 1, pl.ds(h + 1 + dh, 1), :]
        rows[dh] = jnp.broadcast_to(row, (SUB, LANES))
    return rows


def end_rows(ref, c, l, h, first_sub):
    rows = {}
    for dh in (-1, 0, 1):
        at = pl.ds(h + 1 + dh, 1)
        before = jnp.broadcast_to(ref[c, l, at, :], (SUB, LANES))
        after = jnp.broadcast_to(ref[c, l + 2, at, :], (SUB, LANES))
        rows[dh] = jnp.where(first_sub, before, after)
    return rows


def fill_y(pad, own, before, after, at):
    rows, cols = own.shape[1], own.shape[2]
    for c in range(3):
        for l in range(rows):
            row = at + c * rows + l
            pad[c, l + 1, 0:1, :] = before[row : row + 1]
            pad[c, l + 1, 1 : cols + 1, :] = own[c, l]
            pad[c, l + 1, cols + 1 : cols + 2, :] = after[row : row + 1]


def fill_x(pad, rows, cols, before, after, at):
    for c in range(3):
        row = at + c * (cols + 2)
        pad[c, 0, 0 : cols + 2, :] = before[row : row + cols + 2]
        pad[c, rows + 1, 0 : cols + 2, :] = after[row : row + cols + 2]


def fill_x_shared(jpad, dpad, rows, cols, before, after, at):
    for c in range(3):
        row = at + c * (cols + 2)
        for message, l, low in ((before, 0, False), (after, rows + 1, True)):
            both = message[row : row + cols + 2]
            jpad[c, l, 0 : cols + 2, :] = jnp.where(wall_lanes(both, low), both, 0.0)
            moved = pltpu.roll(both, LANES - 3 if low else 3, 1)
            dpad[c, l, 0 : cols + 2, :] = moved


def lattice_rows():
    index = lax.broadcasted_iota(jnp.int32, (1, LANES), 1)
    places = (index % 8, index // 8 % 4, index // 32)
    return [v.astype(F32) * (1.0 / REACH) for v in places]


SPAN = 8.0 / REACH
RISE = 4.0 / REACH


def own_columns(ref, lattice, rows, cols):
    places = []
    for l in range(rows):
        for h in range(cols):
            for c in range(3):
                places.append(ref[c, l + 1, h + 1 : h + 2, :] * (1.0 / REACH) + lattice[c])
    spare = -len(places) % SUB
    if spare:
        places.append(jnp.zeros((spare, LANES), F32))
    return jnp.transpose(jnp.concatenate(places, axis=0))


def bond_row(weight, others, mine):
    for c in range(3):
        diff = others[c] - mine[c]
        weight = weight - diff * diff
    return jnp.maximum(weight, 0.0)


def tile_pass(l, h, cols, columns, others, pulls, weight_of, weights, acc):
    place = 0
    first = 3 * (l * cols + h)
    for g in range(LANES // SUB):
        span = slice(g * SUB, (g + 1) * SUB)
        mine = [jnp.broadcast_to(columns[span, first + c : first + c + 1], (SUB, LANES)) for c in range(3)]
        sums = [None] * 4
        for order, dh in enumerate(reached(g)):
            here = [others[c][dh] for c in range(3)]
            weight = weight_of(g, order, dh, here, mine)
            weights[l, h, place] = weight
            place += 1
            terms = [weight * pulls[c][dh] for c in range(3)] + [weight]
            sums = [t if v is None else v + t for v, t in zip(sums, terms)]
        for c in range(4):
            acc[l, h, c, span, :] = sums[c]


def tile_sums(acc, l, h, count):
    ones = jnp.ones((2 * SUB, 2 * LANES), BF16)
    terms = [jnp.concatenate(two_terms(acc[l, h, c]), axis=1) for c in range(count)]
    sums = lax.dot_general(
        ones,
        jnp.concatenate(terms, axis=0),
        (((1,), (1,)), ((), ())),
        preferred_element_type=F32,
    )[0:1]
    return [sums[:, c * LANES : (c + 1) * LANES] for c in range(count)]


def by_quantity(tiles):
    return [jnp.concatenate(rows, axis=0) for rows in zip(*tiles)]


def quotient(v, n):
    return ((v.astype(F32) + 0.5) * (1.0 / n)).astype(jnp.int32)


def center_kernel(
    wy_count, masks_in, p_in, q_in, s_in, device_in, tile_in, wall, wyo, wye,
    weights, part, bits, target, columns, p, q, s, jpad, dpad, acc, masks, route, sems,
):
    rows, cols = wall.shape[2], wall.shape[3]
    cx = p.shape[0]
    copies = {}
    pairs = [(device_in, route.at[0]), (tile_in, route.at[1])]
    pairs = [(p_in, p), (q_in, q), (s_in, s)] + pairs
    for k, pair in enumerate(pairs):
        copies[k] = pltpu.make_async_copy(*pair, sems.at[k])
    for k, first in enumerate((3, 0, 6)):
        span = slice(first, first + 3)
        copies["masks", first] = pltpu.make_async_copy(
            masks_in.at[:, :, span], masks.at[:, :, span], sems.at[5 + k]
        )
    order = [3, 4, ("masks", 3), ("masks", 0), ("masks", 6), 0, 1, 2]
    for k in order:
        copies[k].start()
    first_sub = lax.broadcasted_iota(jnp.int32, (SUB, LANES), 0) < SUB // 2
    copies[3].wait()
    copies[4].wait()
    device, tile = route[0], route[1]
    a, t = quotient(device, wy_count), quotient(tile, cols)
    b, u = device - a * wy_count, tile - t * cols
    target[...] = (a * rows + t) * (wy_count * cols) + b * cols + u
    before, after = before_after("wy", wye, wyo)
    fill_y(jpad, wall.at[0], before, after, 4 * cx)
    fill_y(dpad, wall.at[1], before, after, 4 * cx + 3 * rows)
    lattice = lattice_rows()
    columns[...] = own_columns(jpad, lattice, rows, cols)

    def one_tile(l, h):
        others = []
        for c in range(3):
            mid = mid_rows(jpad, c, l, h)
            for dh in (-1, 0, 1):
                mid[dh] = mid[dh] * (1.0 / REACH) + lattice[c]
                if c == 1:
                    mid[dh] = mid[dh] + RISE * dh
            others.append(mid)
        pulls = [mid_rows(dpad, c, l, h) for c in range(3)]

        def weight_of(g, order, dh, here, mine):
            span = slice(g * SUB, (g + 1) * SUB)
            return bond_row(masks[l, h, 4 + dh, span, :].astype(F32), here, mine)

        tile_pass(l, h, cols, columns, others, pulls, weight_of, weights, acc)

    def put_sums(l, h):
        for c, sums in enumerate(tile_sums(acc, l, h, 4)):
            part[l, c, h : h + 1, :] = sums

    def put_bits(l, h):
        words = [jnp.zeros((SUB, LANES), jnp.int32) for _ in range(2)]
        for g in range(LANES // SUB):
            span = slice(g * SUB, (g + 1) * SUB)
            for order, dh in enumerate(reached(g)):
                before = masks[l, h, 1 + dh, span, :]
                after = masks[l, h, 7 + dh, span, :]
                place = 3 * (g % 8) + order
                words[g // 8] = words[g // 8] + jnp.where(first_sub, before, after) * (1 << place)
        for k in range(2):
            bits[l, h, k] = words[k]

    tiles = [(l, h) for l in range(rows) for h in range(cols)]
    copies["masks", 3].wait()
    for l, h in tiles:
        one_tile(l, h)
        put_sums(l, h)
    copies["masks", 0].wait()
    copies["masks", 6].wait()
    for l, h in tiles:
        put_bits(l, h)
    for k in range(3):
        copies[k].wait()


def wall_center(wy_count, masks, grids, device, tile, wall, wy_got):
    rows, cols = wall.shape[2], wall.shape[3]
    return pl.pallas_call(
        functools.partial(center_kernel, wy_count),
        in_specs=[HBM] * 6 + [whole()] * 3,
        out_specs=[whole()] * 8,
        out_shape=[
            jax.ShapeDtypeStruct((rows, cols, STORED, SUB, LANES), F32),
            vmem(rows, 4, cols, LANES),
            pltpu.VMEM((rows, cols, 2, SUB, LANES), jnp.int32),
            pltpu.VMEM(device.shape, jnp.int32),
            vmem(LANES, pad8(3 * rows * cols)),
        ]
        + [vmem(*grids[0].shape)] * 3,
        scratch_shapes=[
            vmem(3, rows + 2, SUB, LANES),
            vmem(3, rows + 2, SUB, LANES),
            vmem(rows, cols, 4, LANES, LANES),
            pltpu.VMEM(masks.shape, jnp.int32),
            pltpu.VMEM((2,) + device.shape, jnp.int32),
            pltpu.SemaphoreType.DMA((8,)),
        ],
        compiler_params=params(),
        name="wall_center",
    )(*in_hbm(masks, *grids, device, tile), wall, *wy_got)


def wall_kernel(
    cx, cy, wall, wyo, wye, fxo, fxe, part, bits, columns, weights, vel1, base1, totals, to_odd, to_even,
    jpad, dpad, acc,
):
    rows, cols = wall.shape[2], wall.shape[3]
    first_sub = lax.broadcasted_iota(jnp.int32, (SUB, LANES), 0) < SUB // 2
    before, after = before_after("wy", wye, wyo)
    fill_y(jpad, wall.at[0], before, after, 4 * cx)
    fill_y(dpad, wall.at[1], before, after, 4 * cx + 3 * rows)
    before, after = before_after("fx", fxe, fxo)
    fill_x_shared(jpad, dpad, rows, cols, before, after, 3 * cy)
    lattice = lattice_rows()

    def one_tile(l, h):
        others = []
        for c in range(3):
            ends = end_rows(jpad, c, l, h, first_sub)
            for dh in (-1, 0, 1):
                ends[dh] = ends[dh] * (1.0 / REACH) + lattice[c]
                if c == 0:
                    ends[dh] = ends[dh] + jnp.where(first_sub, -SPAN, SPAN)
                if c == 1:
                    ends[dh] = ends[dh] + RISE * dh
            others.append(ends)
        pulls = [end_rows(dpad, c, l, h, first_sub) for c in range(3)]

        def weight_of(g, order, dh, here, mine):
            bonded = (bits[l, h, g // 8] & (1 << (3 * (g % 8) + order))) != 0
            return jnp.where(bonded, bond_row(1.0, here, mine), 0.0)

        tile_pass(l, h, cols, columns, others, pulls, weight_of, weights, acc)

    for l in range(rows):
        sums = []
        for h in range(cols):
            one_tile(l, h)
            sums.append(tile_sums(acc, l, h, 4))
        pulled = [v + part[l, c] for c, v in enumerate(by_quantity(sums))]
        totals[l] = pulled[3]
        for c in range(3):
            mine = wall[1, c, l]
            fresh = wall[2, c, l] + STIFFNESS * (pulled[c] - pulled[3] * mine)
            vel1[c, l] = fresh
            base1[c, l] = mine + fresh

    def edge(at):
        def write(out):
            for c in range(3):
                for k in range(rows):
                    out[c * rows + k : c * rows + k + 1, :] = base1[c, k, at : at + 1, :]
            for spare in range(3 * rows, out.shape[0]):
                out[spare : spare + 1, :] = jnp.zeros((1, LANES), F32)

        return write

    place_edges(even_at("wy"), edge(0), edge(cols - 1), to_even, to_odd)


def wall_first(cx, cy, wall, wy_got, fx_got, part, bits, columns):
    rows, cols = wall.shape[2], wall.shape[3]
    edge = (pad8(3 * rows), LANES)
    field = vmem(*wall.shape[1:])
    return pl.pallas_call(
        functools.partial(wall_kernel, cx, cy),
        in_specs=[whole()] * 8,
        out_specs=[whole()] * 6,
        out_shape=[
            jax.ShapeDtypeStruct((rows, cols, STORED, SUB, LANES), F32),
            field,
            field,
            vmem(rows, cols, LANES),
            vmem(*edge),
            vmem(*edge),
        ],
        scratch_shapes=[
            pltpu.VMEM((3, rows + 2, SUB, LANES), F32),
            pltpu.VMEM((3, rows + 2, SUB, LANES), F32),
            pltpu.VMEM((rows, cols, 4, LANES, LANES), F32),
        ],
        compiler_params=params(),
        name="wall_first",
    )(wall, *wy_got, *fx_got, part, bits, columns)


def pack_base_kernel(base1, got_odd, got_even, to_odd, to_even):
    rows, cols = base1.shape[1], base1.shape[2]
    before, after = before_after("wy", got_even, got_odd)

    def edge(l):
        def write(out):
            at = 0
            for c in range(3):
                side = c * rows + l
                out[at : at + 1, :] = before[side : side + 1]
                out[at + 1 : at + 1 + cols, :] = base1[c, l]
                out[at + 1 + cols : at + 2 + cols, :] = after[side : side + 1]
                at += cols + 2
            for spare in range(at, out.shape[0]):
                out[spare : spare + 1, :] = jnp.zeros((1, LANES), F32)

        return write

    place_edges(even_at("fx"), edge(0), edge(rows - 1), to_even, to_odd)


def pack_base(base1, got):
    cols = base1.shape[2]
    out = vmem(pad8(3 * (cols + 2)), LANES)
    return pl.pallas_call(
        pack_base_kernel,
        in_specs=[whole()] * 3,
        out_specs=[whole()] * 2,
        out_shape=[out, out],
        compiler_params=params(),
        name="pack_base",
    )(base1, *got)


def last_kernel(
    weights, end_weights, got, base1, vel1, totals, wyo, wye, fxo, fxe, disp_out, vel_out,
    dpad, acc,
):
    rows, cols = base1.shape[1], base1.shape[2]
    first_sub = lax.broadcasted_iota(jnp.int32, (SUB, LANES), 0) < SUB // 2
    before, after = before_after("wy", wye, wyo)
    fill_y(dpad, base1, before, after, 0)
    before, after = before_after("fx", fxe, fxo)
    fill_x(dpad, rows, cols, before, after, 0)
    total = got[0]
    for d in range(1, got.shape[0]):
        total = total + got[d]
    one, two = unpack_slots(total, cols)
    for k in range(rows + 2):
        here = dpad[0, k, 0 : cols + 2, :] + LOADING * one[k][0 : cols + 2]
        dpad[0, k, 0 : cols + 2, :] = here

    def one_tile(l, h):
        mids = [mid_rows(dpad, c, l, h) for c in range(3)]
        ends = [end_rows(dpad, c, l, h, first_sub) for c in range(3)]
        place = 0
        for g in range(LANES // SUB):
            sums = [None] * 3
            for dh in reached(g):
                for weight, pulls in (
                    (weights[l, h, place], mids), (end_weights[l, h, place], ends)
                ):
                    terms = [weight * pulls[c][dh] for c in range(3)]
                    sums = [t if v is None else v + t for v, t in zip(sums, terms)]
                place += 1
            for c in range(3):
                acc[l, h, c, g * SUB : (g + 1) * SUB, :] = sums[c]

    for l in range(rows):
        sums = []
        for h in range(cols):
            one_tile(l, h)
            sums.append(tile_sums(acc, l, h, 3))
        pulled = by_quantity(sums)
        for c in range(3):
            mine = dpad[c, l + 1, 1 : cols + 1, :]
            force = STIFFNESS * (pulled[c] - totals[l] * mine)
            if c == 0:
                force = force + LOADING * (one[l + 1][1 : cols + 1] + two[l])
            fresh = vel1[c, l] + force
            vel_out[c, l] = fresh
            disp_out[c, l] = mine + fresh


def wall_last(weights, end_weights, got, base1, vel1, totals, wy_got, fx_got):
    rows, cols = base1.shape[1], base1.shape[2]
    return pl.pallas_call(
        last_kernel,
        in_specs=[whole()] * 10,
        out_specs=[whole()] * 2,
        out_shape=[jax.ShapeDtypeStruct(base1.shape, F32)] * 2,
        scratch_shapes=[
            pltpu.VMEM((3, rows + 2, SUB, LANES), F32),
            pltpu.VMEM((rows, cols, 3, LANES, LANES), F32),
        ],
        compiler_params=params(),
        name="wall_last",
    )(weights, end_weights, got, base1, vel1, totals, *wy_got, *fx_got)


def per_device(
    displacement,
    velocity,
    jitter,
    bond_masks,
    pressure,
    pressure_prev,
    speed_sq,
    route_device,
    route_tile,
):
    fx_count, wy_count = lax.axis_size("fx"), lax.axis_size("wy")
    cols = displacement.shape[2]
    device = route_device.reshape(-1, LANES)
    tile = route_tile.reshape(-1, LANES)
    cx, cy = pressure.shape[0], pressure.shape[1]
    *sends, ends, wall = pack_wy(
        pressure, pressure_prev, speed_sq, jitter, displacement, velocity
    )
    wy_got = exchange("wy", *sends)
    sends = pack_fx(cx, ends, wall, wy_got)
    fx_got = exchange("fx", *sends)
    grids = (pressure, pressure_prev, speed_sq)
    weights, part, bits, target, columns, *grids = wall_center(
        wy_count, bond_masks, grids, device, tile, wall, wy_got
    )
    pressure_out, slots = grid_steps(*grids, wy_got, fx_got, target, fx_count, wy_count)
    got = lax.all_to_all(slots, ("fx", "wy"), split_axis=0, concat_axis=0, tiled=True)
    end_weights, vel1, base1, totals, *sends = wall_first(
        cx, cy, wall, wy_got, fx_got, part, bits, columns
    )
    base_wy = exchange("wy", *sends)
    sends = pack_base(base1, base_wy)
    base_fx = exchange("fx", *sends)
    disp_out, vel_out = wall_last(
        weights, end_weights, got, base1, vel1, totals, base_wy, base_fx
    )
    return (disp_out, vel_out, pressure_out)


def solution(mesh):
    placed = (
        P(None, "fx", "wy", None),
        P(None, "fx", "wy", None),
        P(None, "fx", "wy", None),
        P("fx", "wy", None, None, None),
        P("fx", "wy", None),
        P("fx", "wy", None),
        P("fx", "wy", None),
        P(("fx", "wy"), None),
        P(("fx", "wy")),
    )
    return jax.shard_map(
        per_device,
        mesh=mesh,
        in_specs=placed,
        out_specs=(P(None, "fx", "wy", None), P(None, "fx", "wy", None), P("fx", "wy", None)),
        check_vma=False,
    )
```

```python
import functools

import jax
import jax.numpy as jnp
from jax import lax
from jax.experimental import pallas as pl
from jax.experimental.pallas import tpu as pltpu
from jax.sharding import PartitionSpec as P

STIFFNESS = 0.02
LOADING = 0.05
REACH = 3.0
LANES = 128
SUB = 8
VMEM_BYTES = 32 * 1024 * 1024
HBM = pl.BlockSpec(memory_space=pltpu.HBM)

F32 = jnp.float32
BF16 = jnp.bfloat16


def whole():
    return pl.BlockSpec(memory_space=pltpu.VMEM)


def params():
    return pltpu.CompilerParams(vmem_limit_bytes=VMEM_BYTES)


def vmem(*shape):
    return pltpu.VMEM(shape, F32)


def even_at(axis):
    return lax.rem(lax.axis_index(axis), 2) == 0


def swap_pairs(axis, sizes, first):
    count, others = sizes[axis], sizes[1 - axis]
    pairs = []

    def join(*two):
        a, b = [place * sizes[1] + other for place, other in two]
        pairs.extend([(a, b), (b, a)])

    def at(place, other):
        return (place, other) if axis == 0 else (other, place)

    met = set()
    for low in range(first, count - 1, 2):
        met.update((low, low + 1))
        for other in range(others):
            join(at(low, other), at(low + 1, other))
    for place in range(count):
        if place not in met and others % 2 == 0:
            for other in range(0, others, 2):
                join(at(place, other), at(place, other + 1))
    return pairs


def exchange(axis, to_odd, to_even):
    names = ("fx", "wy")
    sizes = [lax.axis_size(name) for name in names]
    along = names.index(axis)
    got_odd = lax.ppermute(to_odd, names, swap_pairs(along, sizes, 1))
    got_even = lax.ppermute(to_even, names, swap_pairs(along, sizes, 0))
    return got_odd, got_even


def place_edges(even, low, high, to_even, to_odd):
    @pl.when(even)
    def _():
        high(to_even)
        low(to_odd)

    @pl.when(jnp.logical_not(even))
    def _():
        low(to_even)
        high(to_odd)


def before_after(axis, got_even, got_odd):
    even = even_at(axis)
    place, last = lax.axis_index(axis), lax.axis_size(axis) - 1
    a, b = got_even[...], got_odd[...]
    before = jnp.where(place == 0, 0.0, jnp.where(even, b, a))
    after = jnp.where(place == last, 0.0, jnp.where(even, a, b))
    return before, after


def pack_wy_kernel(
    p, q, s, jit_in, disp_in, vel_in, wy_odd, wy_even, ends, wall, edges, sems
):
    cx, cy = p.shape[0], p.shape[1]
    rows, cols = jit_in.shape[1], jit_in.shape[2]
    pairs = []
    for k, field in enumerate((p, q, s)):
        for side, first in enumerate((0, cy - SUB)):
            pairs.append((field.at[:, first : first + SUB, :], edges.at[2 * k + side]))
    pairs.append((p.at[0:2], ends.at[0, 0:2]))
    pairs.append((p.at[cx - 2 : cx], ends.at[1, 0:2]))
    for k, field in enumerate((q, s)):
        pairs.append((field.at[0], ends.at[0, 2 + k]))
        pairs.append((field.at[cx - 1], ends.at[1, 2 + k]))
    for k, field in enumerate((jit_in, disp_in, vel_in)):
        pairs.append((field, wall.at[k]))
    copies = [pltpu.make_async_copy(a, b, sems.at[k]) for k, (a, b) in enumerate(pairs)]
    for copy in copies:
        copy.start()
    for copy in copies:
        copy.wait()

    def edge(side, near, far, h):
        def write(out):
            out[0:cx, :] = edges[side, :, near, :]
            out[cx : 2 * cx, :] = edges[side, :, far, :]
            out[2 * cx : 3 * cx, :] = edges[2 + side, :, near, :]
            out[3 * cx : 4 * cx, :] = edges[4 + side, :, near, :]
            at = 4 * cx
            for field in range(2):
                for c in range(3):
                    for l in range(rows):
                        out[at : at + 1, :] = wall[field, c, l, h : h + 1, :]
                        at += 1
            for spare in range(at, out.shape[0]):
                out[spare : spare + 1, :] = jnp.zeros((1, LANES), F32)

        return write

    place_edges(
        even_at("wy"),
        edge(0, 0, 1, 0),
        edge(1, SUB - 1, SUB - 2, cols - 1),
        wy_even,
        wy_odd,
    )


def in_hbm(*arrays):
    return [pltpu.with_memory_space_constraint(v, pltpu.HBM) for v in arrays]


def pad8(count):
    return (count + 7) // 8 * 8


def pack_wy(p, q, s, jit, disp, vel):
    cx, cy = p.shape[0], p.shape[1]
    rows = jit.shape[1]
    wy_out = vmem(pad8(4 * cx + 6 * rows), LANES)
    return pl.pallas_call(
        pack_wy_kernel,
        in_specs=[HBM] * 6,
        out_specs=[whole()] * 4,
        out_shape=[wy_out, wy_out, vmem(2, 4, cy, LANES), vmem(3, *jit.shape)],
        scratch_shapes=[
            pltpu.VMEM((6, cx, SUB, LANES), F32),
            pltpu.SemaphoreType.DMA((15,)),
        ],
        compiler_params=params(),
        name="pack_wy",
    )(*in_hbm(p, q, s, jit, disp, vel))


def wall_lanes(field, low):
    lane = lax.broadcasted_iota(jnp.int32, field.shape, 1) % 8
    return lane < 3 if low else lane > 4


def pack_fx_kernel(cx, ends, wall, got_odd, got_even, to_odd, to_even, line):
    cy = ends.shape[2]
    rows, cols = wall.shape[2], wall.shape[3]
    before, after = before_after("wy", got_even, got_odd)

    def edge(side, near, far, x, l):
        def write(out):
            line[SUB - 1 : SUB, :] = before[x : x + 1]
            line[SUB : SUB + cy, :] = ends[side, near]
            line[SUB + cy : SUB + cy + 1, :] = after[x : x + 1]
            mine, speed = ends[side, near], ends[side, 3]
            beside = ends[side, far] + line[SUB - 1 : SUB - 1 + cy, :] + line[SUB + 1 : SUB + 1 + cy, :]
            out[0:cy, :] = mine
            out[cy : 2 * cy, :] = update(mine, ends[side, 2], speed, beside)
            out[2 * cy : 3 * cy, :] = speed
            at = 3 * cy
            for c in range(3):
                pair = []
                for field in range(2):
                    row = 4 * cx + (field * 3 + c) * rows + l
                    parts = (before[row : row + 1], wall[field, c, l], after[row : row + 1])
                    pair.append(jnp.concatenate(parts, axis=0))
                moved = pltpu.roll(pair[1], 3 if side == 0 else LANES - 3, 1)
                out[at : at + cols + 2, :] = jnp.where(wall_lanes(moved, side == 0), pair[0], moved)
                at += cols + 2
            out[at : at + 1, :] = before[x : x + 1]
            out[at + 1 : at + 2, :] = after[x : x + 1]
            for spare in range(at + 2, out.shape[0]):
                out[spare : spare + 1, :] = jnp.zeros((1, LANES), F32)

        return write

    place_edges(
        even_at("fx"), edge(0, 0, 1, 0, 0), edge(1, 1, 0, cx - 1, rows - 1), to_even, to_odd
    )


def pack_fx(cx, ends, wall, got):
    cy, cols = ends.shape[2], wall.shape[3]
    out = vmem(pad8(3 * cy + 3 * (cols + 2) + 2), LANES)
    return pl.pallas_call(
        functools.partial(pack_fx_kernel, cx),
        in_specs=[whole()] * 4,
        out_specs=[whole()] * 2,
        out_shape=[out, out],
        scratch_shapes=[vmem(cy + 2 * SUB, LANES)],
        compiler_params=params(),
        name="pack_fx",
    )(ends, wall, *got)


def along_z(v):
    lane = lax.broadcasted_iota(jnp.int32, v.shape, 1)
    up = jnp.where(lane == LANES - 1, 0.0, pltpu.roll(v, LANES - 1, 1))
    down = jnp.where(lane == 0, 0.0, pltpu.roll(v, 1, 1))
    return up + down


def update(v, old, speed, beside):
    return 2.0 * v - old + speed * (beside + along_z(v) - 6.0 * v)


def two_terms(v):
    high = v.astype(BF16)
    return high, (v - high.astype(F32)).astype(BF16)


def grid_kernel(
    p, q, s, wyo, wye, fxo, fxe, target, out_to, keep, send, s0, s1, rhs, part1, part2, out, slots, sem
):
    cx, cy = p.shape[0], p.shape[1]
    ahead, behind = SUB, SUB + cy
    fx_count = part1.shape[0] // 2 - 1
    cols = 4
    tall = part2.shape[0]
    high = part1.shape[1] - 2 * SUB
    wy_count = high // cols
    before_y, after_y = before_after("wy", wye, wyo)
    before_x, after_x = before_after("fx", fxe, fxo)
    corner = 3 * cy + 3 * (cols + 2)

    s0[1 : cx + 1, ahead:behind, :] = p[...]
    for x, side in ((0, before_x), (cx + 1, after_x)):
        s0[x, ahead:behind, :] = side[0:cy]
        s0[x, ahead - 1 : ahead, :] = side[corner : corner + 1]
        s0[x, behind : behind + 1, :] = side[corner + 1 : corner + 2]
    s0[1 : cx + 1, ahead - 1, :] = before_y[0:cx]
    s0[1 : cx + 1, behind, :] = after_y[0:cx]

    for side, y, inner in ((before_y, ahead - 1, ahead), (after_y, behind, behind - 1)):
        near, far = side[0:cx], side[cx : 2 * cx]
        old, speed = side[2 * cx : 3 * cx], side[3 * cx : 4 * cx]
        beside = s0[0:cx, y, :] + s0[2 : cx + 2, y, :] + far + s0[1 : cx + 1, inner, :]
        s1[1 : cx + 1, y, :] = update(near, old, speed, beside)
    for side, x, inner in ((before_x, 0, 1), (after_x, cx + 1, cx)):
        part, speed = side[cy : 2 * cy], side[2 * cy : 3 * cy]
        s1[x, ahead:behind, :] = part + speed * s0[inner, ahead:behind, :]

    def sweep(now, old, x):
        beside = now[x, ahead:behind, :] + now[x + 2, ahead:behind, :]
        beside = beside + now[x + 1, ahead - 1 : behind - 1, :]
        beside = beside + now[x + 1, ahead + 1 : behind + 1, :]
        return update(now[x + 1, ahead:behind, :], old, s[x], beside)

    for x in range(cx):
        fresh = sweep(s0, q[x], x)
        s1[x + 1, ahead:behind, :] = fresh
        a, b = two_terms(fresh)
        rhs[x * cy : (x + 1) * cy, 0:LANES] = a
        rhs[x * cy : (x + 1) * cy, LANES : 2 * LANES] = b
    for x in range(cx):
        fresh = sweep(s1, p[x], x)
        out[x] = fresh
        a, b = two_terms(fresh)
        rhs[x * cy : (x + 1) * cy, 2 * LANES : 3 * LANES] = a
        rhs[x * cy : (x + 1) * cy, 3 * LANES : 4 * LANES] = b

    out_copy = pltpu.make_async_copy(out, out_to, sem)
    out_copy.start()

    part1[...] = jnp.zeros(part1.shape, F32)
    part2[:, 0:SUB, :] = jnp.zeros((tall, SUB, LANES), F32)
    chunk = 256
    for first in range(0, tall * high, chunk):
        tile = lax.broadcasted_iota(jnp.int32, (chunk, LANES), 0) + first
        picks = []
        for piece in range(target.shape[0]):
            picks.append(jnp.where(tile == target[piece : piece + 1, :], 1.0, 0.0).astype(BF16))
        sums = jnp.dot(jnp.concatenate(picks, axis=1), rhs[...], preferred_element_type=F32)
        one = sums[:, 0:LANES] + sums[:, LANES : 2 * LANES]
        two = sums[:, 2 * LANES : 3 * LANES] + sums[:, 3 * LANES : 4 * LANES]
        l = first // high
        part1[1 + l : 1 + l + chunk // high, SUB : SUB + high, :] = one.reshape(-1, high, LANES)
        part2[l : l + chunk // high, SUB : SUB + high, :] = two.reshape(-1, high, LANES)
    sub = lax.broadcasted_iota(jnp.int32, (SUB, LANES), 0)
    lane = lax.broadcasted_iota(jnp.int32, (SUB, LANES), 1)
    step1 = sub < cols + 2
    for a in range(fx_count):
        for b in range(wy_count):
            h = SUB + cols * b
            slot = a * (wy_count // 2) + b // 2
            one = [part1[2 * a + l, h - 1 : h - 1 + SUB, :] for l in range(4)]
            ends = jnp.where(lane % 8 < 4, one[3], one[0])
            two = [
                part2[2 * a + l, h + at - 6 : h + at - 6 + SUB, :]
                for l, at in ((0, 0), (0, 2), (1, 0))
            ]
            x = jnp.broadcast_to(part2[2 * a + 1, h + 2 : h + 3, :], (SUB, LANES))
            y = jnp.broadcast_to(part2[2 * a + 1, h + 3 : h + 4, :], (SUB, LANES))
            for r in range(4):
                moved = pltpu.roll(y, (3 - 2 * r) % LANES, 1)
                ends = jnp.where((sub == 1 + r) & free_ends(lane), moved, ends)
            low, high_free = (sub == 0) & (lane // 8 % 4 == 0), (sub == cols + 1) & (lane // 8 % 4 == 3)
            own0 = jnp.where(low | high_free, x, one[1])
            own1 = jnp.where(low, pltpu.roll(x, LANES - 8, 1), one[2])
            own1 = jnp.where(high_free, pltpu.roll(x, 8, 1), own1)
            for k, group in enumerate((ends, own0, own1)):
                slots[b % 2, slot, k * SUB : (k + 1) * SUB, :] = jnp.where(step1, group, two[k])

    @pl.when(even_at("wy"))
    def _():
        keep[...] = slots[0]
        send[...] = slots[1]

    @pl.when(jnp.logical_not(even_at("wy")))
    def _():
        keep[...] = slots[1]
        send[...] = slots[0]

    out_copy.wait()


def free_ends(lane):
    return (lane % 8 == 3) | (lane % 8 == 4)


def unpack_slots(total, cols):
    ends, own0, own1 = [total[k * SUB : (k + 1) * SUB] for k in range(3)]
    lane = lax.broadcasted_iota(jnp.int32, (1, LANES), 1)
    two = [[ends[6:7], ends[7:8], own0[6:7], own0[7:8]], [own1[6:7], own1[7:8]]]
    q = lane // 8 % 4
    last = cols + 1
    x = jnp.where(q == 0, own0[0:1], own0[last : last + 1])
    x = jnp.where(q == 1, pltpu.roll(own1[0:1], 8, 1), x)
    x = jnp.where(q == 2, pltpu.roll(own1[last : last + 1], LANES - 8, 1), x)
    y = None
    for r in range(4):
        moved = pltpu.roll(ends[1 + r : 2 + r], (2 * r - 3) % LANES, 1)
        y = moved if y is None else jnp.where(lane % 8 // 2 == r, moved, y)
    two[1].extend([x, y])
    two = [jnp.concatenate(v, axis=0) for v in two]
    return (ends, own0, own1, ends), two


def grid_steps(p, q, s, wy_got, fx_got, target, fx_count, wy_count):
    cx, cy = p.shape[0], p.shape[1]
    tall, high = fx_count * 2, wy_count * 4
    half = (fx_count * wy_count // 2, 3 * SUB, LANES)
    return pl.pallas_call(
        grid_kernel,
        in_specs=[whole()] * 8,
        out_specs=[HBM, whole(), whole()],
        out_shape=[
            jax.ShapeDtypeStruct(p.shape, F32),
            vmem(*half),
            vmem(*half),
        ],
        scratch_shapes=[
            pltpu.VMEM((cx + 2, cy + 2 * SUB, LANES), F32),
            pltpu.VMEM((cx + 2, cy + 2 * SUB, LANES), F32),
            pltpu.VMEM((cx * cy, 4 * LANES), BF16),
            pltpu.VMEM((tall + 2, high + 2 * SUB, LANES), F32),
            pltpu.VMEM((tall, high + 2 * SUB, LANES), F32),
            vmem(*p.shape),
            vmem(2, *half),
            pltpu.SemaphoreType.DMA(()),
        ],
        compiler_params=params(),
        name="grid_steps",
    )(p, q, s, *wy_got, *fx_got, target)


def pair_sum_kernel(keep, got, after, out):
    out[...] = keep[...] + got[...]


def pair_sum(keep, got, after):
    return pl.pallas_call(
        pair_sum_kernel,
        in_specs=[whole()] * 3,
        out_specs=whole(),
        out_shape=jax.ShapeDtypeStruct(keep.shape, F32),
        compiler_params=params(),
        name="pair_sum",
    )(keep, got, after)


def parity_groups(fx_count, wy_count):
    whole_row = range(fx_count * wy_count)
    return [[d for d in whole_row if d % wy_count % 2 == parity] for parity in range(2)]


def reached(g):
    groups = []
    for dh in (-1, 0, 1):
        if (dh == -1 and g % 4 == 3) or (dh == 1 and g % 4 == 0):
            continue
        groups.append(dh)
    return groups


STORED = sum(len(reached(g)) for g in range(LANES // SUB))


def mid_rows(ref, c, l, h):
    rows = {}
    for dh in (-1, 0, 1):
        row = ref[c, l + 1, pl.ds(h + 1 + dh, 1), :]
        rows[dh] = jnp.broadcast_to(row, (SUB, LANES))
    return rows


def end_rows(ref, c, l, h, first_sub):
    rows = {}
    for dh in (-1, 0, 1):
        at = pl.ds(h + 1 + dh, 1)
        before = jnp.broadcast_to(ref[c, l, at, :], (SUB, LANES))
        after = jnp.broadcast_to(ref[c, l + 2, at, :], (SUB, LANES))
        rows[dh] = jnp.where(first_sub, before, after)
    return rows


def fill_y(pad, own, before, after, at):
    rows, cols = own.shape[1], own.shape[2]
    for c in range(3):
        for l in range(rows):
            row = at + c * rows + l
            pad[c, l + 1, 0:1, :] = before[row : row + 1]
            pad[c, l + 1, 1 : cols + 1, :] = own[c, l]
            pad[c, l + 1, cols + 1 : cols + 2, :] = after[row : row + 1]


def fill_x(pad, rows, cols, before, after, at):
    for c in range(3):
        row = at + c * (cols + 2)
        pad[c, 0, 0 : cols + 2, :] = before[row : row + cols + 2]
        pad[c, rows + 1, 0 : cols + 2, :] = after[row : row + cols + 2]


def fill_x_shared(jpad, dpad, rows, cols, before, after, at):
    for c in range(3):
        row = at + c * (cols + 2)
        for message, l, low in ((before, 0, False), (after, rows + 1, True)):
            both = message[row : row + cols + 2]
            jpad[c, l, 0 : cols + 2, :] = jnp.where(wall_lanes(both, low), both, 0.0)
            moved = pltpu.roll(both, LANES - 3 if low else 3, 1)
            dpad[c, l, 0 : cols + 2, :] = moved


def lattice_rows():
    index = lax.broadcasted_iota(jnp.int32, (1, LANES), 1)
    places = (index % 8, index // 8 % 4, index // 32)
    return [v.astype(F32) * (1.0 / REACH) for v in places]


SPAN = 8.0 / REACH
RISE = 4.0 / REACH


def own_columns(ref, lattice, rows, cols):
    places = []
    for l in range(rows):
        for h in range(cols):
            for c in range(3):
                places.append(ref[c, l + 1, h + 1 : h + 2, :] * (1.0 / REACH) + lattice[c])
    spare = -len(places) % SUB
    if spare:
        places.append(jnp.zeros((spare, LANES), F32))
    return jnp.transpose(jnp.concatenate(places, axis=0))


def bond_row(weight, others, mine):
    for c in range(3):
        diff = others[c] - mine[c]
        weight = weight - diff * diff
    return jnp.maximum(weight, 0.0)


def tile_pass(l, h, cols, columns, others, pulls, weight_of, weights, acc):
    place = 0
    first = 3 * (l * cols + h)
    for g in range(LANES // SUB):
        span = slice(g * SUB, (g + 1) * SUB)
        mine = [jnp.broadcast_to(columns[span, first + c : first + c + 1], (SUB, LANES)) for c in range(3)]
        sums = [None] * 4
        for order, dh in enumerate(reached(g)):
            here = [others[c][dh] for c in range(3)]
            weight = weight_of(g, order, dh, here, mine)
            weights[l, h, place] = weight
            place += 1
            terms = [weight * pulls[c][dh] for c in range(3)] + [weight]
            sums = [t if v is None else v + t for v, t in zip(sums, terms)]
        for c in range(4):
            acc[l, h, c, span, :] = sums[c]


def tile_sums(acc, l, h, count):
    ones = jnp.ones((2 * SUB, 2 * LANES), BF16)
    terms = [jnp.concatenate(two_terms(acc[l, h, c]), axis=1) for c in range(count)]
    sums = lax.dot_general(
        ones,
        jnp.concatenate(terms, axis=0),
        (((1,), (1,)), ((), ())),
        preferred_element_type=F32,
    )[0:1]
    return [sums[:, c * LANES : (c + 1) * LANES] for c in range(count)]


def by_quantity(tiles):
    return [jnp.concatenate(rows, axis=0) for rows in zip(*tiles)]


def quotient(v, n):
    return ((v.astype(F32) + 0.5) * (1.0 / n)).astype(jnp.int32)


def center_kernel(
    wy_count, masks_in, p_in, q_in, s_in, device_in, tile_in, wall, wyo, wye,
    weights, part, bits, target, columns, p, q, s, jpad, dpad, acc, masks, route, sems,
):
    rows, cols = wall.shape[2], wall.shape[3]
    cx = p.shape[0]
    copies = {}
    pairs = [(device_in, route.at[0]), (tile_in, route.at[1])]
    pairs = [(p_in, p), (q_in, q), (s_in, s)] + pairs
    for k, pair in enumerate(pairs):
        copies[k] = pltpu.make_async_copy(*pair, sems.at[k])
    for k, first in enumerate((3, 0, 6)):
        span = slice(first, first + 3)
        copies["masks", first] = pltpu.make_async_copy(
            masks_in.at[:, :, span], masks.at[:, :, span], sems.at[5 + k]
        )
    order = [3, 4, ("masks", 3), ("masks", 0), ("masks", 6), 0, 1, 2]
    for k in order:
        copies[k].start()
    first_sub = lax.broadcasted_iota(jnp.int32, (SUB, LANES), 0) < SUB // 2
    copies[3].wait()
    copies[4].wait()
    device, tile = route[0], route[1]
    a, t = quotient(device, wy_count), quotient(tile, cols)
    b, u = device - a * wy_count, tile - t * cols
    target[...] = (a * rows + t) * (wy_count * cols) + b * cols + u
    before, after = before_after("wy", wye, wyo)
    fill_y(jpad, wall.at[0], before, after, 4 * cx)
    fill_y(dpad, wall.at[1], before, after, 4 * cx + 3 * rows)
    lattice = lattice_rows()
    columns[...] = own_columns(jpad, lattice, rows, cols)

    def one_tile(l, h):
        others = []
        for c in range(3):
            mid = mid_rows(jpad, c, l, h)
            for dh in (-1, 0, 1):
                mid[dh] = mid[dh] * (1.0 / REACH) + lattice[c]
                if c == 1:
                    mid[dh] = mid[dh] + RISE * dh
            others.append(mid)
        pulls = [mid_rows(dpad, c, l, h) for c in range(3)]

        def weight_of(g, order, dh, here, mine):
            span = slice(g * SUB, (g + 1) * SUB)
            return bond_row(masks[l, h, 4 + dh, span, :].astype(F32), here, mine)

        tile_pass(l, h, cols, columns, others, pulls, weight_of, weights, acc)

    def put_sums(l, h):
        for c, sums in enumerate(tile_sums(acc, l, h, 4)):
            part[l, c, h : h + 1, :] = sums

    def put_bits(l, h):
        words = [jnp.zeros((SUB, LANES), jnp.int32) for _ in range(2)]
        for g in range(LANES // SUB):
            span = slice(g * SUB, (g + 1) * SUB)
            for order, dh in enumerate(reached(g)):
                before = masks[l, h, 1 + dh, span, :]
                after = masks[l, h, 7 + dh, span, :]
                place = 3 * (g % 8) + order
                words[g // 8] = words[g // 8] + jnp.where(first_sub, before, after) * (1 << place)
        for k in range(2):
            bits[l, h, k] = words[k]

    tiles = [(l, h) for l in range(rows) for h in range(cols)]
    copies["masks", 3].wait()
    for l, h in tiles:
        one_tile(l, h)
        put_sums(l, h)
    copies["masks", 0].wait()
    copies["masks", 6].wait()
    for l, h in tiles:
        put_bits(l, h)
    for k in range(3):
        copies[k].wait()


def wall_center(wy_count, masks, grids, device, tile, wall, wy_got):
    rows, cols = wall.shape[2], wall.shape[3]
    return pl.pallas_call(
        functools.partial(center_kernel, wy_count),
        in_specs=[HBM] * 6 + [whole()] * 3,
        out_specs=[whole()] * 8,
        out_shape=[
            jax.ShapeDtypeStruct((rows, cols, STORED, SUB, LANES), F32),
            vmem(rows, 4, cols, LANES),
            pltpu.VMEM((rows, cols, 2, SUB, LANES), jnp.int32),
            pltpu.VMEM(device.shape, jnp.int32),
            vmem(LANES, pad8(3 * rows * cols)),
        ]
        + [vmem(*grids[0].shape)] * 3,
        scratch_shapes=[
            vmem(3, rows + 2, SUB, LANES),
            vmem(3, rows + 2, SUB, LANES),
            vmem(rows, cols, 4, LANES, LANES),
            pltpu.VMEM(masks.shape, jnp.int32),
            pltpu.VMEM((2,) + device.shape, jnp.int32),
            pltpu.SemaphoreType.DMA((8,)),
        ],
        compiler_params=params(),
        name="wall_center",
    )(*in_hbm(masks, *grids, device, tile), wall, *wy_got)


def wall_kernel(
    cx, cy, wall, wyo, wye, fxo, fxe, part, bits, columns, weights, vel1, base1, totals, to_odd, to_even,
    jpad, dpad, acc,
):
    rows, cols = wall.shape[2], wall.shape[3]
    first_sub = lax.broadcasted_iota(jnp.int32, (SUB, LANES), 0) < SUB // 2
    before, after = before_after("wy", wye, wyo)
    fill_y(jpad, wall.at[0], before, after, 4 * cx)
    fill_y(dpad, wall.at[1], before, after, 4 * cx + 3 * rows)
    before, after = before_after("fx", fxe, fxo)
    fill_x_shared(jpad, dpad, rows, cols, before, after, 3 * cy)
    lattice = lattice_rows()

    def one_tile(l, h):
        others = []
        for c in range(3):
            ends = end_rows(jpad, c, l, h, first_sub)
            for dh in (-1, 0, 1):
                ends[dh] = ends[dh] * (1.0 / REACH) + lattice[c]
                if c == 0:
                    ends[dh] = ends[dh] + jnp.where(first_sub, -SPAN, SPAN)
                if c == 1:
                    ends[dh] = ends[dh] + RISE * dh
            others.append(ends)
        pulls = [end_rows(dpad, c, l, h, first_sub) for c in range(3)]

        def weight_of(g, order, dh, here, mine):
            bonded = (bits[l, h, g // 8] & (1 << (3 * (g % 8) + order))) != 0
            return jnp.where(bonded, bond_row(1.0, here, mine), 0.0)

        tile_pass(l, h, cols, columns, others, pulls, weight_of, weights, acc)

    for l in range(rows):
        sums = []
        for h in range(cols):
            one_tile(l, h)
            sums.append(tile_sums(acc, l, h, 4))
        pulled = [v + part[l, c] for c, v in enumerate(by_quantity(sums))]
        totals[l] = pulled[3]
        for c in range(3):
            mine = wall[1, c, l]
            fresh = wall[2, c, l] + STIFFNESS * (pulled[c] - pulled[3] * mine)
            vel1[c, l] = fresh
            base1[c, l] = mine + fresh

    def edge(at):
        def write(out):
            for c in range(3):
                for k in range(rows):
                    out[c * rows + k : c * rows + k + 1, :] = base1[c, k, at : at + 1, :]
            for spare in range(3 * rows, out.shape[0]):
                out[spare : spare + 1, :] = jnp.zeros((1, LANES), F32)

        return write

    place_edges(even_at("wy"), edge(0), edge(cols - 1), to_even, to_odd)


def wall_first(cx, cy, wall, wy_got, fx_got, part, bits, columns):
    rows, cols = wall.shape[2], wall.shape[3]
    edge = (pad8(3 * rows), LANES)
    field = vmem(*wall.shape[1:])
    return pl.pallas_call(
        functools.partial(wall_kernel, cx, cy),
        in_specs=[whole()] * 8,
        out_specs=[whole()] * 6,
        out_shape=[
            jax.ShapeDtypeStruct((rows, cols, STORED, SUB, LANES), F32),
            field,
            field,
            vmem(rows, cols, LANES),
            vmem(*edge),
            vmem(*edge),
        ],
        scratch_shapes=[
            pltpu.VMEM((3, rows + 2, SUB, LANES), F32),
            pltpu.VMEM((3, rows + 2, SUB, LANES), F32),
            pltpu.VMEM((rows, cols, 4, LANES, LANES), F32),
        ],
        compiler_params=params(),
        name="wall_first",
    )(wall, *wy_got, *fx_got, part, bits, columns)


def pack_base_kernel(base1, got_odd, got_even, to_odd, to_even):
    rows, cols = base1.shape[1], base1.shape[2]
    before, after = before_after("wy", got_even, got_odd)

    def edge(l):
        def write(out):
            at = 0
            for c in range(3):
                side = c * rows + l
                out[at : at + 1, :] = before[side : side + 1]
                out[at + 1 : at + 1 + cols, :] = base1[c, l]
                out[at + 1 + cols : at + 2 + cols, :] = after[side : side + 1]
                at += cols + 2
            for spare in range(at, out.shape[0]):
                out[spare : spare + 1, :] = jnp.zeros((1, LANES), F32)

        return write

    place_edges(even_at("fx"), edge(0), edge(rows - 1), to_even, to_odd)


def pack_base(base1, got):
    cols = base1.shape[2]
    out = vmem(pad8(3 * (cols + 2)), LANES)
    return pl.pallas_call(
        pack_base_kernel,
        in_specs=[whole()] * 3,
        out_specs=[whole()] * 2,
        out_shape=[out, out],
        compiler_params=params(),
        name="pack_base",
    )(base1, *got)


def last_kernel(
    weights, end_weights, got, base1, vel1, totals, wyo, wye, fxo, fxe, disp_out, vel_out,
    dpad, acc,
):
    rows, cols = base1.shape[1], base1.shape[2]
    first_sub = lax.broadcasted_iota(jnp.int32, (SUB, LANES), 0) < SUB // 2
    before, after = before_after("wy", wye, wyo)
    fill_y(dpad, base1, before, after, 0)
    before, after = before_after("fx", fxe, fxo)
    fill_x(dpad, rows, cols, before, after, 0)
    total = got[0]
    for d in range(1, got.shape[0]):
        total = total + got[d]
    one, two = unpack_slots(total, cols)
    for k in range(rows + 2):
        here = dpad[0, k, 0 : cols + 2, :] + LOADING * one[k][0 : cols + 2]
        dpad[0, k, 0 : cols + 2, :] = here

    def one_tile(l, h):
        mids = [mid_rows(dpad, c, l, h) for c in range(3)]
        ends = [end_rows(dpad, c, l, h, first_sub) for c in range(3)]
        place = 0
        for g in range(LANES // SUB):
            sums = [None] * 3
            for dh in reached(g):
                for weight, pulls in (
                    (weights[l, h, place], mids), (end_weights[l, h, place], ends)
                ):
                    terms = [weight * pulls[c][dh] for c in range(3)]
                    sums = [t if v is None else v + t for v, t in zip(sums, terms)]
                place += 1
            for c in range(3):
                acc[l, h, c, g * SUB : (g + 1) * SUB, :] = sums[c]

    for l in range(rows):
        sums = []
        for h in range(cols):
            one_tile(l, h)
            sums.append(tile_sums(acc, l, h, 3))
        pulled = by_quantity(sums)
        for c in range(3):
            mine = dpad[c, l + 1, 1 : cols + 1, :]
            force = STIFFNESS * (pulled[c] - totals[l] * mine)
            if c == 0:
                force = force + LOADING * (one[l + 1][1 : cols + 1] + two[l])
            fresh = vel1[c, l] + force
            vel_out[c, l] = fresh
            disp_out[c, l] = mine + fresh


def wall_last(weights, end_weights, got, base1, vel1, totals, wy_got, fx_got):
    rows, cols = base1.shape[1], base1.shape[2]
    return pl.pallas_call(
        last_kernel,
        in_specs=[whole()] * 10,
        out_specs=[whole()] * 2,
        out_shape=[jax.ShapeDtypeStruct(base1.shape, F32)] * 2,
        scratch_shapes=[
            pltpu.VMEM((3, rows + 2, SUB, LANES), F32),
            pltpu.VMEM((rows, cols, 3, LANES, LANES), F32),
        ],
        compiler_params=params(),
        name="wall_last",
    )(weights, end_weights, got, base1, vel1, totals, *wy_got, *fx_got)


def per_device(
    displacement,
    velocity,
    jitter,
    bond_masks,
    pressure,
    pressure_prev,
    speed_sq,
    route_device,
    route_tile,
):
    fx_count, wy_count = lax.axis_size("fx"), lax.axis_size("wy")
    cols = displacement.shape[2]
    device = route_device.reshape(-1, LANES)
    tile = route_tile.reshape(-1, LANES)
    cx, cy = pressure.shape[0], pressure.shape[1]
    *sends, ends, wall = pack_wy(
        pressure, pressure_prev, speed_sq, jitter, displacement, velocity
    )
    wy_got = exchange("wy", *sends)
    sends = pack_fx(cx, ends, wall, wy_got)
    fx_got = exchange("fx", *sends)
    grids = (pressure, pressure_prev, speed_sq)
    weights, part, bits, target, columns, *grids = wall_center(
        wy_count, bond_masks, grids, device, tile, wall, wy_got
    )
    pressure_out, keep, send = grid_steps(*grids, wy_got, fx_got, target, fx_count, wy_count)
    names = ("fx", "wy")
    other = lax.ppermute(send, names, swap_pairs(1, (fx_count, wy_count), 0))
    end_weights, vel1, base1, totals, *sends = wall_first(
        cx, cy, wall, wy_got, fx_got, part, bits, columns
    )
    slots = pair_sum(keep, other, totals)
    got = lax.all_to_all(
        slots,
        names,
        split_axis=0,
        concat_axis=0,
        tiled=True,
        axis_index_groups=parity_groups(fx_count, wy_count),
    )
    base_wy = exchange("wy", *sends)
    sends = pack_base(base1, base_wy)
    base_fx = exchange("fx", *sends)
    disp_out, vel_out = wall_last(
        weights, end_weights, got, base1, vel1, totals, base_wy, base_fx
    )
    return (disp_out, vel_out, pressure_out)


def solution(mesh):
    placed = (
        P(None, "fx", "wy", None),
        P(None, "fx", "wy", None),
        P(None, "fx", "wy", None),
        P("fx", "wy", None, None, None),
        P("fx", "wy", None),
        P("fx", "wy", None),
        P("fx", "wy", None),
        P(("fx", "wy"), None),
        P(("fx", "wy")),
    )
    return jax.shard_map(
        per_device,
        mesh=mesh,
        in_specs=placed,
        out_specs=(P(None, "fx", "wy", None), P(None, "fx", "wy", None), P("fx", "wy", None)),
        check_vma=False,
    )
```

```python
import functools

import jax
import jax.numpy as jnp
from jax import lax
from jax.experimental import pallas as pl
from jax.experimental.pallas import tpu as pltpu
from jax.sharding import PartitionSpec as P

STIFFNESS = 0.02
LOADING = 0.05
REACH = 3.0
LANES = 128
SUB = 8
VMEM_BYTES = 32 * 1024 * 1024
HBM = pl.BlockSpec(memory_space=pltpu.HBM)

F32 = jnp.float32
BF16 = jnp.bfloat16


def whole():
    return pl.BlockSpec(memory_space=pltpu.VMEM)


def params():
    return pltpu.CompilerParams(vmem_limit_bytes=VMEM_BYTES)


def vmem(*shape):
    return pltpu.VMEM(shape, F32)


def even_at(axis):
    return lax.rem(lax.axis_index(axis), 2) == 0


def swap_pairs(axis, sizes, first):
    count, others = sizes[axis], sizes[1 - axis]
    pairs = []

    def join(*two):
        a, b = [place * sizes[1] + other for place, other in two]
        pairs.extend([(a, b), (b, a)])

    def at(place, other):
        return (place, other) if axis == 0 else (other, place)

    met = set()
    for low in range(first, count - 1, 2):
        met.update((low, low + 1))
        for other in range(others):
            join(at(low, other), at(low + 1, other))
    for place in range(count):
        if place not in met and others % 2 == 0:
            for other in range(0, others, 2):
                join(at(place, other), at(place, other + 1))
    return pairs


def exchange(axis, to_odd, to_even):
    names = ("fx", "wy")
    sizes = [lax.axis_size(name) for name in names]
    along = names.index(axis)
    got_odd = lax.ppermute(to_odd, names, swap_pairs(along, sizes, 1))
    got_even = lax.ppermute(to_even, names, swap_pairs(along, sizes, 0))
    return got_odd, got_even


def place_edges(even, low, high, to_even, to_odd):
    @pl.when(even)
    def _():
        high(to_even)
        low(to_odd)

    @pl.when(jnp.logical_not(even))
    def _():
        low(to_even)
        high(to_odd)


def before_after(axis, got_even, got_odd):
    even = even_at(axis)
    place, last = lax.axis_index(axis), lax.axis_size(axis) - 1
    a, b = got_even[...], got_odd[...]
    before = jnp.where(place == 0, 0.0, jnp.where(even, b, a))
    after = jnp.where(place == last, 0.0, jnp.where(even, a, b))
    return before, after


def pack_wy_kernel(
    p, q, s, jit_in, disp_in, vel_in, wy_odd, wy_even, ends, wall, edges, sems
):
    cx, cy = p.shape[0], p.shape[1]
    rows, cols = jit_in.shape[1], jit_in.shape[2]
    pairs = []
    for k, field in enumerate((p, q, s)):
        for side, first in enumerate((0, cy - SUB)):
            pairs.append((field.at[:, first : first + SUB, :], edges.at[2 * k + side]))
    pairs.append((p.at[0:2], ends.at[0, 0:2]))
    pairs.append((p.at[cx - 2 : cx], ends.at[1, 0:2]))
    for k, field in enumerate((q, s)):
        pairs.append((field.at[0], ends.at[0, 2 + k]))
        pairs.append((field.at[cx - 1], ends.at[1, 2 + k]))
    for k, field in enumerate((jit_in, disp_in, vel_in)):
        pairs.append((field, wall.at[k]))
    copies = [pltpu.make_async_copy(a, b, sems.at[k]) for k, (a, b) in enumerate(pairs)]
    for copy in copies:
        copy.start()
    for copy in copies:
        copy.wait()

    def edge(side, near, far, h):
        def write(out):
            out[0:cx, :] = edges[side, :, near, :]
            out[cx : 2 * cx, :] = edges[side, :, far, :]
            out[2 * cx : 3 * cx, :] = edges[2 + side, :, near, :]
            out[3 * cx : 4 * cx, :] = edges[4 + side, :, near, :]
            at = 4 * cx
            for field in range(2):
                for c in range(3):
                    for l in range(rows):
                        out[at : at + 1, :] = wall[field, c, l, h : h + 1, :]
                        at += 1
            for spare in range(at, out.shape[0]):
                out[spare : spare + 1, :] = jnp.zeros((1, LANES), F32)

        return write

    place_edges(
        even_at("wy"),
        edge(0, 0, 1, 0),
        edge(1, SUB - 1, SUB - 2, cols - 1),
        wy_even,
        wy_odd,
    )


def in_hbm(*arrays):
    return [pltpu.with_memory_space_constraint(v, pltpu.HBM) for v in arrays]


def pad8(count):
    return (count + 7) // 8 * 8


def pack_wy(p, q, s, jit, disp, vel):
    cx, cy = p.shape[0], p.shape[1]
    rows = jit.shape[1]
    wy_out = vmem(pad8(4 * cx + 6 * rows), LANES)
    return pl.pallas_call(
        pack_wy_kernel,
        in_specs=[HBM] * 6,
        out_specs=[whole()] * 4,
        out_shape=[wy_out, wy_out, vmem(2, 4, cy, LANES), vmem(3, *jit.shape)],
        scratch_shapes=[
            pltpu.VMEM((6, cx, SUB, LANES), F32),
            pltpu.SemaphoreType.DMA((15,)),
        ],
        compiler_params=params(),
        name="pack_wy",
    )(*in_hbm(p, q, s, jit, disp, vel))


def wall_lanes(field, low):
    lane = lax.broadcasted_iota(jnp.int32, field.shape, 1) % 8
    return lane < 3 if low else lane > 4


def pack_fx_kernel(cx, ends, wall, got_odd, got_even, to_odd, to_even, line):
    cy = ends.shape[2]
    rows, cols = wall.shape[2], wall.shape[3]
    before, after = before_after("wy", got_even, got_odd)

    def edge(side, near, far, x, l):
        def write(out):
            line[SUB - 1 : SUB, :] = before[x : x + 1]
            line[SUB : SUB + cy, :] = ends[side, near]
            line[SUB + cy : SUB + cy + 1, :] = after[x : x + 1]
            mine, speed = ends[side, near], ends[side, 3]
            beside = ends[side, far] + line[SUB - 1 : SUB - 1 + cy, :] + line[SUB + 1 : SUB + 1 + cy, :]
            out[0:cy, :] = mine
            out[cy : 2 * cy, :] = update(mine, ends[side, 2], speed, beside)
            out[2 * cy : 3 * cy, :] = speed
            at = 3 * cy
            for c in range(3):
                pair = []
                for field in range(2):
                    row = 4 * cx + (field * 3 + c) * rows + l
                    parts = (before[row : row + 1], wall[field, c, l], after[row : row + 1])
                    pair.append(jnp.concatenate(parts, axis=0))
                moved = pltpu.roll(pair[1], 3 if side == 0 else LANES - 3, 1)
                out[at : at + cols + 2, :] = jnp.where(wall_lanes(moved, side == 0), pair[0], moved)
                at += cols + 2
            out[at : at + 1, :] = before[x : x + 1]
            out[at + 1 : at + 2, :] = after[x : x + 1]
            for spare in range(at + 2, out.shape[0]):
                out[spare : spare + 1, :] = jnp.zeros((1, LANES), F32)

        return write

    place_edges(
        even_at("fx"), edge(0, 0, 1, 0, 0), edge(1, 1, 0, cx - 1, rows - 1), to_even, to_odd
    )


def pack_fx(cx, ends, wall, got):
    cy, cols = ends.shape[2], wall.shape[3]
    out = vmem(pad8(3 * cy + 3 * (cols + 2) + 2), LANES)
    return pl.pallas_call(
        functools.partial(pack_fx_kernel, cx),
        in_specs=[whole()] * 4,
        out_specs=[whole()] * 2,
        out_shape=[out, out],
        scratch_shapes=[vmem(cy + 2 * SUB, LANES)],
        compiler_params=params(),
        name="pack_fx",
    )(ends, wall, *got)


def along_z(v):
    lane = lax.broadcasted_iota(jnp.int32, v.shape, 1)
    up = jnp.where(lane == LANES - 1, 0.0, pltpu.roll(v, LANES - 1, 1))
    down = jnp.where(lane == 0, 0.0, pltpu.roll(v, 1, 1))
    return up + down


def update(v, old, speed, beside):
    return 2.0 * v - old + speed * (beside + along_z(v) - 6.0 * v)


def two_terms(v):
    high = v.astype(BF16)
    return high, (v - high.astype(F32)).astype(BF16)


def grid_kernel(
    p, q, s, wyo, wye, fxo, fxe, target, out, keep, send, s0, s1, rhs, part1, part2, slots
):
    cx, cy = p.shape[0], p.shape[1]
    ahead, behind = SUB, SUB + cy
    fx_count = part1.shape[0] // 2 - 1
    cols = 4
    tall = part2.shape[0]
    high = part1.shape[1] - 2 * SUB
    wy_count = high // cols
    before_y, after_y = before_after("wy", wye, wyo)
    before_x, after_x = before_after("fx", fxe, fxo)
    corner = 3 * cy + 3 * (cols + 2)

    s0[1 : cx + 1, ahead:behind, :] = p[...]
    for x, side in ((0, before_x), (cx + 1, after_x)):
        s0[x, ahead:behind, :] = side[0:cy]
        s0[x, ahead - 1 : ahead, :] = side[corner : corner + 1]
        s0[x, behind : behind + 1, :] = side[corner + 1 : corner + 2]
    s0[1 : cx + 1, ahead - 1, :] = before_y[0:cx]
    s0[1 : cx + 1, behind, :] = after_y[0:cx]

    for side, y, inner in ((before_y, ahead - 1, ahead), (after_y, behind, behind - 1)):
        near, far = side[0:cx], side[cx : 2 * cx]
        old, speed = side[2 * cx : 3 * cx], side[3 * cx : 4 * cx]
        beside = s0[0:cx, y, :] + s0[2 : cx + 2, y, :] + far + s0[1 : cx + 1, inner, :]
        s1[1 : cx + 1, y, :] = update(near, old, speed, beside)
    for side, x, inner in ((before_x, 0, 1), (after_x, cx + 1, cx)):
        part, speed = side[cy : 2 * cy], side[2 * cy : 3 * cy]
        s1[x, ahead:behind, :] = part + speed * s0[inner, ahead:behind, :]

    def sweep(now, old, x):
        beside = now[x, ahead:behind, :] + now[x + 2, ahead:behind, :]
        beside = beside + now[x + 1, ahead - 1 : behind - 1, :]
        beside = beside + now[x + 1, ahead + 1 : behind + 1, :]
        return update(now[x + 1, ahead:behind, :], old, s[x], beside)

    for x in range(cx):
        fresh = sweep(s0, q[x], x)
        s1[x + 1, ahead:behind, :] = fresh
        a, b = two_terms(fresh)
        rhs[x * cy : (x + 1) * cy, 0:LANES] = a
        rhs[x * cy : (x + 1) * cy, LANES : 2 * LANES] = b
    for x in range(cx):
        fresh = sweep(s1, p[x], x)
        out[x] = fresh
        a, b = two_terms(fresh)
        rhs[x * cy : (x + 1) * cy, 2 * LANES : 3 * LANES] = a
        rhs[x * cy : (x + 1) * cy, 3 * LANES : 4 * LANES] = b

    part1[...] = jnp.zeros(part1.shape, F32)
    part2[:, 0:SUB, :] = jnp.zeros((tall, SUB, LANES), F32)
    chunk = 256
    for first in range(0, tall * high, chunk):
        tile = lax.broadcasted_iota(jnp.int32, (chunk, LANES), 0) + first
        picks = []
        for piece in range(target.shape[0]):
            picks.append(jnp.where(tile == target[piece : piece + 1, :], 1.0, 0.0).astype(BF16))
        sums = jnp.dot(jnp.concatenate(picks, axis=1), rhs[...], preferred_element_type=F32)
        one = sums[:, 0:LANES] + sums[:, LANES : 2 * LANES]
        two = sums[:, 2 * LANES : 3 * LANES] + sums[:, 3 * LANES : 4 * LANES]
        l = first // high
        part1[1 + l : 1 + l + chunk // high, SUB : SUB + high, :] = one.reshape(-1, high, LANES)
        part2[l : l + chunk // high, SUB : SUB + high, :] = two.reshape(-1, high, LANES)
    sub = lax.broadcasted_iota(jnp.int32, (SUB, LANES), 0)
    lane = lax.broadcasted_iota(jnp.int32, (SUB, LANES), 1)
    step1 = sub < cols + 2
    for a in range(fx_count):
        for b in range(wy_count):
            h = SUB + cols * b
            slot = a * (wy_count // 2) + b // 2
            one = [part1[2 * a + l, h - 1 : h - 1 + SUB, :] for l in range(4)]
            ends = jnp.where(lane % 8 < 4, one[3], one[0])
            two = [
                part2[2 * a + l, h + at - 6 : h + at - 6 + SUB, :]
                for l, at in ((0, 0), (0, 2), (1, 0))
            ]
            x = jnp.broadcast_to(part2[2 * a + 1, h + 2 : h + 3, :], (SUB, LANES))
            y = jnp.broadcast_to(part2[2 * a + 1, h + 3 : h + 4, :], (SUB, LANES))
            for r in range(4):
                moved = pltpu.roll(y, (3 - 2 * r) % LANES, 1)
                ends = jnp.where((sub == 1 + r) & free_ends(lane), moved, ends)
            low, high_free = (sub == 0) & (lane // 8 % 4 == 0), (sub == cols + 1) & (lane // 8 % 4 == 3)
            own0 = jnp.where(low | high_free, x, one[1])
            own1 = jnp.where(low, pltpu.roll(x, LANES - 8, 1), one[2])
            own1 = jnp.where(high_free, pltpu.roll(x, 8, 1), own1)
            for k, group in enumerate((ends, own0, own1)):
                slots[b % 2, slot, k * SUB : (k + 1) * SUB, :] = jnp.where(step1, group, two[k])

    @pl.when(even_at("wy"))
    def _():
        keep[...] = slots[0]
        send[...] = slots[1]

    @pl.when(jnp.logical_not(even_at("wy")))
    def _():
        keep[...] = slots[1]
        send[...] = slots[0]


def free_ends(lane):
    return (lane % 8 == 3) | (lane % 8 == 4)


def unpack_slots(total, cols):
    ends, own0, own1 = [total[k * SUB : (k + 1) * SUB] for k in range(3)]
    lane = lax.broadcasted_iota(jnp.int32, (1, LANES), 1)
    two = [[ends[6:7], ends[7:8], own0[6:7], own0[7:8]], [own1[6:7], own1[7:8]]]
    q = lane // 8 % 4
    last = cols + 1
    x = jnp.where(q == 0, own0[0:1], own0[last : last + 1])
    x = jnp.where(q == 1, pltpu.roll(own1[0:1], 8, 1), x)
    x = jnp.where(q == 2, pltpu.roll(own1[last : last + 1], LANES - 8, 1), x)
    y = None
    for r in range(4):
        moved = pltpu.roll(ends[1 + r : 2 + r], (2 * r - 3) % LANES, 1)
        y = moved if y is None else jnp.where(lane % 8 // 2 == r, moved, y)
    two[1].extend([x, y])
    two = [jnp.concatenate(v, axis=0) for v in two]
    return (ends, own0, own1, ends), two


def grid_steps(p, q, s, wy_got, fx_got, target, fx_count, wy_count):
    cx, cy = p.shape[0], p.shape[1]
    tall, high = fx_count * 2, wy_count * 4
    half = (fx_count * wy_count // 2, 3 * SUB, LANES)
    return pl.pallas_call(
        grid_kernel,
        in_specs=[whole()] * 8,
        out_specs=[whole()] * 3,
        out_shape=[
            vmem(*p.shape),
            vmem(*half),
            vmem(*half),
        ],
        scratch_shapes=[
            pltpu.VMEM((cx + 2, cy + 2 * SUB, LANES), F32),
            pltpu.VMEM((cx + 2, cy + 2 * SUB, LANES), F32),
            pltpu.VMEM((cx * cy, 4 * LANES), BF16),
            pltpu.VMEM((tall + 2, high + 2 * SUB, LANES), F32),
            pltpu.VMEM((tall, high + 2 * SUB, LANES), F32),
            vmem(2, *half),
        ],
        compiler_params=params(),
        name="grid_steps",
    )(p, q, s, *wy_got, *fx_got, target)


def pair_sum_kernel(keep, got, after, out):
    out[...] = keep[...] + got[...]


def pair_sum(keep, got, after):
    return pl.pallas_call(
        pair_sum_kernel,
        in_specs=[whole()] * 3,
        out_specs=whole(),
        out_shape=jax.ShapeDtypeStruct(keep.shape, F32),
        compiler_params=params(),
        name="pair_sum",
    )(keep, got, after)


def parity_groups(fx_count, wy_count):
    whole_row = range(fx_count * wy_count)
    return [[d for d in whole_row if d % wy_count % 2 == parity] for parity in range(2)]


def reached(g):
    groups = []
    for dh in (-1, 0, 1):
        if (dh == -1 and g % 4 == 3) or (dh == 1 and g % 4 == 0):
            continue
        groups.append(dh)
    return groups


STORED = sum(len(reached(g)) for g in range(LANES // SUB))


def mid_rows(ref, c, l, h):
    rows = {}
    for dh in (-1, 0, 1):
        row = ref[c, l + 1, pl.ds(h + 1 + dh, 1), :]
        rows[dh] = jnp.broadcast_to(row, (SUB, LANES))
    return rows


def end_rows(ref, c, l, h, first_sub):
    rows = {}
    for dh in (-1, 0, 1):
        at = pl.ds(h + 1 + dh, 1)
        before = jnp.broadcast_to(ref[c, l, at, :], (SUB, LANES))
        after = jnp.broadcast_to(ref[c, l + 2, at, :], (SUB, LANES))
        rows[dh] = jnp.where(first_sub, before, after)
    return rows


def fill_y(pad, own, before, after, at):
    rows, cols = own.shape[1], own.shape[2]
    for c in range(3):
        for l in range(rows):
            row = at + c * rows + l
            pad[c, l + 1, 0:1, :] = before[row : row + 1]
            pad[c, l + 1, 1 : cols + 1, :] = own[c, l]
            pad[c, l + 1, cols + 1 : cols + 2, :] = after[row : row + 1]


def fill_x(pad, rows, cols, before, after, at):
    for c in range(3):
        row = at + c * (cols + 2)
        pad[c, 0, 0 : cols + 2, :] = before[row : row + cols + 2]
        pad[c, rows + 1, 0 : cols + 2, :] = after[row : row + cols + 2]


def fill_x_shared(jpad, dpad, rows, cols, before, after, at):
    for c in range(3):
        row = at + c * (cols + 2)
        for message, l, low in ((before, 0, False), (after, rows + 1, True)):
            both = message[row : row + cols + 2]
            jpad[c, l, 0 : cols + 2, :] = jnp.where(wall_lanes(both, low), both, 0.0)
            moved = pltpu.roll(both, LANES - 3 if low else 3, 1)
            dpad[c, l, 0 : cols + 2, :] = moved


def lattice_rows():
    index = lax.broadcasted_iota(jnp.int32, (1, LANES), 1)
    places = (index % 8, index // 8 % 4, index // 32)
    return [v.astype(F32) * (1.0 / REACH) for v in places]


SPAN = 8.0 / REACH
RISE = 4.0 / REACH


def own_columns(ref, lattice, rows, cols):
    places = []
    for l in range(rows):
        for h in range(cols):
            for c in range(3):
                places.append(ref[c, l + 1, h + 1 : h + 2, :] * (1.0 / REACH) + lattice[c])
    spare = -len(places) % SUB
    if spare:
        places.append(jnp.zeros((spare, LANES), F32))
    return jnp.transpose(jnp.concatenate(places, axis=0))


def bond_row(weight, others, mine):
    for c in range(3):
        diff = others[c] - mine[c]
        weight = weight - diff * diff
    return jnp.maximum(weight, 0.0)


def tile_pass(l, h, cols, columns, others, pulls, weight_of, weights, acc):
    place = 0
    first = 3 * (l * cols + h)
    for g in range(LANES // SUB):
        span = slice(g * SUB, (g + 1) * SUB)
        mine = [jnp.broadcast_to(columns[span, first + c : first + c + 1], (SUB, LANES)) for c in range(3)]
        sums = [None] * 4
        for order, dh in enumerate(reached(g)):
            here = [others[c][dh] for c in range(3)]
            weight = weight_of(g, order, dh, here, mine)
            weights[l, h, place] = weight
            place += 1
            terms = [weight * pulls[c][dh] for c in range(3)] + [weight]
            sums = [t if v is None else v + t for v, t in zip(sums, terms)]
        for c in range(4):
            acc[l, h, c, span, :] = sums[c]


def tile_sums(acc, l, h, count):
    ones = jnp.ones((2 * SUB, 2 * LANES), BF16)
    terms = [jnp.concatenate(two_terms(acc[l, h, c]), axis=1) for c in range(count)]
    sums = lax.dot_general(
        ones,
        jnp.concatenate(terms, axis=0),
        (((1,), (1,)), ((), ())),
        preferred_element_type=F32,
    )[0:1]
    return [sums[:, c * LANES : (c + 1) * LANES] for c in range(count)]


def by_quantity(tiles):
    return [jnp.concatenate(rows, axis=0) for rows in zip(*tiles)]


def quotient(v, n):
    return ((v.astype(F32) + 0.5) * (1.0 / n)).astype(jnp.int32)


def center_kernel(
    wy_count, masks_in, p_in, q_in, s_in, device_in, tile_in, wall, wyo, wye,
    weights, part, bits, target, columns, p, q, s, jpad, dpad, acc, masks, route, sems,
):
    rows, cols = wall.shape[2], wall.shape[3]
    cx = p.shape[0]
    copies = {}
    pairs = [(device_in, route.at[0]), (tile_in, route.at[1])]
    pairs = [(p_in, p), (q_in, q), (s_in, s)] + pairs
    for k, pair in enumerate(pairs):
        copies[k] = pltpu.make_async_copy(*pair, sems.at[k])
    for k, first in enumerate((3, 0, 6)):
        span = slice(first, first + 3)
        copies["masks", first] = pltpu.make_async_copy(
            masks_in.at[:, :, span], masks.at[:, :, span], sems.at[5 + k]
        )
    order = [3, 4, ("masks", 3), ("masks", 0), ("masks", 6), 0, 1, 2]
    for k in order:
        copies[k].start()
    first_sub = lax.broadcasted_iota(jnp.int32, (SUB, LANES), 0) < SUB // 2
    copies[3].wait()
    copies[4].wait()
    device, tile = route[0], route[1]
    a, t = quotient(device, wy_count), quotient(tile, cols)
    b, u = device - a * wy_count, tile - t * cols
    target[...] = (a * rows + t) * (wy_count * cols) + b * cols + u
    before, after = before_after("wy", wye, wyo)
    fill_y(jpad, wall.at[0], before, after, 4 * cx)
    fill_y(dpad, wall.at[1], before, after, 4 * cx + 3 * rows)
    lattice = lattice_rows()
    columns[...] = own_columns(jpad, lattice, rows, cols)

    def one_tile(l, h):
        others = []
        for c in range(3):
            mid = mid_rows(jpad, c, l, h)
            for dh in (-1, 0, 1):
                mid[dh] = mid[dh] * (1.0 / REACH) + lattice[c]
                if c == 1:
                    mid[dh] = mid[dh] + RISE * dh
            others.append(mid)
        pulls = [mid_rows(dpad, c, l, h) for c in range(3)]

        def weight_of(g, order, dh, here, mine):
            span = slice(g * SUB, (g + 1) * SUB)
            return bond_row(masks[l, h, 4 + dh, span, :].astype(F32), here, mine)

        tile_pass(l, h, cols, columns, others, pulls, weight_of, weights, acc)

    def put_sums(l, h):
        for c, sums in enumerate(tile_sums(acc, l, h, 4)):
            part[l, c, h : h + 1, :] = sums

    def put_bits(l, h):
        words = [jnp.zeros((SUB, LANES), jnp.int32) for _ in range(2)]
        for g in range(LANES // SUB):
            span = slice(g * SUB, (g + 1) * SUB)
            for order, dh in enumerate(reached(g)):
                before = masks[l, h, 1 + dh, span, :]
                after = masks[l, h, 7 + dh, span, :]
                place = 3 * (g % 8) + order
                words[g // 8] = words[g // 8] + jnp.where(first_sub, before, after) * (1 << place)
        for k in range(2):
            bits[l, h, k] = words[k]

    tiles = [(l, h) for l in range(rows) for h in range(cols)]
    copies["masks", 3].wait()
    for l, h in tiles:
        one_tile(l, h)
        put_sums(l, h)
    copies["masks", 0].wait()
    copies["masks", 6].wait()
    for l, h in tiles:
        put_bits(l, h)
    for k in range(3):
        copies[k].wait()


def wall_center(wy_count, masks, grids, device, tile, wall, wy_got):
    rows, cols = wall.shape[2], wall.shape[3]
    return pl.pallas_call(
        functools.partial(center_kernel, wy_count),
        in_specs=[HBM] * 6 + [whole()] * 3,
        out_specs=[whole()] * 8,
        out_shape=[
            jax.ShapeDtypeStruct((rows, cols, STORED, SUB, LANES), F32),
            vmem(rows, 4, cols, LANES),
            pltpu.VMEM((rows, cols, 2, SUB, LANES), jnp.int32),
            pltpu.VMEM(device.shape, jnp.int32),
            vmem(LANES, pad8(3 * rows * cols)),
        ]
        + [vmem(*grids[0].shape)] * 3,
        scratch_shapes=[
            vmem(3, rows + 2, SUB, LANES),
            vmem(3, rows + 2, SUB, LANES),
            vmem(rows, cols, 4, LANES, LANES),
            pltpu.VMEM(masks.shape, jnp.int32),
            pltpu.VMEM((2,) + device.shape, jnp.int32),
            pltpu.SemaphoreType.DMA((8,)),
        ],
        compiler_params=params(),
        name="wall_center",
    )(*in_hbm(masks, *grids, device, tile), wall, *wy_got)


def wall_kernel(
    cx, cy, wall, wyo, wye, fxo, fxe, part, bits, columns, pressure,
    weights, vel1, base1, totals, to_odd, to_even, pressure_out, jpad, dpad, acc, sem,
):
    rows, cols = wall.shape[2], wall.shape[3]
    copy = pltpu.make_async_copy(pressure, pressure_out, sem)
    copy.start()
    first_sub = lax.broadcasted_iota(jnp.int32, (SUB, LANES), 0) < SUB // 2
    before, after = before_after("wy", wye, wyo)
    fill_y(jpad, wall.at[0], before, after, 4 * cx)
    fill_y(dpad, wall.at[1], before, after, 4 * cx + 3 * rows)
    before, after = before_after("fx", fxe, fxo)
    fill_x_shared(jpad, dpad, rows, cols, before, after, 3 * cy)
    lattice = lattice_rows()

    def one_tile(l, h):
        others = []
        for c in range(3):
            ends = end_rows(jpad, c, l, h, first_sub)
            for dh in (-1, 0, 1):
                ends[dh] = ends[dh] * (1.0 / REACH) + lattice[c]
                if c == 0:
                    ends[dh] = ends[dh] + jnp.where(first_sub, -SPAN, SPAN)
                if c == 1:
                    ends[dh] = ends[dh] + RISE * dh
            others.append(ends)
        pulls = [end_rows(dpad, c, l, h, first_sub) for c in range(3)]

        def weight_of(g, order, dh, here, mine):
            bonded = (bits[l, h, g // 8] & (1 << (3 * (g % 8) + order))) != 0
            return jnp.where(bonded, bond_row(1.0, here, mine), 0.0)

        tile_pass(l, h, cols, columns, others, pulls, weight_of, weights, acc)

    for l in range(rows):
        sums = []
        for h in range(cols):
            one_tile(l, h)
            sums.append(tile_sums(acc, l, h, 4))
        pulled = [v + part[l, c] for c, v in enumerate(by_quantity(sums))]
        totals[l] = pulled[3]
        for c in range(3):
            mine = wall[1, c, l]
            fresh = wall[2, c, l] + STIFFNESS * (pulled[c] - pulled[3] * mine)
            vel1[c, l] = fresh
            base1[c, l] = mine + fresh

    def edge(at):
        def write(out):
            for c in range(3):
                for k in range(rows):
                    out[c * rows + k : c * rows + k + 1, :] = base1[c, k, at : at + 1, :]
            for spare in range(3 * rows, out.shape[0]):
                out[spare : spare + 1, :] = jnp.zeros((1, LANES), F32)

        return write

    place_edges(even_at("wy"), edge(0), edge(cols - 1), to_even, to_odd)
    copy.wait()


def wall_first(wall, wy_got, fx_got, part, bits, columns, pressure):
    cx, cy = pressure.shape[0], pressure.shape[1]
    rows, cols = wall.shape[2], wall.shape[3]
    edge = (pad8(3 * rows), LANES)
    field = vmem(*wall.shape[1:])
    return pl.pallas_call(
        functools.partial(wall_kernel, cx, cy),
        in_specs=[whole()] * 9,
        out_specs=[whole()] * 6 + [HBM],
        out_shape=[
            jax.ShapeDtypeStruct((rows, cols, STORED, SUB, LANES), F32),
            field,
            field,
            vmem(rows, cols, LANES),
            vmem(*edge),
            vmem(*edge),
            jax.ShapeDtypeStruct(pressure.shape, F32),
        ],
        scratch_shapes=[
            pltpu.VMEM((3, rows + 2, SUB, LANES), F32),
            pltpu.VMEM((3, rows + 2, SUB, LANES), F32),
            pltpu.VMEM((rows, cols, 4, LANES, LANES), F32),
            pltpu.SemaphoreType.DMA(()),
        ],
        compiler_params=params(),
        name="wall_first",
    )(wall, *wy_got, *fx_got, part, bits, columns, pressure)


def pack_base_kernel(base1, got_odd, got_even, to_odd, to_even):
    rows, cols = base1.shape[1], base1.shape[2]
    before, after = before_after("wy", got_even, got_odd)

    def edge(l):
        def write(out):
            at = 0
            for c in range(3):
                side = c * rows + l
                out[at : at + 1, :] = before[side : side + 1]
                out[at + 1 : at + 1 + cols, :] = base1[c, l]
                out[at + 1 + cols : at + 2 + cols, :] = after[side : side + 1]
                at += cols + 2
            for spare in range(at, out.shape[0]):
                out[spare : spare + 1, :] = jnp.zeros((1, LANES), F32)

        return write

    place_edges(even_at("fx"), edge(0), edge(rows - 1), to_even, to_odd)


def pack_base(base1, got):
    cols = base1.shape[2]
    out = vmem(pad8(3 * (cols + 2)), LANES)
    return pl.pallas_call(
        pack_base_kernel,
        in_specs=[whole()] * 3,
        out_specs=[whole()] * 2,
        out_shape=[out, out],
        compiler_params=params(),
        name="pack_base",
    )(base1, *got)


def last_kernel(
    weights, end_weights, got, base1, vel1, totals, wyo, wye, fxo, fxe, disp_out, vel_out,
    dpad, acc,
):
    rows, cols = base1.shape[1], base1.shape[2]
    first_sub = lax.broadcasted_iota(jnp.int32, (SUB, LANES), 0) < SUB // 2
    before, after = before_after("wy", wye, wyo)
    fill_y(dpad, base1, before, after, 0)
    before, after = before_after("fx", fxe, fxo)
    fill_x(dpad, rows, cols, before, after, 0)
    total = got[0]
    for d in range(1, got.shape[0]):
        total = total + got[d]
    one, two = unpack_slots(total, cols)
    for k in range(rows + 2):
        here = dpad[0, k, 0 : cols + 2, :] + LOADING * one[k][0 : cols + 2]
        dpad[0, k, 0 : cols + 2, :] = here

    def one_tile(l, h):
        mids = [mid_rows(dpad, c, l, h) for c in range(3)]
        ends = [end_rows(dpad, c, l, h, first_sub) for c in range(3)]
        place = 0
        for g in range(LANES // SUB):
            sums = [None] * 3
            for dh in reached(g):
                for weight, pulls in (
                    (weights[l, h, place], mids), (end_weights[l, h, place], ends)
                ):
                    terms = [weight * pulls[c][dh] for c in range(3)]
                    sums = [t if v is None else v + t for v, t in zip(sums, terms)]
                place += 1
            for c in range(3):
                acc[l, h, c, g * SUB : (g + 1) * SUB, :] = sums[c]

    for l in range(rows):
        sums = []
        for h in range(cols):
            one_tile(l, h)
            sums.append(tile_sums(acc, l, h, 3))
        pulled = by_quantity(sums)
        for c in range(3):
            mine = dpad[c, l + 1, 1 : cols + 1, :]
            force = STIFFNESS * (pulled[c] - totals[l] * mine)
            if c == 0:
                force = force + LOADING * (one[l + 1][1 : cols + 1] + two[l])
            fresh = vel1[c, l] + force
            vel_out[c, l] = fresh
            disp_out[c, l] = mine + fresh


def wall_last(weights, end_weights, got, base1, vel1, totals, wy_got, fx_got):
    rows, cols = base1.shape[1], base1.shape[2]
    return pl.pallas_call(
        last_kernel,
        in_specs=[whole()] * 10,
        out_specs=[whole()] * 2,
        out_shape=[jax.ShapeDtypeStruct(base1.shape, F32)] * 2,
        scratch_shapes=[
            pltpu.VMEM((3, rows + 2, SUB, LANES), F32),
            pltpu.VMEM((rows, cols, 3, LANES, LANES), F32),
        ],
        compiler_params=params(),
        name="wall_last",
    )(weights, end_weights, got, base1, vel1, totals, *wy_got, *fx_got)


def per_device(
    displacement,
    velocity,
    jitter,
    bond_masks,
    pressure,
    pressure_prev,
    speed_sq,
    route_device,
    route_tile,
):
    fx_count, wy_count = lax.axis_size("fx"), lax.axis_size("wy")
    cols = displacement.shape[2]
    device = route_device.reshape(-1, LANES)
    tile = route_tile.reshape(-1, LANES)
    cx = pressure.shape[0]
    *sends, ends, wall = pack_wy(
        pressure, pressure_prev, speed_sq, jitter, displacement, velocity
    )
    wy_got = exchange("wy", *sends)
    sends = pack_fx(cx, ends, wall, wy_got)
    fx_got = exchange("fx", *sends)
    grids = (pressure, pressure_prev, speed_sq)
    weights, part, bits, target, columns, *grids = wall_center(
        wy_count, bond_masks, grids, device, tile, wall, wy_got
    )
    fresh, keep, send = grid_steps(*grids, wy_got, fx_got, target, fx_count, wy_count)
    names = ("fx", "wy")
    other = lax.ppermute(send, names, swap_pairs(1, (fx_count, wy_count), 0))
    end_weights, vel1, base1, totals, *sends, pressure_out = wall_first(
        wall, wy_got, fx_got, part, bits, columns, fresh
    )
    slots = pair_sum(keep, other, totals)
    got = lax.all_to_all(
        slots,
        names,
        split_axis=0,
        concat_axis=0,
        tiled=True,
        axis_index_groups=parity_groups(fx_count, wy_count),
    )
    base_wy = exchange("wy", *sends)
    sends = pack_base(base1, base_wy)
    base_fx = exchange("fx", *sends)
    disp_out, vel_out = wall_last(
        weights, end_weights, got, base1, vel1, totals, base_wy, base_fx
    )
    return (disp_out, vel_out, pressure_out)


def solution(mesh):
    placed = (
        P(None, "fx", "wy", None),
        P(None, "fx", "wy", None),
        P(None, "fx", "wy", None),
        P("fx", "wy", None, None, None),
        P("fx", "wy", None),
        P("fx", "wy", None),
        P("fx", "wy", None),
        P(("fx", "wy"), None),
        P(("fx", "wy")),
    )
    return jax.shard_map(
        per_device,
        mesh=mesh,
        in_specs=placed,
        out_specs=(P(None, "fx", "wy", None), P(None, "fx", "wy", None), P("fx", "wy", None)),
        check_vma=False,
    )
```

```python
import functools

import jax
import jax.numpy as jnp
from jax import lax
from jax.experimental import pallas as pl
from jax.experimental.pallas import tpu as pltpu
from jax.sharding import PartitionSpec as P

STIFFNESS = 0.02
LOADING = 0.05
REACH = 3.0
LANES = 128
SUB = 8
VMEM_BYTES = 32 * 1024 * 1024
HBM = pl.BlockSpec(memory_space=pltpu.HBM)

F32 = jnp.float32
BF16 = jnp.bfloat16


def whole():
    return pl.BlockSpec(memory_space=pltpu.VMEM)


def params():
    return pltpu.CompilerParams(vmem_limit_bytes=VMEM_BYTES)


def vmem(*shape):
    return pltpu.VMEM(shape, F32)


def even_at(axis):
    return lax.rem(lax.axis_index(axis), 2) == 0


def swap_pairs(axis, sizes, first):
    count, others = sizes[axis], sizes[1 - axis]
    pairs = []

    def join(*two):
        a, b = [place * sizes[1] + other for place, other in two]
        pairs.extend([(a, b), (b, a)])

    def at(place, other):
        return (place, other) if axis == 0 else (other, place)

    met = set()
    for low in range(first, count - 1, 2):
        met.update((low, low + 1))
        for other in range(others):
            join(at(low, other), at(low + 1, other))
    for place in range(count):
        if place not in met and others % 2 == 0:
            for other in range(0, others, 2):
                join(at(place, other), at(place, other + 1))
    return pairs


def exchange(axis, to_odd, to_even):
    names = ("fx", "wy")
    sizes = [lax.axis_size(name) for name in names]
    along = names.index(axis)
    got_odd = lax.ppermute(to_odd, names, swap_pairs(along, sizes, 1))
    got_even = lax.ppermute(to_even, names, swap_pairs(along, sizes, 0))
    return got_odd, got_even


def place_edges(even, low, high, to_even, to_odd):
    @pl.when(even)
    def _():
        high(to_even)
        low(to_odd)

    @pl.when(jnp.logical_not(even))
    def _():
        low(to_even)
        high(to_odd)


def before_after(axis, got_even, got_odd):
    even = even_at(axis)
    place, last = lax.axis_index(axis), lax.axis_size(axis) - 1
    a, b = got_even[...], got_odd[...]
    before = jnp.where(place == 0, 0.0, jnp.where(even, b, a))
    after = jnp.where(place == last, 0.0, jnp.where(even, a, b))
    return before, after


def pack_wy_kernel(
    p_in, q_in, s_in, jit_in, disp_in, vel_in, wy_odd, wy_even, p, q, s, wall, sems
):
    cx, cy = p.shape[0], p.shape[1]
    rows, cols = jit_in.shape[1], jit_in.shape[2]
    pairs = [(p_in, p), (q_in, q), (s_in, s)]
    for k, field in enumerate((jit_in, disp_in, vel_in)):
        pairs.append((field, wall.at[k]))
    copies = [pltpu.make_async_copy(a, b, sems.at[k]) for k, (a, b) in enumerate(pairs)]
    for copy in copies:
        copy.start()
    for copy in copies:
        copy.wait()

    def edge(near, far, h):
        def write(out):
            out[0:cx, :] = p[:, near, :]
            out[cx : 2 * cx, :] = p[:, far, :]
            out[2 * cx : 3 * cx, :] = q[:, near, :]
            out[3 * cx : 4 * cx, :] = s[:, near, :]
            at = 4 * cx
            for field in range(2):
                for c in range(3):
                    for l in range(rows):
                        out[at : at + 1, :] = wall[field, c, l, h : h + 1, :]
                        at += 1
            for spare in range(at, out.shape[0]):
                out[spare : spare + 1, :] = jnp.zeros((1, LANES), F32)

        return write

    place_edges(
        even_at("wy"),
        edge(0, 1, 0),
        edge(cy - 1, cy - 2, cols - 1),
        wy_even,
        wy_odd,
    )


def in_hbm(*arrays):
    return [pltpu.with_memory_space_constraint(v, pltpu.HBM) for v in arrays]


def pad8(count):
    return (count + 7) // 8 * 8


def pack_wy(p, q, s, jit, disp, vel):
    message = vmem(pad8(4 * p.shape[0] + 6 * jit.shape[1]), LANES)
    return pl.pallas_call(
        pack_wy_kernel,
        in_specs=[HBM] * 6,
        out_specs=[whole()] * 6,
        out_shape=[message, message] + [vmem(*p.shape)] * 3 + [vmem(3, *jit.shape)],
        scratch_shapes=[pltpu.SemaphoreType.DMA((6,))],
        compiler_params=params(),
        name="pack_wy",
    )(*in_hbm(p, q, s, jit, disp, vel))


def wall_lanes(field, low):
    lane = lax.broadcasted_iota(jnp.int32, field.shape, 1) % 8
    return lane < 3 if low else lane > 4


def pack_fx_kernel(p, q, s, wall, got_odd, got_even, to_odd, to_even, line):
    cx, cy = p.shape[0], p.shape[1]
    rows, cols = wall.shape[2], wall.shape[3]
    before, after = before_after("wy", got_even, got_odd)

    def edge(low, x, far, l):
        def write(out):
            line[SUB - 1 : SUB, :] = before[x : x + 1]
            line[SUB : SUB + cy, :] = p[x]
            line[SUB + cy : SUB + cy + 1, :] = after[x : x + 1]
            mine, speed = p[x], s[x]
            beside = p[far] + line[SUB - 1 : SUB - 1 + cy, :] + line[SUB + 1 : SUB + 1 + cy, :]
            out[0:cy, :] = mine
            out[cy : 2 * cy, :] = update(mine, q[x], speed, beside)
            out[2 * cy : 3 * cy, :] = speed
            at = 3 * cy
            for c in range(3):
                pair = []
                for field in range(2):
                    row = 4 * cx + (field * 3 + c) * rows + l
                    parts = (before[row : row + 1], wall[field, c, l], after[row : row + 1])
                    pair.append(jnp.concatenate(parts, axis=0))
                moved = pltpu.roll(pair[1], 3 if low else LANES - 3, 1)
                out[at : at + cols + 2, :] = jnp.where(wall_lanes(moved, low), pair[0], moved)
                at += cols + 2
            out[at : at + 1, :] = before[x : x + 1]
            out[at + 1 : at + 2, :] = after[x : x + 1]
            for spare in range(at + 2, out.shape[0]):
                out[spare : spare + 1, :] = jnp.zeros((1, LANES), F32)

        return write

    place_edges(
        even_at("fx"), edge(True, 0, 1, 0), edge(False, cx - 1, cx - 2, rows - 1), to_even, to_odd
    )


def pack_fx(grids, wall, got):
    cy, cols = grids[0].shape[1], wall.shape[3]
    out = vmem(pad8(3 * cy + 3 * (cols + 2) + 2), LANES)
    return pl.pallas_call(
        pack_fx_kernel,
        in_specs=[whole()] * 6,
        out_specs=[whole()] * 2,
        out_shape=[out, out],
        scratch_shapes=[vmem(cy + 2 * SUB, LANES)],
        compiler_params=params(),
        name="pack_fx",
    )(*grids, wall, *got)


def along_z(v):
    lane = lax.broadcasted_iota(jnp.int32, v.shape, 1)
    up = jnp.where(lane == LANES - 1, 0.0, pltpu.roll(v, LANES - 1, 1))
    down = jnp.where(lane == 0, 0.0, pltpu.roll(v, 1, 1))
    return up + down


def update(v, old, speed, beside):
    return 2.0 * v - old + speed * (beside + along_z(v) - 6.0 * v)


def two_terms(v):
    high = v.astype(BF16)
    return high, (v - high.astype(F32)).astype(BF16)


def grid_kernel(
    p, q, s, wyo, wye, fxo, fxe, target, out, keep, send, s0, s1, rhs, part1, part2, slots
):
    cx, cy = p.shape[0], p.shape[1]
    ahead, behind = SUB, SUB + cy
    fx_count = part1.shape[0] // 2 - 1
    cols = 4
    tall = part2.shape[0]
    high = part1.shape[1] - 2 * SUB
    wy_count = high // cols
    before_y, after_y = before_after("wy", wye, wyo)
    before_x, after_x = before_after("fx", fxe, fxo)
    corner = 3 * cy + 3 * (cols + 2)

    s0[1 : cx + 1, ahead:behind, :] = p[...]
    for x, side in ((0, before_x), (cx + 1, after_x)):
        s0[x, ahead:behind, :] = side[0:cy]
        s0[x, ahead - 1 : ahead, :] = side[corner : corner + 1]
        s0[x, behind : behind + 1, :] = side[corner + 1 : corner + 2]
    s0[1 : cx + 1, ahead - 1, :] = before_y[0:cx]
    s0[1 : cx + 1, behind, :] = after_y[0:cx]

    for side, y, inner in ((before_y, ahead - 1, ahead), (after_y, behind, behind - 1)):
        near, far = side[0:cx], side[cx : 2 * cx]
        old, speed = side[2 * cx : 3 * cx], side[3 * cx : 4 * cx]
        beside = s0[0:cx, y, :] + s0[2 : cx + 2, y, :] + far + s0[1 : cx + 1, inner, :]
        s1[1 : cx + 1, y, :] = update(near, old, speed, beside)
    for side, x, inner in ((before_x, 0, 1), (after_x, cx + 1, cx)):
        part, speed = side[cy : 2 * cy], side[2 * cy : 3 * cy]
        s1[x, ahead:behind, :] = part + speed * s0[inner, ahead:behind, :]

    def sweep(now, old, x):
        beside = now[x, ahead:behind, :] + now[x + 2, ahead:behind, :]
        beside = beside + now[x + 1, ahead - 1 : behind - 1, :]
        beside = beside + now[x + 1, ahead + 1 : behind + 1, :]
        return update(now[x + 1, ahead:behind, :], old, s[x], beside)

    for x in range(cx):
        fresh = sweep(s0, q[x], x)
        s1[x + 1, ahead:behind, :] = fresh
        a, b = two_terms(fresh)
        rhs[x * cy : (x + 1) * cy, 0:LANES] = a
        rhs[x * cy : (x + 1) * cy, LANES : 2 * LANES] = b
    for x in range(cx):
        fresh = sweep(s1, p[x], x)
        out[x] = fresh
        a, b = two_terms(fresh)
        rhs[x * cy : (x + 1) * cy, 2 * LANES : 3 * LANES] = a
        rhs[x * cy : (x + 1) * cy, 3 * LANES : 4 * LANES] = b

    part1[...] = jnp.zeros(part1.shape, F32)
    part2[:, 0:SUB, :] = jnp.zeros((tall, SUB, LANES), F32)
    chunk = 256
    for first in range(0, tall * high, chunk):
        tile = lax.broadcasted_iota(jnp.int32, (chunk, LANES), 0) + first
        picks = []
        for piece in range(target.shape[0]):
            picks.append(jnp.where(tile == target[piece : piece + 1, :], 1.0, 0.0).astype(BF16))
        sums = jnp.dot(jnp.concatenate(picks, axis=1), rhs[...], preferred_element_type=F32)
        one = sums[:, 0:LANES] + sums[:, LANES : 2 * LANES]
        two = sums[:, 2 * LANES : 3 * LANES] + sums[:, 3 * LANES : 4 * LANES]
        l = first // high
        part1[1 + l : 1 + l + chunk // high, SUB : SUB + high, :] = one.reshape(-1, high, LANES)
        part2[l : l + chunk // high, SUB : SUB + high, :] = two.reshape(-1, high, LANES)
    sub = lax.broadcasted_iota(jnp.int32, (SUB, LANES), 0)
    lane = lax.broadcasted_iota(jnp.int32, (SUB, LANES), 1)
    step1 = sub < cols + 2
    for a in range(fx_count):
        for b in range(wy_count):
            h = SUB + cols * b
            slot = a * wy_count + b
            one = [part1[2 * a + l, h - 1 : h - 1 + SUB, :] for l in range(4)]
            ends = jnp.where(lane % 8 < 4, one[3], one[0])
            two = [
                part2[2 * a + l, h + at - 6 : h + at - 6 + SUB, :]
                for l, at in ((0, 0), (0, 2), (1, 0))
            ]
            x = jnp.broadcast_to(part2[2 * a + 1, h + 2 : h + 3, :], (SUB, LANES))
            y = jnp.broadcast_to(part2[2 * a + 1, h + 3 : h + 4, :], (SUB, LANES))
            for r in range(4):
                moved = pltpu.roll(y, (3 - 2 * r) % LANES, 1)
                ends = jnp.where((sub == 1 + r) & free_ends(lane), moved, ends)
            low, high_free = (sub == 0) & (lane // 8 % 4 == 0), (sub == cols + 1) & (lane // 8 % 4 == 3)
            own0 = jnp.where(low | high_free, x, one[1])
            own1 = jnp.where(low, pltpu.roll(x, LANES - 8, 1), one[2])
            own1 = jnp.where(high_free, pltpu.roll(x, 8, 1), own1)
            for k, group in enumerate((ends, own0, own1)):
                slots[slot, k * SUB : (k + 1) * SUB, :] = jnp.where(step1, group, two[k])

    def halve(first, second):
        for to, at in ((first, 0), (second, 3)):
            for k in range(3):
                to[:, k] = slots[:, 4 * (at + k) : 4 * (at + k + 1), :]

    @pl.when(even_at("wy"))
    def _():
        halve(keep, send)

    @pl.when(jnp.logical_not(even_at("wy")))
    def _():
        halve(send, keep)


def free_ends(lane):
    return (lane % 8 == 3) | (lane % 8 == 4)


def unpack_slots(total, cols):
    ends, own0, own1 = [total[k * SUB : (k + 1) * SUB] for k in range(3)]
    lane = lax.broadcasted_iota(jnp.int32, (1, LANES), 1)
    two = [[ends[6:7], ends[7:8], own0[6:7], own0[7:8]], [own1[6:7], own1[7:8]]]
    q = lane // 8 % 4
    last = cols + 1
    x = jnp.where(q == 0, own0[0:1], own0[last : last + 1])
    x = jnp.where(q == 1, pltpu.roll(own1[0:1], 8, 1), x)
    x = jnp.where(q == 2, pltpu.roll(own1[last : last + 1], LANES - 8, 1), x)
    y = None
    for r in range(4):
        moved = pltpu.roll(ends[1 + r : 2 + r], (2 * r - 3) % LANES, 1)
        y = moved if y is None else jnp.where(lane % 8 // 2 == r, moved, y)
    two[1].extend([x, y])
    two = [jnp.concatenate(v, axis=0) for v in two]
    return (ends, own0, own1, ends), two


def grid_steps(p, q, s, wy_got, fx_got, target, fx_count, wy_count):
    cx, cy = p.shape[0], p.shape[1]
    tall, high = fx_count * 2, wy_count * 4
    devices = fx_count * wy_count
    half = (devices, 3, 4, LANES)
    return pl.pallas_call(
        grid_kernel,
        in_specs=[whole()] * 8,
        out_specs=[whole()] * 3,
        out_shape=[
            vmem(*p.shape),
            vmem(*half),
            vmem(*half),
        ],
        scratch_shapes=[
            pltpu.VMEM((cx + 2, cy + 2 * SUB, LANES), F32),
            pltpu.VMEM((cx + 2, cy + 2 * SUB, LANES), F32),
            pltpu.VMEM((cx * cy, 4 * LANES), BF16),
            pltpu.VMEM((tall + 2, high + 2 * SUB, LANES), F32),
            pltpu.VMEM((tall, high + 2 * SUB, LANES), F32),
            vmem(devices, 3 * SUB, LANES),
        ],
        compiler_params=params(),
        name="grid_steps",
    )(p, q, s, *wy_got, *fx_got, target)


def pair_sum_kernel(keep, got, after, out):
    out[...] = keep[...] + got[...]


def pair_sum(keep, got, after):
    return pl.pallas_call(
        pair_sum_kernel,
        in_specs=[whole()] * 3,
        out_specs=whole(),
        out_shape=jax.ShapeDtypeStruct(keep.shape, F32),
        compiler_params=params(),
        name="pair_sum",
    )(keep, got, after)


def reached(g):
    groups = []
    for dh in (-1, 0, 1):
        if (dh == -1 and g % 4 == 3) or (dh == 1 and g % 4 == 0):
            continue
        groups.append(dh)
    return groups


STORED = sum(len(reached(g)) for g in range(LANES // SUB))


def mid_rows(ref, c, l, h):
    rows = {}
    for dh in (-1, 0, 1):
        row = ref[c, l + 1, pl.ds(h + 1 + dh, 1), :]
        rows[dh] = jnp.broadcast_to(row, (SUB, LANES))
    return rows


def end_rows(ref, c, l, h, first_sub):
    rows = {}
    for dh in (-1, 0, 1):
        at = pl.ds(h + 1 + dh, 1)
        before = jnp.broadcast_to(ref[c, l, at, :], (SUB, LANES))
        after = jnp.broadcast_to(ref[c, l + 2, at, :], (SUB, LANES))
        rows[dh] = jnp.where(first_sub, before, after)
    return rows


def fill_y(pad, own, before, after, at):
    rows, cols = own.shape[1], own.shape[2]
    for c in range(3):
        for l in range(rows):
            row = at + c * rows + l
            pad[c, l + 1, 0:1, :] = before[row : row + 1]
            pad[c, l + 1, 1 : cols + 1, :] = own[c, l]
            pad[c, l + 1, cols + 1 : cols + 2, :] = after[row : row + 1]


def fill_x(pad, rows, cols, before, after, at):
    for c in range(3):
        row = at + c * (cols + 2)
        pad[c, 0, 0 : cols + 2, :] = before[row : row + cols + 2]
        pad[c, rows + 1, 0 : cols + 2, :] = after[row : row + cols + 2]


def fill_x_shared(jpad, dpad, rows, cols, before, after, at):
    for c in range(3):
        row = at + c * (cols + 2)
        for message, l, low in ((before, 0, False), (after, rows + 1, True)):
            both = message[row : row + cols + 2]
            jpad[c, l, 0 : cols + 2, :] = jnp.where(wall_lanes(both, low), both, 0.0)
            moved = pltpu.roll(both, LANES - 3 if low else 3, 1)
            dpad[c, l, 0 : cols + 2, :] = moved


def lattice_rows():
    index = lax.broadcasted_iota(jnp.int32, (1, LANES), 1)
    places = (index % 8, index // 8 % 4, index // 32)
    return [v.astype(F32) * (1.0 / REACH) for v in places]


SPAN = 8.0 / REACH
RISE = 4.0 / REACH


def own_columns(ref, lattice, rows, cols):
    places = []
    for l in range(rows):
        for h in range(cols):
            for c in range(3):
                places.append(ref[c, l + 1, h + 1 : h + 2, :] * (1.0 / REACH) + lattice[c])
    spare = -len(places) % SUB
    if spare:
        places.append(jnp.zeros((spare, LANES), F32))
    return jnp.transpose(jnp.concatenate(places, axis=0))


def bond_row(weight, others, mine):
    for c in range(3):
        diff = others[c] - mine[c]
        weight = weight - diff * diff
    return jnp.maximum(weight, 0.0)


def tile_pass(l, h, cols, columns, others, pulls, weight_of, weights, acc):
    place = 0
    first = 3 * (l * cols + h)
    for g in range(LANES // SUB):
        span = slice(g * SUB, (g + 1) * SUB)
        mine = [jnp.broadcast_to(columns[span, first + c : first + c + 1], (SUB, LANES)) for c in range(3)]
        sums = [None] * 4
        for order, dh in enumerate(reached(g)):
            here = [others[c][dh] for c in range(3)]
            weight = weight_of(g, order, dh, here, mine)
            weights[l, h, place] = weight
            place += 1
            terms = [weight * pulls[c][dh] for c in range(3)] + [weight]
            sums = [t if v is None else v + t for v, t in zip(sums, terms)]
        for c in range(4):
            acc[l, h, c, span, :] = sums[c]


def tile_sums(acc, l, h, count):
    ones = jnp.ones((2 * SUB, 2 * LANES), BF16)
    terms = [jnp.concatenate(two_terms(acc[l, h, c]), axis=1) for c in range(count)]
    sums = lax.dot_general(
        ones,
        jnp.concatenate(terms, axis=0),
        (((1,), (1,)), ((), ())),
        preferred_element_type=F32,
    )[0:1]
    return [sums[:, c * LANES : (c + 1) * LANES] for c in range(count)]


def by_quantity(tiles):
    return [jnp.concatenate(rows, axis=0) for rows in zip(*tiles)]


def quotient(v, n):
    return ((v.astype(F32) + 0.5) * (1.0 / n)).astype(jnp.int32)


def center_kernel(
    cx, wy_count, masks_in, device_in, tile_in, wall, wyo, wye,
    weights, part, bits, target, columns, jpad, dpad, acc, masks, route, sems,
):
    rows, cols = wall.shape[2], wall.shape[3]
    copies = {}
    for k, pair in enumerate(((device_in, route.at[0]), (tile_in, route.at[1]))):
        copies[k] = pltpu.make_async_copy(*pair, sems.at[k])
    for k, first in enumerate((3, 0, 6)):
        span = slice(first, first + 3)
        copies["masks", first] = pltpu.make_async_copy(
            masks_in.at[:, :, span], masks.at[:, :, span], sems.at[2 + k]
        )
    order = [0, 1, ("masks", 3), ("masks", 0), ("masks", 6)]
    for k in order:
        copies[k].start()
    first_sub = lax.broadcasted_iota(jnp.int32, (SUB, LANES), 0) < SUB // 2
    copies[0].wait()
    copies[1].wait()
    device, tile = route[0], route[1]
    a, t = quotient(device, wy_count), quotient(tile, cols)
    b, u = device - a * wy_count, tile - t * cols
    target[...] = (a * rows + t) * (wy_count * cols) + b * cols + u
    before, after = before_after("wy", wye, wyo)
    fill_y(jpad, wall.at[0], before, after, 4 * cx)
    fill_y(dpad, wall.at[1], before, after, 4 * cx + 3 * rows)
    lattice = lattice_rows()
    columns[...] = own_columns(jpad, lattice, rows, cols)

    def one_tile(l, h):
        others = []
        for c in range(3):
            mid = mid_rows(jpad, c, l, h)
            for dh in (-1, 0, 1):
                mid[dh] = mid[dh] * (1.0 / REACH) + lattice[c]
                if c == 1:
                    mid[dh] = mid[dh] + RISE * dh
            others.append(mid)
        pulls = [mid_rows(dpad, c, l, h) for c in range(3)]

        def weight_of(g, order, dh, here, mine):
            span = slice(g * SUB, (g + 1) * SUB)
            return bond_row(masks[l, h, 4 + dh, span, :].astype(F32), here, mine)

        tile_pass(l, h, cols, columns, others, pulls, weight_of, weights, acc)

    def put_sums(l, h):
        for c, sums in enumerate(tile_sums(acc, l, h, 4)):
            part[l, c, h : h + 1, :] = sums

    def put_bits(l, h):
        words = [jnp.zeros((SUB, LANES), jnp.int32) for _ in range(2)]
        for g in range(LANES // SUB):
            span = slice(g * SUB, (g + 1) * SUB)
            for order, dh in enumerate(reached(g)):
                before = masks[l, h, 1 + dh, span, :]
                after = masks[l, h, 7 + dh, span, :]
                place = 3 * (g % 8) + order
                words[g // 8] = words[g // 8] + jnp.where(first_sub, before, after) * (1 << place)
        for k in range(2):
            bits[l, h, k] = words[k]

    tiles = [(l, h) for l in range(rows) for h in range(cols)]
    copies["masks", 3].wait()
    for l, h in tiles:
        one_tile(l, h)
        put_sums(l, h)
    copies["masks", 0].wait()
    copies["masks", 6].wait()
    for l, h in tiles:
        put_bits(l, h)


def wall_center(cx, wy_count, masks, device, tile, wall, wy_got):
    rows, cols = wall.shape[2], wall.shape[3]
    return pl.pallas_call(
        functools.partial(center_kernel, cx, wy_count),
        in_specs=[HBM] * 3 + [whole()] * 3,
        out_specs=[whole()] * 5,
        out_shape=[
            jax.ShapeDtypeStruct((rows, cols, STORED, SUB, LANES), F32),
            vmem(rows, 4, cols, LANES),
            pltpu.VMEM((rows, cols, 2, SUB, LANES), jnp.int32),
            pltpu.VMEM(device.shape, jnp.int32),
            vmem(LANES, pad8(3 * rows * cols)),
        ],
        scratch_shapes=[
            vmem(3, rows + 2, SUB, LANES),
            vmem(3, rows + 2, SUB, LANES),
            vmem(rows, cols, 4, LANES, LANES),
            pltpu.VMEM(masks.shape, jnp.int32),
            pltpu.VMEM((2,) + device.shape, jnp.int32),
            pltpu.SemaphoreType.DMA((5,)),
        ],
        compiler_params=params(),
        name="wall_center",
    )(*in_hbm(masks, device, tile), wall, *wy_got)


def wall_kernel(
    cx, cy, wall, wyo, wye, fxo, fxe, part, bits, columns, pressure,
    weights, vel1, base1, totals, to_odd, to_even, pressure_out, jpad, dpad, acc, sem,
):
    rows, cols = wall.shape[2], wall.shape[3]
    copy = pltpu.make_async_copy(pressure, pressure_out, sem)
    copy.start()
    first_sub = lax.broadcasted_iota(jnp.int32, (SUB, LANES), 0) < SUB // 2
    before, after = before_after("wy", wye, wyo)
    fill_y(jpad, wall.at[0], before, after, 4 * cx)
    fill_y(dpad, wall.at[1], before, after, 4 * cx + 3 * rows)
    before, after = before_after("fx", fxe, fxo)
    fill_x_shared(jpad, dpad, rows, cols, before, after, 3 * cy)
    lattice = lattice_rows()

    def one_tile(l, h):
        others = []
        for c in range(3):
            ends = end_rows(jpad, c, l, h, first_sub)
            for dh in (-1, 0, 1):
                ends[dh] = ends[dh] * (1.0 / REACH) + lattice[c]
                if c == 0:
                    ends[dh] = ends[dh] + jnp.where(first_sub, -SPAN, SPAN)
                if c == 1:
                    ends[dh] = ends[dh] + RISE * dh
            others.append(ends)
        pulls = [end_rows(dpad, c, l, h, first_sub) for c in range(3)]

        def weight_of(g, order, dh, here, mine):
            bonded = (bits[l, h, g // 8] & (1 << (3 * (g % 8) + order))) != 0
            return jnp.where(bonded, bond_row(1.0, here, mine), 0.0)

        tile_pass(l, h, cols, columns, others, pulls, weight_of, weights, acc)

    for l in range(rows):
        sums = []
        for h in range(cols):
            one_tile(l, h)
            sums.append(tile_sums(acc, l, h, 4))
        pulled = [v + part[l, c] for c, v in enumerate(by_quantity(sums))]
        totals[l] = pulled[3]
        for c in range(3):
            mine = wall[1, c, l]
            fresh = wall[2, c, l] + STIFFNESS * (pulled[c] - pulled[3] * mine)
            vel1[c, l] = fresh
            base1[c, l] = mine + fresh

    def edge(at):
        def write(out):
            for c in range(3):
                for k in range(rows):
                    out[c * rows + k : c * rows + k + 1, :] = base1[c, k, at : at + 1, :]
            for spare in range(3 * rows, out.shape[0]):
                out[spare : spare + 1, :] = jnp.zeros((1, LANES), F32)

        return write

    place_edges(even_at("wy"), edge(0), edge(cols - 1), to_even, to_odd)
    copy.wait()


def wall_first(wall, wy_got, fx_got, part, bits, columns, pressure):
    cx, cy = pressure.shape[0], pressure.shape[1]
    rows, cols = wall.shape[2], wall.shape[3]
    edge = (pad8(3 * rows), LANES)
    field = vmem(*wall.shape[1:])
    return pl.pallas_call(
        functools.partial(wall_kernel, cx, cy),
        in_specs=[whole()] * 9,
        out_specs=[whole()] * 6 + [HBM],
        out_shape=[
            jax.ShapeDtypeStruct((rows, cols, STORED, SUB, LANES), F32),
            field,
            field,
            vmem(rows, cols, LANES),
            vmem(*edge),
            vmem(*edge),
            jax.ShapeDtypeStruct(pressure.shape, F32),
        ],
        scratch_shapes=[
            pltpu.VMEM((3, rows + 2, SUB, LANES), F32),
            pltpu.VMEM((3, rows + 2, SUB, LANES), F32),
            pltpu.VMEM((rows, cols, 4, LANES, LANES), F32),
            pltpu.SemaphoreType.DMA(()),
        ],
        compiler_params=params(),
        name="wall_first",
    )(wall, *wy_got, *fx_got, part, bits, columns, pressure)


def pack_base_kernel(base1, got_odd, got_even, to_odd, to_even):
    rows, cols = base1.shape[1], base1.shape[2]
    before, after = before_after("wy", got_even, got_odd)

    def edge(l):
        def write(out):
            at = 0
            for c in range(3):
                side = c * rows + l
                out[at : at + 1, :] = before[side : side + 1]
                out[at + 1 : at + 1 + cols, :] = base1[c, l]
                out[at + 1 + cols : at + 2 + cols, :] = after[side : side + 1]
                at += cols + 2
            for spare in range(at, out.shape[0]):
                out[spare : spare + 1, :] = jnp.zeros((1, LANES), F32)

        return write

    place_edges(even_at("fx"), edge(0), edge(rows - 1), to_even, to_odd)


def pack_base(base1, got):
    cols = base1.shape[2]
    out = vmem(pad8(3 * (cols + 2)), LANES)
    return pl.pallas_call(
        pack_base_kernel,
        in_specs=[whole()] * 3,
        out_specs=[whole()] * 2,
        out_shape=[out, out],
        compiler_params=params(),
        name="pack_base",
    )(base1, *got)


def last_kernel(
    weights, end_weights, got, base1, vel1, totals, wyo, wye, fxo, fxe, disp_out, vel_out,
    dpad, acc,
):
    rows, cols = base1.shape[1], base1.shape[2]
    first_sub = lax.broadcasted_iota(jnp.int32, (SUB, LANES), 0) < SUB // 2
    before, after = before_after("wy", wye, wyo)
    fill_y(dpad, base1, before, after, 0)
    before, after = before_after("fx", fxe, fxo)
    fill_x(dpad, rows, cols, before, after, 0)
    pieces = []
    for half in range(2):
        for k in range(3):
            total = got[half, k]
            for d in range(half + 2, got.shape[0], 2):
                total = total + got[d, k]
            pieces.append(total)
    total = jnp.concatenate(pieces, axis=0)
    one, two = unpack_slots(total, cols)
    for k in range(rows + 2):
        here = dpad[0, k, 0 : cols + 2, :] + LOADING * one[k][0 : cols + 2]
        dpad[0, k, 0 : cols + 2, :] = here

    def one_tile(l, h):
        mids = [mid_rows(dpad, c, l, h) for c in range(3)]
        ends = [end_rows(dpad, c, l, h, first_sub) for c in range(3)]
        place = 0
        for g in range(LANES // SUB):
            sums = [None] * 3
            for dh in reached(g):
                for weight, pulls in (
                    (weights[l, h, place], mids), (end_weights[l, h, place], ends)
                ):
                    terms = [weight * pulls[c][dh] for c in range(3)]
                    sums = [t if v is None else v + t for v, t in zip(sums, terms)]
                place += 1
            for c in range(3):
                acc[l, h, c, g * SUB : (g + 1) * SUB, :] = sums[c]

    for l in range(rows):
        sums = []
        for h in range(cols):
            one_tile(l, h)
            sums.append(tile_sums(acc, l, h, 3))
        pulled = by_quantity(sums)
        for c in range(3):
            mine = dpad[c, l + 1, 1 : cols + 1, :]
            force = STIFFNESS * (pulled[c] - totals[l] * mine)
            if c == 0:
                force = force + LOADING * (one[l + 1][1 : cols + 1] + two[l])
            fresh = vel1[c, l] + force
            vel_out[c, l] = fresh
            disp_out[c, l] = mine + fresh


def wall_last(weights, end_weights, got, base1, vel1, totals, wy_got, fx_got):
    rows, cols = base1.shape[1], base1.shape[2]
    return pl.pallas_call(
        last_kernel,
        in_specs=[whole()] * 10,
        out_specs=[whole()] * 2,
        out_shape=[jax.ShapeDtypeStruct(base1.shape, F32)] * 2,
        scratch_shapes=[
            pltpu.VMEM((3, rows + 2, SUB, LANES), F32),
            pltpu.VMEM((rows, cols, 3, LANES, LANES), F32),
        ],
        compiler_params=params(),
        name="wall_last",
    )(weights, end_weights, got, base1, vel1, totals, *wy_got, *fx_got)


def per_device(
    displacement,
    velocity,
    jitter,
    bond_masks,
    pressure,
    pressure_prev,
    speed_sq,
    route_device,
    route_tile,
):
    fx_count, wy_count = lax.axis_size("fx"), lax.axis_size("wy")
    cols = displacement.shape[2]
    device = route_device.reshape(-1, LANES)
    tile = route_tile.reshape(-1, LANES)
    cx = pressure.shape[0]
    *sends, p, q, s, wall = pack_wy(
        pressure, pressure_prev, speed_sq, jitter, displacement, velocity
    )
    grids = (p, q, s)
    wy_got = exchange("wy", *sends)
    sends = pack_fx(grids, wall, wy_got)
    fx_got = exchange("fx", *sends)
    weights, part, bits, target, columns = wall_center(
        cx, wy_count, bond_masks, device, tile, wall, wy_got
    )
    fresh, keep, send = grid_steps(*grids, wy_got, fx_got, target, fx_count, wy_count)
    names = ("fx", "wy")
    other = lax.ppermute(send, names, swap_pairs(1, (fx_count, wy_count), 0))
    end_weights, vel1, base1, totals, *sends, pressure_out = wall_first(
        wall, wy_got, fx_got, part, bits, columns, fresh
    )
    slots = pair_sum(keep, other, totals)
    got = lax.all_to_all(slots, names, split_axis=0, concat_axis=0, tiled=True)
    base_wy = exchange("wy", *sends)
    sends = pack_base(base1, base_wy)
    base_fx = exchange("fx", *sends)
    disp_out, vel_out = wall_last(
        weights, end_weights, got, base1, vel1, totals, base_wy, base_fx
    )
    return (disp_out, vel_out, pressure_out)


def solution(mesh):
    placed = (
        P(None, "fx", "wy", None),
        P(None, "fx", "wy", None),
        P(None, "fx", "wy", None),
        P("fx", "wy", None, None, None),
        P("fx", "wy", None),
        P("fx", "wy", None),
        P("fx", "wy", None),
        P(("fx", "wy"), None),
        P(("fx", "wy")),
    )
    return jax.shard_map(
        per_device,
        mesh=mesh,
        in_specs=placed,
        out_specs=(P(None, "fx", "wy", None), P(None, "fx", "wy", None), P("fx", "wy", None)),
        check_vma=False,
    )
```

```python
import functools

import jax
import jax.numpy as jnp
from jax import lax
from jax.experimental import pallas as pl
from jax.experimental.pallas import tpu as pltpu
from jax.sharding import PartitionSpec as P

STIFFNESS = 0.02
LOADING = 0.05
REACH = 3.0
LANES = 128
SUB = 8
VMEM_BYTES = 32 * 1024 * 1024
HBM = pl.BlockSpec(memory_space=pltpu.HBM)

F32 = jnp.float32
BF16 = jnp.bfloat16


def whole():
    return pl.BlockSpec(memory_space=pltpu.VMEM)


def params():
    return pltpu.CompilerParams(vmem_limit_bytes=VMEM_BYTES)


def vmem(*shape):
    return pltpu.VMEM(shape, F32)


def even_at(axis):
    return lax.rem(lax.axis_index(axis), 2) == 0


def swap_pairs(axis, sizes, first):
    count, others = sizes[axis], sizes[1 - axis]
    pairs = []

    def join(*two):
        a, b = [place * sizes[1] + other for place, other in two]
        pairs.extend([(a, b), (b, a)])

    def at(place, other):
        return (place, other) if axis == 0 else (other, place)

    met = set()
    for low in range(first, count - 1, 2):
        met.update((low, low + 1))
        for other in range(others):
            join(at(low, other), at(low + 1, other))
    for place in range(count):
        if place not in met and others % 2 == 0:
            for other in range(0, others, 2):
                join(at(place, other), at(place, other + 1))
    return pairs


def exchange(axis, to_odd, to_even):
    names = ("fx", "wy")
    sizes = [lax.axis_size(name) for name in names]
    along = names.index(axis)
    got_odd = lax.ppermute(to_odd, names, swap_pairs(along, sizes, 1))
    got_even = lax.ppermute(to_even, names, swap_pairs(along, sizes, 0))
    return got_odd, got_even


def place_edges(even, low, high, to_even, to_odd):
    @pl.when(even)
    def _():
        high(to_even)
        low(to_odd)

    @pl.when(jnp.logical_not(even))
    def _():
        low(to_even)
        high(to_odd)


def before_after(axis, got_even, got_odd):
    even = even_at(axis)
    place, last = lax.axis_index(axis), lax.axis_size(axis) - 1
    a, b = got_even[...], got_odd[...]
    before = jnp.where(place == 0, 0.0, jnp.where(even, b, a))
    after = jnp.where(place == last, 0.0, jnp.where(even, a, b))
    return before, after


def pack_wy_kernel(
    p_in, q_in, s_in, jit_in, disp_in, vel_in, wy_odd, wy_even, p, q, s, wall, sems
):
    cx, cy = p.shape[0], p.shape[1]
    rows, cols = jit_in.shape[1], jit_in.shape[2]
    pairs = [(p_in, p), (q_in, q), (s_in, s)]
    for k, field in enumerate((jit_in, disp_in, vel_in)):
        pairs.append((field, wall.at[k]))
    copies = [pltpu.make_async_copy(a, b, sems.at[k]) for k, (a, b) in enumerate(pairs)]
    for copy in copies:
        copy.start()
    for copy in copies:
        copy.wait()

    def edge(near, far, h):
        def write(out):
            out[0:cx, :] = p[:, near, :]
            out[cx : 2 * cx, :] = p[:, far, :]
            out[2 * cx : 3 * cx, :] = q[:, near, :]
            out[3 * cx : 4 * cx, :] = s[:, near, :]
            at = 4 * cx
            for field in range(2):
                for c in range(3):
                    for l in range(rows):
                        out[at : at + 1, :] = wall[field, c, l, h : h + 1, :]
                        at += 1
            for spare in range(at, out.shape[0]):
                out[spare : spare + 1, :] = jnp.zeros((1, LANES), F32)

        return write

    place_edges(
        even_at("wy"),
        edge(0, 1, 0),
        edge(cy - 1, cy - 2, cols - 1),
        wy_even,
        wy_odd,
    )


def in_hbm(*arrays):
    return [pltpu.with_memory_space_constraint(v, pltpu.HBM) for v in arrays]


def pad8(count):
    return (count + 7) // 8 * 8


def pack_wy(p, q, s, jit, disp, vel):
    message = vmem(pad8(4 * p.shape[0] + 6 * jit.shape[1]), LANES)
    return pl.pallas_call(
        pack_wy_kernel,
        in_specs=[HBM] * 6,
        out_specs=[whole()] * 6,
        out_shape=[message, message] + [vmem(*p.shape)] * 3 + [vmem(3, *jit.shape)],
        scratch_shapes=[pltpu.SemaphoreType.DMA((6,))],
        compiler_params=params(),
        name="pack_wy",
    )(*in_hbm(p, q, s, jit, disp, vel))


def wall_lanes(field, low):
    lane = lax.broadcasted_iota(jnp.int32, field.shape, 1) % 8
    return lane < 3 if low else lane > 4


def pack_fx_kernel(p, q, s, wall, got_odd, got_even, to_odd, to_even, line):
    cx, cy = p.shape[0], p.shape[1]
    rows, cols = wall.shape[2], wall.shape[3]
    before, after = before_after("wy", got_even, got_odd)

    def edge(low, x, far, l):
        def write(out):
            line[SUB - 1 : SUB, :] = before[x : x + 1]
            line[SUB : SUB + cy, :] = p[x]
            line[SUB + cy : SUB + cy + 1, :] = after[x : x + 1]
            mine, speed = p[x], s[x]
            beside = p[far] + line[SUB - 1 : SUB - 1 + cy, :] + line[SUB + 1 : SUB + 1 + cy, :]
            out[0:cy, :] = mine
            out[cy : 2 * cy, :] = update(mine, q[x], speed, beside)
            out[2 * cy : 3 * cy, :] = speed
            at = 3 * cy
            for c in range(3):
                pair = []
                for field in range(2):
                    row = 4 * cx + (field * 3 + c) * rows + l
                    parts = (before[row : row + 1], wall[field, c, l], after[row : row + 1])
                    pair.append(jnp.concatenate(parts, axis=0))
                moved = pltpu.roll(pair[1], 3 if low else LANES - 3, 1)
                out[at : at + cols + 2, :] = jnp.where(wall_lanes(moved, low), pair[0], moved)
                at += cols + 2
            out[at : at + 1, :] = before[x : x + 1]
            out[at + 1 : at + 2, :] = after[x : x + 1]
            for spare in range(at + 2, out.shape[0]):
                out[spare : spare + 1, :] = jnp.zeros((1, LANES), F32)

        return write

    place_edges(
        even_at("fx"), edge(True, 0, 1, 0), edge(False, cx - 1, cx - 2, rows - 1), to_even, to_odd
    )


def pack_fx(grids, wall, got):
    cy, cols = grids[0].shape[1], wall.shape[3]
    out = vmem(pad8(3 * cy + 3 * (cols + 2) + 2), LANES)
    return pl.pallas_call(
        pack_fx_kernel,
        in_specs=[whole()] * 6,
        out_specs=[whole()] * 2,
        out_shape=[out, out],
        scratch_shapes=[vmem(cy + 2 * SUB, LANES)],
        compiler_params=params(),
        name="pack_fx",
    )(*grids, wall, *got)


def along_z(v):
    lane = lax.broadcasted_iota(jnp.int32, v.shape, 1)
    up = jnp.where(lane == LANES - 1, 0.0, pltpu.roll(v, LANES - 1, 1))
    down = jnp.where(lane == 0, 0.0, pltpu.roll(v, 1, 1))
    return up + down


def update(v, old, speed, beside):
    return 2.0 * v - old + speed * (beside + along_z(v) - 6.0 * v)


def two_terms(v):
    high = v.astype(BF16)
    return high, (v - high.astype(F32)).astype(BF16)


def grid_kernel(
    p, q, s, wyo, wye, fxo, fxe, target, out, keep, send, s0, s1, rhs, part1, part2, slots
):
    cx, cy = p.shape[0], p.shape[1]
    ahead, behind = SUB, SUB + cy
    fx_count = part1.shape[0] // 2 - 1
    cols = 4
    tall = part2.shape[0]
    high = part1.shape[1] - 2 * SUB
    wy_count = high // cols
    before_y, after_y = before_after("wy", wye, wyo)
    before_x, after_x = before_after("fx", fxe, fxo)
    corner = 3 * cy + 3 * (cols + 2)

    s0[1 : cx + 1, ahead:behind, :] = p[...]
    for x, side in ((0, before_x), (cx + 1, after_x)):
        s0[x, ahead:behind, :] = side[0:cy]
        s0[x, ahead - 1 : ahead, :] = side[corner : corner + 1]
        s0[x, behind : behind + 1, :] = side[corner + 1 : corner + 2]
    s0[1 : cx + 1, ahead - 1, :] = before_y[0:cx]
    s0[1 : cx + 1, behind, :] = after_y[0:cx]

    for side, y, inner in ((before_y, ahead - 1, ahead), (after_y, behind, behind - 1)):
        near, far = side[0:cx], side[cx : 2 * cx]
        old, speed = side[2 * cx : 3 * cx], side[3 * cx : 4 * cx]
        beside = s0[0:cx, y, :] + s0[2 : cx + 2, y, :] + far + s0[1 : cx + 1, inner, :]
        s1[1 : cx + 1, y, :] = update(near, old, speed, beside)
    for side, x, inner in ((before_x, 0, 1), (after_x, cx + 1, cx)):
        part, speed = side[cy : 2 * cy], side[2 * cy : 3 * cy]
        s1[x, ahead:behind, :] = part + speed * s0[inner, ahead:behind, :]

    def sweep(now, old, x):
        beside = now[x, ahead:behind, :] + now[x + 2, ahead:behind, :]
        beside = beside + now[x + 1, ahead - 1 : behind - 1, :]
        beside = beside + now[x + 1, ahead + 1 : behind + 1, :]
        return update(now[x + 1, ahead:behind, :], old, s[x], beside)

    for x in range(cx):
        fresh = sweep(s0, q[x], x)
        s1[x + 1, ahead:behind, :] = fresh
        a, b = two_terms(fresh)
        rhs[x * cy : (x + 1) * cy, 0:LANES] = a
        rhs[x * cy : (x + 1) * cy, LANES : 2 * LANES] = b
    for x in range(cx):
        fresh = sweep(s1, p[x], x)
        out[x] = fresh
        a, b = two_terms(fresh)
        rhs[x * cy : (x + 1) * cy, 2 * LANES : 3 * LANES] = a
        rhs[x * cy : (x + 1) * cy, 3 * LANES : 4 * LANES] = b

    part1[...] = jnp.zeros(part1.shape, F32)
    part2[:, 0:SUB, :] = jnp.zeros((tall, SUB, LANES), F32)
    chunk = 256
    for first in range(0, tall * high, chunk):
        tile = lax.broadcasted_iota(jnp.int32, (chunk, LANES), 0) + first
        picks = []
        for piece in range(target.shape[0]):
            picks.append(jnp.where(tile == target[piece : piece + 1, :], 1.0, 0.0).astype(BF16))
        sums = jnp.dot(jnp.concatenate(picks, axis=1), rhs[...], preferred_element_type=F32)
        one = sums[:, 0:LANES] + sums[:, LANES : 2 * LANES]
        two = sums[:, 2 * LANES : 3 * LANES] + sums[:, 3 * LANES : 4 * LANES]
        l = first // high
        part1[1 + l : 1 + l + chunk // high, SUB : SUB + high, :] = one.reshape(-1, high, LANES)
        part2[l : l + chunk // high, SUB : SUB + high, :] = two.reshape(-1, high, LANES)
    sub = lax.broadcasted_iota(jnp.int32, (SUB, LANES), 0)
    lane = lax.broadcasted_iota(jnp.int32, (SUB, LANES), 1)
    step1 = sub < cols + 2
    for a in range(fx_count):
        for b in range(wy_count):
            h = SUB + cols * b
            slot = a * wy_count + b
            one = [part1[2 * a + l, h - 1 : h - 1 + SUB, :] for l in range(4)]
            ends = jnp.where(lane % 8 < 4, one[3], one[0])
            two = [
                part2[2 * a + l, h + at - 6 : h + at - 6 + SUB, :]
                for l, at in ((0, 0), (0, 2), (1, 0))
            ]
            x = jnp.broadcast_to(part2[2 * a + 1, h + 2 : h + 3, :], (SUB, LANES))
            y = jnp.broadcast_to(part2[2 * a + 1, h + 3 : h + 4, :], (SUB, LANES))
            for r in range(4):
                moved = pltpu.roll(y, (3 - 2 * r) % LANES, 1)
                ends = jnp.where((sub == 1 + r) & free_ends(lane), moved, ends)
            low, high_free = (sub == 0) & (lane // 8 % 4 == 0), (sub == cols + 1) & (lane // 8 % 4 == 3)
            own0 = jnp.where(low | high_free, x, one[1])
            own1 = jnp.where(low, pltpu.roll(x, LANES - 8, 1), one[2])
            own1 = jnp.where(high_free, pltpu.roll(x, 8, 1), own1)
            for k, group in enumerate((ends, own0, own1)):
                slots[slot, k * SUB : (k + 1) * SUB, :] = jnp.where(step1, group, two[k])

    def halve(first, second):
        for to, at in ((first, 0), (second, 3)):
            for k in range(3):
                to[:, k] = slots[:, 4 * (at + k) : 4 * (at + k + 1), :]

    @pl.when(even_at("wy"))
    def _():
        halve(keep, send)

    @pl.when(jnp.logical_not(even_at("wy")))
    def _():
        halve(send, keep)


def free_ends(lane):
    return (lane % 8 == 3) | (lane % 8 == 4)


def unpack_slots(total, cols):
    ends, own0, own1 = [total[k * SUB : (k + 1) * SUB] for k in range(3)]
    lane = lax.broadcasted_iota(jnp.int32, (1, LANES), 1)
    two = [[ends[6:7], ends[7:8], own0[6:7], own0[7:8]], [own1[6:7], own1[7:8]]]
    q = lane // 8 % 4
    last = cols + 1
    x = jnp.where(q == 0, own0[0:1], own0[last : last + 1])
    x = jnp.where(q == 1, pltpu.roll(own1[0:1], 8, 1), x)
    x = jnp.where(q == 2, pltpu.roll(own1[last : last + 1], LANES - 8, 1), x)
    y = None
    for r in range(4):
        moved = pltpu.roll(ends[1 + r : 2 + r], (2 * r - 3) % LANES, 1)
        y = moved if y is None else jnp.where(lane % 8 // 2 == r, moved, y)
    two[1].extend([x, y])
    two = [jnp.concatenate(v, axis=0) for v in two]
    return (ends, own0, own1, ends), two


def grid_steps(p, q, s, wy_got, fx_got, target, fx_count, wy_count):
    cx, cy = p.shape[0], p.shape[1]
    tall, high = fx_count * 2, wy_count * 4
    devices = fx_count * wy_count
    half = (devices, 3, 4, LANES)
    return pl.pallas_call(
        grid_kernel,
        in_specs=[whole()] * 8,
        out_specs=[whole()] * 3,
        out_shape=[
            vmem(*p.shape),
            vmem(*half),
            vmem(*half),
        ],
        scratch_shapes=[
            pltpu.VMEM((cx + 2, cy + 2 * SUB, LANES), F32),
            pltpu.VMEM((cx + 2, cy + 2 * SUB, LANES), F32),
            pltpu.VMEM((cx * cy, 4 * LANES), BF16),
            pltpu.VMEM((tall + 2, high + 2 * SUB, LANES), F32),
            pltpu.VMEM((tall, high + 2 * SUB, LANES), F32),
            vmem(devices, 3 * SUB, LANES),
        ],
        compiler_params=params(),
        name="grid_steps",
    )(p, q, s, *wy_got, *fx_got, target)


def pair_sum_kernel(keep, got, after, out):
    out[...] = keep[...] + got[...]


def pair_sum(keep, got, after):
    return pl.pallas_call(
        pair_sum_kernel,
        in_specs=[whole()] * 3,
        out_specs=whole(),
        out_shape=jax.ShapeDtypeStruct(keep.shape, F32),
        compiler_params=params(),
        name="pair_sum",
    )(keep, got, after)


def reached(g):
    groups = []
    for dh in (-1, 0, 1):
        if (dh == -1 and g % 4 == 3) or (dh == 1 and g % 4 == 0):
            continue
        groups.append(dh)
    return groups


STORED = sum(len(reached(g)) for g in range(LANES // SUB))


def mid_rows(ref, c, l, h):
    rows = {}
    for dh in (-1, 0, 1):
        row = ref[c, l + 1, pl.ds(h + 1 + dh, 1), :]
        rows[dh] = jnp.broadcast_to(row, (SUB, LANES))
    return rows


def end_rows(ref, c, l, h, first_sub):
    rows = {}
    for dh in (-1, 0, 1):
        at = pl.ds(h + 1 + dh, 1)
        before = jnp.broadcast_to(ref[c, l, at, :], (SUB, LANES))
        after = jnp.broadcast_to(ref[c, l + 2, at, :], (SUB, LANES))
        rows[dh] = jnp.where(first_sub, before, after)
    return rows


def fill_y(pad, own, before, after, at):
    rows, cols = own.shape[1], own.shape[2]
    for c in range(3):
        for l in range(rows):
            row = at + c * rows + l
            pad[c, l + 1, 0:1, :] = before[row : row + 1]
            pad[c, l + 1, 1 : cols + 1, :] = own[c, l]
            pad[c, l + 1, cols + 1 : cols + 2, :] = after[row : row + 1]


def fill_x(pad, rows, cols, before, after, at):
    for c in range(3):
        row = at + c * (cols + 2)
        pad[c, 0, 0 : cols + 2, :] = before[row : row + cols + 2]
        pad[c, rows + 1, 0 : cols + 2, :] = after[row : row + cols + 2]


def fill_x_shared(jpad, dpad, rows, cols, before, after, at):
    for c in range(3):
        row = at + c * (cols + 2)
        for message, l, low in ((before, 0, False), (after, rows + 1, True)):
            both = message[row : row + cols + 2]
            jpad[c, l, 0 : cols + 2, :] = jnp.where(wall_lanes(both, low), both, 0.0)
            moved = pltpu.roll(both, LANES - 3 if low else 3, 1)
            dpad[c, l, 0 : cols + 2, :] = moved


def lattice_rows():
    index = lax.broadcasted_iota(jnp.int32, (1, LANES), 1)
    places = (index % 8, index // 8 % 4, index // 32)
    return [v.astype(F32) * (1.0 / REACH) for v in places]


SPAN = 8.0 / REACH
RISE = 4.0 / REACH


def own_columns(ref, lattice, rows, cols):
    places = []
    for l in range(rows):
        for h in range(cols):
            for c in range(3):
                places.append(ref[c, l + 1, h + 1 : h + 2, :] * (1.0 / REACH) + lattice[c])
    spare = -len(places) % SUB
    if spare:
        places.append(jnp.zeros((spare, LANES), F32))
    return jnp.transpose(jnp.concatenate(places, axis=0))


def bond_row(weight, others, mine):
    for c in range(3):
        diff = others[c] - mine[c]
        weight = weight - diff * diff
    return jnp.maximum(weight, 0.0)


def tile_pass(l, h, cols, columns, others, pulls, mask_at, weights, acc):
    place = 0
    first = 3 * (l * cols + h)
    for g in range(LANES // SUB):
        span = slice(g * SUB, (g + 1) * SUB)
        mine = [jnp.broadcast_to(columns[span, first + c : first + c + 1], (SUB, LANES)) for c in range(3)]
        sums = [None] * 4
        for dh in reached(g):
            here = [others[c][dh] for c in range(3)]
            weight = bond_row(mask_at(dh, span, place), here, mine)
            weights[l, h, place] = weight
            place += 1
            terms = [weight * pulls[c][dh] for c in range(3)] + [weight]
            sums = [t if v is None else v + t for v, t in zip(sums, terms)]
        for c in range(4):
            acc[l, h, c, span, :] = sums[c]


def tile_sums(acc, l, h, count):
    ones = jnp.ones((2 * SUB, 2 * LANES), BF16)
    terms = [jnp.concatenate(two_terms(acc[l, h, c]), axis=1) for c in range(count)]
    sums = lax.dot_general(
        ones,
        jnp.concatenate(terms, axis=0),
        (((1,), (1,)), ((), ())),
        preferred_element_type=F32,
    )[0:1]
    return [sums[:, c * LANES : (c + 1) * LANES] for c in range(count)]


def by_quantity(tiles):
    return [jnp.concatenate(rows, axis=0) for rows in zip(*tiles)]


def quotient(v, n):
    return ((v.astype(F32) + 0.5) * (1.0 / n)).astype(jnp.int32)


def center_kernel(
    cx, wy_count, masks_in, device_in, tile_in, wall, wyo, wye,
    weights, part, end_masks, target, columns, jpad, dpad, acc, masks, route, sems,
):
    rows, cols = wall.shape[2], wall.shape[3]
    copies = {}
    for k, pair in enumerate(((device_in, route.at[0]), (tile_in, route.at[1]))):
        copies[k] = pltpu.make_async_copy(*pair, sems.at[k])
    for k, first in enumerate((3, 0, 6)):
        span = slice(first, first + 3)
        copies["masks", first] = pltpu.make_async_copy(
            masks_in.at[:, :, span], masks.at[:, :, span], sems.at[2 + k]
        )
    order = [0, 1, ("masks", 3), ("masks", 0), ("masks", 6)]
    for k in order:
        copies[k].start()
    first_sub = lax.broadcasted_iota(jnp.int32, (SUB, LANES), 0) < SUB // 2
    copies[0].wait()
    copies[1].wait()
    device, tile = route[0], route[1]
    a, t = quotient(device, wy_count), quotient(tile, cols)
    b, u = device - a * wy_count, tile - t * cols
    target[...] = (a * rows + t) * (wy_count * cols) + b * cols + u
    before, after = before_after("wy", wye, wyo)
    fill_y(jpad, wall.at[0], before, after, 4 * cx)
    fill_y(dpad, wall.at[1], before, after, 4 * cx + 3 * rows)
    lattice = lattice_rows()
    columns[...] = own_columns(jpad, lattice, rows, cols)

    def one_tile(l, h):
        others = []
        for c in range(3):
            mid = mid_rows(jpad, c, l, h)
            for dh in (-1, 0, 1):
                mid[dh] = mid[dh] * (1.0 / REACH) + lattice[c]
                if c == 1:
                    mid[dh] = mid[dh] + RISE * dh
            others.append(mid)
        pulls = [mid_rows(dpad, c, l, h) for c in range(3)]

        def mask_at(dh, span, place):
            return masks[l, h, 4 + dh, span, :].astype(F32)

        tile_pass(l, h, cols, columns, others, pulls, mask_at, weights, acc)

    def put_sums(l, h):
        for c, sums in enumerate(tile_sums(acc, l, h, 4)):
            part[l, c, h : h + 1, :] = sums

    def put_masks(l, h):
        place = 0
        for g in range(LANES // SUB):
            span = slice(g * SUB, (g + 1) * SUB)
            for dh in reached(g):
                before = masks[l, h, 1 + dh, span, :]
                after = masks[l, h, 7 + dh, span, :]
                end_masks[l, h, place] = jnp.where(first_sub, before, after).astype(F32)
                place += 1

    tiles = [(l, h) for l in range(rows) for h in range(cols)]
    copies["masks", 3].wait()
    for l, h in tiles:
        one_tile(l, h)
        put_sums(l, h)
    copies["masks", 0].wait()
    copies["masks", 6].wait()
    for l, h in tiles:
        put_masks(l, h)


def wall_center(cx, wy_count, masks, device, tile, wall, wy_got):
    rows, cols = wall.shape[2], wall.shape[3]
    return pl.pallas_call(
        functools.partial(center_kernel, cx, wy_count),
        in_specs=[HBM] * 3 + [whole()] * 3,
        out_specs=[whole()] * 5,
        out_shape=[
            jax.ShapeDtypeStruct((rows, cols, STORED, SUB, LANES), F32),
            vmem(rows, 4, cols, LANES),
            vmem(rows, cols, STORED, SUB, LANES),
            pltpu.VMEM(device.shape, jnp.int32),
            vmem(LANES, pad8(3 * rows * cols)),
        ],
        scratch_shapes=[
            vmem(3, rows + 2, SUB, LANES),
            vmem(3, rows + 2, SUB, LANES),
            vmem(rows, cols, 4, LANES, LANES),
            pltpu.VMEM(masks.shape, jnp.int32),
            pltpu.VMEM((2,) + device.shape, jnp.int32),
            pltpu.SemaphoreType.DMA((5,)),
        ],
        compiler_params=params(),
        name="wall_center",
    )(*in_hbm(masks, device, tile), wall, *wy_got)


def wall_kernel(
    cx, cy, wall, wyo, wye, fxo, fxe, part, end_masks, columns, pressure,
    weights, vel1, base1, totals, to_odd, to_even, pressure_out, jpad, dpad, acc, sem,
):
    rows, cols = wall.shape[2], wall.shape[3]
    copy = pltpu.make_async_copy(pressure, pressure_out, sem)
    copy.start()
    first_sub = lax.broadcasted_iota(jnp.int32, (SUB, LANES), 0) < SUB // 2
    before, after = before_after("wy", wye, wyo)
    fill_y(jpad, wall.at[0], before, after, 4 * cx)
    fill_y(dpad, wall.at[1], before, after, 4 * cx + 3 * rows)
    before, after = before_after("fx", fxe, fxo)
    fill_x_shared(jpad, dpad, rows, cols, before, after, 3 * cy)
    lattice = lattice_rows()

    def one_tile(l, h):
        others = []
        for c in range(3):
            ends = end_rows(jpad, c, l, h, first_sub)
            for dh in (-1, 0, 1):
                ends[dh] = ends[dh] * (1.0 / REACH) + lattice[c]
                if c == 0:
                    ends[dh] = ends[dh] + jnp.where(first_sub, -SPAN, SPAN)
                if c == 1:
                    ends[dh] = ends[dh] + RISE * dh
            others.append(ends)
        pulls = [end_rows(dpad, c, l, h, first_sub) for c in range(3)]

        def mask_at(dh, span, place):
            return end_masks[l, h, place]

        tile_pass(l, h, cols, columns, others, pulls, mask_at, weights, acc)

    for l in range(rows):
        sums = []
        for h in range(cols):
            one_tile(l, h)
            sums.append(tile_sums(acc, l, h, 4))
        pulled = [v + part[l, c] for c, v in enumerate(by_quantity(sums))]
        totals[l] = pulled[3]
        for c in range(3):
            mine = wall[1, c, l]
            fresh = wall[2, c, l] + STIFFNESS * (pulled[c] - pulled[3] * mine)
            vel1[c, l] = fresh
            base1[c, l] = mine + fresh

    def edge(at):
        def write(out):
            for c in range(3):
                for k in range(rows):
                    out[c * rows + k : c * rows + k + 1, :] = base1[c, k, at : at + 1, :]
            for spare in range(3 * rows, out.shape[0]):
                out[spare : spare + 1, :] = jnp.zeros((1, LANES), F32)

        return write

    place_edges(even_at("wy"), edge(0), edge(cols - 1), to_even, to_odd)
    copy.wait()


def wall_first(wall, wy_got, fx_got, part, end_masks, columns, pressure):
    cx, cy = pressure.shape[0], pressure.shape[1]
    rows, cols = wall.shape[2], wall.shape[3]
    edge = (pad8(3 * rows), LANES)
    field = vmem(*wall.shape[1:])
    return pl.pallas_call(
        functools.partial(wall_kernel, cx, cy),
        in_specs=[whole()] * 9,
        out_specs=[whole()] * 6 + [HBM],
        out_shape=[
            jax.ShapeDtypeStruct((rows, cols, STORED, SUB, LANES), F32),
            field,
            field,
            vmem(rows, cols, LANES),
            vmem(*edge),
            vmem(*edge),
            jax.ShapeDtypeStruct(pressure.shape, F32),
        ],
        scratch_shapes=[
            pltpu.VMEM((3, rows + 2, SUB, LANES), F32),
            pltpu.VMEM((3, rows + 2, SUB, LANES), F32),
            pltpu.VMEM((rows, cols, 4, LANES, LANES), F32),
            pltpu.SemaphoreType.DMA(()),
        ],
        compiler_params=params(),
        name="wall_first",
    )(wall, *wy_got, *fx_got, part, end_masks, columns, pressure)


def pack_base_kernel(base1, got_odd, got_even, to_odd, to_even):
    rows, cols = base1.shape[1], base1.shape[2]
    before, after = before_after("wy", got_even, got_odd)

    def edge(l):
        def write(out):
            at = 0
            for c in range(3):
                side = c * rows + l
                out[at : at + 1, :] = before[side : side + 1]
                out[at + 1 : at + 1 + cols, :] = base1[c, l]
                out[at + 1 + cols : at + 2 + cols, :] = after[side : side + 1]
                at += cols + 2
            for spare in range(at, out.shape[0]):
                out[spare : spare + 1, :] = jnp.zeros((1, LANES), F32)

        return write

    place_edges(even_at("fx"), edge(0), edge(rows - 1), to_even, to_odd)


def pack_base(base1, got):
    cols = base1.shape[2]
    out = vmem(pad8(3 * (cols + 2)), LANES)
    return pl.pallas_call(
        pack_base_kernel,
        in_specs=[whole()] * 3,
        out_specs=[whole()] * 2,
        out_shape=[out, out],
        compiler_params=params(),
        name="pack_base",
    )(base1, *got)


def middle_kernel(weights, base1, wyo, wye, after_this, part, dpad, acc):
    rows, cols = base1.shape[1], base1.shape[2]
    before, after = before_after("wy", wye, wyo)
    fill_y(dpad, base1, before, after, 0)
    for l in range(rows):
        for h in range(cols):
            mids = [mid_rows(dpad, c, l, h) for c in range(3)]
            place = 0
            for g in range(LANES // SUB):
                sums = [None] * 3
                for dh in reached(g):
                    weight = weights[l, h, place]
                    terms = [weight * mids[c][dh] for c in range(3)]
                    sums = [t if v is None else v + t for v, t in zip(sums, terms)]
                    place += 1
                for c in range(3):
                    acc[l, h, c, g * SUB : (g + 1) * SUB, :] = sums[c]
            for c, row in enumerate(tile_sums(acc, l, h, 3)):
                part[l, c, h : h + 1, :] = row


def wall_middle(weights, base1, wy_got, after):
    rows, cols = base1.shape[1], base1.shape[2]
    return pl.pallas_call(
        middle_kernel,
        in_specs=[whole()] * 5,
        out_specs=whole(),
        out_shape=vmem(rows, 3, cols, LANES),
        scratch_shapes=[vmem(3, rows + 2, SUB, LANES), vmem(rows, cols, 3, LANES, LANES)],
        compiler_params=params(),
        name="wall_middle",
    )(weights, base1, *wy_got, after)


def last_kernel(
    weights, end_weights, part, got, base1, vel1, totals, wyo, wye, fxo, fxe, disp_out, vel_out,
    dpad, load_pad, acc,
):
    rows, cols = base1.shape[1], base1.shape[2]
    first_sub = lax.broadcasted_iota(jnp.int32, (SUB, LANES), 0) < SUB // 2
    before, after = before_after("wy", wye, wyo)
    fill_y(dpad, base1, before, after, 0)
    before, after = before_after("fx", fxe, fxo)
    fill_x(dpad, rows, cols, before, after, 0)
    pieces = []
    for half in range(2):
        for k in range(3):
            total = got[half, k]
            for d in range(half + 2, got.shape[0], 2):
                total = total + got[d, k]
            pieces.append(total)
    total = jnp.concatenate(pieces, axis=0)
    one, two = unpack_slots(total, cols)
    for k in range(rows + 2):
        loads = LOADING * one[k][0 : cols + 2]
        load_pad[0, k, 0 : cols + 2, :] = loads
        dpad[0, k, 0 : cols + 2, :] = dpad[0, k, 0 : cols + 2, :] + loads

    def one_tile(l, h):
        mid = mid_rows(load_pad, 0, l, h)
        ends = [end_rows(dpad, c, l, h, first_sub) for c in range(3)]
        place = 0
        for g in range(LANES // SUB):
            sums = [None] * 3
            for dh in reached(g):
                weight = end_weights[l, h, place]
                terms = [weight * ends[c][dh] for c in range(3)]
                terms[0] = terms[0] + weights[l, h, place] * mid[dh]
                sums = [t if v is None else v + t for v, t in zip(sums, terms)]
                place += 1
            for c in range(3):
                acc[l, h, c, g * SUB : (g + 1) * SUB, :] = sums[c]

    for l in range(rows):
        sums = []
        for h in range(cols):
            one_tile(l, h)
            sums.append(tile_sums(acc, l, h, 3))
        pulled = by_quantity(sums)
        for c in range(3):
            mine = dpad[c, l + 1, 1 : cols + 1, :]
            force = STIFFNESS * (pulled[c] + part[l, c] - totals[l] * mine)
            if c == 0:
                force = force + LOADING * (one[l + 1][1 : cols + 1] + two[l])
            fresh = vel1[c, l] + force
            vel_out[c, l] = fresh
            disp_out[c, l] = mine + fresh


def wall_last(weights, end_weights, part, got, base1, vel1, totals, wy_got, fx_got):
    rows, cols = base1.shape[1], base1.shape[2]
    return pl.pallas_call(
        last_kernel,
        in_specs=[whole()] * 11,
        out_specs=[whole()] * 2,
        out_shape=[jax.ShapeDtypeStruct(base1.shape, F32)] * 2,
        scratch_shapes=[
            vmem(3, rows + 2, SUB, LANES),
            vmem(1, rows + 2, SUB, LANES),
            pltpu.VMEM((rows, cols, 3, LANES, LANES), F32),
        ],
        compiler_params=params(),
        name="wall_last",
    )(weights, end_weights, part, got, base1, vel1, totals, *wy_got, *fx_got)


def per_device(
    displacement,
    velocity,
    jitter,
    bond_masks,
    pressure,
    pressure_prev,
    speed_sq,
    route_device,
    route_tile,
):
    fx_count, wy_count = lax.axis_size("fx"), lax.axis_size("wy")
    cols = displacement.shape[2]
    device = route_device.reshape(-1, LANES)
    tile = route_tile.reshape(-1, LANES)
    cx = pressure.shape[0]
    *sends, p, q, s, wall = pack_wy(
        pressure, pressure_prev, speed_sq, jitter, displacement, velocity
    )
    grids = (p, q, s)
    wy_got = exchange("wy", *sends)
    sends = pack_fx(grids, wall, wy_got)
    fx_got = exchange("fx", *sends)
    weights, part, end_masks, target, columns = wall_center(
        cx, wy_count, bond_masks, device, tile, wall, wy_got
    )
    fresh, keep, send = grid_steps(*grids, wy_got, fx_got, target, fx_count, wy_count)
    names = ("fx", "wy")
    other = lax.ppermute(send, names, swap_pairs(1, (fx_count, wy_count), 0))
    end_weights, vel1, base1, totals, *sends, pressure_out = wall_first(
        wall, wy_got, fx_got, part, end_masks, columns, fresh
    )
    slots = pair_sum(keep, other, totals)
    got = lax.all_to_all(slots, names, split_axis=0, concat_axis=0, tiled=True)
    base_wy = exchange("wy", *sends)
    sends = pack_base(base1, base_wy)
    base_fx = exchange("fx", *sends)
    middle = wall_middle(weights, base1, base_wy, sends[0])
    disp_out, vel_out = wall_last(
        weights, end_weights, middle, got, base1, vel1, totals, base_wy, base_fx
    )
    return (disp_out, vel_out, pressure_out)


def solution(mesh):
    placed = (
        P(None, "fx", "wy", None),
        P(None, "fx", "wy", None),
        P(None, "fx", "wy", None),
        P("fx", "wy", None, None, None),
        P("fx", "wy", None),
        P("fx", "wy", None),
        P("fx", "wy", None),
        P(("fx", "wy"), None),
        P(("fx", "wy")),
    )
    return jax.shard_map(
        per_device,
        mesh=mesh,
        in_specs=placed,
        out_specs=(P(None, "fx", "wy", None), P(None, "fx", "wy", None), P("fx", "wy", None)),
        check_vma=False,
    )
```

```python
import functools

import jax
import jax.numpy as jnp
from jax import lax
from jax.experimental import pallas as pl
from jax.experimental.pallas import tpu as pltpu
from jax.sharding import PartitionSpec as P

STIFFNESS = 0.02
LOADING = 0.05
REACH = 3.0
LANES = 128
SUB = 8
VMEM_BYTES = 32 * 1024 * 1024
HBM = pl.BlockSpec(memory_space=pltpu.HBM)

F32 = jnp.float32
BF16 = jnp.bfloat16


def whole():
    return pl.BlockSpec(memory_space=pltpu.VMEM)


def params():
    return pltpu.CompilerParams(vmem_limit_bytes=VMEM_BYTES)


def vmem(*shape):
    return pltpu.VMEM(shape, F32)


def even_at(axis):
    return lax.rem(lax.axis_index(axis), 2) == 0


def swap_pairs(axis, sizes, first):
    count, others = sizes[axis], sizes[1 - axis]
    pairs = []

    def join(*two):
        a, b = [place * sizes[1] + other for place, other in two]
        pairs.extend([(a, b), (b, a)])

    def at(place, other):
        return (place, other) if axis == 0 else (other, place)

    met = set()
    for low in range(first, count - 1, 2):
        met.update((low, low + 1))
        for other in range(others):
            join(at(low, other), at(low + 1, other))
    for place in range(count):
        if place not in met and others % 2 == 0:
            for other in range(0, others, 2):
                join(at(place, other), at(place, other + 1))
    return pairs


def exchange(axis, to_odd, to_even):
    names = ("fx", "wy")
    sizes = [lax.axis_size(name) for name in names]
    along = names.index(axis)
    got_odd = lax.ppermute(to_odd, names, swap_pairs(along, sizes, 1))
    got_even = lax.ppermute(to_even, names, swap_pairs(along, sizes, 0))
    return got_odd, got_even


def place_edges(even, low, high, to_even, to_odd):
    @pl.when(even)
    def _():
        high(to_even)
        low(to_odd)

    @pl.when(jnp.logical_not(even))
    def _():
        low(to_even)
        high(to_odd)


def before_after(axis, got_even, got_odd):
    even = even_at(axis)
    place, last = lax.axis_index(axis), lax.axis_size(axis) - 1
    a, b = got_even[...], got_odd[...]
    before = jnp.where(place == 0, 0.0, jnp.where(even, b, a))
    after = jnp.where(place == last, 0.0, jnp.where(even, a, b))
    return before, after


def pack_wy_kernel(
    p_in, q_in, s_in, jit_in, disp_in, vel_in, wy_odd, wy_even, p, q, s, wall, sems
):
    cx, cy = p.shape[0], p.shape[1]
    rows, cols = jit_in.shape[1], jit_in.shape[2]
    pairs = [(p_in, p), (q_in, q), (s_in, s)]
    for k, field in enumerate((jit_in, disp_in, vel_in)):
        pairs.append((field, wall.at[k]))
    copies = [pltpu.make_async_copy(a, b, sems.at[k]) for k, (a, b) in enumerate(pairs)]
    for copy in copies:
        copy.start()
    for copy in copies:
        copy.wait()

    def edge(near, far, h):
        def write(out):
            out[0:cx, :] = p[:, near, :]
            out[cx : 2 * cx, :] = p[:, far, :]
            out[2 * cx : 3 * cx, :] = q[:, near, :]
            out[3 * cx : 4 * cx, :] = s[:, near, :]
            at = 4 * cx
            for field in range(2):
                for c in range(3):
                    for l in range(rows):
                        out[at : at + 1, :] = wall[field, c, l, h : h + 1, :]
                        at += 1
            for spare in range(at, out.shape[0]):
                out[spare : spare + 1, :] = jnp.zeros((1, LANES), F32)

        return write

    place_edges(
        even_at("wy"),
        edge(0, 1, 0),
        edge(cy - 1, cy - 2, cols - 1),
        wy_even,
        wy_odd,
    )


def in_hbm(*arrays):
    return [pltpu.with_memory_space_constraint(v, pltpu.HBM) for v in arrays]


def pad8(count):
    return (count + 7) // 8 * 8


def pack_wy(p, q, s, jit, disp, vel):
    message = vmem(pad8(4 * p.shape[0] + 6 * jit.shape[1]), LANES)
    return pl.pallas_call(
        pack_wy_kernel,
        in_specs=[HBM] * 6,
        out_specs=[whole()] * 6,
        out_shape=[message, message] + [vmem(*p.shape)] * 3 + [vmem(3, *jit.shape)],
        scratch_shapes=[pltpu.SemaphoreType.DMA((6,))],
        compiler_params=params(),
        name="pack_wy",
    )(*in_hbm(p, q, s, jit, disp, vel))


def wall_lanes(field, low):
    lane = lax.broadcasted_iota(jnp.int32, field.shape, 1) % 8
    return lane < 3 if low else lane > 4


def pack_fx_kernel(p, q, s, wall, got_odd, got_even, to_odd, to_even, line):
    cx, cy = p.shape[0], p.shape[1]
    rows, cols = wall.shape[2], wall.shape[3]
    before, after = before_after("wy", got_even, got_odd)

    def edge(low, x, far, l):
        def write(out):
            line[SUB - 1 : SUB, :] = before[x : x + 1]
            line[SUB : SUB + cy, :] = p[x]
            line[SUB + cy : SUB + cy + 1, :] = after[x : x + 1]
            mine, speed = p[x], s[x]
            beside = p[far] + line[SUB - 1 : SUB - 1 + cy, :] + line[SUB + 1 : SUB + 1 + cy, :]
            out[0:cy, :] = mine
            out[cy : 2 * cy, :] = update(mine, q[x], speed, beside)
            out[2 * cy : 3 * cy, :] = speed
            at = 3 * cy
            for c in range(3):
                pair = []
                for field in range(2):
                    row = 4 * cx + (field * 3 + c) * rows + l
                    parts = (before[row : row + 1], wall[field, c, l], after[row : row + 1])
                    pair.append(jnp.concatenate(parts, axis=0))
                moved = pltpu.roll(pair[1], 3 if low else LANES - 3, 1)
                out[at : at + cols + 2, :] = jnp.where(wall_lanes(moved, low), pair[0], moved)
                at += cols + 2
            out[at : at + 1, :] = before[x : x + 1]
            out[at + 1 : at + 2, :] = after[x : x + 1]
            for spare in range(at + 2, out.shape[0]):
                out[spare : spare + 1, :] = jnp.zeros((1, LANES), F32)

        return write

    place_edges(
        even_at("fx"), edge(True, 0, 1, 0), edge(False, cx - 1, cx - 2, rows - 1), to_even, to_odd
    )


def pack_fx(grids, wall, got):
    cy, cols = grids[0].shape[1], wall.shape[3]
    out = vmem(pad8(3 * cy + 3 * (cols + 2) + 2), LANES)
    return pl.pallas_call(
        pack_fx_kernel,
        in_specs=[whole()] * 6,
        out_specs=[whole()] * 2,
        out_shape=[out, out],
        scratch_shapes=[vmem(cy + 2 * SUB, LANES)],
        compiler_params=params(),
        name="pack_fx",
    )(*grids, wall, *got)


def along_z(v):
    lane = lax.broadcasted_iota(jnp.int32, v.shape, 1)
    up = jnp.where(lane == LANES - 1, 0.0, pltpu.roll(v, LANES - 1, 1))
    down = jnp.where(lane == 0, 0.0, pltpu.roll(v, 1, 1))
    return up + down


def update(v, old, speed, beside):
    return 2.0 * v - old + speed * (beside + along_z(v) - 6.0 * v)


def two_terms(v):
    high = v.astype(BF16)
    return high, (v - high.astype(F32)).astype(BF16)


def grid_kernel(
    p, q, s, wyo, wye, fxo, fxe, target, out, keep, send, s0, s1, rhs, part1, part2, slots
):
    cx, cy = p.shape[0], p.shape[1]
    ahead, behind = SUB, SUB + cy
    fx_count = part1.shape[0] // 2 - 1
    cols = 4
    tall = part2.shape[0]
    high = part1.shape[1] - 2 * SUB
    wy_count = high // cols
    before_y, after_y = before_after("wy", wye, wyo)
    before_x, after_x = before_after("fx", fxe, fxo)
    corner = 3 * cy + 3 * (cols + 2)

    s0[1 : cx + 1, ahead:behind, :] = p[...]
    for x, side in ((0, before_x), (cx + 1, after_x)):
        s0[x, ahead:behind, :] = side[0:cy]
        s0[x, ahead - 1 : ahead, :] = side[corner : corner + 1]
        s0[x, behind : behind + 1, :] = side[corner + 1 : corner + 2]
    s0[1 : cx + 1, ahead - 1, :] = before_y[0:cx]
    s0[1 : cx + 1, behind, :] = after_y[0:cx]

    for side, y, inner in ((before_y, ahead - 1, ahead), (after_y, behind, behind - 1)):
        near, far = side[0:cx], side[cx : 2 * cx]
        old, speed = side[2 * cx : 3 * cx], side[3 * cx : 4 * cx]
        beside = s0[0:cx, y, :] + s0[2 : cx + 2, y, :] + far + s0[1 : cx + 1, inner, :]
        s1[1 : cx + 1, y, :] = update(near, old, speed, beside)
    for side, x, inner in ((before_x, 0, 1), (after_x, cx + 1, cx)):
        part, speed = side[cy : 2 * cy], side[2 * cy : 3 * cy]
        s1[x, ahead:behind, :] = part + speed * s0[inner, ahead:behind, :]

    def sweep(now, old, x):
        beside = now[x, ahead:behind, :] + now[x + 2, ahead:behind, :]
        beside = beside + now[x + 1, ahead - 1 : behind - 1, :]
        beside = beside + now[x + 1, ahead + 1 : behind + 1, :]
        return update(now[x + 1, ahead:behind, :], old, s[x], beside)

    for x in range(cx):
        fresh = sweep(s0, q[x], x)
        s1[x + 1, ahead:behind, :] = fresh
        a, b = two_terms(fresh)
        rhs[x * cy : (x + 1) * cy, 0:LANES] = a
        rhs[x * cy : (x + 1) * cy, LANES : 2 * LANES] = b
    for x in range(cx):
        fresh = sweep(s1, p[x], x)
        out[x] = fresh
        a, b = two_terms(fresh)
        rhs[x * cy : (x + 1) * cy, 2 * LANES : 3 * LANES] = a
        rhs[x * cy : (x + 1) * cy, 3 * LANES : 4 * LANES] = b

    part1[...] = jnp.zeros(part1.shape, F32)
    part2[:, 0:SUB, :] = jnp.zeros((tall, SUB, LANES), F32)
    chunk = 256
    for first in range(0, tall * high, chunk):
        tile = lax.broadcasted_iota(jnp.int32, (chunk, LANES), 0) + first
        picks = []
        for piece in range(target.shape[0]):
            picks.append(jnp.where(tile == target[piece : piece + 1, :], 1.0, 0.0).astype(BF16))
        sums = jnp.dot(jnp.concatenate(picks, axis=1), rhs[...], preferred_element_type=F32)
        one = sums[:, 0:LANES] + sums[:, LANES : 2 * LANES]
        two = sums[:, 2 * LANES : 3 * LANES] + sums[:, 3 * LANES : 4 * LANES]
        l = first // high
        part1[1 + l : 1 + l + chunk // high, SUB : SUB + high, :] = one.reshape(-1, high, LANES)
        part2[l : l + chunk // high, SUB : SUB + high, :] = two.reshape(-1, high, LANES)
    sub = lax.broadcasted_iota(jnp.int32, (SUB, LANES), 0)
    lane = lax.broadcasted_iota(jnp.int32, (SUB, LANES), 1)
    step1 = sub < cols + 2
    for a in range(fx_count):
        for b in range(wy_count):
            h = SUB + cols * b
            slot = a * wy_count + b
            one = [part1[2 * a + l, h - 1 : h - 1 + SUB, :] for l in range(4)]
            ends = jnp.where(lane % 8 < 4, one[3], one[0])
            two = [
                part2[2 * a + l, h + at - 6 : h + at - 6 + SUB, :]
                for l, at in ((0, 0), (0, 2), (1, 0))
            ]
            x = jnp.broadcast_to(part2[2 * a + 1, h + 2 : h + 3, :], (SUB, LANES))
            y = jnp.broadcast_to(part2[2 * a + 1, h + 3 : h + 4, :], (SUB, LANES))
            for r in range(4):
                moved = pltpu.roll(y, (3 - 2 * r) % LANES, 1)
                ends = jnp.where((sub == 1 + r) & free_ends(lane), moved, ends)
            low, high_free = (sub == 0) & (lane // 8 % 4 == 0), (sub == cols + 1) & (lane // 8 % 4 == 3)
            own0 = jnp.where(low | high_free, x, one[1])
            own1 = jnp.where(low, pltpu.roll(x, LANES - 8, 1), one[2])
            own1 = jnp.where(high_free, pltpu.roll(x, 8, 1), own1)
            for k, group in enumerate((ends, own0, own1)):
                slots[slot, k * SUB : (k + 1) * SUB, :] = jnp.where(step1, group, two[k])

    def halve(first, second):
        for to, at in ((first, 0), (second, 3)):
            for k in range(3):
                to[:, k] = slots[:, 4 * (at + k) : 4 * (at + k + 1), :]

    @pl.when(even_at("wy"))
    def _():
        halve(keep, send)

    @pl.when(jnp.logical_not(even_at("wy")))
    def _():
        halve(send, keep)


def free_ends(lane):
    return (lane % 8 == 3) | (lane % 8 == 4)


def unpack_slots(total, cols):
    ends, own0, own1 = [total[k * SUB : (k + 1) * SUB] for k in range(3)]
    lane = lax.broadcasted_iota(jnp.int32, (1, LANES), 1)
    two = [[ends[6:7], ends[7:8], own0[6:7], own0[7:8]], [own1[6:7], own1[7:8]]]
    q = lane // 8 % 4
    last = cols + 1
    x = jnp.where(q == 0, own0[0:1], own0[last : last + 1])
    x = jnp.where(q == 1, pltpu.roll(own1[0:1], 8, 1), x)
    x = jnp.where(q == 2, pltpu.roll(own1[last : last + 1], LANES - 8, 1), x)
    y = None
    for r in range(4):
        moved = pltpu.roll(ends[1 + r : 2 + r], (2 * r - 3) % LANES, 1)
        y = moved if y is None else jnp.where(lane % 8 // 2 == r, moved, y)
    two[1].extend([x, y])
    two = [jnp.concatenate(v, axis=0) for v in two]
    return (ends, own0, own1, ends), two


def grid_steps(p, q, s, wy_got, fx_got, target, fx_count, wy_count):
    cx, cy = p.shape[0], p.shape[1]
    tall, high = fx_count * 2, wy_count * 4
    devices = fx_count * wy_count
    half = (devices, 3, 4, LANES)
    return pl.pallas_call(
        grid_kernel,
        in_specs=[whole()] * 8,
        out_specs=[whole()] * 3,
        out_shape=[
            vmem(*p.shape),
            vmem(*half),
            vmem(*half),
        ],
        scratch_shapes=[
            pltpu.VMEM((cx + 2, cy + 2 * SUB, LANES), F32),
            pltpu.VMEM((cx + 2, cy + 2 * SUB, LANES), F32),
            pltpu.VMEM((cx * cy, 4 * LANES), BF16),
            pltpu.VMEM((tall + 2, high + 2 * SUB, LANES), F32),
            pltpu.VMEM((tall, high + 2 * SUB, LANES), F32),
            vmem(devices, 3 * SUB, LANES),
        ],
        compiler_params=params(),
        name="grid_steps",
    )(p, q, s, *wy_got, *fx_got, target)


def pair_sum_kernel(keep, got, after, out):
    out[...] = keep[...] + got[...]


def pair_sum(keep, got, after):
    return pl.pallas_call(
        pair_sum_kernel,
        in_specs=[whole()] * 3,
        out_specs=whole(),
        out_shape=jax.ShapeDtypeStruct(keep.shape, F32),
        compiler_params=params(),
        name="pair_sum",
    )(keep, got, after)


def reached(g):
    groups = []
    for dh in (-1, 0, 1):
        if (dh == -1 and g % 4 == 3) or (dh == 1 and g % 4 == 0):
            continue
        groups.append(dh)
    return groups


STORED = sum(len(reached(g)) for g in range(LANES // SUB))


def mid_rows(ref, c, l, h):
    rows = {}
    for dh in (-1, 0, 1):
        row = ref[c, l + 1, pl.ds(h + 1 + dh, 1), :]
        rows[dh] = jnp.broadcast_to(row, (SUB, LANES))
    return rows


def end_rows(ref, c, l, h, first_sub):
    rows = {}
    for dh in (-1, 0, 1):
        at = pl.ds(h + 1 + dh, 1)
        before = jnp.broadcast_to(ref[c, l, at, :], (SUB, LANES))
        after = jnp.broadcast_to(ref[c, l + 2, at, :], (SUB, LANES))
        rows[dh] = jnp.where(first_sub, before, after)
    return rows


def fill_y(pad, own, before, after, at):
    rows, cols = own.shape[1], own.shape[2]
    for c in range(3):
        for l in range(rows):
            row = at + c * rows + l
            pad[c, l + 1, 0:1, :] = before[row : row + 1]
            pad[c, l + 1, 1 : cols + 1, :] = own[c, l]
            pad[c, l + 1, cols + 1 : cols + 2, :] = after[row : row + 1]


def fill_x(pad, rows, cols, before, after, at):
    for c in range(3):
        row = at + c * (cols + 2)
        pad[c, 0, 0 : cols + 2, :] = before[row : row + cols + 2]
        pad[c, rows + 1, 0 : cols + 2, :] = after[row : row + cols + 2]


def fill_x_shared(jpad, dpad, rows, cols, before, after, at):
    for c in range(3):
        row = at + c * (cols + 2)
        for message, l, low in ((before, 0, False), (after, rows + 1, True)):
            both = message[row : row + cols + 2]
            jpad[c, l, 0 : cols + 2, :] = jnp.where(wall_lanes(both, low), both, 0.0)
            moved = pltpu.roll(both, LANES - 3 if low else 3, 1)
            dpad[c, l, 0 : cols + 2, :] = moved


def lattice_rows():
    index = lax.broadcasted_iota(jnp.int32, (1, LANES), 1)
    places = (index % 8, index // 8 % 4, index // 32)
    return [v.astype(F32) * (1.0 / REACH) for v in places]


SPAN = 8.0 / REACH
RISE = 4.0 / REACH


def own_columns(ref, lattice, rows, cols):
    places = []
    for l in range(rows):
        for h in range(cols):
            for c in range(3):
                places.append(ref[c, l + 1, h + 1 : h + 2, :] * (1.0 / REACH) + lattice[c])
    spare = -len(places) % SUB
    if spare:
        places.append(jnp.zeros((spare, LANES), F32))
    return jnp.transpose(jnp.concatenate(places, axis=0))


def bond_row(weight, others, mine):
    for c in range(3):
        diff = others[c] - mine[c]
        weight = weight - diff * diff
    return jnp.maximum(weight, 0.0)


def tile_pass(l, h, cols, columns, others, pulls, mask_at, weights, acc):
    place = 0
    first = 3 * (l * cols + h)
    for g in range(LANES // SUB):
        span = slice(g * SUB, (g + 1) * SUB)
        mine = [jnp.broadcast_to(columns[span, first + c : first + c + 1], (SUB, LANES)) for c in range(3)]
        sums = [None] * 4
        for dh in reached(g):
            here = [others[c][dh] for c in range(3)]
            weight = bond_row(mask_at(dh, span, place), here, mine)
            weights[l, h, place] = weight
            place += 1
            terms = [weight * pulls[c][dh] for c in range(3)] + [weight]
            sums = [t if v is None else v + t for v, t in zip(sums, terms)]
        for c in range(4):
            acc[l, h, c, span, :] = sums[c]


def tile_sums(acc, l, h, count):
    ones = jnp.ones((2 * SUB, 2 * LANES), BF16)
    terms = [jnp.concatenate(two_terms(acc[l, h, c]), axis=1) for c in range(count)]
    sums = lax.dot_general(
        ones,
        jnp.concatenate(terms, axis=0),
        (((1,), (1,)), ((), ())),
        preferred_element_type=F32,
    )[0:1]
    return [sums[:, c * LANES : (c + 1) * LANES] for c in range(count)]


def by_quantity(tiles):
    return [jnp.concatenate(rows, axis=0) for rows in zip(*tiles)]


def quotient(v, n):
    return ((v.astype(F32) + 0.5) * (1.0 / n)).astype(jnp.int32)


def center_kernel(
    cx, wy_count, masks_in, device_in, tile_in, wall, wyo, wye,
    weights, part, end_masks, target, columns, jpad, dpad, acc, masks, route, sems,
):
    rows, cols = wall.shape[2], wall.shape[3]
    copies = {}
    for k, pair in enumerate(((device_in, route.at[0]), (tile_in, route.at[1]))):
        copies[k] = pltpu.make_async_copy(*pair, sems.at[k])
    for k, first in enumerate((3, 0, 6)):
        span = slice(first, first + 3)
        copies["masks", first] = pltpu.make_async_copy(
            masks_in.at[:, :, span], masks.at[:, :, span], sems.at[2 + k]
        )
    order = [0, 1, ("masks", 3), ("masks", 0), ("masks", 6)]
    for k in order:
        copies[k].start()
    first_sub = lax.broadcasted_iota(jnp.int32, (SUB, LANES), 0) < SUB // 2
    copies[0].wait()
    copies[1].wait()
    device, tile = route[0], route[1]
    a, t = quotient(device, wy_count), quotient(tile, cols)
    b, u = device - a * wy_count, tile - t * cols
    target[...] = (a * rows + t) * (wy_count * cols) + b * cols + u
    before, after = before_after("wy", wye, wyo)
    fill_y(jpad, wall.at[0], before, after, 4 * cx)
    fill_y(dpad, wall.at[1], before, after, 4 * cx + 3 * rows)
    lattice = lattice_rows()
    columns[...] = own_columns(jpad, lattice, rows, cols)

    def one_tile(l, h):
        others = []
        for c in range(3):
            mid = mid_rows(jpad, c, l, h)
            for dh in (-1, 0, 1):
                mid[dh] = mid[dh] * (1.0 / REACH) + lattice[c]
                if c == 1:
                    mid[dh] = mid[dh] + RISE * dh
            others.append(mid)
        pulls = [mid_rows(dpad, c, l, h) for c in range(3)]

        def mask_at(dh, span, place):
            return masks[l, h, 4 + dh, span, :].astype(F32)

        tile_pass(l, h, cols, columns, others, pulls, mask_at, weights, acc)

    def put_sums(l, h):
        for c, sums in enumerate(tile_sums(acc, l, h, 4)):
            part[l, c, h : h + 1, :] = sums

    def put_masks(l, h):
        place = 0
        for g in range(LANES // SUB):
            span = slice(g * SUB, (g + 1) * SUB)
            for dh in reached(g):
                before = masks[l, h, 1 + dh, span, :]
                after = masks[l, h, 7 + dh, span, :]
                end_masks[l, h, place] = jnp.where(first_sub, before, after).astype(F32)
                place += 1

    tiles = [(l, h) for l in range(rows) for h in range(cols)]
    copies["masks", 3].wait()
    for l, h in tiles:
        one_tile(l, h)
        put_sums(l, h)
    copies["masks", 0].wait()
    copies["masks", 6].wait()
    for l, h in tiles:
        put_masks(l, h)


def wall_center(cx, wy_count, masks, device, tile, wall, wy_got):
    rows, cols = wall.shape[2], wall.shape[3]
    return pl.pallas_call(
        functools.partial(center_kernel, cx, wy_count),
        in_specs=[HBM] * 3 + [whole()] * 3,
        out_specs=[whole()] * 5,
        out_shape=[
            jax.ShapeDtypeStruct((rows, cols, STORED, SUB, LANES), F32),
            vmem(rows, 4, cols, LANES),
            vmem(rows, cols, STORED, SUB, LANES),
            pltpu.VMEM(device.shape, jnp.int32),
            vmem(LANES, pad8(3 * rows * cols)),
        ],
        scratch_shapes=[
            vmem(3, rows + 2, SUB, LANES),
            vmem(3, rows + 2, SUB, LANES),
            vmem(rows, cols, 4, LANES, LANES),
            pltpu.VMEM(masks.shape, jnp.int32),
            pltpu.VMEM((2,) + device.shape, jnp.int32),
            pltpu.SemaphoreType.DMA((5,)),
        ],
        compiler_params=params(),
        name="wall_center",
    )(*in_hbm(masks, device, tile), wall, *wy_got)


def wall_kernel(
    cx, cy, wall, wyo, wye, fxo, fxe, part, end_masks, columns, pressure,
    weights, vel1, base1, totals, to_odd, to_even, pressure_out, jpad, dpad, acc, sem,
):
    rows, cols = wall.shape[2], wall.shape[3]
    copy = pltpu.make_async_copy(pressure, pressure_out, sem)
    copy.start()
    first_sub = lax.broadcasted_iota(jnp.int32, (SUB, LANES), 0) < SUB // 2
    before, after = before_after("wy", wye, wyo)
    fill_y(jpad, wall.at[0], before, after, 4 * cx)
    fill_y(dpad, wall.at[1], before, after, 4 * cx + 3 * rows)
    before, after = before_after("fx", fxe, fxo)
    fill_x_shared(jpad, dpad, rows, cols, before, after, 3 * cy)
    lattice = lattice_rows()

    def one_tile(l, h):
        others = []
        for c in range(3):
            ends = end_rows(jpad, c, l, h, first_sub)
            for dh in (-1, 0, 1):
                ends[dh] = ends[dh] * (1.0 / REACH) + lattice[c]
                if c == 0:
                    ends[dh] = ends[dh] + jnp.where(first_sub, -SPAN, SPAN)
                if c == 1:
                    ends[dh] = ends[dh] + RISE * dh
            others.append(ends)
        pulls = [end_rows(dpad, c, l, h, first_sub) for c in range(3)]

        def mask_at(dh, span, place):
            return end_masks[l, h, place]

        tile_pass(l, h, cols, columns, others, pulls, mask_at, weights, acc)

    for l in range(rows):
        sums = []
        for h in range(cols):
            one_tile(l, h)
            sums.append(tile_sums(acc, l, h, 4))
        pulled = [v + part[l, c] for c, v in enumerate(by_quantity(sums))]
        totals[l] = pulled[3]
        for c in range(3):
            mine = wall[1, c, l]
            fresh = wall[2, c, l] + STIFFNESS * (pulled[c] - pulled[3] * mine)
            vel1[c, l] = fresh
            base1[c, l] = mine + fresh

    def edge(at):
        def write(out):
            for c in range(3):
                for k in range(rows):
                    out[c * rows + k : c * rows + k + 1, :] = base1[c, k, at : at + 1, :]
            for spare in range(3 * rows, out.shape[0]):
                out[spare : spare + 1, :] = jnp.zeros((1, LANES), F32)

        return write

    place_edges(even_at("wy"), edge(0), edge(cols - 1), to_even, to_odd)
    copy.wait()


def wall_first(wall, wy_got, fx_got, part, end_masks, columns, pressure):
    cx, cy = pressure.shape[0], pressure.shape[1]
    rows, cols = wall.shape[2], wall.shape[3]
    edge = (pad8(3 * rows), LANES)
    field = vmem(*wall.shape[1:])
    return pl.pallas_call(
        functools.partial(wall_kernel, cx, cy),
        in_specs=[whole()] * 9,
        out_specs=[whole()] * 6 + [HBM],
        out_shape=[
            jax.ShapeDtypeStruct((rows, cols, STORED, SUB, LANES), F32),
            field,
            field,
            vmem(rows, cols, LANES),
            vmem(*edge),
            vmem(*edge),
            jax.ShapeDtypeStruct(pressure.shape, F32),
        ],
        scratch_shapes=[
            pltpu.VMEM((3, rows + 2, SUB, LANES), F32),
            pltpu.VMEM((3, rows + 2, SUB, LANES), F32),
            pltpu.VMEM((rows, cols, 4, LANES, LANES), F32),
            pltpu.SemaphoreType.DMA(()),
        ],
        compiler_params=params(),
        name="wall_first",
    )(wall, *wy_got, *fx_got, part, end_masks, columns, pressure)


def pack_base_kernel(base1, got_odd, got_even, to_odd, to_even):
    rows, cols = base1.shape[1], base1.shape[2]
    before, after = before_after("wy", got_even, got_odd)

    def edge(l):
        def write(out):
            at = 0
            for c in range(3):
                side = c * rows + l
                out[at : at + 1, :] = before[side : side + 1]
                out[at + 1 : at + 1 + cols, :] = base1[c, l]
                out[at + 1 + cols : at + 2 + cols, :] = after[side : side + 1]
                at += cols + 2
            for spare in range(at, out.shape[0]):
                out[spare : spare + 1, :] = jnp.zeros((1, LANES), F32)

        return write

    place_edges(even_at("fx"), edge(0), edge(rows - 1), to_even, to_odd)


def pack_base(base1, got):
    cols = base1.shape[2]
    out = vmem(pad8(3 * (cols + 2)), LANES)
    return pl.pallas_call(
        pack_base_kernel,
        in_specs=[whole()] * 3,
        out_specs=[whole()] * 2,
        out_shape=[out, out],
        compiler_params=params(),
        name="pack_base",
    )(base1, *got)


def middle_kernel(weights, base1, wyo, wye, after_this, part, dpad, acc):
    rows, cols = base1.shape[1], base1.shape[2]
    before, after = before_after("wy", wye, wyo)
    fill_y(dpad, base1, before, after, 0)
    for l in range(rows):
        for h in range(cols):
            mids = [mid_rows(dpad, c, l, h) for c in range(3)]
            place = 0
            for g in range(LANES // SUB):
                sums = [None] * 3
                for dh in reached(g):
                    weight = weights[l, h, place]
                    terms = [weight * mids[c][dh] for c in range(3)]
                    sums = [t if v is None else v + t for v, t in zip(sums, terms)]
                    place += 1
                for c in range(3):
                    acc[l, h, c, g * SUB : (g + 1) * SUB, :] = sums[c]
            for c, row in enumerate(tile_sums(acc, l, h, 3)):
                part[l, c, h : h + 1, :] = row


def wall_middle(weights, base1, wy_got, after):
    rows, cols = base1.shape[1], base1.shape[2]
    return pl.pallas_call(
        middle_kernel,
        in_specs=[whole()] * 5,
        out_specs=whole(),
        out_shape=vmem(rows, 3, cols, LANES),
        scratch_shapes=[vmem(3, rows + 2, SUB, LANES), vmem(rows, cols, 3, LANES, LANES)],
        compiler_params=params(),
        name="wall_middle",
    )(weights, base1, *wy_got, after)


def ends_kernel(weights, base1, fxo, fxe, wyo, wye, middle, part, dpad, acc):
    rows, cols = base1.shape[1], base1.shape[2]
    first_sub = lax.broadcasted_iota(jnp.int32, (SUB, LANES), 0) < SUB // 2
    before, after = before_after("wy", wye, wyo)
    fill_y(dpad, base1, before, after, 0)
    before, after = before_after("fx", fxe, fxo)
    fill_x(dpad, rows, cols, before, after, 0)
    for l in range(rows):
        sums = []
        for h in range(cols):
            ends = [end_rows(dpad, c, l, h, first_sub) for c in range(3)]
            weigh(weights, ends, l, h, acc)
            sums.append(tile_sums(acc, l, h, 3))
        for c, rows_c in enumerate(by_quantity(sums)):
            part[l, c] = middle[l, c] + rows_c


def weigh(weights, fields, l, h, acc):
    place = 0
    for g in range(LANES // SUB):
        sums = [None] * len(fields)
        for dh in reached(g):
            weight = weights[l, h, place]
            terms = [weight * field[dh] for field in fields]
            sums = [t if v is None else v + t for v, t in zip(sums, terms)]
            place += 1
        for c, value in enumerate(sums):
            acc[l, h, c, g * SUB : (g + 1) * SUB, :] = value


def wall_ends(weights, base1, wy_got, fx_got, middle):
    rows, cols = base1.shape[1], base1.shape[2]
    return pl.pallas_call(
        ends_kernel,
        in_specs=[whole()] * 7,
        out_specs=whole(),
        out_shape=vmem(rows, 3, cols, LANES),
        scratch_shapes=[vmem(3, rows + 2, SUB, LANES), vmem(rows, cols, 3, LANES, LANES)],
        compiler_params=params(),
        name="wall_ends",
    )(weights, base1, *fx_got, *wy_got, middle)


def last_kernel(weights, end_weights, part, got, base1, vel1, totals, disp_out, vel_out, load_pad, acc):
    rows, cols = base1.shape[1], base1.shape[2]
    first_sub = lax.broadcasted_iota(jnp.int32, (SUB, LANES), 0) < SUB // 2
    pieces = []
    for half in range(2):
        for k in range(3):
            total = got[half, k]
            for d in range(half + 2, got.shape[0], 2):
                total = total + got[d, k]
            pieces.append(total)
    one, two = unpack_slots(jnp.concatenate(pieces, axis=0), cols)
    for k in range(rows + 2):
        load_pad[0, k, 0 : cols + 2, :] = LOADING * one[k][0 : cols + 2]

    def one_tile(l, h):
        mid = mid_rows(load_pad, 0, l, h)
        ends = end_rows(load_pad, 0, l, h, first_sub)
        place = 0
        for g in range(LANES // SUB):
            total = None
            for dh in reached(g):
                term = weights[l, h, place] * mid[dh] + end_weights[l, h, place] * ends[dh]
                total = term if total is None else total + term
                place += 1
            acc[l, h, 0, g * SUB : (g + 1) * SUB, :] = total

    for l in range(rows):
        sums = []
        for h in range(cols):
            one_tile(l, h)
            sums.append(tile_sums(acc, l, h, 1))
        loads = by_quantity(sums)[0]
        for c in range(3):
            mine, pulled = base1[c, l], part[l, c]
            if c == 0:
                mine, pulled = mine + load_pad[0, l + 1, 1 : cols + 1, :], pulled + loads
            force = STIFFNESS * (pulled - totals[l] * mine)
            if c == 0:
                force = force + LOADING * (one[l + 1][1 : cols + 1] + two[l])
            fresh = vel1[c, l] + force
            vel_out[c, l] = fresh
            disp_out[c, l] = mine + fresh


def wall_last(weights, end_weights, part, got, base1, vel1, totals):
    rows, cols = base1.shape[1], base1.shape[2]
    return pl.pallas_call(
        last_kernel,
        in_specs=[whole()] * 7,
        out_specs=[whole()] * 2,
        out_shape=[jax.ShapeDtypeStruct(base1.shape, F32)] * 2,
        scratch_shapes=[vmem(1, rows + 2, SUB, LANES), vmem(rows, cols, 1, LANES, LANES)],
        compiler_params=params(),
        name="wall_last",
    )(weights, end_weights, part, got, base1, vel1, totals)


def per_device(
    displacement,
    velocity,
    jitter,
    bond_masks,
    pressure,
    pressure_prev,
    speed_sq,
    route_device,
    route_tile,
):
    fx_count, wy_count = lax.axis_size("fx"), lax.axis_size("wy")
    cols = displacement.shape[2]
    device = route_device.reshape(-1, LANES)
    tile = route_tile.reshape(-1, LANES)
    cx = pressure.shape[0]
    *sends, p, q, s, wall = pack_wy(
        pressure, pressure_prev, speed_sq, jitter, displacement, velocity
    )
    grids = (p, q, s)
    wy_got = exchange("wy", *sends)
    sends = pack_fx(grids, wall, wy_got)
    fx_got = exchange("fx", *sends)
    weights, part, end_masks, target, columns = wall_center(
        cx, wy_count, bond_masks, device, tile, wall, wy_got
    )
    fresh, keep, send = grid_steps(*grids, wy_got, fx_got, target, fx_count, wy_count)
    names = ("fx", "wy")
    other = lax.ppermute(send, names, swap_pairs(1, (fx_count, wy_count), 0))
    end_weights, vel1, base1, totals, *sends, pressure_out = wall_first(
        wall, wy_got, fx_got, part, end_masks, columns, fresh
    )
    slots = pair_sum(keep, other, totals)
    got = lax.all_to_all(slots, names, split_axis=0, concat_axis=0, tiled=True)
    base_wy = exchange("wy", *sends)
    sends = pack_base(base1, base_wy)
    base_fx = exchange("fx", *sends)
    middle = wall_middle(weights, base1, base_wy, sends[0])
    part = wall_ends(end_weights, base1, base_wy, base_fx, middle)
    disp_out, vel_out = wall_last(weights, end_weights, part, got, base1, vel1, totals)
    return (disp_out, vel_out, pressure_out)


def solution(mesh):
    placed = (
        P(None, "fx", "wy", None),
        P(None, "fx", "wy", None),
        P(None, "fx", "wy", None),
        P("fx", "wy", None, None, None),
        P("fx", "wy", None),
        P("fx", "wy", None),
        P("fx", "wy", None),
        P(("fx", "wy"), None),
        P(("fx", "wy")),
    )
    return jax.shard_map(
        per_device,
        mesh=mesh,
        in_specs=placed,
        out_specs=(P(None, "fx", "wy", None), P(None, "fx", "wy", None), P("fx", "wy", None)),
        check_vma=False,
    )
```
